32 devices in a mesh: req: 2 (over y), ctx: 4 (over x, core), tp: 4 (over z).
Axes of the slice: x: 2, y: 2, z: 4, core: 2. Of those that a mesh axis runs over, the one named last changes fastest.
Arguments:
- hidden_in: bfloat16 [4096, 6144], P(('req', 'ctx', 'tp')), parts along dimension 0, may hold values from -5 to 5
- queries: bfloat16 [4096, 4096], P(('req', 'ctx', 'tp')), parts along dimension 0, may hold values from -40 to 40
- keys: bfloat16 [4096, 1024], P(('req', 'ctx', 'tp')), parts along dimension 0, may hold values from -8 to 8
- values: bfloat16 [4096, 1024], P(('req', 'ctx', 'tp')), parts along dimension 0, may hold values from -6 to 6
- block_order: int32 [8], P('req'), parts along dimension 0, may hold values from 0 to 3, each once
- routes: int32 [4096, 2], P(('req', 'ctx')), parts along dimension 0, may hold values from 0 to 7, as said below
- out_weight: bfloat16 [4096, 6144], P('tp'), may hold values from -0.09375 to 0.09375
- norm_gain: float32 [6144], replicated, may hold values from 0.1 to 1.9
- router_weight: bfloat16 [6144, 8], replicated, may hold values from -0.078125 to 0.078125
- gate_weight: bfloat16 [6144, 8192], P(None, 'tp'), may hold values from -0.078125 to 0.078125
- up_weight: bfloat16 [6144, 8192], P(None, 'tp'), may hold values from -0.078125 to 0.078125
- down_weight: bfloat16 [8192, 6144], P('tp'), may hold values from -0.0625 to 0.0625
Outputs:
- attended: bfloat16 [4096, 6144], P(('req', 'ctx', 'tp')), parts along dimension 0
- expert_out: bfloat16 [4096, 6144], P(('req', 'ctx', 'tp')), parts along dimension 0
The draws below stay inside these ranges and needn't reach their ends.
There are 2 independent parts, one for each index of `req`. The reference program is written for one: setup_inputs(seed, part) draws one part's arguments, and reference() takes and returns one part's arrays. A program takes and returns all parts, laid end to end along the dimension named above; an argument that names none is the same for every part. Nothing has to cross between parts.
Inputs may be any that keep to these rules, and one draw needn't show every extreme that they name: `routes`: each row names two different experts. In each block of 512 rows at most 192 rows name expert 0, and exactly 192 in at least one block.
All inputs are finite; a program needn't handle non-finite values.
Results may differ from the reference program's by a relative error of at most 0.023.
Values may be sent and summed in bfloat16 or wider, within the bound.
No kernel may reach another device: no remote copies, remote signals or barrier semaphores. Data moves between devices by JAX's collectives and lax.ppermute only.
A program may use at most 256 MiB of HBM per device.

```python
import math
import jax
import jax.numpy as jnp
from jax import lax

D = 6144
HEADS = 32
KV_HEADS = 8
HD = 128
FF = 8192
EXPERTS = 8
BLOCK = 512
CAP = 192
TOKENS = 2048
N_CTX = 4
N_TP = 4


def draw_queries(key, part):
    key = jax.random.fold_in(key, 3)
    result = 3.0 * jnp.clip(jax.random.normal(key, (TOKENS, HEADS * HD), jnp.float32), -4.0, 4.0)
    return result.astype(jnp.bfloat16)


def draw_keys(key, part):
    key = jax.random.fold_in(key, 7)
    result = jnp.clip(jax.random.normal(key, (TOKENS, KV_HEADS * HD), jnp.float32), -5.0, 5.0)
    return result.astype(jnp.bfloat16)


def draw_hidden_in(key, part):
    key = jax.random.fold_in(key, 5)
    keys_all = jax.random.split(key, 3)
    result = jnp.clip(jax.random.normal(keys_all[2], (TOKENS, D), jnp.float32), -4.0, 4.0)
    return result.astype(jnp.bfloat16)


def draw_routes(key, part):
    key = jax.random.fold_in(key, 9)
    keys_all = jax.random.split(key, 6)
    blocks = TOKENS // BLOCK
    counts = jax.random.randint(keys_all[0], (blocks,), CAP // 2, CAP + 1)
    fullest = jax.random.randint(keys_all[1], (), 0, blocks)
    counts = jnp.where(jnp.arange(blocks) == fullest, CAP, counts)
    ranks = jax.vmap(lambda subkey: jax.random.permutation(subkey, BLOCK))(jax.random.split(keys_all[2], blocks))
    picked = (ranks < counts[:, None]).reshape(TOKENS)
    other = jax.random.randint(keys_all[3], (TOKENS,), 1, EXPERTS)
    second = 1 + (other - 1 + jax.random.randint(keys_all[4], (TOKENS,), 1, EXPERTS - 1)) % (EXPERTS - 1)
    first_slot = jnp.where(picked, 0, other)
    second_slot = jnp.where(picked, other, second)
    swapped = jax.random.randint(keys_all[5], (TOKENS,), 0, 2) == 1
    return jnp.stack([jnp.where(swapped, second_slot, first_slot), jnp.where(swapped, first_slot, second_slot)], axis=1).astype(jnp.int32)


def block_scale(rng, extent, pieces, low, largest):
    gain = 1.0
    for axis_at, parts in pieces:
        heights = jax.random.uniform(jax.random.fold_in(jax.random.fold_in(rng, 6), axis_at), (parts,), jnp.float32, low / len(pieces), largest / len(pieces))
        gain = gain * jnp.repeat(jnp.exp(heights), extent[axis_at] // parts).reshape((-1,) + (1,) * (len(extent) - 1 - axis_at))
    return gain


def centred(rng, dims, deviation, most, shards=(), kind=jnp.bfloat16):
    drawn = jax.random.normal(rng, dims, jnp.float32) * deviation
    if len(shards) > 0:
        drawn = block_scale(rng, dims, shards, -0.22, 0.18) * drawn
    return jnp.clip(drawn, min=-most, max=most).astype(kind)


def setup_inputs(seed: int = 0, part: int = 0) -> dict:
    streams_of = jax.random.split(jax.random.key(seed), 13)
    part_splits = jax.random.split(jax.random.fold_in(streams_of[12], part), 13)
    hidden_in = draw_hidden_in(jax.random.fold_in(jax.random.fold_in(streams_of[12], part), 71), part)
    queries = draw_queries(jax.random.fold_in(jax.random.fold_in(streams_of[12], part), 71), part)
    keys = draw_keys(jax.random.fold_in(jax.random.fold_in(streams_of[12], part), 71), part)
    values = centred(part_splits[3], (TOKENS, KV_HEADS * HD), 1.0, 6.0, ((0, 16),))
    block_order = jax.random.permutation(part_splits[4], N_CTX).astype(jnp.int32)
    routes = draw_routes(jax.random.fold_in(jax.random.fold_in(streams_of[12], part), 71), part)
    out_weight = centred(streams_of[6], (HEADS * HD, D), (HEADS * HD) ** -0.5, 0.09375, ((0, 4),))
    norm_gain = jnp.clip(1.0 + 0.18 * jax.random.normal(streams_of[7], (D,), jnp.float32), 0.1, 1.9)
    router_weight = centred(streams_of[8], (D, EXPERTS), D ** -0.5, 0.078125)
    gate_weight = centred(streams_of[9], (D, FF), D ** -0.5, 0.078125, ((1, 4),))
    up_weight = centred(streams_of[10], (D, FF), D ** -0.5, 0.078125, ((1, 4),))
    down_weight = centred(streams_of[11], (FF, D), FF ** -0.5, 0.0625, ((0, 4),))
    return dict(hidden_in=hidden_in, queries=queries, keys=keys, values=values, block_order=block_order, routes=routes, out_weight=out_weight, norm_gain=norm_gain, router_weight=router_weight, gate_weight=gate_weight, up_weight=up_weight, down_weight=down_weight)


def route_share(normed, routes, router_weight):
    logits = jnp.dot(normed, router_weight, preferred_element_type=jnp.float32)
    expert_ids = jnp.arange(router_weight.shape[1], dtype=jnp.int32)
    first = lax.optimization_barrier(jnp.sum(jnp.where(routes[:, 0:1] == expert_ids[None, :], logits, 0.0), axis=1))
    second = lax.optimization_barrier(jnp.sum(jnp.where(routes[:, 1:2] == expert_ids[None, :], logits, 0.0), axis=1))
    share = jnp.where(routes[:, 0] == 0, 1.0 / (1.0 + jnp.exp(second - first)), 0.0)
    return share + jnp.where(routes[:, 1] == 0, 1.0 / (1.0 + jnp.exp(first - second)), 0.0)

def add_term(total, pair):
    term = jnp.dot(pair[0], pair[1], preferred_element_type=jnp.float32).astype(jnp.bfloat16)
    term = lax.optimization_barrier(term)
    return (total + term.astype(jnp.float32), None)

def reference(hidden_in, queries, keys, values, block_order, routes, out_weight, norm_gain, router_weight, gate_weight, up_weight, down_weight):
    tokens = hidden_in.shape[0]
    row_ids = jnp.arange(tokens, dtype=jnp.int32)
    position = block_order[row_ids // BLOCK].astype(jnp.int32) * BLOCK + row_ids % BLOCK
    visible = position[None, :] <= position[:, None]
    grouping = HEADS // KV_HEADS
    factor = 1.0 / math.sqrt(HD)
    query_all = queries.reshape(tokens, HEADS, HD).transpose(1, 0, 2)
    key_all = keys.reshape(tokens, KV_HEADS, HD).transpose(1, 0, 2)
    value_all = values.reshape(tokens, KV_HEADS, HD).transpose(1, 0, 2)

    def one_head(index):
        query = query_all[index]
        key = key_all[index // grouping]
        value = value_all[index // grouping]
        scores = jnp.dot(query, key.T, preferred_element_type=jnp.float32) * factor
        scores = jnp.where(visible, scores, -1e+30)
        highest = lax.optimization_barrier(jnp.max(scores, axis=1, keepdims=True))
        weights = jnp.where(visible, jnp.exp(scores - highest), 0.0)
        norm = lax.optimization_barrier(jnp.sum(weights, axis=1, keepdims=True))
        mixed = jnp.dot(weights.astype(jnp.bfloat16), value, preferred_element_type=jnp.float32) / norm
        return mixed.astype(jnp.bfloat16)
    heads = lax.map(one_head, jnp.arange(HEADS, dtype=jnp.int32))
    heads_out = heads.transpose(1, 0, 2).reshape(tokens, HEADS * HD)
    per_device = HEADS // N_TP
    grouped_heads = heads_out.reshape(tokens, N_TP, per_device * HD).transpose(1, 0, 2)
    grouped_out = out_weight.reshape(N_TP, per_device * HD, D)
    head_sum, _ = lax.scan(add_term, jnp.zeros((tokens, D), jnp.float32), (grouped_heads, grouped_out))
    attended = (hidden_in.astype(jnp.float32) + head_sum).astype(jnp.bfloat16)
    widened = attended.astype(jnp.float32)
    normed = (widened * lax.rsqrt(lax.optimization_barrier(jnp.mean(widened * widened, axis=1, keepdims=True)) + 1e-05) * norm_gain).astype(jnp.bfloat16)
    share = route_share(normed, routes, router_weight)
    picked = (routes[:, 0] == 0) | (routes[:, 1] == 0)
    slots_all = N_CTX * CAP
    chosen = jnp.nonzero(picked, size=slots_all, fill_value=0)[0].astype(jnp.int32)
    filled = jnp.arange(slots_all, dtype=jnp.int32) < jnp.sum(picked.astype(jnp.int32))
    chosen_rows = normed[chosen]
    chosen_share = jnp.where(filled, share[chosen], 0.0)
    gate = jnp.dot(chosen_rows, gate_weight, preferred_element_type=jnp.float32)
    upward = jnp.dot(chosen_rows, up_weight, preferred_element_type=jnp.float32)
    act = (jax.nn.silu(gate) * upward * chosen_share[:, None]).astype(jnp.bfloat16)
    hidden_part = FF // N_TP
    grouped_act = act.reshape(slots_all, N_TP, hidden_part).transpose(1, 0, 2)
    grouped_down = down_weight.reshape(N_TP, hidden_part, D)
    expert_rows, _ = lax.scan(add_term, jnp.zeros((slots_all, D), jnp.float32), (grouped_act, grouped_down))
    placed = jnp.zeros((tokens, D), jnp.float32).at[chosen].add(jnp.where(filled[:, None], expert_rows, 0.0))
    return (attended, placed.astype(jnp.bfloat16))
```

```python
import functools
import math

import jax
import jax.numpy as jnp
from jax import lax
from jax.experimental import pallas as pl
from jax.experimental.pallas import tpu as pltpu
from jax.sharding import PartitionSpec as P

HEADS = 32
KV_HEADS = 8
HD = 128
FACTOR = math.log2(math.e) / math.sqrt(HD)


def attention_kernel(pairs, sharing, block_rows, info, q_ref, place_ref, kv_ref, out_ref):
    half = q_ref.shape[1]
    tall = sharing * half
    my_block = info[0]
    place = jnp.concatenate([place_ref[0]] * sharing, axis=0)
    ones = jnp.ones((block_rows, HD), jnp.bfloat16)
    queries = []
    for p in range(pairs):
        heads = [q_ref[0, :, (p * sharing + g) * HD : (p * sharing + g + 1) * HD] for g in range(sharing)]
        queries.append(jnp.concatenate(heads, axis=0))

    def scores_of(p, start):
        key = kv_ref[pl.ds(start, block_rows), p * HD : (p + 1) * HD]
        return lax.dot_general(queries[p], key, (((1,), (1,)), ((), ())), preferred_element_type=jnp.float32)

    def mixed_of(p, start, weights):
        value = kv_ref[pl.ds(start, block_rows), (pairs + p) * HD : (pairs + p + 1) * HD]
        return jnp.dot(weights, jnp.concatenate([value, ones], axis=1), preferred_element_type=jnp.float32)

    def start_of(place_in_prompt):
        return pl.multiple_of(info[1 + place_in_prompt] * block_rows, block_rows)

    own = start_of(my_block)
    key_place = lax.broadcasted_iota(jnp.int32, (tall, block_rows), 1)
    state = []
    for p in range(pairs):
        scores = jnp.where(key_place <= place, scores_of(p, own), -1e30)
        top = jnp.max(scores, axis=1, keepdims=True)
        weights = jnp.exp2((scores - top) * FACTOR).astype(jnp.bfloat16)
        state.append((top, mixed_of(p, own, weights)))

    def earlier(step, state):
        start = start_of(step)
        new = []
        for p in range(pairs):
            top, total = state[p]
            scores = scores_of(p, start)
            raised = jnp.maximum(top, jnp.max(scores, axis=1, keepdims=True))
            weights = jnp.exp2((scores - raised) * FACTOR).astype(jnp.bfloat16)
            total = total * jnp.exp2((top - raised) * FACTOR) + mixed_of(p, start, weights)
            new.append((raised, total))
        return new

    state = lax.fori_loop(0, my_block, earlier, state)
    for p in range(pairs):
        total = state[p][1]
        mixed = (total[:, :HD] / total[:, HD:]).astype(jnp.bfloat16)
        for g in range(sharing):
            at = (p * sharing + g) * HD
            out_ref[0, :, at : at + HD] = mixed[g * half : (g + 1) * half]


def attend(info, queries, places, pairs_all, which, half, pairs, sharing, block_rows):
    shards, _, width = queries.shape
    count = pairs_all.shape[0]
    flops = 4 * shards * half * width * count
    return pl.pallas_call(
        functools.partial(attention_kernel, pairs, sharing, block_rows),
        grid_spec=pltpu.PrefetchScalarGridSpec(
            num_scalar_prefetch=1,
            grid=(shards,),
            in_specs=[
                pl.BlockSpec((1, half, width), lambda s, info: (s, which, 0)),
                pl.BlockSpec((1, half, 1), lambda s, info: (s, which, 0)),
                pl.BlockSpec(pairs_all.shape, lambda s, info: (0, 0)),
            ],
            out_specs=pl.BlockSpec((1, half, width), lambda s, info: (s, 0, 0)),
        ),
        out_shape=jax.ShapeDtypeStruct((shards, half, width), jnp.bfloat16),
        compiler_params=pltpu.CompilerParams(vmem_limit_bytes=24 * 1024 * 1024),
        cost_estimate=pl.CostEstimate(
            flops=flops,
            bytes_accessed=2 * (2 * shards * half * width + pairs_all.size),
            transcendentals=shards * half * width // HD * count,
        ),
    )(info, queries, places, pairs_all)


def on_device(
    hidden_in,
    queries,
    keys,
    values,
    block_order,
    routes,
    out_weight,
    norm_gain,
    router_weight,
    gate_weight,
    up_weight,
    down_weight,
):
    shards = lax.axis_size("tp")
    rows = hidden_in.shape[0]
    block_rows = rows * shards
    per_device = HEADS // shards
    grouping = HEADS // KV_HEADS
    repeat_by = max(1, grouping // per_device)
    pairs = max(1, per_device // grouping)
    sharing = per_device // pairs
    half = rows // 2 if rows % 32 == 0 else rows
    halves = rows // half

    def spread(source):
        widened = jnp.repeat(source.reshape(rows, KV_HEADS, HD), repeat_by, axis=1)
        return widened.reshape(rows, shards, pairs, HD)

    sent_pairs = jnp.stack([spread(keys), spread(values)], axis=2).reshape(rows, shards, 2 * pairs * HD)
    got_pairs = lax.all_to_all(sent_pairs, "tp", split_axis=1, concat_axis=0, tiled=True)
    pairs_all = lax.all_gather(got_pairs.reshape(block_rows, 2 * pairs * HD), "ctx", axis=0, tiled=True)

    picked = ((routes[:, 0] == 0) | (routes[:, 1] == 0)).reshape(shards, rows)
    row_ids = jnp.arange(rows, dtype=jnp.int32)
    up_to = (row_ids[:, None] <= row_ids[None, :]).astype(jnp.bfloat16)
    seen = jnp.dot(picked.astype(jnp.bfloat16), up_to, preferred_element_type=jnp.float32).astype(jnp.int32)
    count = seen[:, -1:]
    slot = jnp.where(picked, seen - 1, count + row_ids[None, :] - seen)
    fullest = lax.pmax(jnp.max(count), ("req", "ctx"))
    at_slot = slot[:, None, :] == row_ids[None, :, None]
    row_of_slot = jnp.sum(jnp.where(at_slot, row_ids[None, None, :], 0), axis=2)
    places = (row_of_slot + jnp.arange(shards, dtype=jnp.int32)[:, None] * rows)[:, :, None]
    me = lax.axis_index("tp")
    my_slot = lax.dynamic_index_in_dim(slot, me, 0, keepdims=False)
    order = (my_slot[None, :] == row_ids[:, None]).astype(jnp.bfloat16)

    def reorder(source):
        return jnp.dot(order, source, preferred_element_type=jnp.float32).astype(jnp.bfloat16)

    def restore(parts):
        whole = jnp.concatenate(parts, axis=0) if len(parts) > 1 else parts[0]
        return lax.dot_general(
            order, whole, (((0,), (0,)), ((), ())), preferred_element_type=jnp.float32
        ).astype(jnp.bfloat16)

    sent_query = reorder(queries).reshape(rows, shards, per_device * HD)
    got_query = lax.all_to_all(sent_query, "tp", split_axis=1, concat_axis=0, tiled=True)
    got_query = got_query.reshape(shards, rows, per_device * HD)

    ctx_ids = jnp.arange(block_order.shape[0], dtype=jnp.int32)
    my_block = jnp.sum(jnp.where(ctx_ids == lax.axis_index("ctx"), block_order, 0))
    holder = jnp.sum(jnp.where(block_order[None, :] == ctx_ids[:, None], ctx_ids[None, :], 0), axis=1)
    info = jnp.concatenate([my_block[None], holder])

    hidden = reorder(hidden_in).astype(jnp.float32)
    my_routes = lax.dynamic_slice_in_dim(routes, me * rows, rows, 0)
    my_routes = jnp.sum(
        jnp.where((my_slot[None, :] == row_ids[:, None])[:, :, None], my_routes[None, :, :], 0), axis=1
    )
    expert_ids = jnp.arange(router_weight.shape[1], dtype=jnp.int32)

    def project(which):
        heads = attend(info, got_query, places, pairs_all, which, half, pairs, sharing, block_rows)
        heads = heads.reshape(shards * half, per_device * HD)
        return jnp.dot(heads, out_weight, preferred_element_type=jnp.float32).astype(jnp.bfloat16)

    def gather_sum(term):
        return lax.psum_scatter(term, "tp", scatter_dimension=0, tiled=True)

    def finish(which, head_sum):
        return (hidden[which * half : (which + 1) * half] + head_sum.astype(jnp.float32)).astype(jnp.bfloat16)

    def expert(which, attended):
        widened = attended.astype(jnp.float32)
        normed = (
            widened * lax.rsqrt(jnp.mean(widened * widened, axis=1, keepdims=True) + 1e-05) * norm_gain
        ).astype(jnp.bfloat16)
        chosen = lax.all_gather(normed, "tp", axis=0, tiled=True)
        logits = jnp.dot(normed, router_weight, preferred_element_type=jnp.float32)
        slots = my_routes[which * half : (which + 1) * half]
        first = jnp.sum(jnp.where(slots[:, 0:1] == expert_ids[None, :], logits, 0.0), axis=1)
        second = jnp.sum(jnp.where(slots[:, 1:2] == expert_ids[None, :], logits, 0.0), axis=1)
        share = jnp.where(slots[:, 0] == 0, 1.0 / (1.0 + jnp.exp(second - first)), 0.0)
        share = share + jnp.where(slots[:, 1] == 0, 1.0 / (1.0 + jnp.exp(first - second)), 0.0)
        gate = jnp.dot(chosen, gate_weight, preferred_element_type=jnp.float32)
        upward = jnp.dot(chosen, up_weight, preferred_element_type=jnp.float32)
        acts = (jax.nn.silu(gate) * upward).astype(jnp.bfloat16)
        total = gather_sum(jnp.dot(acts, down_weight, preferred_element_type=jnp.float32).astype(jnp.bfloat16))
        return (total.astype(jnp.float32) * share[:, None]).astype(jnp.bfloat16)

    attended = [finish(0, gather_sum(project(0)))]
    experts = [expert(0, attended[0])]
    if halves > 1:
        attended.append(finish(1, gather_sum(project(1))))
        experts.append(
            lax.cond(
                fullest > half,
                lambda source: expert(1, source),
                jnp.zeros_like,
                attended[1],
            )
        )
    return (restore(attended), restore(experts))


def solution(mesh):
    return jax.shard_map(
        on_device,
        mesh=mesh,
        in_specs=(
            P(("req", "ctx", "tp"), None),
            P(("req", "ctx", "tp"), None),
            P(("req", "ctx", "tp"), None),
            P(("req", "ctx", "tp"), None),
            P("req"),
            P(("req", "ctx"), None),
            P("tp", None),
            P(),
            P(),
            P(None, "tp"),
            P(None, "tp"),
            P("tp", None),
        ),
        out_specs=(P(("req", "ctx", "tp"), None), P(("req", "ctx", "tp"), None)),
        check_vma=False,
    )
```

```python
import functools
import math

import jax
import jax.numpy as jnp
from jax import lax
from jax.experimental import pallas as pl
from jax.experimental.pallas import tpu as pltpu
from jax.sharding import PartitionSpec as P

HEADS = 32
KV_HEADS = 8
HD = 128
FACTOR = math.log2(math.e) / math.sqrt(HD)
LINE = 4


def attention_kernel(slots, held, pairs, sharing, block_rows, *refs):
    (order, mine), refs = refs[:2], refs[2:]
    query_refs, refs = refs[:slots], refs[slots:]
    place_ref, key_place_ref, refs = refs[0], refs[1], refs[2:]
    pair_refs, refs = refs[: len(held)], refs[len(held) :]
    out_ref, query_ref, top_ref, total_ref = refs
    half = out_ref.shape[1]
    tall = sharing * half
    me = mine[0]
    my_block = order[me]
    ones = jnp.ones((block_rows, HD), jnp.bfloat16)

    for at in range(slots):

        @pl.when(pl.program_id(0) == at)
        def _():
            for p in range(pairs):
                for g in range(sharing):
                    column = (p * sharing + g) * HD
                    query_ref[p, g * half : (g + 1) * half, :] = query_refs[at][:, column : column + HD]

    def scores_of(p, ref, start):
        key = ref[start : start + block_rows, p * HD : (p + 1) * HD]
        return lax.dot_general(
            query_ref[p], key, (((1,), (1,)), ((), ())), preferred_element_type=jnp.float32
        )

    def mixed_of(p, ref, start, weights):
        value = ref[start : start + block_rows, (pairs + p) * HD : (pairs + p + 1) * HD]
        return jnp.dot(weights, jnp.concatenate([value, ones], axis=1), preferred_element_type=jnp.float32)

    place = jnp.concatenate([place_ref[0]] * sharing, axis=0)
    visible = key_place_ref[...] <= place
    for p in range(pairs):
        scores = jnp.where(visible, scores_of(p, pair_refs[0], 0), -1e30)
        top = jnp.max(scores, axis=1, keepdims=True)
        weights = jnp.exp2((scores - top) * FACTOR).astype(jnp.bfloat16)
        top_ref[p] = jnp.broadcast_to(top, (tall, HD))
        total_ref[p] = mixed_of(p, pair_refs[0], 0, weights)

    for ref, offsets in list(zip(pair_refs, held))[1:]:
        for index, offset in enumerate(offsets):

            @pl.when(order[me ^ offset] < my_block)
            def _():
                for p in range(pairs):
                    top = top_ref[p][:, :1]
                    scores = scores_of(p, ref, index * block_rows)
                    raised = jnp.maximum(top, jnp.max(scores, axis=1, keepdims=True))
                    weights = jnp.exp2((scores - raised) * FACTOR).astype(jnp.bfloat16)
                    top_ref[p] = jnp.broadcast_to(raised, (tall, HD))
                    total_ref[p] = total_ref[p] * jnp.exp2((top - raised) * FACTOR) + mixed_of(
                        p, ref, index * block_rows, weights
                    )

    for p in range(pairs):
        total = total_ref[p]
        mixed = (total[:, :HD] / total[:, HD:]).astype(jnp.bfloat16)
        for g in range(sharing):
            column = (p * sharing + g) * HD
            out_ref[0, :, column : column + HD] = mixed[g * half : (g + 1) * half]


def attend(order, mine, queries, places, key_places, pair_list, held, which, half, pairs, sharing, block_rows):
    slots = len(queries)
    width = queries[0].shape[1]
    tall = sharing * half
    count = sum(pair.shape[0] for pair in pair_list)
    kernel = functools.partial(attention_kernel, slots, held, pairs, sharing, block_rows)
    whole = [pl.BlockSpec(pair.shape, lambda s, *_: (0, 0)) for pair in pair_list]
    return pl.pallas_call(
        kernel,
        grid_spec=pltpu.PrefetchScalarGridSpec(
            num_scalar_prefetch=2,
            grid=(slots,),
            in_specs=[pl.BlockSpec((half, width), lambda s, *_: (which, 0))] * slots
            + [
                pl.BlockSpec((1, half, 1), lambda s, *_: (s, which, 0)),
                pl.BlockSpec((1, block_rows), lambda s, *_: (0, 0)),
            ]
            + whole,
            out_specs=pl.BlockSpec((1, half, width), lambda s, *_: (s, 0, 0)),
            scratch_shapes=[
                pltpu.VMEM((pairs, tall, HD), jnp.bfloat16),
                pltpu.VMEM((pairs, tall, HD), jnp.float32),
                pltpu.VMEM((pairs, tall, 2 * HD), jnp.float32),
            ],
        ),
        out_shape=jax.ShapeDtypeStruct((slots, half, width), jnp.bfloat16),
        compiler_params=pltpu.CompilerParams(vmem_limit_bytes=24 * 1024 * 1024),
        cost_estimate=pl.CostEstimate(
            flops=4 * slots * half * width * count,
            bytes_accessed=2 * (2 * slots * half * width + count * 2 * pairs * HD),
            transcendentals=slots * half * width // HD * count,
        ),
    )(order, mine, *queries, places, key_places, *pair_list)


def on_device(
    hidden_in,
    queries,
    keys,
    values,
    block_order,
    routes,
    out_weight,
    norm_gain,
    router_weight,
    gate_weight,
    up_weight,
    down_weight,
):
    shards = lax.axis_size("tp")
    blocks = lax.axis_size("ctx")
    me = lax.axis_index("tp")
    rows, model = hidden_in.shape
    block_rows = rows * shards
    per_device = HEADS // shards
    grouping = HEADS // KV_HEADS
    repeat_by = max(1, grouping // per_device)
    pairs = max(1, per_device // grouping)
    sharing = per_device // pairs
    half = rows // 2 if rows % 32 == 0 else rows
    halves = rows // half
    line = shards <= LINE
    pieces = 2 if line else 1
    cuts = [slice(c * (model // pieces), (c + 1) * (model // pieces)) for c in range(pieces)]
    shard_of = lax.rem(me - jnp.arange(shards, dtype=jnp.int32) + shards, shards)

    def exchange(source):
        if not line:
            got = lax.all_to_all(source, "tp", split_axis=1, concat_axis=0, tiled=True)
            got = got.reshape(shards, rows, source.shape[2])
            return [lax.dynamic_index_in_dim(got, shard_of[s], 0, keepdims=False) for s in range(shards)]
        got = []
        for s in range(shards):
            part = lax.dynamic_index_in_dim(source, lax.rem(me + s, shards), 1, keepdims=False)
            if s > 0:
                part = lax.ppermute(part, "tp", [(i, (i + s) % shards) for i in range(shards)])
            got.append(part)
        return got

    def reduce_line(terms, after=None):
        if not line:
            by_shard = jnp.take(jnp.stack(terms), shard_of, axis=0).reshape(-1, terms[0].shape[1])
            return lax.psum_scatter(by_shard, "tp", scatter_dimension=0, tiled=True).astype(jnp.float32)
        right = left = None
        for s in range(1, shards):
            to_right, to_left = terms[s], terms[shards - s]
            if right is not None:
                to_right = to_right + right
                to_left = to_left + left
            if after is not None:
                to_right, to_left, _ = lax.optimization_barrier((to_right, to_left, after[s - 1]))
            right = lax.ppermute(to_right, "tp", [(i, i + 1) for i in range(s)])
            left = lax.ppermute(to_left, "tp", [(i, i - 1) for i in range(shards - s, shards)])
        return terms[0].astype(jnp.float32) + right.astype(jnp.float32) + left.astype(jnp.float32)

    def gather_line(source):
        if not line:
            got = lax.all_gather(source, "tp", axis=0)
            return jnp.take(got, shard_of, axis=0), None
        right = left = source
        rights, lefts = [source], [source]
        for s in range(1, shards):
            right = lax.ppermute(right, "tp", [(i, i + 1) for i in range(s - 1, shards - 1)])
            left = lax.ppermute(left, "tp", [(i, i - 1) for i in range(1, shards - s + 1)])
            rights.append(right)
            lefts.append(left)
        got = [source] + [jnp.where(me >= s, rights[s], lefts[shards - s]) for s in range(1, shards)]
        return jnp.stack(got), list(zip(rights[1:], lefts[1:]))

    def spread(source):
        widened = jnp.repeat(source.reshape(rows, KV_HEADS, HD), repeat_by, axis=1)
        return widened.reshape(rows, shards, pairs * HD)

    own_pairs = jnp.concatenate(exchange(jnp.concatenate([spread(keys), spread(values)], axis=2)), axis=0)
    key_places = (shard_of[:, None] * rows + jnp.arange(rows, dtype=jnp.int32)[None, :]).reshape(1, block_rows)
    pair_list, held = [own_pairs], [[0]]
    offset = blocks // 2
    while offset >= 1:
        sent = pair_list[0] if len(pair_list) == 1 else jnp.concatenate(pair_list, axis=0)
        pair_list.append(lax.ppermute(sent, "ctx", [(i, i ^ offset) for i in range(blocks)]))
        held.append([other ^ offset for group in held for other in group])
        offset //= 2

    picked = ((routes[:, 0] == 0) | (routes[:, 1] == 0)).reshape(shards, rows)
    row_ids = jnp.arange(rows, dtype=jnp.int32)
    up_to = (row_ids[:, None] <= row_ids[None, :]).astype(jnp.bfloat16)
    seen = jnp.dot(picked.astype(jnp.bfloat16), up_to, preferred_element_type=jnp.float32).astype(jnp.int32)
    count = seen[:, -1:]
    slot = jnp.where(picked, seen - 1, count + row_ids[None, :] - seen)
    at_slot = slot[:, None, :] == row_ids[None, :, None]
    row_of_slot = jnp.sum(jnp.where(at_slot, row_ids[None, None, :], 0), axis=2)
    places = (row_of_slot + jnp.arange(shards, dtype=jnp.int32)[:, None] * rows)[:, :, None]
    places = jnp.take(places, shard_of, axis=0)
    my_slot = lax.dynamic_index_in_dim(slot, me, 0, keepdims=False)
    order = (my_slot[None, :] == row_ids[:, None]).astype(jnp.bfloat16)

    fullest = jnp.full((8, 128), jnp.max(count), jnp.float32)
    for axis in ("req", "ctx"):
        size = lax.axis_size(axis)
        step = 1
        while step < size:
            other = lax.ppermute(fullest, axis, [(i, i ^ step) for i in range(size)])
            fullest = jnp.maximum(fullest, other)
            step *= 2
    crowded = fullest[0, 0] > half

    def reorder(source):
        return jnp.dot(order, source, preferred_element_type=jnp.float32).astype(jnp.bfloat16)

    def restore(parts):
        whole = jnp.concatenate(parts, axis=0) if len(parts) > 1 else parts[0]
        return lax.dot_general(
            order, whole, (((0,), (0,)), ((), ())), preferred_element_type=jnp.float32
        ).astype(jnp.bfloat16)

    got_query = exchange(reorder(queries).reshape(rows, shards, per_device * HD))
    mine = lax.axis_index("ctx").astype(jnp.int32)[None]
    hidden = reorder(hidden_in).astype(jnp.float32)
    my_routes = lax.dynamic_slice_in_dim(routes, me * rows, rows, 0)
    my_routes = jnp.sum(
        jnp.where((my_slot[None, :] == row_ids[:, None])[:, :, None], my_routes[None, :, :], 0), axis=1
    )
    expert_ids = jnp.arange(router_weight.shape[1], dtype=jnp.int32)

    def project(which, groups):
        terms = [[None] * shards for _ in cuts]
        for group in groups:
            heads = attend(
                block_order,
                mine,
                [got_query[s] for s in group],
                jnp.stack([places[s] for s in group]),
                key_places,
                pair_list,
                held,
                which,
                half,
                pairs,
                sharing,
                block_rows,
            ).reshape(len(group) * half, per_device * HD)
            for c, cut in enumerate(cuts):
                term = jnp.dot(heads, out_weight[:, cut], preferred_element_type=jnp.float32)
                term = term.astype(jnp.bfloat16)
                for at, s in enumerate(group):
                    terms[c][s] = term[at * half : (at + 1) * half]
        return terms

    def finish(which, head_sums):
        base = hidden[which * half : (which + 1) * half]
        return jnp.concatenate(
            [(base[:, cut] + head_sum).astype(jnp.bfloat16) for cut, head_sum in zip(cuts, head_sums)], axis=1
        )

    def expert(which, attended):
        widened = attended.astype(jnp.float32)
        normed = (
            widened * lax.rsqrt(jnp.mean(widened * widened, axis=1, keepdims=True) + 1e-05) * norm_gain
        ).astype(jnp.bfloat16)
        gate = upward = 0.0
        marks = []
        for cut in cuts:
            chosen, mark = gather_line(normed[:, cut])
            chosen = chosen.reshape(shards * half, -1)
            marks.append(mark)
            gate = gate + jnp.dot(chosen, gate_weight[cut], preferred_element_type=jnp.float32)
            upward = upward + jnp.dot(chosen, up_weight[cut], preferred_element_type=jnp.float32)
        logits = jnp.dot(normed, router_weight, preferred_element_type=jnp.float32)
        named = my_routes[which * half : (which + 1) * half]
        first = jnp.sum(jnp.where(named[:, 0:1] == expert_ids[None, :], logits, 0.0), axis=1)
        second = jnp.sum(jnp.where(named[:, 1:2] == expert_ids[None, :], logits, 0.0), axis=1)
        share = jnp.where(named[:, 0] == 0, 1.0 / (1.0 + jnp.exp(second - first)), 0.0)
        share = share + jnp.where(named[:, 1] == 0, 1.0 / (1.0 + jnp.exp(first - second)), 0.0)
        acts = (jax.nn.silu(gate) * upward).astype(jnp.bfloat16)
        parts = []
        for cut in cuts:
            term = jnp.dot(acts, down_weight[:, cut], preferred_element_type=jnp.float32)
            term = term.astype(jnp.bfloat16).reshape(shards, half, -1)
            total = reduce_line([term[s] for s in range(shards)])
            parts.append((total * share[:, None]).astype(jnp.bfloat16))
        return jnp.concatenate(parts, axis=1), marks

    groups = [[1, 3], [2, 0]] if shards == 4 else [list(range(shards))]
    attended = [finish(0, [reduce_line(terms) for terms in project(0, groups)])]
    part, marks = expert(0, attended[0])
    experts = [part]
    if halves > 1:
        sums = [reduce_line(terms, mark) for terms, mark in zip(project(1, groups), marks)]
        attended.append(finish(1, sums))
        experts.append(lax.cond(crowded, lambda source: expert(1, source)[0], jnp.zeros_like, attended[1]))
    return (restore(attended), restore(experts))


def solution(mesh):
    return jax.shard_map(
        on_device,
        mesh=mesh,
        in_specs=(
            P(("req", "ctx", "tp"), None),
            P(("req", "ctx", "tp"), None),
            P(("req", "ctx", "tp"), None),
            P(("req", "ctx", "tp"), None),
            P("req"),
            P(("req", "ctx"), None),
            P("tp", None),
            P(),
            P(),
            P(None, "tp"),
            P(None, "tp"),
            P("tp", None),
        ),
        out_specs=(P(("req", "ctx", "tp"), None), P(("req", "ctx", "tp"), None)),
        check_vma=False,
    )
```

```python
import functools
import math

import jax
import jax.numpy as jnp
from jax import lax
from jax.experimental import pallas as pl
from jax.experimental.pallas import tpu as pltpu
from jax.sharding import PartitionSpec as P

HEADS = 32
KV_HEADS = 8
HD = 128
FACTOR = math.log2(math.e) / math.sqrt(HD)
LINE = 4
SUM_ROWS = 16


def attention_kernel(slots, held, pairs, sharing, block_rows, *refs):
    (order, mine), refs = refs[:2], refs[2:]
    query_refs, refs = refs[:slots], refs[slots:]
    place_ref, key_place_ref, refs = refs[0], refs[1], refs[2:]
    pair_refs, refs = refs[: len(held)], refs[len(held) :]
    out_ref, query_ref, value_ref, top_ref, total_ref = refs
    half = out_ref.shape[1]
    me = mine[0]
    my_block = order[me]
    blocks = [(ref, index, offset) for ref, group in zip(pair_refs, held) for index, offset in enumerate(group)]

    @pl.when(pl.program_id(0) == 0)
    def _():
        value_ref[:, :, HD:, :] = jnp.ones((len(blocks), pairs, SUM_ROWS, block_rows), jnp.bfloat16)

    for at, (ref, index, offset) in enumerate(blocks):

        @pl.when((pl.program_id(0) == 0) & (order[me ^ offset] <= my_block))
        def _():
            for p in range(pairs):
                columns = slice((pairs + p) * HD, (pairs + p + 1) * HD)
                value_ref[at, p, :HD, :] = ref[index * block_rows : (index + 1) * block_rows, columns].T

    for at in range(slots):

        @pl.when(pl.program_id(0) == at)
        def _():
            for p in range(pairs):
                for g in range(sharing):
                    column = (p * sharing + g) * HD
                    query_ref[p, g * half : (g + 1) * half, :] = query_refs[at][:, column : column + HD]

    def scores_of(p, at):
        ref, index, _ = blocks[at]
        key = ref[index * block_rows : (index + 1) * block_rows, p * HD : (p + 1) * HD]
        return lax.dot_general(
            key, query_ref[p], (((1,), (1,)), ((), ())), preferred_element_type=jnp.float32
        )

    def mixed_of(p, at, weights):
        return jnp.dot(value_ref[at, p], weights, preferred_element_type=jnp.float32)

    place = jnp.concatenate([place_ref[0]] * sharing, axis=1)
    visible = key_place_ref[...] <= place
    for p in range(pairs):
        scores = jnp.where(visible, scores_of(p, 0), -1e30)
        top = jnp.max(scores, axis=0, keepdims=True)
        weights = jnp.exp2((scores - top) * FACTOR).astype(jnp.bfloat16)
        top_ref[p, 0:1, :] = top
        total_ref[p] = mixed_of(p, 0, weights)

    for at in range(1, len(blocks)):

        @pl.when(order[me ^ blocks[at][2]] < my_block)
        def _():
            for p in range(pairs):
                top = top_ref[p, 0:1, :]
                scores = scores_of(p, at)
                raised = jnp.maximum(top, jnp.max(scores, axis=0, keepdims=True))
                weights = jnp.exp2((scores - raised) * FACTOR).astype(jnp.bfloat16)
                top_ref[p, 0:1, :] = raised
                total_ref[p] = total_ref[p] * jnp.exp2((top - raised) * FACTOR) + mixed_of(p, at, weights)

    for p in range(pairs):
        mixed = (total_ref[p, :HD, :] / total_ref[p, HD : HD + 1, :]).T.astype(jnp.bfloat16)
        for g in range(sharing):
            column = (p * sharing + g) * HD
            out_ref[0, :, column : column + HD] = mixed[g * half : (g + 1) * half]


def attend(order, mine, queries, places, key_places, pair_list, held, which, half, pairs, sharing, block_rows):
    slots = len(queries)
    width = queries[0].shape[1]
    tall = sharing * half
    blocks = sum(len(group) for group in held)
    count = blocks * block_rows
    kernel = functools.partial(attention_kernel, slots, held, pairs, sharing, block_rows)
    whole = [pl.BlockSpec(pair.shape, lambda s, *_: (0, 0)) for pair in pair_list]
    return pl.pallas_call(
        kernel,
        grid_spec=pltpu.PrefetchScalarGridSpec(
            num_scalar_prefetch=2,
            grid=(slots,),
            in_specs=[pl.BlockSpec((half, width), lambda s, *_: (which, 0))] * slots
            + [
                pl.BlockSpec((1, 1, half), lambda s, *_: (s, 0, 0)),
                pl.BlockSpec((block_rows, 1), lambda s, *_: (0, 0)),
            ]
            + whole,
            out_specs=pl.BlockSpec((1, half, width), lambda s, *_: (s, 0, 0)),
            scratch_shapes=[
                pltpu.VMEM((pairs, tall, HD), jnp.bfloat16),
                pltpu.VMEM((blocks, pairs, HD + SUM_ROWS, block_rows), jnp.bfloat16),
                pltpu.VMEM((pairs, 8, tall), jnp.float32),
                pltpu.VMEM((pairs, HD + SUM_ROWS, tall), jnp.float32),
            ],
        ),
        out_shape=jax.ShapeDtypeStruct((slots, half, width), jnp.bfloat16),
        compiler_params=pltpu.CompilerParams(vmem_limit_bytes=24 * 1024 * 1024),
        cost_estimate=pl.CostEstimate(
            flops=4 * slots * half * width * count,
            bytes_accessed=2 * (2 * slots * half * width + count * 2 * pairs * HD),
            transcendentals=slots * half * width // HD * count,
        ),
    )(order, mine, *queries, places, key_places, *pair_list)


def hidden_kernel(plan, started, last, *refs):
    mine, refs = refs[0], refs[1:]
    sources, refs = refs[: plan], refs[plan:]
    gate_weight, up_weight, refs = refs[0], refs[1], refs[2:]
    if started:
        gate_before, up_before, refs = refs[0], refs[1], refs[2:]
    outs, chosen = refs[:-1], refs[-1]

    @pl.when(pl.program_id(0) == 0)
    def _():
        if plan == 1:
            chosen[...] = sources[0][...]
        else:
            shards = (plan + 1) // 2
            rows = sources[0].shape[0]
            chosen[:rows] = sources[0][...]
            for s in range(1, shards):
                right, left = sources[s], sources[plan - s]

                @pl.when(mine[0] >= s)
                def _():
                    chosen[s * rows : (s + 1) * rows] = right[...]

                @pl.when(mine[0] < s)
                def _():
                    chosen[s * rows : (s + 1) * rows] = left[...]

    gate = jnp.dot(chosen[...], gate_weight[...], preferred_element_type=jnp.float32)
    upward = jnp.dot(chosen[...], up_weight[...], preferred_element_type=jnp.float32)
    if started:
        gate = gate + gate_before[...]
        upward = upward + up_before[...]
    if last:
        outs[0][...] = (gate / (1.0 + jnp.exp(-gate)) * upward).astype(jnp.bfloat16)
    else:
        outs[0][...] = gate
        outs[1][...] = upward


def hidden_units(mine, sources, gate_weight, up_weight, cut, before, last):
    shards = (len(sources) + 1) // 2
    rows = sources[0].shape[0] * shards
    depth = sources[0].shape[1]
    width = gate_weight.shape[1]
    tile = min(256, width)
    weight = pl.BlockSpec((depth, tile), lambda n, *_: (cut, n))
    out = pl.BlockSpec((rows, tile), lambda n, *_: (0, n))
    kinds = [jnp.bfloat16] if last else [jnp.float32] * 2
    return pl.pallas_call(
        functools.partial(hidden_kernel, len(sources), len(before) > 0, last),
        grid_spec=pltpu.PrefetchScalarGridSpec(
            num_scalar_prefetch=1,
            grid=(width // tile,),
            in_specs=[pl.BlockSpec(source.shape, lambda n, *_: (0, 0)) for source in sources]
            + [weight, weight]
            + [out] * len(before),
            out_specs=[out] * len(kinds),
            scratch_shapes=[pltpu.VMEM((rows, depth), jnp.bfloat16)],
        ),
        out_shape=[jax.ShapeDtypeStruct((rows, width), kind) for kind in kinds],
        compiler_params=pltpu.CompilerParams(vmem_limit_bytes=40 * 1024 * 1024),
        cost_estimate=pl.CostEstimate(
            flops=4 * rows * depth * width, bytes_accessed=4 * depth * width, transcendentals=rows * width
        ),
    )(mine, *sources, gate_weight, up_weight, *before)


def product_kernel(left_ref, right_ref, out_ref):
    out_ref[...] = jnp.dot(left_ref[...], right_ref[...], preferred_element_type=jnp.float32).astype(
        jnp.bfloat16
    )


def product(left, weight, cut, pieces):
    rows, depth = left.shape
    width = weight.shape[1] // pieces
    tile = 512
    return pl.pallas_call(
        product_kernel,
        grid=(width // tile,),
        in_specs=[
            pl.BlockSpec((rows, depth), lambda n: (0, 0)),
            pl.BlockSpec((depth, tile), lambda n: (0, cut * (width // tile) + n)),
        ],
        out_specs=pl.BlockSpec((rows, tile), lambda n: (0, n)),
        out_shape=jax.ShapeDtypeStruct((rows, width), jnp.bfloat16),
        compiler_params=pltpu.CompilerParams(vmem_limit_bytes=32 * 1024 * 1024),
        cost_estimate=pl.CostEstimate(
            flops=2 * rows * depth * width, bytes_accessed=2 * depth * width, transcendentals=0
        ),
    )(left, weight)


def on_device(
    hidden_in,
    queries,
    keys,
    values,
    block_order,
    routes,
    out_weight,
    norm_gain,
    router_weight,
    gate_weight,
    up_weight,
    down_weight,
):
    shards = lax.axis_size("tp")
    blocks = lax.axis_size("ctx")
    me = lax.axis_index("tp")
    rows, model = hidden_in.shape
    block_rows = rows * shards
    per_device = HEADS // shards
    grouping = HEADS // KV_HEADS
    repeat_by = max(1, grouping // per_device)
    pairs = max(1, per_device // grouping)
    sharing = per_device // pairs
    half = rows // 2 if rows % 32 == 0 else rows
    halves = rows // half
    line = shards <= LINE
    pieces = 2 if line else 1
    cuts = [slice(c * (model // pieces), (c + 1) * (model // pieces)) for c in range(pieces)]
    shard_of = lax.rem(me - jnp.arange(shards, dtype=jnp.int32) + shards, shards)

    def exchange(source):
        if not line:
            got = lax.all_to_all(source, "tp", split_axis=1, concat_axis=0, tiled=True)
            got = got.reshape(shards, rows, source.shape[2])
            return [lax.dynamic_index_in_dim(got, shard_of[s], 0, keepdims=False) for s in range(shards)]
        got = []
        for s in range(shards):
            part = lax.dynamic_index_in_dim(source, lax.rem(me + s, shards), 1, keepdims=False)
            if s > 0:
                part = lax.ppermute(part, "tp", [(i, (i + s) % shards) for i in range(shards)])
            got.append(part)
        return got

    def reduce_line(terms, after=None):
        if not line:
            by_shard = jnp.take(jnp.stack(terms), shard_of, axis=0).reshape(-1, terms[0].shape[1])
            return lax.psum_scatter(by_shard, "tp", scatter_dimension=0, tiled=True).astype(jnp.float32), None
        right = left = None
        marks = []
        for s in range(1, shards):
            to_right, to_left = terms[s], terms[shards - s]
            if right is not None:
                to_right = to_right + right
                to_left = to_left + left
            if after is not None:
                to_right, to_left, _ = lax.optimization_barrier((to_right, to_left, after[s - 1]))
            right = lax.ppermute(to_right, "tp", [(i, i + 1) for i in range(s)])
            left = lax.ppermute(to_left, "tp", [(i, i - 1) for i in range(shards - s, shards)])
            marks.append((right, left))
        return terms[0].astype(jnp.float32) + right.astype(jnp.float32) + left.astype(jnp.float32), marks

    def gather_line(source):
        if not line:
            got = lax.all_gather(source, "tp", axis=0)
            return [jnp.take(got, shard_of, axis=0).reshape(shards * half, -1)], None
        right = left = source
        rights, lefts = [source], [source]
        for s in range(1, shards):
            right = lax.ppermute(right, "tp", [(i, i + 1) for i in range(s - 1, shards - 1)])
            left = lax.ppermute(left, "tp", [(i, i - 1) for i in range(1, shards - s + 1)])
            rights.append(right)
            lefts.append(left)
        return [source] + rights[1:] + lefts[1:], list(zip(rights[1:], lefts[1:]))

    def spread(source):
        widened = jnp.repeat(source.reshape(rows, KV_HEADS, HD), repeat_by, axis=1)
        return widened.reshape(rows, shards, pairs * HD)

    own_pairs = jnp.concatenate(exchange(jnp.concatenate([spread(keys), spread(values)], axis=2)), axis=0)
    key_places = (shard_of[:, None] * rows + jnp.arange(rows, dtype=jnp.int32)[None, :]).reshape(block_rows, 1)
    pair_list, held = [own_pairs], [[0]]
    offset = blocks // 2
    while offset >= 1:
        sent = pair_list[0] if len(pair_list) == 1 else jnp.concatenate(pair_list, axis=0)
        pair_list.append(lax.ppermute(sent, "ctx", [(i, i ^ offset) for i in range(blocks)]))
        held.append([other ^ offset for group in held for other in group])
        offset //= 2

    picked = ((routes[:, 0] == 0) | (routes[:, 1] == 0)).reshape(shards, rows)
    row_ids = jnp.arange(rows, dtype=jnp.int32)
    up_to = (row_ids[:, None] <= row_ids[None, :]).astype(jnp.bfloat16)
    seen = jnp.dot(picked.astype(jnp.bfloat16), up_to, preferred_element_type=jnp.float32).astype(jnp.int32)
    count = seen[:, -1:]
    slot = jnp.where(picked, seen - 1, count + row_ids[None, :] - seen)
    at_slot = slot[:, None, :] == row_ids[None, :, None]
    row_of_slot = jnp.sum(jnp.where(at_slot, row_ids[None, None, :], 0), axis=2)
    places = (row_of_slot + jnp.arange(shards, dtype=jnp.int32)[:, None] * rows)
    places = jnp.take(places, shard_of, axis=0)
    my_slot = lax.dynamic_index_in_dim(slot, me, 0, keepdims=False)
    order = (my_slot[None, :] == row_ids[:, None]).astype(jnp.bfloat16)

    fullest = jnp.full((8, 128), jnp.max(count), jnp.float32)
    for axis in ("req", "ctx"):
        size = lax.axis_size(axis)
        step = 1
        while step < size:
            other = lax.ppermute(fullest, axis, [(i, i ^ step) for i in range(size)])
            fullest = jnp.maximum(fullest, other)
            step *= 2
    crowded = fullest[0, 0] > half

    def reorder(source):
        return jnp.dot(order, source, preferred_element_type=jnp.float32).astype(jnp.bfloat16)

    def restore(parts):
        whole = jnp.concatenate(parts, axis=0) if len(parts) > 1 else parts[0]
        return lax.dot_general(
            order, whole, (((0,), (0,)), ((), ())), preferred_element_type=jnp.float32
        ).astype(jnp.bfloat16)

    got_query = exchange(reorder(queries).reshape(rows, shards, per_device * HD))
    mine = lax.axis_index("ctx").astype(jnp.int32)[None]
    hidden = reorder(hidden_in).astype(jnp.float32)
    my_routes = lax.dynamic_slice_in_dim(routes, me * rows, rows, 0)
    my_routes = jnp.sum(
        jnp.where((my_slot[None, :] == row_ids[:, None])[:, :, None], my_routes[None, :, :], 0), axis=1
    )
    expert_ids = jnp.arange(router_weight.shape[1], dtype=jnp.int32)

    def project(which, slots, asked):
        seen_at = places[:, which * half : (which + 1) * half]
        heads = attend(
            block_order,
            mine,
            asked,
            jnp.stack([seen_at[s] for s in slots])[:, None, :],
            key_places,
            pair_list,
            held,
            which,
            half,
            pairs,
            sharing,
            block_rows,
        ).reshape(shards * half, per_device * HD)
        terms = []
        for cut in cuts:
            term = jnp.dot(heads, out_weight[:, cut], preferred_element_type=jnp.float32)
            term = term.astype(jnp.bfloat16)
            terms.append([term[slots.index(s) * half : (slots.index(s) + 1) * half] for s in range(shards)])
        return terms

    def finish(which, head_sums):
        base = hidden[which * half : (which + 1) * half]
        return jnp.concatenate(
            [(base[:, cut] + head_sum).astype(jnp.bfloat16) for cut, head_sum in zip(cuts, head_sums)], axis=1
        )

    def activate(attended):
        widened = attended.astype(jnp.float32)
        normed = (
            widened * lax.rsqrt(jnp.mean(widened * widened, axis=1, keepdims=True) + 1e-05) * norm_gain
        ).astype(jnp.bfloat16)
        before = []
        marks = []
        for c, cut in enumerate(cuts):
            sources, mark = gather_line(normed[:, cut])
            marks.append(mark)
            before = hidden_units(me[None], sources, gate_weight, up_weight, c, before, c == pieces - 1)
        return normed, before[0], marks

    def share_of(which, normed):
        logits = jnp.dot(normed, router_weight, preferred_element_type=jnp.float32)
        named = my_routes[which * half : (which + 1) * half]
        first = jnp.sum(jnp.where(named[:, 0:1] == expert_ids[None, :], logits, 0.0), axis=1)
        second = jnp.sum(jnp.where(named[:, 1:2] == expert_ids[None, :], logits, 0.0), axis=1)
        share = jnp.where(named[:, 0] == 0, 1.0 / (1.0 + jnp.exp(second - first)), 0.0)
        return share + jnp.where(named[:, 1] == 0, 1.0 / (1.0 + jnp.exp(first - second)), 0.0)

    def deliver(acts, share):
        parts = []
        for c in range(pieces):
            term = product(acts, down_weight, c, pieces).reshape(shards, half, -1)
            total, _ = reduce_line([term[s] for s in range(shards)])
            parts.append((total * share[:, None]).astype(jnp.bfloat16))
        return jnp.concatenate(parts, axis=1)

    def late_expert(source):
        normed, acts, _ = activate(source)
        return deliver(acts, share_of(1, normed))

    slots = [s for s in range(1, shards, 2)] + [s for s in range(2, shards, 2)] + [0]
    asked = [got_query[s] for s in slots]
    reduced = [reduce_line(terms) for terms in project(0, slots, asked)]
    first_half = finish(0, [total for total, _ in reduced])
    normed, acts, marks = activate(first_half)
    share = share_of(0, normed)
    if halves > 1:
        if line:
            asked, _ = lax.optimization_barrier((asked, reduced[0][1][0]))
        sums = [reduce_line(terms, mark)[0] for terms, mark in zip(project(1, slots, asked), marks)]
        second_half = finish(1, sums)
        acts, second_half = lax.optimization_barrier((acts, second_half))
        part = deliver(acts, share)
        part, late = lax.optimization_barrier((part, second_half))
        late = lax.cond(crowded, late_expert, jnp.zeros_like, late)
        return (restore([first_half, second_half]), restore([part, late]))
    return (restore([first_half]), restore([deliver(acts, share)]))


def solution(mesh):
    return jax.shard_map(
        on_device,
        mesh=mesh,
        in_specs=(
            P(("req", "ctx", "tp"), None),
            P(("req", "ctx", "tp"), None),
            P(("req", "ctx", "tp"), None),
            P(("req", "ctx", "tp"), None),
            P("req"),
            P(("req", "ctx"), None),
            P("tp", None),
            P(),
            P(),
            P(None, "tp"),
            P(None, "tp"),
            P("tp", None),
        ),
        out_specs=(P(("req", "ctx", "tp"), None), P(("req", "ctx", "tp"), None)),
        check_vma=False,
    )
```

```python
import functools
import math

import jax
import jax.numpy as jnp
from jax import lax
from jax.experimental import pallas as pl
from jax.experimental.pallas import tpu as pltpu
from jax.sharding import PartitionSpec as P

HEADS = 32
KV_HEADS = 8
HD = 128
FACTOR = math.log2(math.e) / math.sqrt(HD)
LINE = 4
SUM_ROWS = 16
TILE = 256


def attention_kernel(slots, held, pairs, sharing, block_rows, *refs):
    (order, mine), refs = refs[:2], refs[2:]
    query_refs, refs = refs[:slots], refs[slots:]
    place_ref, key_place_ref, refs = refs[0], refs[1], refs[2:]
    pair_refs, refs = refs[: len(held)], refs[len(held) :]
    out_ref, query_ref, value_ref, top_ref, total_ref = refs
    half = out_ref.shape[1]
    me = mine[0]
    my_block = order[me]
    blocks = [(ref, index, offset) for ref, group in zip(pair_refs, held) for index, offset in enumerate(group)]

    @pl.when(pl.program_id(0) == 0)
    def _():
        value_ref[:, :, HD:, :] = jnp.ones((len(blocks), pairs, SUM_ROWS, block_rows), jnp.bfloat16)

    for at, (ref, index, offset) in enumerate(blocks):

        @pl.when((pl.program_id(0) == 0) & (order[me ^ offset] <= my_block))
        def _():
            for p in range(pairs):
                columns = slice((pairs + p) * HD, (pairs + p + 1) * HD)
                value_ref[at, p, :HD, :] = ref[index * block_rows : (index + 1) * block_rows, columns].T

    for at in range(slots):

        @pl.when(pl.program_id(0) == at)
        def _():
            for p in range(pairs):
                for g in range(sharing):
                    column = (p * sharing + g) * HD
                    query_ref[p, g * half : (g + 1) * half, :] = query_refs[at][:, column : column + HD]

    def scores_of(p, at):
        ref, index, _ = blocks[at]
        key = ref[index * block_rows : (index + 1) * block_rows, p * HD : (p + 1) * HD]
        return lax.dot_general(
            key, query_ref[p], (((1,), (1,)), ((), ())), preferred_element_type=jnp.float32
        )

    def mixed_of(p, at, weights):
        return jnp.dot(value_ref[at, p], weights, preferred_element_type=jnp.float32)

    place = jnp.concatenate([place_ref[0]] * sharing, axis=1)
    visible = key_place_ref[...] <= place
    for p in range(pairs):
        scores = jnp.where(visible, scores_of(p, 0), -1e30)
        top = jnp.max(scores, axis=0, keepdims=True)
        weights = jnp.exp2((scores - top) * FACTOR).astype(jnp.bfloat16)
        top_ref[p, 0:1, :] = top
        total_ref[p] = mixed_of(p, 0, weights)

    for at in range(1, len(blocks)):

        @pl.when(order[me ^ blocks[at][2]] < my_block)
        def _():
            for p in range(pairs):
                top = top_ref[p, 0:1, :]
                scores = scores_of(p, at)
                raised = jnp.maximum(top, jnp.max(scores, axis=0, keepdims=True))
                weights = jnp.exp2((scores - raised) * FACTOR).astype(jnp.bfloat16)
                top_ref[p, 0:1, :] = raised
                total_ref[p] = total_ref[p] * jnp.exp2((top - raised) * FACTOR) + mixed_of(p, at, weights)

    for p in range(pairs):
        mixed = (total_ref[p, :HD, :] / total_ref[p, HD : HD + 1, :]).T.astype(jnp.bfloat16)
        for g in range(sharing):
            column = (p * sharing + g) * HD
            out_ref[0, :, column : column + HD] = mixed[g * half : (g + 1) * half]


def attend(order, mine, queries, places, key_places, pair_list, held, pairs, sharing, block_rows):
    slots = len(queries)
    half, width = queries[0].shape
    tall = sharing * half
    blocks = sum(len(group) for group in held)
    count = blocks * block_rows
    kernel = functools.partial(attention_kernel, slots, held, pairs, sharing, block_rows)
    whole = [pl.BlockSpec(pair.shape, lambda s, *_: (0, 0)) for pair in pair_list]
    return pl.pallas_call(
        kernel,
        grid_spec=pltpu.PrefetchScalarGridSpec(
            num_scalar_prefetch=2,
            grid=(slots,),
            in_specs=[pl.BlockSpec((half, width), lambda s, *_: (0, 0))] * slots
            + [
                pl.BlockSpec((1, 1, half), lambda s, *_: (s, 0, 0)),
                pl.BlockSpec((block_rows, 1), lambda s, *_: (0, 0)),
            ]
            + whole,
            out_specs=pl.BlockSpec((1, half, width), lambda s, *_: (s, 0, 0)),
            scratch_shapes=[
                pltpu.VMEM((pairs, tall, HD), jnp.bfloat16),
                pltpu.VMEM((blocks, pairs, HD + SUM_ROWS, block_rows), jnp.bfloat16),
                pltpu.VMEM((pairs, 8, tall), jnp.float32),
                pltpu.VMEM((pairs, HD + SUM_ROWS, tall), jnp.float32),
            ],
        ),
        out_shape=jax.ShapeDtypeStruct((slots, half, width), jnp.bfloat16),
        compiler_params=pltpu.CompilerParams(vmem_limit_bytes=24 * 1024 * 1024),
        cost_estimate=pl.CostEstimate(
            flops=4 * slots * half * width * count,
            bytes_accessed=2 * (2 * slots * half * width + count * 2 * pairs * HD),
            transcendentals=slots * half * width // HD * count,
        ),
    )(order, mine, *queries, places, key_places, *pair_list)


def hidden_kernel(plan, started, last, streams, *refs):
    mine, refs = refs[0], refs[1:]
    sources, refs = refs[:plan], refs[plan:]
    gate_weights, up_weights, refs = refs[:streams], refs[streams : 2 * streams], refs[2 * streams :]
    if started:
        gate_before, up_before, refs = refs[0], refs[1], refs[2:]
    if last:
        out, chosen, gate, upward = refs
    else:
        gate, upward, chosen = refs
    step = pl.program_id(0)
    steps = pl.num_programs(0)
    tile = gate_weights[0].shape[0]

    @pl.when(step == 0)
    def _():
        if plan == 1:
            chosen[...] = sources[0][...]
        else:
            shards = (plan + 1) // 2
            rows = sources[0].shape[0]
            chosen[:rows] = sources[0][...]
            for s in range(1, shards):
                right, left = sources[s], sources[plan - s]

                @pl.when(mine[0] >= s)
                def _():
                    chosen[s * rows : (s + 1) * rows] = right[...]

                @pl.when(mine[0] < s)
                def _():
                    chosen[s * rows : (s + 1) * rows] = left[...]

    parts = []
    for weights in (gate_weights, up_weights):
        total = None
        for j, weight in enumerate(weights):
            columns = pl.ds(pl.multiple_of((j * steps + step) * tile, tile), tile)
            term = jnp.dot(chosen[:, columns], weight[...], preferred_element_type=jnp.float32)
            total = term if total is None else total + term
        parts.append(total)

    @pl.when(step == 0)
    def _():
        gate[...] = parts[0] + gate_before[...] if started else parts[0]
        upward[...] = parts[1] + up_before[...] if started else parts[1]

    @pl.when(step > 0)
    def _():
        gate[...] += parts[0]
        upward[...] += parts[1]

    if last:

        @pl.when(step == steps - 1)
        def _():
            value = gate[...]
            out[...] = (value / (1.0 + jnp.exp(-value)) * upward[...]).astype(jnp.bfloat16)


def hidden_units(mine, sources, gate_weight, up_weight, cut, before, last):
    shards = (len(sources) + 1) // 2
    rows = sources[0].shape[0] * shards
    depth = sources[0].shape[1]
    width = gate_weight.shape[1]
    tile, streams = TILE, 2
    steps = depth // (tile * streams)
    weights = [
        pl.BlockSpec((tile, width), functools.partial(lambda j, k, *_: ((cut * streams + j) * steps + k, 0), j))
        for j in range(streams)
    ]
    out = pl.BlockSpec((rows, width), lambda k, *_: (0, 0))
    kinds = [jnp.bfloat16] if last else [jnp.float32] * 2
    scratch = [pltpu.VMEM((rows, depth), jnp.bfloat16)]
    if last:
        scratch += [pltpu.VMEM((rows, width), jnp.float32)] * 2
    return pl.pallas_call(
        functools.partial(hidden_kernel, len(sources), len(before) > 0, last, streams),
        grid_spec=pltpu.PrefetchScalarGridSpec(
            num_scalar_prefetch=1,
            grid=(steps,),
            in_specs=[pl.BlockSpec(source.shape, lambda k, *_: (0, 0)) for source in sources]
            + weights
            + weights
            + [out] * len(before),
            out_specs=[out] * len(kinds),
            scratch_shapes=scratch,
        ),
        out_shape=[jax.ShapeDtypeStruct((rows, width), kind) for kind in kinds],
        compiler_params=pltpu.CompilerParams(vmem_limit_bytes=40 * 1024 * 1024),
        cost_estimate=pl.CostEstimate(
            flops=4 * rows * depth * width, bytes_accessed=4 * depth * width, transcendentals=rows * width
        ),
    )(mine, *sources, *[gate_weight] * streams, *[up_weight] * streams, *before)


def product_kernel(streams, left_ref, *refs):
    weights, (out_ref, total) = refs[:streams], refs[streams:]
    step = pl.program_id(0)
    steps = pl.num_programs(0)
    tile = weights[0].shape[0]
    value = None
    for j, weight in enumerate(weights):
        columns = pl.ds(pl.multiple_of((j * steps + step) * tile, tile), tile)
        term = jnp.dot(left_ref[:, columns], weight[...], preferred_element_type=jnp.float32)
        value = term if value is None else value + term

    @pl.when(step == 0)
    def _():
        total[...] = value

    @pl.when(step > 0)
    def _():
        total[...] += value

    @pl.when(step == steps - 1)
    def _():
        out_ref[...] = total[...].astype(jnp.bfloat16)


def product(left, weight, cut, pieces):
    rows, depth = left.shape
    width = weight.shape[1] // pieces
    tile = min(TILE, depth)
    streams = 2 if depth % (2 * tile) == 0 else 1
    steps = depth // (tile * streams)
    return pl.pallas_call(
        functools.partial(product_kernel, streams),
        grid=(steps,),
        in_specs=[pl.BlockSpec((rows, depth), lambda k: (0, 0))]
        + [
            pl.BlockSpec((tile, width), functools.partial(lambda j, k: (j * steps + k, cut), j))
            for j in range(streams)
        ],
        out_specs=pl.BlockSpec((rows, width), lambda k: (0, 0)),
        out_shape=jax.ShapeDtypeStruct((rows, width), jnp.bfloat16),
        scratch_shapes=[pltpu.VMEM((rows, width), jnp.float32)],
        compiler_params=pltpu.CompilerParams(vmem_limit_bytes=40 * 1024 * 1024),
        cost_estimate=pl.CostEstimate(
            flops=2 * rows * depth * width, bytes_accessed=2 * depth * width, transcendentals=0
        ),
    )(left, *[weight] * streams)


def pack_pairs_kernel(shards, mine, keys_ref, values_ref, *outs):
    width = keys_ref.shape[1] // shards
    for s in range(shards):
        columns = pl.ds(pl.multiple_of(lax.rem(mine[0] + s, shards) * width, width), width)
        outs[s][:, :width] = keys_ref[:, columns]
        outs[s][:, width:] = values_ref[:, columns]


def pack_pairs(mine, keys, values, shards):
    rows, width = keys.shape
    spec = pl.BlockSpec((rows, width), lambda k, *_: (0, 0))
    out = (rows, 2 * width // shards)
    return pl.pallas_call(
        functools.partial(pack_pairs_kernel, shards),
        grid_spec=pltpu.PrefetchScalarGridSpec(
            num_scalar_prefetch=1,
            grid=(1,),
            in_specs=[spec, spec],
            out_specs=[pl.BlockSpec(out, lambda k, *_: (0, 0))] * shards,
        ),
        out_shape=[jax.ShapeDtypeStruct(out, keys.dtype)] * shards,
    )(mine, keys, values)


def pack_queries_kernel(shards, halves, mine, picked_ref, query_ref, *outs):
    rows = query_ref.shape[0]
    half = rows // halves
    width = query_ref.shape[1] // shards
    packed, (order_ref, places_ref, count_ref) = outs[: halves * shards], outs[halves * shards :]
    me = mine[0]
    across = lax.broadcasted_iota(jnp.int32, (rows, rows), 1)
    down = lax.broadcasted_iota(jnp.int32, (rows, rows), 0)
    up_to = jnp.where(down <= across, 1.0, 0.0).astype(jnp.bfloat16)
    picked = picked_ref[...]
    seen = jnp.dot(picked.astype(jnp.bfloat16), up_to, preferred_element_type=jnp.float32).astype(jnp.int32)
    count = seen[:, rows - 1 : rows]
    row_ids = lax.broadcasted_iota(jnp.int32, seen.shape, 1)
    slot = jnp.where(picked > 0, seen - 1, count + row_ids - seen)
    count_ref[...] = jnp.broadcast_to(jnp.max(count, axis=0, keepdims=True), count_ref.shape).astype(jnp.float32)
    ids = row_ids.astype(jnp.bfloat16)
    for s in range(shards):
        shard = lax.rem(me - s + shards, shards)
        mine_slot = slot[0:1]
        for other in range(1, shards):
            mine_slot = jnp.where(shard == other, slot[other : other + 1], mine_slot)
        at_slot = jnp.where(mine_slot == down, 1.0, 0.0).astype(jnp.bfloat16)
        rows_at = lax.dot_general(ids, at_slot, (((1,), (1,)), ((), ())), preferred_element_type=jnp.float32)
        places_ref[s] = rows_at[0:1].astype(jnp.int32) + shard * rows
        if s == 0:
            order_ref[...] = at_slot
    for s in range(shards):
        columns = pl.ds(pl.multiple_of(lax.rem(me + s, shards) * width, width), width)
        ordered = jnp.dot(order_ref[...], query_ref[:, columns], preferred_element_type=jnp.float32)
        ordered = ordered.astype(jnp.bfloat16)
        for h in range(halves):
            packed[h * shards + s][...] = ordered[h * half : (h + 1) * half]


def pack_queries(mine, picked, queries, shards, halves):
    rows, width = queries.shape
    packed = (rows // halves, width // shards)
    shapes = [jax.ShapeDtypeStruct(packed, jnp.bfloat16)] * (halves * shards) + [
        jax.ShapeDtypeStruct((rows, rows), jnp.bfloat16),
        jax.ShapeDtypeStruct((shards, 1, rows), jnp.int32),
        jax.ShapeDtypeStruct((8, 128), jnp.float32),
    ]

    def whole(shape):
        return pl.BlockSpec(shape, lambda k, *_: (0,) * len(shape))

    got = pl.pallas_call(
        functools.partial(pack_queries_kernel, shards, halves),
        grid_spec=pltpu.PrefetchScalarGridSpec(
            num_scalar_prefetch=1,
            grid=(1,),
            in_specs=[whole(picked.shape), whole(queries.shape)],
            out_specs=[whole(shape.shape) for shape in shapes],
        ),
        out_shape=shapes,
    )(mine, picked, queries)
    return [got[h * shards : (h + 1) * shards] for h in range(halves)], *got[halves * shards :]


def on_device(
    hidden_in,
    queries,
    keys,
    values,
    block_order,
    routes,
    out_weight,
    norm_gain,
    router_weight,
    gate_weight,
    up_weight,
    down_weight,
):
    shards = lax.axis_size("tp")
    blocks = lax.axis_size("ctx")
    me = lax.axis_index("tp")
    rows, model = hidden_in.shape
    block_rows = rows * shards
    per_device = HEADS // shards
    grouping = HEADS // KV_HEADS
    repeat_by = max(1, grouping // per_device)
    pairs = max(1, per_device // grouping)
    sharing = per_device // pairs
    half = rows // 2 if rows % 32 == 0 else rows
    halves = rows // half
    line = shards <= LINE
    pieces = 2 if line else 1
    cuts = [slice(c * (model // pieces), (c + 1) * (model // pieces)) for c in range(pieces)]
    shard_of = lax.rem(me - jnp.arange(shards, dtype=jnp.int32) + shards, shards)

    def shift(parts):
        moves = [[(i, (i + s) % shards) for i in range(shards)] for s in range(shards)]
        return [parts[0]] + [lax.ppermute(parts[s], "tp", moves[s]) for s in range(1, shards)]

    def exchange(source):
        got = lax.all_to_all(source, "tp", split_axis=1, concat_axis=0, tiled=True)
        got = got.reshape(shards, rows, source.shape[2])
        return [lax.dynamic_index_in_dim(got, shard_of[s], 0, keepdims=False) for s in range(shards)]

    def rights(count):
        return [(i, i + 1) for i in range(count)]

    def lefts(count):
        return [(i, i - 1) for i in range(shards - count, shards)]

    def reduce_line(terms):
        if not line:
            by_shard = jnp.take(jnp.stack(terms), shard_of, axis=0).reshape(-1, terms[0].shape[1])
            return lax.psum_scatter(by_shard, "tp", scatter_dimension=0, tiled=True).astype(jnp.float32), None
        right = left = mark = None
        for s in range(1, shards):
            to_right, to_left = terms[s], terms[shards - s]
            if right is not None:
                to_right = to_right + right
                to_left = to_left + left
            right = lax.ppermute(to_right, "tp", rights(s))
            left = lax.ppermute(to_left, "tp", lefts(s))
            right, left = lax.optimization_barrier((right, left))
            mark = right if mark is None else mark
        return terms[0].astype(jnp.float32) + right.astype(jnp.float32) + left.astype(jnp.float32), mark

    def gather_line(source, terms=None):
        if not line:
            got = lax.all_gather(source, "tp", axis=0)
            return [jnp.take(got, shard_of, axis=0).reshape(shards * half, -1)], None
        right = left = source
        from_left, from_right = [], []
        for s in range(1, shards):
            if s > 1 and terms is not None:
                right = jnp.where(me >= s - 1, right, right + terms[s - 1])
                left = jnp.where(me <= shards - s, left, left + terms[shards - s + 1])
            if s == 1 or terms is not None:
                to_right, to_left = rights(shards - 1), lefts(shards - 1)
            else:
                to_right = [(i, i + 1) for i in range(s - 1, shards - 1)]
                to_left = [(i, i - 1) for i in range(1, shards - s + 1)]
            right = lax.ppermute(right, "tp", to_right)
            left = lax.ppermute(left, "tp", to_left)
            right, left = lax.optimization_barrier((right, left))
            from_left.append(right)
            from_right.append(left)
        total = None
        if terms is not None:
            right = lax.ppermute(right + terms[shards - 1], "tp", rights(shards - 1))
            left = lax.ppermute(left + terms[1], "tp", lefts(shards - 1))
            total = terms[0].astype(jnp.float32) + right.astype(jnp.float32) + left.astype(jnp.float32)
        return [source] + from_left + from_right, total

    key_places = (shard_of[:, None] * rows + jnp.arange(rows, dtype=jnp.int32)[None, :]).reshape(block_rows, 1)
    picked = ((routes[:, 0] == 0) | (routes[:, 1] == 0)).reshape(shards, rows)
    if line:
        sent_pairs = pack_pairs(me[None], keys, values, shards)
        own_pairs = jnp.concatenate(shift(sent_pairs), axis=0)
        picked, _ = lax.optimization_barrier((picked.astype(jnp.int32), sent_pairs))
        packed, order, places, fullest = pack_queries(me[None], picked, queries, shards, halves)
        asked = [shift(packed[h]) for h in range(halves)]
    else:

        def spread(source):
            widened = jnp.repeat(source.reshape(rows, KV_HEADS, HD), repeat_by, axis=1)
            return widened.reshape(rows, shards, pairs * HD)

        own_pairs = exchange(jnp.concatenate([spread(keys), spread(values)], axis=2))
        own_pairs = jnp.concatenate(own_pairs, axis=0)
        row_ids = jnp.arange(rows, dtype=jnp.int32)
        seen = jnp.cumsum(picked.astype(jnp.int32), axis=1)
        slot = jnp.where(picked, seen - 1, seen[:, -1:] + row_ids[None, :] - seen)
        at_slot = slot[:, None, :] == row_ids[None, :, None]
        row_of_slot = jnp.sum(jnp.where(at_slot, row_ids[None, None, :], 0), axis=2)
        places = row_of_slot + jnp.arange(shards, dtype=jnp.int32)[:, None] * rows
        places = jnp.take(places, shard_of, axis=0)[:, None, :]
        order = lax.dynamic_index_in_dim(at_slot, me, 0, keepdims=False).astype(jnp.bfloat16)
        ordered = jnp.dot(order, queries, preferred_element_type=jnp.float32).astype(jnp.bfloat16)
        asked = [exchange(ordered.reshape(rows, shards, per_device * HD))]

    pair_list, held = [own_pairs], [[0]]
    offset = blocks // 2
    while offset >= 1:
        pair_list += [lax.ppermute(part, "ctx", [(i, i ^ offset) for i in range(blocks)]) for part in pair_list]
        held += [[other ^ offset for other in group] for group in held]
        offset //= 2

    def reorder(source):
        return jnp.dot(order, source, preferred_element_type=jnp.float32).astype(jnp.bfloat16)

    def restore(parts):
        whole = jnp.concatenate(parts, axis=0) if len(parts) > 1 else parts[0]
        return lax.dot_general(
            order, whole, (((0,), (0,)), ((), ())), preferred_element_type=jnp.float32
        ).astype(jnp.bfloat16)

    mine = lax.axis_index("ctx").astype(jnp.int32)[None]
    expert_ids = jnp.arange(router_weight.shape[1], dtype=jnp.int32)
    slots = [s for s in range(1, shards, 2)] + [s for s in range(2, shards, 2)] + [0]

    def project(which):
        heads = attend(
            block_order,
            mine,
            [asked[which][s] for s in slots],
            jnp.stack([places[s, :, which * half : (which + 1) * half] for s in slots]),
            key_places,
            pair_list,
            held,
            pairs,
            sharing,
            block_rows,
        ).reshape(shards * half, per_device * HD)
        terms = []
        for c in range(pieces):
            term = product(heads, out_weight, c, pieces)
            terms.append([term[slots.index(s) * half : (slots.index(s) + 1) * half] for s in range(shards)])
        return terms

    def finish(which, head_sums):
        base = hidden[which * half : (which + 1) * half].astype(jnp.float32)
        return jnp.concatenate(
            [(base[:, cut] + head_sum).astype(jnp.bfloat16) for cut, head_sum in zip(cuts, head_sums)], axis=1
        )

    def activate(attended, terms=None):
        widened = attended.astype(jnp.float32)
        normed = (
            widened * lax.rsqrt(jnp.mean(widened * widened, axis=1, keepdims=True) + 1e-05) * norm_gain
        ).astype(jnp.bfloat16)
        before = []
        sums = []
        for c, cut in enumerate(cuts):
            sources, total = gather_line(normed[:, cut], None if terms is None else terms[c])
            sums.append(total)
            before = hidden_units(me[None], sources, gate_weight, up_weight, c, before, c == pieces - 1)
        return normed, before[0], sums

    def share_of(which, normed):
        logits = jnp.dot(normed, router_weight, preferred_element_type=jnp.float32)
        named = my_routes[which * half : (which + 1) * half]
        first = jnp.sum(jnp.where(named[:, 0:1] == expert_ids[None, :], logits, 0.0), axis=1)
        second = jnp.sum(jnp.where(named[:, 1:2] == expert_ids[None, :], logits, 0.0), axis=1)
        share = jnp.where(named[:, 0] == 0, 1.0 / (1.0 + jnp.exp(second - first)), 0.0)
        return share + jnp.where(named[:, 1] == 0, 1.0 / (1.0 + jnp.exp(first - second)), 0.0)

    def deliver(acts, share):
        parts = []
        for c in range(pieces):
            term = product(acts, down_weight, c, pieces).reshape(shards, half, -1)
            total, _ = reduce_line([term[s] for s in range(shards)])
            parts.append((total * share[:, None]).astype(jnp.bfloat16))
        return jnp.concatenate(parts, axis=1)

    def late_expert(source):
        normed, acts, _ = activate(source)
        return deliver(acts, share_of(1, normed))

    reduced = [reduce_line(terms) for terms in project(0)]
    if line:
        asked[-1], hidden_in, order, fullest, _ = lax.optimization_barrier(
            (asked[-1], hidden_in, order, fullest, reduced[0][1])
        )
    hidden = reorder(hidden_in)
    my_routes = lax.dynamic_slice_in_dim(routes, me * rows, rows, 0).astype(jnp.bfloat16)
    my_routes = reorder(my_routes).astype(jnp.int32)
    totals = [total for total, _ in reduced]
    if halves == 1:
        first_half = finish(0, totals)
        normed, acts, _ = activate(first_half)
        return (restore([first_half]), restore([deliver(acts, share_of(0, normed))]))
    for axis in ("req", "ctx"):
        size = lax.axis_size(axis)
        step = 1
        while step < size:
            fullest = jnp.maximum(fullest, lax.ppermute(fullest, axis, [(i, i ^ step) for i in range(size)]))
            step *= 2
    terms = project(1)
    totals, terms, fullest = lax.optimization_barrier((totals, terms, fullest))
    first_half = finish(0, totals)
    normed, acts, sums = activate(first_half, terms)
    share = share_of(0, normed)
    second_half = finish(1, sums)
    acts, second_half = lax.optimization_barrier((acts, second_half))
    part = deliver(acts, share)
    part, late = lax.optimization_barrier((part, second_half))
    late = lax.cond(fullest[0, 0] > half, late_expert, jnp.zeros_like, late)
    return (restore([first_half, second_half]), restore([part, late]))


def solution(mesh):
    return jax.shard_map(
        on_device,
        mesh=mesh,
        in_specs=(
            P(("req", "ctx", "tp"), None),
            P(("req", "ctx", "tp"), None),
            P(("req", "ctx", "tp"), None),
            P(("req", "ctx", "tp"), None),
            P("req"),
            P(("req", "ctx"), None),
            P("tp", None),
            P(),
            P(),
            P(None, "tp"),
            P(None, "tp"),
            P("tp", None),
        ),
        out_specs=(P(("req", "ctx", "tp"), None), P(("req", "ctx", "tp"), None)),
        check_vma=False,
    )
```

```python
import functools
import math

import jax
import jax.numpy as jnp
from jax import lax
from jax.experimental import pallas as pl
from jax.experimental.pallas import tpu as pltpu
from jax.sharding import PartitionSpec as P

HEADS = 32
KV_HEADS = 8
HD = 128
FACTOR = math.log2(math.e) / math.sqrt(HD)
LINE = 4
SUM_ROWS = 16
TILE = 256


def attention_kernel(slots, together, held, pairs, sharing, block_rows, *refs):
    (order, mine), refs = refs[:2], refs[2:]
    query_refs, refs = refs[:slots], refs[slots:]
    place_ref, key_place_ref, refs = refs[0], refs[1], refs[2:]
    pair_refs, refs = refs[: len(held)], refs[len(held) :]
    out_ref, query_ref, value_ref, top_ref, total_ref = refs
    half = out_ref.shape[1]
    me = mine[0]
    my_block = order[me]
    blocks = [(ref, index, offset) for ref, group in zip(pair_refs, held) for index, offset in enumerate(group)]

    @pl.when(pl.program_id(0) == 0)
    def _():
        value_ref[:, :, HD:, :] = jnp.ones((len(blocks), pairs, SUM_ROWS, block_rows), jnp.bfloat16)

    for at, (ref, index, offset) in enumerate(blocks):

        @pl.when((pl.program_id(0) == 0) & (order[me ^ offset] <= my_block))
        def _():
            for p in range(pairs):
                columns = slice((pairs + p) * HD, (pairs + p + 1) * HD)
                value_ref[at, p, :HD, :] = ref[index * block_rows : (index + 1) * block_rows, columns].T

    for at in range(slots):

        @pl.when(pl.program_id(0) == at // together)
        def _():
            for p in range(pairs):
                for g in range(sharing):
                    column = (p * sharing + g) * HD
                    row = (at % together * sharing + g) * half
                    query_ref[p, row : row + half, :] = query_refs[at][:, column : column + HD]

    def scores_of(p, at):
        ref, index, _ = blocks[at]
        key = ref[index * block_rows : (index + 1) * block_rows, p * HD : (p + 1) * HD]
        return lax.dot_general(
            key, query_ref[p], (((1,), (1,)), ((), ())), preferred_element_type=jnp.float32
        )

    def mixed_of(p, at, weights):
        return jnp.dot(value_ref[at, p], weights, preferred_element_type=jnp.float32)

    place = jnp.concatenate([place_ref[i] for i in range(together) for _ in range(sharing)], axis=1)
    visible = key_place_ref[...] <= place
    for p in range(pairs):
        scores = jnp.where(visible, scores_of(p, 0), -1e30)
        top = jnp.max(scores, axis=0, keepdims=True)
        weights = jnp.exp2((scores - top) * FACTOR).astype(jnp.bfloat16)
        top_ref[p, 0:1, :] = top
        total_ref[p] = mixed_of(p, 0, weights)

    for at in range(1, len(blocks)):

        @pl.when(order[me ^ blocks[at][2]] < my_block)
        def _():
            for p in range(pairs):
                top = top_ref[p, 0:1, :]
                scores = scores_of(p, at)
                raised = jnp.maximum(top, jnp.max(scores, axis=0, keepdims=True))
                weights = jnp.exp2((scores - raised) * FACTOR).astype(jnp.bfloat16)
                top_ref[p, 0:1, :] = raised
                total_ref[p] = total_ref[p] * jnp.exp2((top - raised) * FACTOR) + mixed_of(p, at, weights)

    for p in range(pairs):
        mixed = (total_ref[p, :HD, :] / total_ref[p, HD : HD + 1, :]).T.astype(jnp.bfloat16)
        for i in range(together):
            for g in range(sharing):
                column = (p * sharing + g) * HD
                row = (i * sharing + g) * half
                out_ref[i, :, column : column + HD] = mixed[row : row + half]


def attend(order, mine, queries, places, key_places, pair_list, held, pairs, sharing, block_rows):
    slots = len(queries)
    half, width = queries[0].shape
    together = 2 if slots <= LINE else 1
    tall = together * sharing * half
    blocks = sum(len(group) for group in held)
    count = blocks * block_rows
    kernel = functools.partial(attention_kernel, slots, together, held, pairs, sharing, block_rows)
    whole = [pl.BlockSpec(pair.shape, lambda s, *_: (0, 0)) for pair in pair_list]
    return pl.pallas_call(
        kernel,
        grid_spec=pltpu.PrefetchScalarGridSpec(
            num_scalar_prefetch=2,
            grid=(slots // together,),
            in_specs=[pl.BlockSpec((half, width), lambda s, *_: (0, 0))] * slots
            + [
                pl.BlockSpec((together, 1, half), lambda s, *_: (s, 0, 0)),
                pl.BlockSpec((block_rows, 1), lambda s, *_: (0, 0)),
            ]
            + whole,
            out_specs=pl.BlockSpec((together, half, width), lambda s, *_: (s, 0, 0)),
            scratch_shapes=[
                pltpu.VMEM((pairs, tall, HD), jnp.bfloat16),
                pltpu.VMEM((blocks, pairs, HD + SUM_ROWS, block_rows), jnp.bfloat16),
                pltpu.VMEM((pairs, 8, tall), jnp.float32),
                pltpu.VMEM((pairs, HD + SUM_ROWS, tall), jnp.float32),
            ],
        ),
        out_shape=jax.ShapeDtypeStruct((slots, half, width), jnp.bfloat16),
        compiler_params=pltpu.CompilerParams(vmem_limit_bytes=12 * 1024 * 1024),
        cost_estimate=pl.CostEstimate(
            flops=40 * slots * half * width * count,
            bytes_accessed=2 * (2 * slots * half * width + count * 2 * pairs * HD),
            transcendentals=slots * half * width // HD * count,
        ),
    )(order, mine, *queries, places, key_places, *pair_list)


def hidden_kernel(plan, started, last, cut, *refs):
    mine, refs = refs[0], refs[1:]
    sources, refs = refs[:plan], refs[plan:]
    gate_weight, up_weight, refs = refs[0], refs[1], refs[2:]
    if started:
        gate_before, up_before, refs = refs[0], refs[1], refs[2:]
    if last:
        out, chosen, gate, upward = refs
    else:
        gate, upward, chosen = refs
    step = pl.program_id(0)
    steps = pl.num_programs(0)
    tile = up_weight.shape[0]
    depth = chosen.shape[1]

    def piece(ref):
        return ref[...] if ref.shape[1] == depth else ref[:, cut * depth : (cut + 1) * depth]

    @pl.when(step == 0)
    def _():
        shards = (plan + 1) // 2
        rows = sources[0].shape[0]
        chosen[:rows] = piece(sources[0])
        for s in range(1, shards):
            right, left = sources[s], sources[plan - s]

            @pl.when(mine[0] >= s)
            def _():
                chosen[s * rows : (s + 1) * rows] = piece(right)

            @pl.when(mine[0] < s)
            def _():
                chosen[s * rows : (s + 1) * rows] = piece(left)

    held = chosen[:, pl.ds(pl.multiple_of(step * tile, tile), tile)]
    if gate_weight.shape[0] == tile:
        gate_tile = gate_weight[...]
    else:
        gate_tile = gate_weight[pl.ds(pl.multiple_of((cut * steps + step) * tile, tile), tile), :]
    parts = [
        jnp.dot(held, gate_tile, preferred_element_type=jnp.float32),
        jnp.dot(held, up_weight[...], preferred_element_type=jnp.float32),
    ]

    @pl.when(step == 0)
    def _():
        gate[...] = parts[0] + gate_before[...] if started else parts[0]
        upward[...] = parts[1] + up_before[...] if started else parts[1]

    @pl.when(step > 0)
    def _():
        gate[...] += parts[0]
        upward[...] += parts[1]

    if last:

        @pl.when(step == steps - 1)
        def _():
            value = gate[...]
            out[...] = (value / (1.0 + jnp.exp(-value)) * upward[...]).astype(jnp.bfloat16)


def hidden_units(mine, sources, gate_weight, up_weight, cut, pieces, before, resident):
    shards = (len(sources) + 1) // 2
    rows = sources[0].shape[0] * shards
    depth = gate_weight.shape[0] // pieces
    width = gate_weight.shape[1]
    last = cut == pieces - 1
    tile = TILE
    steps = depth // tile
    streamed = pl.BlockSpec((tile, width), lambda k, *_: (cut * steps + k, 0))
    in_place = pl.BlockSpec(memory_space=pltpu.VMEM)
    out = pl.BlockSpec(memory_space=pltpu.VMEM)
    kinds = [jnp.bfloat16] if last else [jnp.float32] * 2
    scratch = [pltpu.VMEM((rows, depth), jnp.bfloat16)]
    if last:
        scratch += [pltpu.VMEM((rows, width), jnp.float32)] * 2
    return pl.pallas_call(
        functools.partial(hidden_kernel, len(sources), len(before) > 0, last, cut),
        grid_spec=pltpu.PrefetchScalarGridSpec(
            num_scalar_prefetch=1,
            grid=(steps,),
            in_specs=[in_place] * len(sources)
            + [in_place if resident else streamed, streamed]
            + [in_place] * len(before),
            out_specs=[out] * len(kinds),
            scratch_shapes=scratch,
        ),
        out_shape=[jax.ShapeDtypeStruct((rows, width), kind) for kind in kinds],
        compiler_params=pltpu.CompilerParams(vmem_limit_bytes=24 * 1024 * 1024),
        cost_estimate=pl.CostEstimate(
            flops=4 * rows * depth * width, bytes_accessed=4 * depth * width, transcendentals=rows * width
        ),
    )(mine, *sources, gate_weight, up_weight, *before)


def product_kernel(left_ref, weight, out_ref, total):
    step = pl.program_id(0)
    tile = weight.shape[0]
    columns = pl.ds(pl.multiple_of(step * tile, tile), tile)
    value = jnp.dot(left_ref[:, columns], weight[...], preferred_element_type=jnp.float32)

    @pl.when(step == 0)
    def _():
        total[...] = value

    @pl.when(step > 0)
    def _():
        total[...] += value

    @pl.when(step == pl.num_programs(0) - 1)
    def _():
        out_ref[...] = total[...].astype(jnp.bfloat16)


def resident_product_kernel(cut, left_ref, weight, out_ref):
    tile = out_ref.shape[1]
    columns = pl.ds(pl.multiple_of((cut * pl.num_programs(0) + pl.program_id(0)) * tile, tile), tile)
    out_ref[...] = jnp.dot(left_ref[...], weight[:, columns], preferred_element_type=jnp.float32).astype(
        jnp.bfloat16
    )


def product(left, weight, cut, pieces, resident=False):
    rows, depth = left.shape
    width = weight.shape[1] // pieces
    cost = pl.CostEstimate(flops=2 * rows * depth * width, bytes_accessed=2 * depth * width, transcendentals=0)
    out = jax.ShapeDtypeStruct((rows, width), jnp.bfloat16)
    limit = pltpu.CompilerParams(vmem_limit_bytes=20 * 1024 * 1024)
    if resident:
        tile = 1024
        return pl.pallas_call(
            functools.partial(resident_product_kernel, cut),
            grid=(width // tile,),
            in_specs=[pl.BlockSpec((rows, depth), lambda n: (0, 0)), pl.BlockSpec(memory_space=pltpu.VMEM)],
            out_specs=pl.BlockSpec((rows, tile), lambda n: (0, n)),
            out_shape=out,
            compiler_params=limit,
            cost_estimate=cost,
        )(left, weight)
    tile = min(TILE, depth)
    return pl.pallas_call(
        product_kernel,
        grid=(depth // tile,),
        in_specs=[
            pl.BlockSpec((rows, depth), lambda k: (0, 0)),
            pl.BlockSpec((tile, width), lambda k: (k, cut)),
        ],
        out_specs=pl.BlockSpec((rows, width), lambda k: (0, 0)),
        out_shape=out,
        scratch_shapes=[pltpu.VMEM((rows, width), jnp.float32)],
        compiler_params=limit,
        cost_estimate=cost,
    )(left, weight)


def pack_pairs_kernel(shards, mine, keys_ref, values_ref, *outs):
    width = keys_ref.shape[1] // shards
    for s in range(shards):
        columns = pl.ds(pl.multiple_of(lax.rem(mine[0] + s, shards) * width, width), width)
        outs[s][:, :width] = keys_ref[:, columns]
        outs[s][:, width:] = values_ref[:, columns]


def pack_pairs(mine, keys, values, shards):
    rows, width = keys.shape
    spec = pl.BlockSpec((rows, width), lambda k, *_: (0, 0))
    out = (rows, 2 * width // shards)
    return pl.pallas_call(
        functools.partial(pack_pairs_kernel, shards),
        grid_spec=pltpu.PrefetchScalarGridSpec(
            num_scalar_prefetch=1,
            grid=(1,),
            in_specs=[spec, spec],
            out_specs=[pl.BlockSpec(out, lambda k, *_: (0, 0))] * shards,
        ),
        out_shape=[jax.ShapeDtypeStruct(out, keys.dtype)] * shards,
    )(mine, keys, values)


def pack_queries_kernel(shards, halves, mine, picked_ref, query_ref, *outs):
    rows = query_ref.shape[0]
    half = rows // halves
    width = query_ref.shape[1] // shards
    packed, (order_ref, places_ref, count_ref) = outs[: halves * shards], outs[halves * shards :]
    me = mine[0]
    across = lax.broadcasted_iota(jnp.int32, (rows, rows), 1)
    down = lax.broadcasted_iota(jnp.int32, (rows, rows), 0)
    up_to = jnp.where(down <= across, 1.0, 0.0).astype(jnp.bfloat16)
    picked = picked_ref[...]
    seen = jnp.dot(picked.astype(jnp.bfloat16), up_to, preferred_element_type=jnp.float32).astype(jnp.int32)
    count = seen[:, rows - 1 : rows]
    row_ids = lax.broadcasted_iota(jnp.int32, seen.shape, 1)
    slot = jnp.where(picked > 0, seen - 1, count + row_ids - seen)
    count_ref[...] = jnp.broadcast_to(jnp.max(count, axis=0, keepdims=True), count_ref.shape).astype(jnp.float32)
    ids = row_ids.astype(jnp.bfloat16)
    for s in range(shards):
        shard = lax.rem(me - s + shards, shards)
        mine_slot = slot[0:1]
        for other in range(1, shards):
            mine_slot = jnp.where(shard == other, slot[other : other + 1], mine_slot)
        at_slot = jnp.where(mine_slot == down, 1.0, 0.0).astype(jnp.bfloat16)
        rows_at = lax.dot_general(ids, at_slot, (((1,), (1,)), ((), ())), preferred_element_type=jnp.float32)
        places_ref[s] = rows_at[0:1].astype(jnp.int32) + shard * rows
        if s == 0:
            order_ref[...] = at_slot
    for s in range(shards):
        columns = pl.ds(pl.multiple_of(lax.rem(me + s, shards) * width, width), width)
        ordered = jnp.dot(order_ref[...], query_ref[:, columns], preferred_element_type=jnp.float32)
        ordered = ordered.astype(jnp.bfloat16)
        for h in range(halves):
            packed[h * shards + s][...] = ordered[h * half : (h + 1) * half]


def pack_queries(mine, picked, queries, shards, halves):
    rows, width = queries.shape
    packed = (rows // halves, width // shards)
    shapes = [jax.ShapeDtypeStruct(packed, jnp.bfloat16)] * (halves * shards) + [
        jax.ShapeDtypeStruct((rows, rows), jnp.bfloat16),
        jax.ShapeDtypeStruct((shards, 1, rows), jnp.int32),
        jax.ShapeDtypeStruct((8, 128), jnp.float32),
    ]

    def whole(shape):
        return pl.BlockSpec(shape, lambda k, *_: (0,) * len(shape))

    got = pl.pallas_call(
        functools.partial(pack_queries_kernel, shards, halves),
        grid_spec=pltpu.PrefetchScalarGridSpec(
            num_scalar_prefetch=1,
            grid=(1,),
            in_specs=[whole(picked.shape), whole(queries.shape)],
            out_specs=[whole(shape.shape) for shape in shapes],
        ),
        out_shape=shapes,
    )(mine, picked, queries)
    return [got[h * shards : (h + 1) * shards] for h in range(halves)], *got[halves * shards :]


def on_device(
    hidden_in,
    queries,
    keys,
    values,
    block_order,
    routes,
    out_weight,
    norm_gain,
    router_weight,
    gate_weight,
    up_weight,
    down_weight,
):
    shards = lax.axis_size("tp")
    blocks = lax.axis_size("ctx")
    me = lax.axis_index("tp")
    rows, model = hidden_in.shape
    block_rows = rows * shards
    per_device = HEADS // shards
    grouping = HEADS // KV_HEADS
    repeat_by = max(1, grouping // per_device)
    pairs = max(1, per_device // grouping)
    sharing = per_device // pairs
    half = rows // 2 if rows % 32 == 0 else rows
    halves = rows // half
    line = shards <= LINE
    pieces = 2 if line else 1
    cuts = [slice(c * (model // pieces), (c + 1) * (model // pieces)) for c in range(pieces)]
    shard_of = lax.rem(me - jnp.arange(shards, dtype=jnp.int32) + shards, shards)

    def shift(parts):
        moves = [[(i, (i + s) % shards) for i in range(shards)] for s in range(shards)]
        return [parts[0]] + [lax.ppermute(parts[s], "tp", moves[s]) for s in range(1, shards)]

    def exchange(source):
        got = lax.all_to_all(source, "tp", split_axis=1, concat_axis=0, tiled=True)
        got = got.reshape(shards, rows, source.shape[2])
        return [lax.dynamic_index_in_dim(got, shard_of[s], 0, keepdims=False) for s in range(shards)]

    def rights(count):
        return [(i, i + 1) for i in range(count)]

    def lefts(count):
        return [(i, i - 1) for i in range(shards - count, shards)]

    def reduce_line(terms):
        if not line:
            by_shard = jnp.take(jnp.stack(terms), shard_of, axis=0).reshape(-1, terms[0].shape[1])
            return lax.psum_scatter(by_shard, "tp", scatter_dimension=0, tiled=True).astype(jnp.float32), None
        right = left = None
        marks = []
        for s in range(1, shards):
            to_right, to_left = terms[s], terms[shards - s]
            if right is not None:
                to_right = to_right + right
                to_left = to_left + left
            right = lax.ppermute(to_right, "tp", rights(s))
            left = lax.ppermute(to_left, "tp", lefts(s))
            right, left = lax.optimization_barrier((right, left))
            marks.append(right)
        return terms[0].astype(jnp.float32) + right.astype(jnp.float32) + left.astype(jnp.float32), marks

    def gather_line(source, terms=None):
        if not line:
            got = lax.all_gather(source, "tp", axis=0)
            return [[jnp.take(got, shard_of, axis=0).reshape(shards * half, -1)]], None
        first_right = lax.ppermute(source, "tp", rights(shards - 1))
        first_left = lax.ppermute(source, "tp", lefts(shards - 1))
        first_right, first_left = lax.optimization_barrier((first_right, first_left))
        sources, totals = [], []
        for c, cut in enumerate(cuts):
            right, left = first_right[:, cut], first_left[:, cut]
            from_left, from_right = [first_right], [first_left]
            for s in range(2, shards):
                if terms is None:
                    to_right = [(i, i + 1) for i in range(s - 1, shards - 1)]
                    to_left = [(i, i - 1) for i in range(1, shards - s + 1)]
                else:
                    right = jnp.where(me >= s - 1, right, right + terms[c][s - 1])
                    left = jnp.where(me <= shards - s, left, left + terms[c][shards - s + 1])
                    to_right, to_left = rights(shards - 1), lefts(shards - 1)
                right = lax.ppermute(right, "tp", to_right)
                left = lax.ppermute(left, "tp", to_left)
                right, left = lax.optimization_barrier((right, left))
                from_left.append(right)
                from_right.append(left)
            if terms is not None:
                right = lax.ppermute(right + terms[c][shards - 1], "tp", rights(shards - 1))
                left = lax.ppermute(left + terms[c][1], "tp", lefts(shards - 1))
                totals.append(
                    terms[c][0].astype(jnp.float32) + right.astype(jnp.float32) + left.astype(jnp.float32)
                )
            sources.append([source] + from_left + from_right)
        return sources, totals

    key_places = (shard_of[:, None] * rows + jnp.arange(rows, dtype=jnp.int32)[None, :]).reshape(block_rows, 1)
    picked = ((routes[:, 0] == 0) | (routes[:, 1] == 0)).reshape(shards, rows)
    if line:
        sent_pairs = pack_pairs(me[None], keys, values, shards)
        own_pairs = jnp.concatenate(shift(sent_pairs), axis=0)
        picked, _ = lax.optimization_barrier((picked.astype(jnp.int32), sent_pairs))
        packed, order, places, fullest = pack_queries(me[None], picked, queries, shards, halves)
        asked = [shift(packed[h]) for h in range(halves)]
    else:

        def spread(source):
            widened = jnp.repeat(source.reshape(rows, KV_HEADS, HD), repeat_by, axis=1)
            return widened.reshape(rows, shards, pairs * HD)

        own_pairs = exchange(jnp.concatenate([spread(keys), spread(values)], axis=2))
        own_pairs = jnp.concatenate(own_pairs, axis=0)
        row_ids = jnp.arange(rows, dtype=jnp.int32)
        seen = jnp.cumsum(picked.astype(jnp.int32), axis=1)
        slot = jnp.where(picked, seen - 1, seen[:, -1:] + row_ids[None, :] - seen)
        at_slot = slot[:, None, :] == row_ids[None, :, None]
        row_of_slot = jnp.sum(jnp.where(at_slot, row_ids[None, None, :], 0), axis=2)
        places = row_of_slot + jnp.arange(shards, dtype=jnp.int32)[:, None] * rows
        places = jnp.take(places, shard_of, axis=0)[:, None, :]
        order = lax.dynamic_index_in_dim(at_slot, me, 0, keepdims=False).astype(jnp.bfloat16)
        ordered = jnp.dot(order, queries, preferred_element_type=jnp.float32).astype(jnp.bfloat16)
        asked = [exchange(ordered.reshape(rows, shards, per_device * HD))]

    pair_list, held = [own_pairs], [[0]]
    offset = blocks // 2
    while offset >= 1:
        pair_list += [lax.ppermute(part, "ctx", [(i, i ^ offset) for i in range(blocks)]) for part in pair_list]
        held += [[other ^ offset for other in group] for group in held]
        offset //= 2

    def reorder(source):
        return jnp.dot(order, source, preferred_element_type=jnp.float32).astype(jnp.bfloat16)

    def restore(parts):
        whole = jnp.concatenate(parts, axis=0) if len(parts) > 1 else parts[0]
        return lax.dot_general(
            order, whole, (((0,), (0,)), ((), ())), preferred_element_type=jnp.float32
        ).astype(jnp.bfloat16)

    mine = lax.axis_index("ctx").astype(jnp.int32)[None]
    expert_ids = jnp.arange(router_weight.shape[1], dtype=jnp.int32)
    slots = [s for s in range(1, shards, 2)] + [s for s in range(2, shards, 2)] + [0]

    def project(which):
        heads = attend(
            block_order,
            mine,
            [asked[which][s] for s in slots],
            jnp.stack([places[s, :, which * half : (which + 1) * half] for s in slots]),
            key_places,
            pair_list,
            held,
            pairs,
            sharing,
            block_rows,
        ).reshape(shards * half, per_device * HD)
        terms = []
        for c in range(pieces):
            term = product(heads, out_weight, c, pieces)
            terms.append([term[slots.index(s) * half : (slots.index(s) + 1) * half] for s in range(shards)])
        return terms

    def finish(which, head_sums):
        base = hidden[which * half : (which + 1) * half].astype(jnp.float32)
        return jnp.concatenate(
            [(base[:, cut] + head_sum).astype(jnp.bfloat16) for cut, head_sum in zip(cuts, head_sums)], axis=1
        )

    def normalise(attended):
        widened = attended.astype(jnp.float32)
        return (
            widened * lax.rsqrt(jnp.mean(widened * widened, axis=1, keepdims=True) + 1e-05) * norm_gain
        ).astype(jnp.bfloat16)

    def activate(normed, terms=None, resident=False):
        sources, sums = gather_line(normed, terms)
        before = []
        for c in range(pieces):
            before = hidden_units(me[None], sources[c], gate_weight, up_weight, c, pieces, before, resident)
        return before[0], sums

    def share_of(which, normed):
        logits = jnp.dot(normed, router_weight, preferred_element_type=jnp.float32)
        named = my_routes[which * half : (which + 1) * half]
        first = jnp.sum(jnp.where(named[:, 0:1] == expert_ids[None, :], logits, 0.0), axis=1)
        second = jnp.sum(jnp.where(named[:, 1:2] == expert_ids[None, :], logits, 0.0), axis=1)
        share = jnp.where(named[:, 0] == 0, 1.0 / (1.0 + jnp.exp(second - first)), 0.0)
        return share + jnp.where(named[:, 1] == 0, 1.0 / (1.0 + jnp.exp(first - second)), 0.0)

    def deliver(acts, share):
        parts = []
        for c in range(pieces):
            term = product(acts, down_weight, c, pieces).reshape(shards, half, -1)
            total, _ = reduce_line([term[s] for s in range(shards)])
            parts.append((total * share[:, None]).astype(jnp.bfloat16))
        return jnp.concatenate(parts, axis=1)

    def late_expert(source):
        normed = normalise(source)
        acts, _ = activate(normed, None, False)
        return deliver(acts, share_of(1, normed))

    terms = project(0)
    if halves > 1:
        terms, asked[1] = lax.optimization_barrier((terms, asked[1]))
    reduced = [reduce_line(term) for term in terms]
    if line:
        hidden_in, order, _ = lax.optimization_barrier((hidden_in, order, reduced[0][1][0]))
    hidden = reorder(hidden_in)
    my_routes = lax.dynamic_slice_in_dim(routes, me * rows, rows, 0).astype(jnp.bfloat16)
    my_routes = reorder(my_routes).astype(jnp.int32)
    totals = [total for total, _ in reduced]
    first_half = finish(0, totals)
    normed = normalise(first_half)
    share = share_of(0, normed)
    if halves == 1:
        acts, _ = activate(normed)
        return (restore([first_half]), restore([deliver(acts, share)]))
    asked[1], _ = lax.optimization_barrier((asked[1], normed))
    acts, sums = activate(normed, project(1))
    second_half = finish(1, sums)
    acts, second_half = lax.optimization_barrier((acts, second_half))
    part = deliver(acts, share)
    part, late = lax.optimization_barrier((part, second_half))
    late = lax.cond(fullest[0, 0] > half, late_expert, jnp.zeros_like, late)
    return (restore([first_half, second_half]), restore([part, late]))


def solution(mesh):
    return jax.shard_map(
        on_device,
        mesh=mesh,
        in_specs=(
            P(("req", "ctx", "tp"), None),
            P(("req", "ctx", "tp"), None),
            P(("req", "ctx", "tp"), None),
            P(("req", "ctx", "tp"), None),
            P("req"),
            P(("req", "ctx"), None),
            P("tp", None),
            P(),
            P(),
            P(None, "tp"),
            P(None, "tp"),
            P("tp", None),
        ),
        out_specs=(P(("req", "ctx", "tp"), None), P(("req", "ctx", "tp"), None)),
        check_vma=False,
    )
```

```python
import functools
import math

import jax
import jax.numpy as jnp
from jax import lax
from jax.experimental import pallas as pl
from jax.experimental.pallas import tpu as pltpu
from jax.sharding import PartitionSpec as P

HEADS = 32
KV_HEADS = 8
HD = 128
FACTOR = math.log2(math.e) / math.sqrt(HD)
LINE = 4
SUM_ROWS = 16
TILE = 256
VMEM_SMALL = 12 * 1024 * 1024
VMEM_HELD = 20 * 1024 * 1024
VMEM_LARGE = 40 * 1024 * 1024


def attention_kernel(slots, together, held, pairs, sharing, block_rows, *refs):
    (order, mine), refs = refs[:2], refs[2:]
    query_refs, refs = refs[:slots], refs[slots:]
    place_ref, key_place_ref, refs = refs[0], refs[1], refs[2:]
    pair_refs, refs = refs[: len(held)], refs[len(held) :]
    out_ref, query_ref, key_ref, value_ref, top_ref, total_ref = refs
    half = out_ref.shape[1]
    me = mine[0]
    my_block = order[me]
    blocks = [(ref, index, offset) for ref, group in zip(pair_refs, held) for index, offset in enumerate(group)]

    @pl.when(pl.program_id(0) == 0)
    def _():
        value_ref[:, :, HD:, :] = jnp.ones((len(blocks), pairs, SUM_ROWS, block_rows), jnp.bfloat16)

    for at, (ref, index, offset) in enumerate(blocks):

        @pl.when((pl.program_id(0) == 0) & (order[me ^ offset] <= my_block))
        def _():
            for p in range(pairs):
                rows = slice(index * block_rows, (index + 1) * block_rows)
                key_ref[at, p] = ref[rows, p * HD : (p + 1) * HD]
                value_ref[at, p, :HD, :] = ref[rows, (pairs + p) * HD : (pairs + p + 1) * HD].T

    for at in range(slots):

        @pl.when(pl.program_id(0) == at // together)
        def _():
            for p in range(pairs):
                for g in range(sharing):
                    column = (p * sharing + g) * HD
                    row = (at % together * sharing + g) * half
                    query_ref[p, row : row + half, :] = query_refs[at][:, column : column + HD]

    def scores_of(p, at):
        return lax.dot_general(
            key_ref[at, p], query_ref[p], (((1,), (1,)), ((), ())), preferred_element_type=jnp.float32
        )

    def mixed_of(p, at, weights):
        return jnp.dot(value_ref[at, p], weights, preferred_element_type=jnp.float32)

    place = jnp.concatenate([place_ref[i] for i in range(together) for _ in range(sharing)], axis=1)
    visible = key_place_ref[...] <= place
    for p in range(pairs):
        scores = jnp.where(visible, scores_of(p, 0), -1e30)
        top = jnp.max(scores, axis=0, keepdims=True)
        weights = jnp.exp2((scores - top) * FACTOR).astype(jnp.bfloat16)
        top_ref[p, 0:1, :] = top
        total_ref[p] = mixed_of(p, 0, weights)

    @pl.loop(1, len(blocks))
    def _(at):
        offset = blocks[1][2] if len(blocks) > 1 else 0
        for other in range(2, len(blocks)):
            offset = jnp.where(at == other, blocks[other][2], offset)

        @pl.when(order[me ^ offset] < my_block)
        def _():
            for p in range(pairs):
                top = top_ref[p, 0:1, :]
                scores = scores_of(p, at)
                raised = jnp.maximum(top, jnp.max(scores, axis=0, keepdims=True))
                weights = jnp.exp2((scores - raised) * FACTOR).astype(jnp.bfloat16)
                top_ref[p, 0:1, :] = raised
                total_ref[p] = total_ref[p] * jnp.exp2((top - raised) * FACTOR) + mixed_of(p, at, weights)

    for p in range(pairs):
        mixed = (total_ref[p, :HD, :] / total_ref[p, HD : HD + 1, :]).T.astype(jnp.bfloat16)
        for i in range(together):
            for g in range(sharing):
                column = (p * sharing + g) * HD
                row = (i * sharing + g) * half
                out_ref[i, :, column : column + HD] = mixed[row : row + half]


def attend(order, mine, queries, places, key_places, pair_list, held, pairs, sharing, block_rows):
    slots = len(queries)
    half, width = queries[0].shape
    together = 2 if slots <= LINE else 1
    tall = together * sharing * half
    blocks = sum(len(group) for group in held)
    count = blocks * block_rows
    kernel = functools.partial(attention_kernel, slots, together, held, pairs, sharing, block_rows)
    whole = [pl.BlockSpec(memory_space=pltpu.VMEM) for _ in pair_list]
    return pl.pallas_call(
        kernel,
        grid_spec=pltpu.PrefetchScalarGridSpec(
            num_scalar_prefetch=2,
            grid=(slots // together,),
            in_specs=[pl.BlockSpec((half, width), lambda s, *_: (0, 0))] * slots
            + [
                pl.BlockSpec((together, 1, half), lambda s, *_: (s, 0, 0)),
                pl.BlockSpec((block_rows, 1), lambda s, *_: (0, 0)),
            ]
            + whole,
            out_specs=pl.BlockSpec((together, half, width), lambda s, *_: (s, 0, 0)),
            scratch_shapes=[
                pltpu.VMEM((pairs, tall, HD), jnp.bfloat16),
                pltpu.VMEM((blocks, pairs, block_rows, HD), jnp.bfloat16),
                pltpu.VMEM((blocks, pairs, HD + SUM_ROWS, block_rows), jnp.bfloat16),
                pltpu.VMEM((pairs, 8, tall), jnp.float32),
                pltpu.VMEM((pairs, HD + SUM_ROWS, tall), jnp.float32),
            ],
        ),
        out_shape=jax.ShapeDtypeStruct((slots, half, width), jnp.bfloat16),
        compiler_params=pltpu.CompilerParams(vmem_limit_bytes=12 * 1024 * 1024),
        cost_estimate=pl.CostEstimate(
            flops=40 * slots * half * width * count,
            bytes_accessed=2 * (2 * slots * half * width + count * 2 * pairs * HD),
            transcendentals=slots * half * width // HD * count,
        ),
    )(order, mine, *queries, places, key_places, *pair_list)


def hidden_kernel(plan, started, last, cut, *refs):
    mine, refs = refs[0], refs[1:]
    sources, refs = refs[:plan], refs[plan:]
    gate_weight, up_weight, refs = refs[0], refs[1], refs[2:]
    if started:
        gate_before, up_before, refs = refs[0], refs[1], refs[2:]
    outs, chosen = refs[:-1], refs[-1]
    step = pl.program_id(0)
    tile = up_weight.shape[1]
    depth = chosen.shape[1]

    def piece(ref):
        return ref[...] if ref.shape[1] == depth else ref[:, cut * depth : (cut + 1) * depth]

    @pl.when(step == 0)
    def _():
        shards = (plan + 1) // 2
        rows = sources[0].shape[0]
        chosen[:rows] = piece(sources[0])
        for s in range(1, shards):
            right, left = sources[s], sources[plan - s]

            @pl.when(mine[0] >= s)
            def _():
                chosen[s * rows : (s + 1) * rows] = piece(right)

            @pl.when(mine[0] < s)
            def _():
                chosen[s * rows : (s + 1) * rows] = piece(left)

    if gate_weight.shape == up_weight.shape:
        gate_tile = gate_weight[...]
    else:
        columns = pl.ds(pl.multiple_of(step * tile, tile), tile)
        gate_tile = gate_weight[cut * depth : (cut + 1) * depth, columns]
    gate = jnp.dot(chosen[...], gate_tile, preferred_element_type=jnp.float32)
    upward = jnp.dot(chosen[...], up_weight[...], preferred_element_type=jnp.float32)
    if started:
        gate = gate + gate_before[...]
        upward = upward + up_before[...]
    if last:
        outs[0][...] = (gate / (1.0 + jnp.exp(-gate)) * upward).astype(jnp.bfloat16)
    else:
        outs[0][...] = gate
        outs[1][...] = upward


def hidden_units(mine, sources, gate_weight, up_weight, cut, pieces, before, resident):
    shards = (len(sources) + 1) // 2
    rows = sources[0].shape[0] * shards
    depth = gate_weight.shape[0] // pieces
    width = gate_weight.shape[1]
    last = cut == pieces - 1
    tile = min(TILE, width)
    streamed = pl.BlockSpec((depth, tile), lambda n, *_: (cut, n))
    in_place = pl.BlockSpec(memory_space=pltpu.VMEM)
    out = pl.BlockSpec((rows, tile), lambda n, *_: (0, n))
    kinds = [jnp.bfloat16] if last else [jnp.float32] * 2
    return pl.pallas_call(
        functools.partial(hidden_kernel, len(sources), len(before) > 0, last, cut),
        grid_spec=pltpu.PrefetchScalarGridSpec(
            num_scalar_prefetch=1,
            grid=(width // tile,),
            in_specs=[in_place] * len(sources)
            + [in_place if resident else streamed, streamed]
            + [out] * len(before),
            out_specs=[out] * len(kinds),
            scratch_shapes=[pltpu.VMEM((rows, depth), jnp.bfloat16)],
        ),
        out_shape=[jax.ShapeDtypeStruct((rows, width), kind) for kind in kinds],
        compiler_params=pltpu.CompilerParams(vmem_limit_bytes=VMEM_LARGE),
        cost_estimate=pl.CostEstimate(
            flops=4 * rows * depth * width, bytes_accessed=4 * depth * width, transcendentals=rows * width
        ),
    )(mine, *sources, gate_weight, up_weight, *before)


def product_kernel(left_ref, weight, out_ref):
    out_ref[...] = jnp.dot(left_ref[...], weight[...], preferred_element_type=jnp.float32).astype(jnp.bfloat16)


def resident_product_kernel(cut, left_ref, weight, out_ref):
    tile = out_ref.shape[1]
    columns = pl.ds(pl.multiple_of((cut * pl.num_programs(0) + pl.program_id(0)) * tile, tile), tile)
    out_ref[...] = jnp.dot(left_ref[...], weight[:, columns], preferred_element_type=jnp.float32).astype(
        jnp.bfloat16
    )


def product(left, weight, cut, pieces, resident=False):
    rows, depth = left.shape
    width = weight.shape[1] // pieces
    tile = 2 * TILE
    in_place = pl.BlockSpec(memory_space=pltpu.VMEM)
    streamed = pl.BlockSpec((depth, tile), lambda n: (0, cut * (width // tile) + n))
    return pl.pallas_call(
        functools.partial(resident_product_kernel, cut) if resident else product_kernel,
        grid=(width // tile,),
        in_specs=[in_place, in_place if resident else streamed],
        out_specs=pl.BlockSpec((rows, tile), lambda n: (0, n)),
        out_shape=jax.ShapeDtypeStruct((rows, width), jnp.bfloat16),
        compiler_params=pltpu.CompilerParams(vmem_limit_bytes=VMEM_HELD if resident else VMEM_SMALL),
        cost_estimate=pl.CostEstimate(
            flops=2 * rows * depth * width, bytes_accessed=2 * depth * width, transcendentals=0
        ),
    )(left, weight)


def pack_pairs_kernel(shards, mine, keys_ref, values_ref, *outs):
    width = keys_ref.shape[1] // shards
    for s in range(shards):
        columns = pl.ds(pl.multiple_of(lax.rem(mine[0] + s, shards) * width, width), width)
        outs[s][:, :width] = keys_ref[:, columns]
        outs[s][:, width:] = values_ref[:, columns]


def pack_pairs(mine, keys, values, shards):
    rows, width = keys.shape
    spec = pl.BlockSpec((rows, width), lambda k, *_: (0, 0))
    out = (rows, 2 * width // shards)
    return pl.pallas_call(
        functools.partial(pack_pairs_kernel, shards),
        grid_spec=pltpu.PrefetchScalarGridSpec(
            num_scalar_prefetch=1,
            grid=(1,),
            in_specs=[spec, spec],
            out_specs=[pl.BlockSpec(out, lambda k, *_: (0, 0))] * shards,
        ),
        out_shape=[jax.ShapeDtypeStruct(out, keys.dtype)] * shards,
    )(mine, keys, values)


def pack_queries_kernel(shards, halves, mine, picked_ref, query_ref, *outs):
    rows = query_ref.shape[0]
    half = rows // halves
    width = query_ref.shape[1] // shards
    packed, (order_ref, places_ref, count_ref) = outs[: halves * shards], outs[halves * shards :]
    me = mine[0]
    across = lax.broadcasted_iota(jnp.int32, (rows, rows), 1)
    down = lax.broadcasted_iota(jnp.int32, (rows, rows), 0)
    up_to = jnp.where(down <= across, 1.0, 0.0).astype(jnp.bfloat16)
    picked = picked_ref[...]
    seen = jnp.dot(picked.astype(jnp.bfloat16), up_to, preferred_element_type=jnp.float32).astype(jnp.int32)
    count = seen[:, rows - 1 : rows]
    row_ids = lax.broadcasted_iota(jnp.int32, seen.shape, 1)
    slot = jnp.where(picked > 0, seen - 1, count + row_ids - seen)
    count_ref[...] = jnp.broadcast_to(jnp.max(count, axis=0, keepdims=True), count_ref.shape).astype(jnp.float32)
    ids = row_ids.astype(jnp.bfloat16)
    for s in range(shards):
        shard = lax.rem(me - s + shards, shards)
        mine_slot = slot[0:1]
        for other in range(1, shards):
            mine_slot = jnp.where(shard == other, slot[other : other + 1], mine_slot)
        at_slot = jnp.where(mine_slot == down, 1.0, 0.0).astype(jnp.bfloat16)
        rows_at = lax.dot_general(ids, at_slot, (((1,), (1,)), ((), ())), preferred_element_type=jnp.float32)
        places_ref[s] = rows_at[0:1].astype(jnp.int32) + shard * rows
        if s == 0:
            order_ref[...] = at_slot
    for s in range(shards):
        columns = pl.ds(pl.multiple_of(lax.rem(me + s, shards) * width, width), width)
        ordered = jnp.dot(order_ref[...], query_ref[:, columns], preferred_element_type=jnp.float32)
        ordered = ordered.astype(jnp.bfloat16)
        for h in range(halves):
            packed[h * shards + s][...] = ordered[h * half : (h + 1) * half]


def pack_queries(mine, picked, queries, shards, halves):
    rows, width = queries.shape
    packed = (rows // halves, width // shards)
    shapes = [jax.ShapeDtypeStruct(packed, jnp.bfloat16)] * (halves * shards) + [
        jax.ShapeDtypeStruct((rows, rows), jnp.bfloat16),
        jax.ShapeDtypeStruct((shards, 1, rows), jnp.int32),
        jax.ShapeDtypeStruct((8, 128), jnp.float32),
    ]

    def whole(shape):
        return pl.BlockSpec(shape, lambda k, *_: (0,) * len(shape))

    got = pl.pallas_call(
        functools.partial(pack_queries_kernel, shards, halves),
        grid_spec=pltpu.PrefetchScalarGridSpec(
            num_scalar_prefetch=1,
            grid=(1,),
            in_specs=[whole(picked.shape), whole(queries.shape)],
            out_specs=[whole(shape.shape) for shape in shapes],
        ),
        out_shape=shapes,
    )(mine, picked, queries)
    return [got[h * shards : (h + 1) * shards] for h in range(halves)], *got[halves * shards :]


def on_device(
    hidden_in,
    queries,
    keys,
    values,
    block_order,
    routes,
    out_weight,
    norm_gain,
    router_weight,
    gate_weight,
    up_weight,
    down_weight,
):
    shards = lax.axis_size("tp")
    blocks = lax.axis_size("ctx")
    me = lax.axis_index("tp")
    rows, model = hidden_in.shape
    block_rows = rows * shards
    per_device = HEADS // shards
    grouping = HEADS // KV_HEADS
    repeat_by = max(1, grouping // per_device)
    pairs = max(1, per_device // grouping)
    sharing = per_device // pairs
    half = rows // 2 if rows % 32 == 0 else rows
    halves = rows // half
    line = shards <= LINE
    pieces = 2 if line else 1
    cuts = [slice(c * (model // pieces), (c + 1) * (model // pieces)) for c in range(pieces)]
    shard_of = lax.rem(me - jnp.arange(shards, dtype=jnp.int32) + shards, shards)

    def shift(parts):
        moves = [[(i, (i + s) % shards) for i in range(shards)] for s in range(shards)]
        return [parts[0]] + [lax.ppermute(parts[s], "tp", moves[s]) for s in range(1, shards)]

    def exchange(source):
        got = lax.all_to_all(source, "tp", split_axis=1, concat_axis=0, tiled=True)
        got = got.reshape(shards, rows, source.shape[2])
        return [lax.dynamic_index_in_dim(got, shard_of[s], 0, keepdims=False) for s in range(shards)]

    def rights(count):
        return [(i, i + 1) for i in range(count)]

    def lefts(count):
        return [(i, i - 1) for i in range(shards - count, shards)]

    def reduce_line(pieces_terms):
        if not line:
            by_shard = [jnp.take(jnp.stack(terms), shard_of, axis=0).reshape(-1, terms[0].shape[1]) for terms in pieces_terms]
            return [
                lax.psum_scatter(term, "tp", scatter_dimension=0, tiled=True).astype(jnp.float32) for term in by_shard
            ], None
        got = [None] * len(pieces_terms)
        marks = []
        for s in range(1, shards):
            ahead = None
            for c, terms in enumerate(pieces_terms):
                if got[c] is None:
                    sent = (terms[s], terms[shards - s])
                else:
                    arrived = got[c] if ahead is None else lax.optimization_barrier((got[c], ahead))[0]
                    sent = (terms[s] + arrived[0], terms[shards - s] + arrived[1])
                ahead = sent
                right = lax.ppermute(sent[0], "tp", rights(s))
                left = lax.ppermute(sent[1], "tp", lefts(s))
                got[c] = lax.optimization_barrier((right, left))
            marks.append(got[0])
        return [
            terms[0].astype(jnp.float32) + right.astype(jnp.float32) + left.astype(jnp.float32)
            for terms, (right, left) in zip(pieces_terms, got)
        ], marks

    def gather_line(source, terms=None):
        if not line:
            got = lax.all_gather(source, "tp", axis=0)
            return [[jnp.take(got, shard_of, axis=0).reshape(shards * half, -1)]], None
        first_right = lax.ppermute(source, "tp", rights(shards - 1))
        first_left = lax.ppermute(source, "tp", lefts(shards - 1))
        first_right, first_left = lax.optimization_barrier((first_right, first_left))
        got = [(first_right[:, cut], first_left[:, cut]) for cut in cuts]
        sources = [([source, first_right], [first_left]) for _ in cuts]
        for s in range(2, shards):
            ahead = None
            for c in range(pieces):
                right, left = got[c] if ahead is None else lax.optimization_barrier((got[c], ahead))[0]
                if terms is None:
                    to_right = [(i, i + 1) for i in range(s - 1, shards - 1)]
                    to_left = [(i, i - 1) for i in range(1, shards - s + 1)]
                else:
                    right = jnp.where(me >= s - 1, right, right + terms[c][s - 1])
                    left = jnp.where(me <= shards - s, left, left + terms[c][shards - s + 1])
                    to_right, to_left = rights(shards - 1), lefts(shards - 1)
                ahead = (right, left)
                right = lax.ppermute(right, "tp", to_right)
                left = lax.ppermute(left, "tp", to_left)
                got[c] = lax.optimization_barrier((right, left))
                sources[c][0].append(got[c][0])
                sources[c][1].append(got[c][1])
        totals = []
        if terms is not None:
            for c, (right, left) in enumerate(got):
                right = lax.ppermute(right + terms[c][shards - 1], "tp", rights(shards - 1))
                left = lax.ppermute(left + terms[c][1], "tp", lefts(shards - 1))
                totals.append(
                    terms[c][0].astype(jnp.float32) + right.astype(jnp.float32) + left.astype(jnp.float32)
                )
        return [right + left for right, left in sources], totals

    key_places = (shard_of[:, None] * rows + jnp.arange(rows, dtype=jnp.int32)[None, :]).reshape(block_rows, 1)
    picked = ((routes[:, 0] == 0) | (routes[:, 1] == 0)).reshape(shards, rows)
    if line:
        sent_pairs = pack_pairs(me[None], keys, values, shards)
        own_pairs = jnp.concatenate(shift(sent_pairs), axis=0)
        picked, _ = lax.optimization_barrier((picked.astype(jnp.int32), sent_pairs))
        packed, order, places, fullest = pack_queries(me[None], picked, queries, shards, halves)
        asked = [shift(packed[h]) for h in range(halves)]
    else:

        def spread(source):
            widened = jnp.repeat(source.reshape(rows, KV_HEADS, HD), repeat_by, axis=1)
            return widened.reshape(rows, shards, pairs * HD)

        own_pairs = exchange(jnp.concatenate([spread(keys), spread(values)], axis=2))
        own_pairs = jnp.concatenate(own_pairs, axis=0)
        row_ids = jnp.arange(rows, dtype=jnp.int32)
        seen = jnp.cumsum(picked.astype(jnp.int32), axis=1)
        slot = jnp.where(picked, seen - 1, seen[:, -1:] + row_ids[None, :] - seen)
        at_slot = slot[:, None, :] == row_ids[None, :, None]
        row_of_slot = jnp.sum(jnp.where(at_slot, row_ids[None, None, :], 0), axis=2)
        places = row_of_slot + jnp.arange(shards, dtype=jnp.int32)[:, None] * rows
        places = jnp.take(places, shard_of, axis=0)[:, None, :]
        order = lax.dynamic_index_in_dim(at_slot, me, 0, keepdims=False).astype(jnp.bfloat16)
        ordered = jnp.dot(order, queries, preferred_element_type=jnp.float32).astype(jnp.bfloat16)
        asked = [exchange(ordered.reshape(rows, shards, per_device * HD))]

    pair_list, held = [own_pairs], [[0]]
    offset = blocks // 2
    while offset >= 1:
        pair_list += [lax.ppermute(part, "ctx", [(i, i ^ offset) for i in range(blocks)]) for part in pair_list]
        held += [[other ^ offset for other in group] for group in held]
        offset //= 2

    def reorder(source):
        return jnp.dot(order, source, preferred_element_type=jnp.float32).astype(jnp.bfloat16)

    def restore(parts):
        whole = jnp.concatenate(parts, axis=0) if len(parts) > 1 else parts[0]
        return lax.dot_general(
            order, whole, (((0,), (0,)), ((), ())), preferred_element_type=jnp.float32
        ).astype(jnp.bfloat16)

    mine = lax.axis_index("ctx").astype(jnp.int32)[None]
    expert_ids = jnp.arange(router_weight.shape[1], dtype=jnp.int32)
    slots = [s for s in range(1, shards, 2)] + [s for s in range(2, shards, 2)] + [0]

    def project(which):
        heads = attend(
            block_order,
            mine,
            [asked[which][s] for s in slots],
            jnp.stack([places[s, :, which * half : (which + 1) * half] for s in slots]),
            key_places,
            pair_list,
            held,
            pairs,
            sharing,
            block_rows,
        ).reshape(shards * half, per_device * HD)
        terms = []
        for c in range(pieces):
            term = product(heads, out_weight, c, pieces, True)
            terms.append([term[slots.index(s) * half : (slots.index(s) + 1) * half] for s in range(shards)])
        return terms

    def finish(which, head_sums):
        base = hidden[which * half : (which + 1) * half].astype(jnp.float32)
        return jnp.concatenate(
            [(base[:, cut] + head_sum).astype(jnp.bfloat16) for cut, head_sum in zip(cuts, head_sums)], axis=1
        )

    def normalise(attended):
        widened = attended.astype(jnp.float32)
        return (
            widened * lax.rsqrt(jnp.mean(widened * widened, axis=1, keepdims=True) + 1e-05) * norm_gain
        ).astype(jnp.bfloat16)

    def activate(normed, terms=None, resident=False):
        sources, sums = gather_line(normed, terms)
        before = []
        for c in range(pieces):
            if before and line:
                sources[c], before = lax.optimization_barrier((sources[c], before))
            before = hidden_units(me[None], sources[c], gate_weight, up_weight, c, pieces, before, resident)
        return before[0], sums

    def share_of(which, normed):
        logits = jnp.dot(normed, router_weight, preferred_element_type=jnp.float32)
        named = my_routes[which * half : (which + 1) * half]
        first = jnp.sum(jnp.where(named[:, 0:1] == expert_ids[None, :], logits, 0.0), axis=1)
        second = jnp.sum(jnp.where(named[:, 1:2] == expert_ids[None, :], logits, 0.0), axis=1)
        share = jnp.where(named[:, 0] == 0, 1.0 / (1.0 + jnp.exp(second - first)), 0.0)
        return share + jnp.where(named[:, 1] == 0, 1.0 / (1.0 + jnp.exp(first - second)), 0.0)

    def deliver(acts, share):
        terms = [product(acts, down_weight, c, pieces).reshape(shards, half, -1) for c in range(pieces)]
        sums, _ = reduce_line([[term[s] for s in range(shards)] for term in terms])
        return jnp.concatenate([(total * share[:, None]).astype(jnp.bfloat16) for total in sums], axis=1)

    def late_expert(source):
        normed = normalise(source)
        acts, _ = activate(normed, None, False)
        return deliver(acts, share_of(1, normed))

    terms = project(0)
    if halves > 1:
        terms, asked[1] = lax.optimization_barrier((terms, asked[1]))
    totals, marks = reduce_line(terms)
    if line:
        hidden_in, order, _ = lax.optimization_barrier((hidden_in, order, marks[0]))
    hidden = reorder(hidden_in)
    my_routes = lax.dynamic_slice_in_dim(routes, me * rows, rows, 0).astype(jnp.bfloat16)
    my_routes = reorder(my_routes).astype(jnp.int32)
    first_half = finish(0, totals)
    normed = normalise(first_half)
    share = share_of(0, normed)
    if halves == 1:
        acts, _ = activate(normed)
        return (restore([first_half]), restore([deliver(acts, share)]))
    asked[1], _ = lax.optimization_barrier((asked[1], normed))
    acts, sums = activate(normed, project(1))
    second_half = finish(1, sums)
    acts, second_half = lax.optimization_barrier((acts, second_half))
    part = deliver(acts, share)
    part, late = lax.optimization_barrier((part, second_half))
    late = lax.cond(fullest[0, 0] > half, late_expert, jnp.zeros_like, late)
    return (restore([first_half, second_half]), restore([part, late]))


def solution(mesh):
    return jax.shard_map(
        on_device,
        mesh=mesh,
        in_specs=(
            P(("req", "ctx", "tp"), None),
            P(("req", "ctx", "tp"), None),
            P(("req", "ctx", "tp"), None),
            P(("req", "ctx", "tp"), None),
            P("req"),
            P(("req", "ctx"), None),
            P("tp", None),
            P(),
            P(),
            P(None, "tp"),
            P(None, "tp"),
            P("tp", None),
        ),
        out_specs=(P(("req", "ctx", "tp"), None), P(("req", "ctx", "tp"), None)),
        check_vma=False,
    )
```

```python
import functools
import math

import jax
import jax.numpy as jnp
from jax import lax
from jax.experimental import pallas as pl
from jax.experimental.pallas import tpu as pltpu
from jax.sharding import PartitionSpec as P

HEADS = 32
KV_HEADS = 8
HD = 128
FACTOR = math.log2(math.e) / math.sqrt(HD)
LINE = 4
SUM_ROWS = 16
TILE = 256
VMEM_SMALL = 12 * 1024 * 1024
VMEM_HELD = 20 * 1024 * 1024
VMEM_LARGE = 40 * 1024 * 1024


def attention_kernel(slots, together, held, pairs, sharing, block_rows, *refs):
    (order, mine), refs = refs[:2], refs[2:]
    query_refs, refs = refs[:slots], refs[slots:]
    place_ref, key_place_ref, refs = refs[0], refs[1], refs[2:]
    pair_refs, refs = refs[: len(held)], refs[len(held) :]
    out_ref, query_ref, key_ref, value_ref, top_ref, total_ref = refs
    half = out_ref.shape[1]
    me = mine[0]
    my_block = order[me]
    blocks = [(ref, index, offset) for ref, group in zip(pair_refs, held) for index, offset in enumerate(group)]

    @pl.when(pl.program_id(0) == 0)
    def _():
        value_ref[:, :, HD:, :] = jnp.ones((len(blocks), pairs, SUM_ROWS, block_rows), jnp.bfloat16)

    for at, (ref, index, offset) in enumerate(blocks):

        @pl.when((pl.program_id(0) == 0) & (order[me ^ offset] <= my_block))
        def _():
            for p in range(pairs):
                rows = slice(index * block_rows, (index + 1) * block_rows)
                key_ref[at, p] = ref[rows, p * HD : (p + 1) * HD]
                value_ref[at, p, :HD, :] = ref[rows, (pairs + p) * HD : (pairs + p + 1) * HD].T

    for at in range(slots):

        @pl.when(pl.program_id(0) == at // together)
        def _():
            for p in range(pairs):
                for g in range(sharing):
                    column = (p * sharing + g) * HD
                    row = (at % together * sharing + g) * half
                    query_ref[p, row : row + half, :] = query_refs[at][:, column : column + HD]

    def scores_of(p, at):
        return lax.dot_general(
            key_ref[at, p], query_ref[p], (((1,), (1,)), ((), ())), preferred_element_type=jnp.float32
        )

    def mixed_of(p, at, weights):
        return jnp.dot(value_ref[at, p], weights, preferred_element_type=jnp.float32)

    place = jnp.concatenate([place_ref[i] for i in range(together) for _ in range(sharing)], axis=1)
    visible = key_place_ref[...] <= place
    for p in range(pairs):
        scores = jnp.where(visible, scores_of(p, 0), -1e30)
        top = jnp.max(scores, axis=0, keepdims=True)
        weights = jnp.exp2((scores - top) * FACTOR).astype(jnp.bfloat16)
        top_ref[p, 0:1, :] = top
        total_ref[p] = mixed_of(p, 0, weights)

    @pl.loop(1, len(blocks))
    def _(at):
        offset = blocks[1][2] if len(blocks) > 1 else 0
        for other in range(2, len(blocks)):
            offset = jnp.where(at == other, blocks[other][2], offset)

        @pl.when(order[me ^ offset] < my_block)
        def _():
            for p in range(pairs):
                top = top_ref[p, 0:1, :]
                scores = scores_of(p, at)
                raised = jnp.maximum(top, jnp.max(scores, axis=0, keepdims=True))
                weights = jnp.exp2((scores - raised) * FACTOR).astype(jnp.bfloat16)
                top_ref[p, 0:1, :] = raised
                total_ref[p] = total_ref[p] * jnp.exp2((top - raised) * FACTOR) + mixed_of(p, at, weights)

    for p in range(pairs):
        mixed = (total_ref[p, :HD, :] / total_ref[p, HD : HD + 1, :]).T.astype(jnp.bfloat16)
        for i in range(together):
            for g in range(sharing):
                column = (p * sharing + g) * HD
                row = (i * sharing + g) * half
                out_ref[i, :, column : column + HD] = mixed[row : row + half]


def attend(order, mine, queries, places, key_places, pair_list, held, pairs, sharing, block_rows):
    slots = len(queries)
    half, width = queries[0].shape
    together = 2 if slots <= LINE else 1
    tall = together * sharing * half
    blocks = sum(len(group) for group in held)
    count = blocks * block_rows
    kernel = functools.partial(attention_kernel, slots, together, held, pairs, sharing, block_rows)
    whole = [pl.BlockSpec(memory_space=pltpu.VMEM) for _ in pair_list]
    return pl.pallas_call(
        kernel,
        grid_spec=pltpu.PrefetchScalarGridSpec(
            num_scalar_prefetch=2,
            grid=(slots // together,),
            in_specs=[pl.BlockSpec((half, width), lambda s, *_: (0, 0))] * slots
            + [
                pl.BlockSpec((together, 1, half), lambda s, *_: (s, 0, 0)),
                pl.BlockSpec((block_rows, 1), lambda s, *_: (0, 0)),
            ]
            + whole,
            out_specs=pl.BlockSpec((together, half, width), lambda s, *_: (s, 0, 0)),
            scratch_shapes=[
                pltpu.VMEM((pairs, tall, HD), jnp.bfloat16),
                pltpu.VMEM((blocks, pairs, block_rows, HD), jnp.bfloat16),
                pltpu.VMEM((blocks, pairs, HD + SUM_ROWS, block_rows), jnp.bfloat16),
                pltpu.VMEM((pairs, 8, tall), jnp.float32),
                pltpu.VMEM((pairs, HD + SUM_ROWS, tall), jnp.float32),
            ],
        ),
        out_shape=jax.ShapeDtypeStruct((slots, half, width), jnp.bfloat16),
        compiler_params=pltpu.CompilerParams(vmem_limit_bytes=12 * 1024 * 1024),
        cost_estimate=pl.CostEstimate(
            flops=40 * slots * half * width * count,
            bytes_accessed=2 * (2 * slots * half * width + count * 2 * pairs * HD),
            transcendentals=slots * half * width // HD * count,
        ),
    )(order, mine, *queries, places, key_places, *pair_list)


def hidden_kernel(plan, *refs):
    mine, refs = refs[0], refs[1:]
    sources = []
    for count in plan:
        sources.append(refs[:count])
        refs = refs[count:]
    gate_weight, up_weight, out, chosen = refs

    def place(s, source):
        rows, width = source[0].shape
        for c, ref in enumerate(source):
            chosen[s * rows : (s + 1) * rows, c * width : (c + 1) * width] = ref[...]

    @pl.when(pl.program_id(0) == 0)
    def _():
        place(0, sources[0])
        for s in range(1, (len(plan) + 1) // 2):
            right, left = sources[s], sources[len(plan) - s]

            @pl.when(mine[0] >= s)
            def _():
                place(s, right)

            @pl.when(mine[0] < s)
            def _():
                place(s, left)

    gate = jnp.dot(chosen[...], gate_weight[...], preferred_element_type=jnp.float32)
    upward = jnp.dot(chosen[...], up_weight[...], preferred_element_type=jnp.float32)
    out[...] = (gate / (1.0 + jnp.exp(-gate)) * upward).astype(jnp.bfloat16)


def hidden_units(mine, sources, gate_weight, up_weight):
    flat = [piece for source in sources for piece in source]
    rows = flat[0].shape[0] * ((len(sources) + 1) // 2)
    depth, width = gate_weight.shape
    tile = min(TILE, width)
    weight = pl.BlockSpec((depth, tile), lambda n, *_: (0, n))
    return pl.pallas_call(
        functools.partial(hidden_kernel, [len(source) for source in sources]),
        grid_spec=pltpu.PrefetchScalarGridSpec(
            num_scalar_prefetch=1,
            grid=(width // tile,),
            in_specs=[pl.BlockSpec(memory_space=pltpu.VMEM)] * len(flat) + [weight, weight],
            out_specs=pl.BlockSpec((rows, tile), lambda n, *_: (0, n)),
            scratch_shapes=[pltpu.VMEM((rows, depth), jnp.bfloat16)],
        ),
        out_shape=jax.ShapeDtypeStruct((rows, width), jnp.bfloat16),
        compiler_params=pltpu.CompilerParams(vmem_limit_bytes=VMEM_LARGE),
        cost_estimate=pl.CostEstimate(
            flops=4 * rows * depth * width, bytes_accessed=4 * depth * width, transcendentals=rows * width
        ),
    )(mine, *flat, gate_weight, up_weight)


def product_kernel(left_ref, weight, out_ref):
    out_ref[...] = jnp.dot(left_ref[...], weight[...], preferred_element_type=jnp.float32).astype(jnp.bfloat16)


def resident_product_kernel(cut, left_ref, weight, out_ref):
    tile = out_ref.shape[1]
    columns = pl.ds(pl.multiple_of((cut * pl.num_programs(0) + pl.program_id(0)) * tile, tile), tile)
    out_ref[...] = jnp.dot(left_ref[...], weight[:, columns], preferred_element_type=jnp.float32).astype(
        jnp.bfloat16
    )


def product(left, weight, cut, pieces, resident=False):
    rows, depth = left.shape
    width = weight.shape[1] // pieces
    tile = 2 * TILE
    in_place = pl.BlockSpec(memory_space=pltpu.VMEM)
    streamed = pl.BlockSpec((depth, tile), lambda n: (0, cut * (width // tile) + n))
    return pl.pallas_call(
        functools.partial(resident_product_kernel, cut) if resident else product_kernel,
        grid=(width // tile,),
        in_specs=[in_place, in_place if resident else streamed],
        out_specs=pl.BlockSpec((rows, tile), lambda n: (0, n)),
        out_shape=jax.ShapeDtypeStruct((rows, width), jnp.bfloat16),
        compiler_params=pltpu.CompilerParams(vmem_limit_bytes=VMEM_HELD if resident else VMEM_SMALL),
        cost_estimate=pl.CostEstimate(
            flops=2 * rows * depth * width, bytes_accessed=2 * depth * width, transcendentals=0
        ),
    )(left, weight)


def pack_pairs_kernel(shards, mine, keys_ref, values_ref, *outs):
    width = keys_ref.shape[1] // shards
    for s in range(shards):
        columns = pl.ds(pl.multiple_of(lax.rem(mine[0] + s, shards) * width, width), width)
        outs[s][:, :width] = keys_ref[:, columns]
        outs[s][:, width:] = values_ref[:, columns]


def pack_pairs(mine, keys, values, shards):
    rows, width = keys.shape
    spec = pl.BlockSpec((rows, width), lambda k, *_: (0, 0))
    out = (rows, 2 * width // shards)
    return pl.pallas_call(
        functools.partial(pack_pairs_kernel, shards),
        grid_spec=pltpu.PrefetchScalarGridSpec(
            num_scalar_prefetch=1,
            grid=(1,),
            in_specs=[spec, spec],
            out_specs=[pl.BlockSpec(out, lambda k, *_: (0, 0))] * shards,
        ),
        out_shape=[jax.ShapeDtypeStruct(out, keys.dtype)] * shards,
    )(mine, keys, values)


def pack_queries_kernel(shards, halves, mine, picked_ref, query_ref, *outs):
    rows = query_ref.shape[0]
    half = rows // halves
    width = query_ref.shape[1] // shards
    packed, (order_ref, places_ref, count_ref) = outs[: halves * shards], outs[halves * shards :]
    me = mine[0]
    across = lax.broadcasted_iota(jnp.int32, (rows, rows), 1)
    down = lax.broadcasted_iota(jnp.int32, (rows, rows), 0)
    up_to = jnp.where(down <= across, 1.0, 0.0).astype(jnp.bfloat16)
    picked = picked_ref[...]
    seen = jnp.dot(picked.astype(jnp.bfloat16), up_to, preferred_element_type=jnp.float32).astype(jnp.int32)
    count = seen[:, rows - 1 : rows]
    row_ids = lax.broadcasted_iota(jnp.int32, seen.shape, 1)
    slot = jnp.where(picked > 0, seen - 1, count + row_ids - seen)
    count_ref[...] = jnp.broadcast_to(jnp.max(count, axis=0, keepdims=True), count_ref.shape).astype(jnp.float32)
    ids = row_ids.astype(jnp.bfloat16)
    for s in range(shards):
        shard = lax.rem(me - s + shards, shards)
        mine_slot = slot[0:1]
        for other in range(1, shards):
            mine_slot = jnp.where(shard == other, slot[other : other + 1], mine_slot)
        at_slot = jnp.where(mine_slot == down, 1.0, 0.0).astype(jnp.bfloat16)
        rows_at = lax.dot_general(ids, at_slot, (((1,), (1,)), ((), ())), preferred_element_type=jnp.float32)
        places_ref[s] = rows_at[0:1].astype(jnp.int32) + shard * rows
        if s == 0:
            order_ref[...] = at_slot
    for s in range(shards):
        columns = pl.ds(pl.multiple_of(lax.rem(me + s, shards) * width, width), width)
        ordered = jnp.dot(order_ref[...], query_ref[:, columns], preferred_element_type=jnp.float32)
        ordered = ordered.astype(jnp.bfloat16)
        for h in range(halves):
            packed[h * shards + s][...] = ordered[h * half : (h + 1) * half]


def pack_queries(mine, picked, queries, shards, halves):
    rows, width = queries.shape
    packed = (rows // halves, width // shards)
    shapes = [jax.ShapeDtypeStruct(packed, jnp.bfloat16)] * (halves * shards) + [
        jax.ShapeDtypeStruct((rows, rows), jnp.bfloat16),
        jax.ShapeDtypeStruct((shards, 1, rows), jnp.int32),
        jax.ShapeDtypeStruct((8, 128), jnp.float32),
    ]

    def whole(shape):
        return pl.BlockSpec(shape, lambda k, *_: (0,) * len(shape))

    got = pl.pallas_call(
        functools.partial(pack_queries_kernel, shards, halves),
        grid_spec=pltpu.PrefetchScalarGridSpec(
            num_scalar_prefetch=1,
            grid=(1,),
            in_specs=[whole(picked.shape), whole(queries.shape)],
            out_specs=[whole(shape.shape) for shape in shapes],
        ),
        out_shape=shapes,
    )(mine, picked, queries)
    return [got[h * shards : (h + 1) * shards] for h in range(halves)], *got[halves * shards :]


def on_device(
    hidden_in,
    queries,
    keys,
    values,
    block_order,
    routes,
    out_weight,
    norm_gain,
    router_weight,
    gate_weight,
    up_weight,
    down_weight,
):
    shards = lax.axis_size("tp")
    blocks = lax.axis_size("ctx")
    me = lax.axis_index("tp")
    rows, model = hidden_in.shape
    block_rows = rows * shards
    per_device = HEADS // shards
    grouping = HEADS // KV_HEADS
    repeat_by = max(1, grouping // per_device)
    pairs = max(1, per_device // grouping)
    sharing = per_device // pairs
    half = rows // 2 if rows % 32 == 0 else rows
    halves = rows // half
    line = shards <= LINE
    pieces = 2 if line else 1
    cuts = [slice(c * (model // pieces), (c + 1) * (model // pieces)) for c in range(pieces)]
    shard_of = lax.rem(me - jnp.arange(shards, dtype=jnp.int32) + shards, shards)

    def shift(parts):
        moves = [[(i, (i + s) % shards) for i in range(shards)] for s in range(shards)]
        return [parts[0]] + [lax.ppermute(parts[s], "tp", moves[s]) for s in range(1, shards)]

    def exchange(source):
        got = lax.all_to_all(source, "tp", split_axis=1, concat_axis=0, tiled=True)
        got = got.reshape(shards, rows, source.shape[2])
        return [lax.dynamic_index_in_dim(got, shard_of[s], 0, keepdims=False) for s in range(shards)]

    def rights(count):
        return [(i, i + 1) for i in range(count)]

    def lefts(count):
        return [(i, i - 1) for i in range(shards - count, shards)]

    def reduce_line(pieces_terms):
        if not line:
            by_shard = [jnp.take(jnp.stack(terms), shard_of, axis=0).reshape(-1, terms[0].shape[1]) for terms in pieces_terms]
            return [
                lax.psum_scatter(term, "tp", scatter_dimension=0, tiled=True).astype(jnp.float32) for term in by_shard
            ], None
        got = [None] * len(pieces_terms)
        marks = []
        for s in range(1, shards):
            for c, terms in enumerate(pieces_terms):
                if got[c] is None:
                    sent = (terms[s], terms[shards - s])
                else:
                    arrived = got[c]
                    sent = (terms[s] + arrived[0], terms[shards - s] + arrived[1])
                right = lax.ppermute(sent[0], "tp", rights(s))
                left = lax.ppermute(sent[1], "tp", lefts(s))
                got[c] = lax.optimization_barrier((right, left))
            marks.append(got[0])
        return [
            terms[0].astype(jnp.float32) + right.astype(jnp.float32) + left.astype(jnp.float32)
            for terms, (right, left) in zip(pieces_terms, got)
        ], marks

    def gather_line(source, terms=None):
        if not line:
            got = lax.all_gather(source, "tp", axis=0)
            return [[jnp.take(got, shard_of, axis=0).reshape(shards * half, -1)]], None
        first_right = lax.ppermute(source, "tp", rights(shards - 1))
        first_left = lax.ppermute(source, "tp", lefts(shards - 1))
        first_right, first_left = lax.optimization_barrier((first_right, first_left))
        got = [(first_right[:, cut], first_left[:, cut]) for cut in cuts]
        from_left, from_right = [], []
        for s in range(2, shards):
            if terms is None:
                sent = got
                to_right = [(i, i + 1) for i in range(s - 1, shards - 1)]
                to_left = [(i, i - 1) for i in range(1, shards - s + 1)]
            else:
                sent = [
                    (
                        jnp.where(me >= s - 1, right, right + term[s - 1]),
                        jnp.where(me <= shards - s, left, left + term[shards - s + 1]),
                    )
                    for (right, left), term in zip(got, terms)
                ]
                to_right, to_left = rights(shards - 1), lefts(shards - 1)
            from_left.append([right for right, _ in sent])
            from_right.append([left for _, left in sent])
            got = [
                lax.optimization_barrier((lax.ppermute(right, "tp", to_right), lax.ppermute(left, "tp", to_left)))
                for right, left in sent
            ]
        from_left.append([right for right, _ in got])
        from_right.append([left for _, left in got])
        total = None
        if terms is not None:
            right = jnp.concatenate([right + term[shards - 1] for (right, _), term in zip(got, terms)], axis=1)
            left = jnp.concatenate([left + term[1] for (_, left), term in zip(got, terms)], axis=1)
            right = lax.ppermute(right, "tp", rights(shards - 1)).astype(jnp.float32)
            left = lax.ppermute(left, "tp", lefts(shards - 1)).astype(jnp.float32)
            total = jnp.concatenate([term[0] for term in terms], axis=1).astype(jnp.float32) + right + left
        return [[source]] + from_left + from_right, total

    key_places = (shard_of[:, None] * rows + jnp.arange(rows, dtype=jnp.int32)[None, :]).reshape(block_rows, 1)
    picked = ((routes[:, 0] == 0) | (routes[:, 1] == 0)).reshape(shards, rows)
    if line:
        sent_pairs = pack_pairs(me[None], keys, values, shards)
        own_pairs = jnp.concatenate(shift(sent_pairs), axis=0)
        picked, _ = lax.optimization_barrier((picked.astype(jnp.int32), sent_pairs))
        packed, order, places, fullest = pack_queries(me[None], picked, queries, shards, halves)
        asked = [shift(packed[h]) for h in range(halves)]
    else:

        def spread(source):
            widened = jnp.repeat(source.reshape(rows, KV_HEADS, HD), repeat_by, axis=1)
            return widened.reshape(rows, shards, pairs * HD)

        own_pairs = exchange(jnp.concatenate([spread(keys), spread(values)], axis=2))
        own_pairs = jnp.concatenate(own_pairs, axis=0)
        row_ids = jnp.arange(rows, dtype=jnp.int32)
        seen = jnp.cumsum(picked.astype(jnp.int32), axis=1)
        slot = jnp.where(picked, seen - 1, seen[:, -1:] + row_ids[None, :] - seen)
        at_slot = slot[:, None, :] == row_ids[None, :, None]
        row_of_slot = jnp.sum(jnp.where(at_slot, row_ids[None, None, :], 0), axis=2)
        places = row_of_slot + jnp.arange(shards, dtype=jnp.int32)[:, None] * rows
        places = jnp.take(places, shard_of, axis=0)[:, None, :]
        order = lax.dynamic_index_in_dim(at_slot, me, 0, keepdims=False).astype(jnp.bfloat16)
        ordered = jnp.dot(order, queries, preferred_element_type=jnp.float32).astype(jnp.bfloat16)
        asked = [exchange(ordered.reshape(rows, shards, per_device * HD))]

    pair_list, held = [own_pairs], [[0]]
    offset = blocks // 2
    while offset >= 1:
        pair_list += [lax.ppermute(part, "ctx", [(i, i ^ offset) for i in range(blocks)]) for part in pair_list]
        held += [[other ^ offset for other in group] for group in held]
        offset //= 2

    def reorder(source):
        return jnp.dot(order, source, preferred_element_type=jnp.float32).astype(jnp.bfloat16)

    def restore(parts):
        whole = jnp.concatenate(parts, axis=0) if len(parts) > 1 else parts[0]
        return lax.dot_general(
            order, whole, (((0,), (0,)), ((), ())), preferred_element_type=jnp.float32
        ).astype(jnp.bfloat16)

    mine = lax.axis_index("ctx").astype(jnp.int32)[None]
    expert_ids = jnp.arange(router_weight.shape[1], dtype=jnp.int32)
    slots = [s for s in range(1, shards, 2)] + [s for s in range(2, shards, 2)] + [0]

    def project(which):
        heads = attend(
            block_order,
            mine,
            [asked[which][s] for s in slots],
            jnp.stack([places[s, :, which * half : (which + 1) * half] for s in slots]),
            key_places,
            pair_list,
            held,
            pairs,
            sharing,
            block_rows,
        ).reshape(shards * half, per_device * HD)
        terms = []
        for c in range(pieces):
            term = product(heads, out_weight, c, pieces, True)
            terms.append([term[slots.index(s) * half : (slots.index(s) + 1) * half] for s in range(shards)])
        return terms

    def finish(which, head_sums):
        base = hidden[which * half : (which + 1) * half].astype(jnp.float32)
        return jnp.concatenate(
            [(base[:, cut] + head_sum).astype(jnp.bfloat16) for cut, head_sum in zip(cuts, head_sums)], axis=1
        )

    def normalise(attended):
        widened = attended.astype(jnp.float32)
        return (
            widened * lax.rsqrt(jnp.mean(widened * widened, axis=1, keepdims=True) + 1e-05) * norm_gain
        ).astype(jnp.bfloat16)

    def activate(normed, terms=None):
        sources, total = gather_line(normed, terms)
        return hidden_units(me[None], sources, gate_weight, up_weight), total

    def share_of(which, normed):
        logits = jnp.dot(normed, router_weight, preferred_element_type=jnp.float32)
        named = my_routes[which * half : (which + 1) * half]
        first = jnp.sum(jnp.where(named[:, 0:1] == expert_ids[None, :], logits, 0.0), axis=1)
        second = jnp.sum(jnp.where(named[:, 1:2] == expert_ids[None, :], logits, 0.0), axis=1)
        share = jnp.where(named[:, 0] == 0, 1.0 / (1.0 + jnp.exp(second - first)), 0.0)
        return share + jnp.where(named[:, 1] == 0, 1.0 / (1.0 + jnp.exp(first - second)), 0.0)

    def deliver(which, acts, normed):
        terms = [product(acts, down_weight, c, pieces).reshape(shards, half, -1) for c in range(pieces)]
        sums, marks = reduce_line([[term[s] for s in range(shards)] for term in terms])
        if line:
            normed, _ = lax.optimization_barrier((normed, marks[0]))
        share = share_of(which, normed)
        return jnp.concatenate([(total * share[:, None]).astype(jnp.bfloat16) for total in sums], axis=1)

    def late_expert(source):
        normed = normalise(source)
        return deliver(1, activate(normed)[0], normed)

    terms = project(0)
    if halves > 1:
        terms, asked[1] = lax.optimization_barrier((terms, asked[1]))
    totals, marks = reduce_line(terms)
    if line:
        hidden_in, order, _ = lax.optimization_barrier((hidden_in, order, marks[0]))
    hidden = reorder(hidden_in)
    my_routes = lax.dynamic_slice_in_dim(routes, me * rows, rows, 0).astype(jnp.bfloat16)
    my_routes = reorder(my_routes).astype(jnp.int32)
    first_half = finish(0, totals)
    normed = normalise(first_half)
    if halves == 1:
        return (restore([first_half]), restore([deliver(0, activate(normed)[0], normed)]))
    asked[1], _ = lax.optimization_barrier((asked[1], normed))
    acts, second_sum = activate(normed, project(1))
    second_half = (hidden[half:].astype(jnp.float32) + second_sum).astype(jnp.bfloat16)
    acts, second_half = lax.optimization_barrier((acts, second_half))
    part = deliver(0, acts, normed)
    part, late, fullest = lax.optimization_barrier((part, second_half, fullest))
    late = lax.cond(fullest[0, 0] > half, late_expert, jnp.zeros_like, late)
    return (restore([first_half, second_half]), restore([part, late]))


def solution(mesh):
    return jax.shard_map(
        on_device,
        mesh=mesh,
        in_specs=(
            P(("req", "ctx", "tp"), None),
            P(("req", "ctx", "tp"), None),
            P(("req", "ctx", "tp"), None),
            P(("req", "ctx", "tp"), None),
            P("req"),
            P(("req", "ctx"), None),
            P("tp", None),
            P(),
            P(),
            P(None, "tp"),
            P(None, "tp"),
            P("tp", None),
        ),
        out_specs=(P(("req", "ctx", "tp"), None), P(("req", "ctx", "tp"), None)),
        check_vma=False,
    )
```

```python
import functools
import math

import jax
import jax.numpy as jnp
from jax import lax
from jax.experimental import pallas as pl
from jax.experimental.pallas import tpu as pltpu
from jax.sharding import PartitionSpec as P

HEADS = 32
KV_HEADS = 8
HD = 128
FACTOR = math.log2(math.e) / math.sqrt(HD)
LINE = 4
SUM_ROWS = 16
TILE = 256
VMEM_SMALL = 12 * 1024 * 1024
VMEM_HELD = 20 * 1024 * 1024
VMEM_LARGE = 40 * 1024 * 1024


def attention_kernel(slots, together, held, pairs, sharing, block_rows, plan, *refs):
    pieces, grouped = plan
    (order, mine), refs = refs[:2], refs[2:]
    query_refs, refs = refs[:slots], refs[slots:]
    place_ref, key_place_ref, refs = refs[0], refs[1], refs[2:]
    pair_refs, weight, refs = refs[: len(held)], refs[len(held)], refs[len(held) + 1 :]
    outs, refs = refs[: pieces * (slots if grouped else 1)], refs[pieces * (slots if grouped else 1) :]
    query_ref, key_ref, value_ref, top_ref, total_ref, head_ref, weight_ref, arrived = refs
    half = query_refs[0].shape[0]
    step = pl.program_id(0)
    me = mine[0]
    my_block = order[me]
    blocks = [(ref, index, offset) for ref, group in zip(pair_refs, held) for index, offset in enumerate(group)]
    weight_copy = pltpu.make_async_copy(weight, weight_ref, arrived)

    @pl.when(step == 0)
    def _():
        weight_copy.start()
        value_ref[:, :, HD:, :] = jnp.ones((len(blocks), pairs, SUM_ROWS, block_rows), jnp.bfloat16)

    for at, (ref, index, offset) in enumerate(blocks):

        @pl.when((step == 0) & (order[me ^ offset] <= my_block))
        def _():
            for p in range(pairs):
                rows = slice(index * block_rows, (index + 1) * block_rows)
                key_ref[at, p] = ref[rows, p * HD : (p + 1) * HD]
                value_ref[at, p, :HD, :] = ref[rows, (pairs + p) * HD : (pairs + p + 1) * HD].T

    for at in range(slots):

        @pl.when(step == at // together)
        def _():
            for p in range(pairs):
                for g in range(sharing):
                    column = (p * sharing + g) * HD
                    row = (at % together * sharing + g) * half
                    query_ref[p, row : row + half, :] = query_refs[at][:, column : column + HD]

    def scores_of(p, at):
        return lax.dot_general(
            key_ref[at, p], query_ref[p], (((1,), (1,)), ((), ())), preferred_element_type=jnp.float32
        )

    def mixed_of(p, at, weights):
        return jnp.dot(value_ref[at, p], weights, preferred_element_type=jnp.float32)

    place = jnp.concatenate([place_ref[i] for i in range(together) for _ in range(sharing)], axis=1)
    visible = key_place_ref[...] <= place
    for p in range(pairs):
        scores = jnp.where(visible, scores_of(p, 0), -1e30)
        top = jnp.max(scores, axis=0, keepdims=True)
        weights = jnp.exp2((scores - top) * FACTOR).astype(jnp.bfloat16)
        top_ref[p, 0:1, :] = top
        total_ref[p] = mixed_of(p, 0, weights)

    @pl.loop(1, len(blocks))
    def _(at):
        offset = blocks[1][2] if len(blocks) > 1 else 0
        for other in range(2, len(blocks)):
            offset = jnp.where(at == other, blocks[other][2], offset)

        @pl.when(order[me ^ offset] < my_block)
        def _():
            for p in range(pairs):
                top = top_ref[p, 0:1, :]
                scores = scores_of(p, at)
                raised = jnp.maximum(top, jnp.max(scores, axis=0, keepdims=True))
                weights = jnp.exp2((scores - raised) * FACTOR).astype(jnp.bfloat16)
                top_ref[p, 0:1, :] = raised
                total_ref[p] = total_ref[p] * jnp.exp2((top - raised) * FACTOR) + mixed_of(p, at, weights)

    for p in range(pairs):
        mixed = (total_ref[p, :HD, :] / total_ref[p, HD : HD + 1, :]).T.astype(jnp.bfloat16)
        for i in range(together):
            for g in range(sharing):
                column = (p * sharing + g) * HD
                row = (i * sharing + g) * half
                at = pl.multiple_of((step * together + i) * half, half)
                head_ref[pl.ds(at, half), column : column + HD] = mixed[row : row + half]

    @pl.when(step == pl.num_programs(0) - 1)
    def _():
        weight_copy.wait()
        width = weight.shape[1] // pieces
        tile = 2 * TILE
        for c in range(pieces):

            @pl.loop(0, width // tile)
            def _(n):
                columns = pl.ds(pl.multiple_of(c * width + n * tile, tile), tile)
                value = jnp.dot(head_ref[...], weight_ref[:, columns], preferred_element_type=jnp.float32)
                share_out(outs[c * len(outs) // pieces :], pl.ds(pl.multiple_of(n * tile, tile), tile), value)


def share_out(outs, columns, value):
    rows = outs[0].shape[0]
    for g in range(value.shape[0] // rows):
        outs[g][:, columns] = value[g * rows : (g + 1) * rows].astype(jnp.bfloat16)


def piece_shapes(rows, width, slots, pieces, grouped):
    return [jax.ShapeDtypeStruct((rows // slots if grouped else rows, width // pieces), jnp.bfloat16)] * (
        pieces * (slots if grouped else 1)
    )


def by_piece(outs, slots, pieces, grouped):
    if grouped:
        return [outs[c * slots : (c + 1) * slots] for c in range(pieces)]
    return [[out[s * (out.shape[0] // slots) : (s + 1) * (out.shape[0] // slots)] for s in range(slots)] for out in outs]


def attend(order, mine, queries, places, key_places, pair_list, held, pairs, sharing, block_rows, weight, pieces, grouped):
    slots = len(queries)
    half, width = queries[0].shape
    together = 2 if slots <= LINE else 1
    tall = together * sharing * half
    blocks = sum(len(group) for group in held)
    count = blocks * block_rows
    shapes = piece_shapes(slots * half, weight.shape[1], slots, pieces, grouped)
    kernel = functools.partial(
        attention_kernel, slots, together, held, pairs, sharing, block_rows, (pieces, grouped)
    )
    in_place = pl.BlockSpec(memory_space=pltpu.VMEM)
    outs = pl.pallas_call(
        kernel,
        grid_spec=pltpu.PrefetchScalarGridSpec(
            num_scalar_prefetch=2,
            grid=(slots // together,),
            in_specs=[in_place] * slots
            + [
                pl.BlockSpec((together, 1, half), lambda s, *_: (s, 0, 0)),
                pl.BlockSpec((block_rows, 1), lambda s, *_: (0, 0)),
            ]
            + [in_place] * len(pair_list)
            + [pl.BlockSpec(memory_space=pl.ANY)],
            out_specs=[in_place] * len(shapes),
            scratch_shapes=[
                pltpu.VMEM((pairs, tall, HD), jnp.bfloat16),
                pltpu.VMEM((blocks, pairs, block_rows, HD), jnp.bfloat16),
                pltpu.VMEM((blocks, pairs, HD + SUM_ROWS, block_rows), jnp.bfloat16),
                pltpu.VMEM((pairs, 8, tall), jnp.float32),
                pltpu.VMEM((pairs, HD + SUM_ROWS, tall), jnp.float32),
                pltpu.VMEM((slots * half, width), jnp.bfloat16),
                pltpu.VMEM(weight.shape, weight.dtype),
                pltpu.SemaphoreType.DMA,
            ],
        ),
        out_shape=shapes,
        compiler_params=pltpu.CompilerParams(vmem_limit_bytes=VMEM_LARGE),
        cost_estimate=pl.CostEstimate(
            flops=40 * slots * half * width * count,
            bytes_accessed=2 * (2 * slots * half * width + count * 2 * pairs * HD + weight.size),
            transcendentals=slots * half * width // HD * count,
        ),
    )(order, mine, *queries, places, key_places, *pair_list, weight)
    return by_piece(outs, slots, pieces, grouped)


def expert_kernel(plan, pieces, *refs):
    mine, refs = refs[0], refs[1:]
    sources = []
    for count in plan:
        sources.append(refs[:count])
        refs = refs[count:]
    gate_weight, up_weight, down_weight, refs = refs[0], refs[1], refs[2], refs[3:]
    outs, (chosen, acts) = refs[:-2], refs[-2:]
    step = pl.program_id(0)
    tile = gate_weight.shape[1]
    first = acts.shape[1] // tile

    def place(s, source):
        rows, width = source[0].shape
        for c, ref in enumerate(source):
            chosen[s * rows : (s + 1) * rows, c * width : (c + 1) * width] = ref[...]

    @pl.when(step == 0)
    def _():
        place(0, sources[0])
        for s in range(1, (len(plan) + 1) // 2):
            right, left = sources[s], sources[len(plan) - s]

            @pl.when(mine[0] >= s)
            def _():
                place(s, right)

            @pl.when(mine[0] < s)
            def _():
                place(s, left)

    @pl.when(step < first)
    def _():
        gate = jnp.dot(chosen[...], gate_weight[...], preferred_element_type=jnp.float32)
        upward = jnp.dot(chosen[...], up_weight[...], preferred_element_type=jnp.float32)
        columns = pl.ds(pl.multiple_of(step * tile, tile), tile)
        acts[:, columns] = (gate / (1.0 + jnp.exp(-gate)) * upward).astype(jnp.bfloat16)

    @pl.when(step >= first)
    def _():
        value = jnp.dot(acts[...], down_weight[...], preferred_element_type=jnp.float32)
        strip = down_weight.shape[1]
        strips = outs[0].shape[1] // strip
        for c in range(pieces):

            @pl.when((step - first) // strips == c)
            def _():
                columns = pl.ds(pl.multiple_of((step - first - c * strips) * strip, strip), strip)
                share_out(outs[c * len(outs) // pieces :], columns, value)


def expert_rows(mine, sources, gate_weight, up_weight, down_weight, slots, pieces, grouped):
    flat = [piece for source in sources for piece in source]
    rows = flat[0].shape[0] * ((len(sources) + 1) // 2)
    depth, width = gate_weight.shape
    tile, strip = min(TILE, width), 2 * TILE
    first = width // tile
    shapes = piece_shapes(rows, depth, slots, pieces, grouped)
    in_place = pl.BlockSpec(memory_space=pltpu.VMEM)
    weight = pl.BlockSpec((depth, tile), lambda n, *_: (0, jnp.minimum(n, first - 1)))
    outs = pl.pallas_call(
        functools.partial(expert_kernel, [len(source) for source in sources], pieces),
        grid_spec=pltpu.PrefetchScalarGridSpec(
            num_scalar_prefetch=1,
            grid=(first + depth // strip,),
            in_specs=[in_place] * len(flat)
            + [weight, weight, pl.BlockSpec((width, strip), lambda n, *_: (0, jnp.maximum(n - first, 0)))],
            out_specs=[in_place] * len(shapes),
            scratch_shapes=[pltpu.VMEM((rows, depth), jnp.bfloat16), pltpu.VMEM((rows, width), jnp.bfloat16)],
        ),
        out_shape=shapes,
        compiler_params=pltpu.CompilerParams(vmem_limit_bytes=VMEM_LARGE),
        cost_estimate=pl.CostEstimate(
            flops=6 * rows * depth * width, bytes_accessed=6 * depth * width, transcendentals=rows * width
        ),
    )(mine, *flat, gate_weight, up_weight, down_weight)
    return by_piece(outs, slots, pieces, grouped)


def pack_pairs_kernel(shards, mine, keys_ref, values_ref, *outs):
    width = keys_ref.shape[1] // shards
    for s in range(shards):
        columns = pl.ds(pl.multiple_of(lax.rem(mine[0] + s, shards) * width, width), width)
        outs[s][:, :width] = keys_ref[:, columns]
        outs[s][:, width:] = values_ref[:, columns]


def pack_pairs(mine, keys, values, shards):
    rows, width = keys.shape
    spec = pl.BlockSpec((rows, width), lambda k, *_: (0, 0))
    out = (rows, 2 * width // shards)
    return pl.pallas_call(
        functools.partial(pack_pairs_kernel, shards),
        grid_spec=pltpu.PrefetchScalarGridSpec(
            num_scalar_prefetch=1,
            grid=(1,),
            in_specs=[spec, spec],
            out_specs=[pl.BlockSpec(out, lambda k, *_: (0, 0))] * shards,
        ),
        out_shape=[jax.ShapeDtypeStruct(out, keys.dtype)] * shards,
    )(mine, keys, values)


def pack_queries_kernel(slots, halves, mine, picked_ref, query_ref, *outs):
    shards = len(slots)
    rows = query_ref.shape[0]
    half = rows // halves
    width = query_ref.shape[1] // shards
    packed, outs = outs[: halves * shards], outs[halves * shards :]
    place_refs, (order_ref, count_ref) = outs[:halves], outs[halves:]
    me = mine[0]
    across = lax.broadcasted_iota(jnp.int32, (rows, rows), 1)
    down = lax.broadcasted_iota(jnp.int32, (rows, rows), 0)
    up_to = jnp.where(down <= across, 1.0, 0.0).astype(jnp.bfloat16)
    picked = picked_ref[...]
    seen = jnp.dot(picked.astype(jnp.bfloat16), up_to, preferred_element_type=jnp.float32).astype(jnp.int32)
    count = seen[:, rows - 1 : rows]
    row_ids = lax.broadcasted_iota(jnp.int32, seen.shape, 1)
    slot = jnp.where(picked > 0, seen - 1, count + row_ids - seen)
    count_ref[...] = jnp.broadcast_to(jnp.max(count, axis=0, keepdims=True), count_ref.shape).astype(jnp.float32)
    ids = row_ids.astype(jnp.bfloat16)
    for s in range(shards):
        shard = lax.rem(me - s + shards, shards)
        mine_slot = slot[0:1]
        for other in range(1, shards):
            mine_slot = jnp.where(shard == other, slot[other : other + 1], mine_slot)
        at_slot = jnp.where(mine_slot == down, 1.0, 0.0).astype(jnp.bfloat16)
        rows_at = lax.dot_general(ids, at_slot, (((1,), (1,)), ((), ())), preferred_element_type=jnp.float32)
        for h in range(halves):
            here = rows_at[0:1, h * half : (h + 1) * half]
            place_refs[h][slots.index(s)] = here.astype(jnp.int32) + shard * rows
        if s == 0:
            order_ref[...] = at_slot
    for s in range(shards):
        columns = pl.ds(pl.multiple_of(lax.rem(me + s, shards) * width, width), width)
        ordered = jnp.dot(order_ref[...], query_ref[:, columns], preferred_element_type=jnp.float32)
        ordered = ordered.astype(jnp.bfloat16)
        for h in range(halves):
            packed[h * shards + s][...] = ordered[h * half : (h + 1) * half]


def pack_queries(mine, picked, queries, slots, halves):
    shards = len(slots)
    rows, width = queries.shape
    packed = (rows // halves, width // shards)
    shapes = [jax.ShapeDtypeStruct(packed, jnp.bfloat16)] * (halves * shards)
    shapes += [jax.ShapeDtypeStruct((shards, 1, rows // halves), jnp.int32)] * halves
    shapes += [jax.ShapeDtypeStruct((rows, rows), jnp.bfloat16), jax.ShapeDtypeStruct((8, 128), jnp.float32)]

    def whole(shape):
        return pl.BlockSpec(shape, lambda k, *_: (0,) * len(shape))

    got = pl.pallas_call(
        functools.partial(pack_queries_kernel, slots, halves),
        grid_spec=pltpu.PrefetchScalarGridSpec(
            num_scalar_prefetch=1,
            grid=(1,),
            in_specs=[whole(picked.shape), whole(queries.shape)],
            out_specs=[whole(shape.shape) for shape in shapes],
        ),
        out_shape=shapes,
    )(mine, picked, queries)
    packed, got = got[: halves * shards], got[halves * shards :]
    return [packed[h * shards : (h + 1) * shards] for h in range(halves)], got[:halves], *got[halves:]


def on_device(
    hidden_in,
    queries,
    keys,
    values,
    block_order,
    routes,
    out_weight,
    norm_gain,
    router_weight,
    gate_weight,
    up_weight,
    down_weight,
):
    shards = lax.axis_size("tp")
    blocks = lax.axis_size("ctx")
    me = lax.axis_index("tp")
    rows, model = hidden_in.shape
    block_rows = rows * shards
    per_device = HEADS // shards
    grouping = HEADS // KV_HEADS
    repeat_by = max(1, grouping // per_device)
    pairs = max(1, per_device // grouping)
    sharing = per_device // pairs
    half = rows // 2 if rows % 32 == 0 else rows
    halves = rows // half
    line = shards <= LINE
    pieces = 2 if line else 1
    cuts = [slice(c * (model // pieces), (c + 1) * (model // pieces)) for c in range(pieces)]
    slots = [s for s in range(1, shards, 2)] + [s for s in range(2, shards, 2)] + [0]
    shard_of = lax.rem(me - jnp.arange(shards, dtype=jnp.int32) + shards, shards)

    def shift(parts):
        moves = [[(i, (i + s) % shards) for i in range(shards)] for s in range(shards)]
        return [parts[0]] + [lax.ppermute(parts[s], "tp", moves[s]) for s in range(1, shards)]

    def exchange(source):
        got = lax.all_to_all(source, "tp", split_axis=1, concat_axis=0, tiled=True)
        got = got.reshape(shards, rows, source.shape[2])
        return [lax.dynamic_index_in_dim(got, shard_of[s], 0, keepdims=False) for s in range(shards)]

    def rights(count):
        return [(i, i + 1) for i in range(count)]

    def lefts(count):
        return [(i, i - 1) for i in range(shards - count, shards)]

    def reduce_line(pieces_terms):
        if not line:
            by_shard = [jnp.take(jnp.stack(terms), shard_of, axis=0).reshape(-1, terms[0].shape[1]) for terms in pieces_terms]
            return [
                lax.psum_scatter(term, "tp", scatter_dimension=0, tiled=True).astype(jnp.float32) for term in by_shard
            ], None
        got = [None] * len(pieces_terms)
        marks = []
        for s in range(1, shards):
            for c, terms in enumerate(pieces_terms):
                if got[c] is None:
                    sent = (terms[s], terms[shards - s])
                else:
                    arrived = got[c]
                    sent = (terms[s] + arrived[0], terms[shards - s] + arrived[1])
                right = lax.ppermute(sent[0], "tp", rights(s))
                left = lax.ppermute(sent[1], "tp", lefts(s))
                got[c] = lax.optimization_barrier((right, left))
            marks.append(got[0])
        return [
            terms[0].astype(jnp.float32) + right.astype(jnp.float32) + left.astype(jnp.float32)
            for terms, (right, left) in zip(pieces_terms, got)
        ], marks

    def gather_line(source, terms=None):
        if not line:
            got = lax.all_gather(source, "tp", axis=0)
            return [[jnp.take(got, shard_of, axis=0).reshape(shards * half, -1)]], None
        first_right = lax.ppermute(source, "tp", rights(shards - 1))
        first_left = lax.ppermute(source, "tp", lefts(shards - 1))
        first_right, first_left = lax.optimization_barrier((first_right, first_left))
        got = [(first_right[:, cut], first_left[:, cut]) for cut in cuts]
        from_left, from_right = [], []
        for s in range(2, shards):
            if terms is None:
                sent = got
                to_right = [(i, i + 1) for i in range(s - 1, shards - 1)]
                to_left = [(i, i - 1) for i in range(1, shards - s + 1)]
            else:
                sent = [
                    (
                        jnp.where(me >= s - 1, right, right + term[s - 1]),
                        jnp.where(me <= shards - s, left, left + term[shards - s + 1]),
                    )
                    for (right, left), term in zip(got, terms)
                ]
                to_right, to_left = rights(shards - 1), lefts(shards - 1)
            from_left.append([right for right, _ in sent])
            from_right.append([left for _, left in sent])
            got = [
                lax.optimization_barrier((lax.ppermute(right, "tp", to_right), lax.ppermute(left, "tp", to_left)))
                for right, left in sent
            ]
        from_left.append([right for right, _ in got])
        from_right.append([left for _, left in got])
        total = None
        if terms is not None:
            right = jnp.concatenate([right + term[shards - 1] for (right, _), term in zip(got, terms)], axis=1)
            left = jnp.concatenate([left + term[1] for (_, left), term in zip(got, terms)], axis=1)
            right = lax.ppermute(right, "tp", rights(shards - 1)).astype(jnp.float32)
            left = lax.ppermute(left, "tp", lefts(shards - 1)).astype(jnp.float32)
            total = jnp.concatenate([term[0] for term in terms], axis=1).astype(jnp.float32) + right + left
        return [[source]] + from_left + from_right, total

    key_places = (shard_of[:, None] * rows + jnp.arange(rows, dtype=jnp.int32)[None, :]).reshape(block_rows, 1)
    picked = ((routes[:, 0] == 0) | (routes[:, 1] == 0)).reshape(shards, rows)
    if line:
        sent_pairs = pack_pairs(me[None], keys, values, shards)
        own_pairs = jnp.concatenate(shift(sent_pairs), axis=0)
        picked, _ = lax.optimization_barrier((picked.astype(jnp.int32), sent_pairs))
        packed, places, order, fullest = pack_queries(me[None], picked, queries, slots, halves)
        asked = [shift(packed[0])]
    else:

        def spread(source):
            widened = jnp.repeat(source.reshape(rows, KV_HEADS, HD), repeat_by, axis=1)
            return widened.reshape(rows, shards, pairs * HD)

        own_pairs = exchange(jnp.concatenate([spread(keys), spread(values)], axis=2))
        own_pairs = jnp.concatenate(own_pairs, axis=0)
        row_ids = jnp.arange(rows, dtype=jnp.int32)
        seen = jnp.cumsum(picked.astype(jnp.int32), axis=1)
        slot = jnp.where(picked, seen - 1, seen[:, -1:] + row_ids[None, :] - seen)
        at_slot = slot[:, None, :] == row_ids[None, :, None]
        row_of_slot = jnp.sum(jnp.where(at_slot, row_ids[None, None, :], 0), axis=2)
        places = row_of_slot + jnp.arange(shards, dtype=jnp.int32)[:, None] * rows
        places = [jnp.stack([jnp.take(places, shard_of[s], axis=0) for s in slots])[:, None, :]]
        order = lax.dynamic_index_in_dim(at_slot, me, 0, keepdims=False).astype(jnp.bfloat16)
        ordered = jnp.dot(order, queries, preferred_element_type=jnp.float32).astype(jnp.bfloat16)
        asked = [exchange(ordered.reshape(rows, shards, per_device * HD))]

    pair_list, held = [own_pairs], [[0]]
    offset = blocks // 2
    while offset >= 1:
        pair_list += [lax.ppermute(part, "ctx", [(i, i ^ offset) for i in range(blocks)]) for part in pair_list]
        held += [[other ^ offset for other in group] for group in held]
        offset //= 2

    def reorder(source):
        return jnp.dot(order, source, preferred_element_type=jnp.float32).astype(jnp.bfloat16)

    def restore(parts):
        whole = jnp.concatenate(parts, axis=0) if len(parts) > 1 else parts[0]
        return lax.dot_general(
            order, whole, (((0,), (0,)), ((), ())), preferred_element_type=jnp.float32
        ).astype(jnp.bfloat16)

    mine = lax.axis_index("ctx").astype(jnp.int32)[None]
    expert_ids = jnp.arange(router_weight.shape[1], dtype=jnp.int32)

    def project(which):
        terms = attend(
            block_order,
            lax.axis_index("ctx").astype(jnp.int32)[None],
            [asked[which][s] for s in slots],
            places[which],
            key_places,
            pair_list,
            held,
            pairs,
            sharing,
            block_rows,
            out_weight,
            pieces,
            line,
        )
        return [[term[slots.index(s)] for s in range(shards)] for term in terms]

    def finish(which, head_sums):
        base = hidden[which * half : (which + 1) * half].astype(jnp.float32)
        return jnp.concatenate(
            [(base[:, cut] + head_sum).astype(jnp.bfloat16) for cut, head_sum in zip(cuts, head_sums)], axis=1
        )

    def normalise(attended):
        widened = attended.astype(jnp.float32)
        return (
            widened * lax.rsqrt(jnp.mean(widened * widened, axis=1, keepdims=True) + 1e-05) * norm_gain
        ).astype(jnp.bfloat16)

    def share_of(which, normed):
        logits = jnp.dot(normed, router_weight, preferred_element_type=jnp.float32)
        named = my_routes[which * half : (which + 1) * half]
        first = jnp.sum(jnp.where(named[:, 0:1] == expert_ids[None, :], logits, 0.0), axis=1)
        second = jnp.sum(jnp.where(named[:, 1:2] == expert_ids[None, :], logits, 0.0), axis=1)
        share = jnp.where(named[:, 0] == 0, 1.0 / (1.0 + jnp.exp(second - first)), 0.0)
        return share + jnp.where(named[:, 1] == 0, 1.0 / (1.0 + jnp.exp(first - second)), 0.0)

    def expert(which, normed, sources, beside=None):
        terms = expert_rows(me[None], sources, gate_weight, up_weight, down_weight, shards, pieces, line)
        if beside is not None:
            terms, beside = lax.optimization_barrier((terms, beside))
        sums, marks = reduce_line(terms)
        if line:
            normed, _ = lax.optimization_barrier((normed, marks[0]))
        share = share_of(which, normed)
        parts = [(total * share[:, None]).astype(jnp.bfloat16) for total in sums]
        return jnp.concatenate(parts, axis=1), beside

    def late_expert(source):
        normed = normalise(source)
        return expert(1, normed, gather_line(normed)[0])[0]

    terms = project(0)
    if halves > 1:
        asked.append(shift(packed[1]))
        terms, asked[1] = lax.optimization_barrier((terms, asked[1]))
    totals, marks = reduce_line(terms)
    if line:
        hidden_in, order, _ = lax.optimization_barrier((hidden_in, order, marks[0]))
    hidden = reorder(hidden_in)
    my_routes = lax.dynamic_slice_in_dim(routes, me * rows, rows, 0).astype(jnp.bfloat16)
    my_routes = reorder(my_routes).astype(jnp.int32)
    first_half = finish(0, totals)
    normed = normalise(first_half)
    if halves == 1:
        return (restore([first_half]), restore([expert(0, normed, gather_line(normed)[0])[0]]))
    asked[1], _ = lax.optimization_barrier((asked[1], normed))
    sources, second_sum = gather_line(normed, project(1))
    second_half = (hidden[half:].astype(jnp.float32) + second_sum).astype(jnp.bfloat16)
    part, second_half = expert(0, normed, sources, second_half)
    part, late, fullest = lax.optimization_barrier((part, second_half, fullest))
    late = lax.cond(fullest[0, 0] > half, late_expert, jnp.zeros_like, late)
    return (restore([first_half, second_half]), restore([part, late]))


def solution(mesh):
    return jax.shard_map(
        on_device,
        mesh=mesh,
        in_specs=(
            P(("req", "ctx", "tp"), None),
            P(("req", "ctx", "tp"), None),
            P(("req", "ctx", "tp"), None),
            P(("req", "ctx", "tp"), None),
            P("req"),
            P(("req", "ctx"), None),
            P("tp", None),
            P(),
            P(),
            P(None, "tp"),
            P(None, "tp"),
            P("tp", None),
        ),
        out_specs=(P(("req", "ctx", "tp"), None), P(("req", "ctx", "tp"), None)),
        check_vma=False,
    )
```

```python
import functools
import math

import jax
import jax.numpy as jnp
from jax import lax
from jax.experimental import pallas as pl
from jax.experimental.pallas import tpu as pltpu
from jax.sharding import PartitionSpec as P

HEADS = 32
KV_HEADS = 8
HD = 128
FACTOR = math.log2(math.e) / math.sqrt(HD)
LINE = 4
SUM_ROWS = 16
TILE = 256
VMEM_SMALL = 12 * 1024 * 1024
VMEM_HELD = 20 * 1024 * 1024
VMEM_LARGE = 40 * 1024 * 1024


def attention_kernel(slots, together, held, pairs, sharing, block_rows, plan, *refs):
    pieces, grouped = plan
    (order, mine), refs = refs[:2], refs[2:]
    query_refs, refs = refs[:slots], refs[slots:]
    place_ref, refs = refs[0], refs[1:]
    pair_refs, weight, refs = refs[: len(held)], refs[len(held)], refs[len(held) + 1 :]
    outs, refs = refs[: pieces * (slots if grouped else 1)], refs[pieces * (slots if grouped else 1) :]
    query_ref, key_ref, value_ref, top_ref, total_ref, head_ref, weight_ref, arrived = refs
    half = query_refs[0].shape[0]
    step = pl.program_id(0)
    me = mine[0]
    my_block = order[me]
    blocks = [(ref, index, offset) for ref, group in zip(pair_refs, held) for index, offset in enumerate(group)]
    weight_copy = pltpu.make_async_copy(weight, weight_ref, arrived)

    @pl.when(step == 0)
    def _():
        weight_copy.start()
        value_ref[:, :, HD:, :] = jnp.ones((len(blocks), pairs, SUM_ROWS, block_rows), jnp.bfloat16)

    for at, (ref, index, offset) in enumerate(blocks):

        @pl.when((step == 0) & (order[me ^ offset] <= my_block))
        def _():
            for p in range(pairs):
                rows = slice(index * block_rows, (index + 1) * block_rows)
                key_ref[at, p] = ref[rows, p * HD : (p + 1) * HD]
                value_ref[at, p, :HD, :] = ref[rows, (pairs + p) * HD : (pairs + p + 1) * HD].T

    for at in range(slots):

        @pl.when(step == at // together)
        def _():
            for p in range(pairs):
                for g in range(sharing):
                    column = (p * sharing + g) * HD
                    row = (at % together * sharing + g) * half
                    query_ref[p, row : row + half, :] = query_refs[at][:, column : column + HD]

    def scores_of(p, at):
        return lax.dot_general(
            key_ref[at, p], query_ref[p], (((1,), (1,)), ((), ())), preferred_element_type=jnp.float32
        )

    def mixed_of(p, at, weights):
        return jnp.dot(value_ref[at, p], weights, preferred_element_type=jnp.float32)

    place = jnp.concatenate([place_ref[i] for i in range(together) for _ in range(sharing)], axis=1)
    rows = block_rows // slots
    down = lax.broadcasted_iota(jnp.int32, (rows, place.shape[1]), 0)
    visible = jnp.concatenate(
        [down <= place - lax.rem(mine[1] - s + slots, slots) * rows for s in range(slots)], axis=0
    )
    for p in range(pairs):
        scores = jnp.where(visible, scores_of(p, 0), -1e30)
        top = jnp.max(scores, axis=0, keepdims=True)
        weights = jnp.exp2((scores - top) * FACTOR).astype(jnp.bfloat16)
        top_ref[p, 0:1, :] = top
        total_ref[p] = mixed_of(p, 0, weights)

    @pl.loop(1, len(blocks))
    def _(at):
        offset = blocks[1][2] if len(blocks) > 1 else 0
        for other in range(2, len(blocks)):
            offset = jnp.where(at == other, blocks[other][2], offset)

        @pl.when(order[me ^ offset] < my_block)
        def _():
            for p in range(pairs):
                top = top_ref[p, 0:1, :]
                scores = scores_of(p, at)
                raised = jnp.maximum(top, jnp.max(scores, axis=0, keepdims=True))
                weights = jnp.exp2((scores - raised) * FACTOR).astype(jnp.bfloat16)
                top_ref[p, 0:1, :] = raised
                total_ref[p] = total_ref[p] * jnp.exp2((top - raised) * FACTOR) + mixed_of(p, at, weights)

    for p in range(pairs):
        mixed = (total_ref[p, :HD, :] / total_ref[p, HD : HD + 1, :]).T.astype(jnp.bfloat16)
        for i in range(together):
            for g in range(sharing):
                column = (p * sharing + g) * HD
                row = (i * sharing + g) * half
                at = pl.multiple_of((step * together + i) * half, half)
                head_ref[pl.ds(at, half), column : column + HD] = mixed[row : row + half]

    @pl.when(step == pl.num_programs(0) - 1)
    def _():
        weight_copy.wait()
        width = weight.shape[1] // pieces
        tile = 2 * TILE
        for c in range(pieces):

            @pl.loop(0, width // tile)
            def _(n):
                columns = pl.ds(pl.multiple_of(c * width + n * tile, tile), tile)
                value = jnp.dot(head_ref[...], weight_ref[:, columns], preferred_element_type=jnp.float32)
                share_out(outs[c * len(outs) // pieces :], pl.ds(pl.multiple_of(n * tile, tile), tile), value)


def share_out(outs, columns, value):
    rows = outs[0].shape[0]
    for g in range(value.shape[0] // rows):
        outs[g][:, columns] = value[g * rows : (g + 1) * rows].astype(jnp.bfloat16)


def piece_shapes(rows, width, slots, pieces, grouped):
    return [jax.ShapeDtypeStruct((rows // slots if grouped else rows, width // pieces), jnp.bfloat16)] * (
        pieces * (slots if grouped else 1)
    )


def by_piece(outs, slots, pieces, grouped):
    if grouped:
        return [outs[c * slots : (c + 1) * slots] for c in range(pieces)]
    return [[out[s * (out.shape[0] // slots) : (s + 1) * (out.shape[0] // slots)] for s in range(slots)] for out in outs]


def attend(order, mine, queries, places, pair_list, held, pairs, sharing, block_rows, weight, pieces, grouped):
    slots = len(queries)
    half, width = queries[0].shape
    together = 2 if slots <= LINE else 1
    tall = together * sharing * half
    blocks = sum(len(group) for group in held)
    count = blocks * block_rows
    shapes = piece_shapes(slots * half, weight.shape[1], slots, pieces, grouped)
    kernel = functools.partial(
        attention_kernel, slots, together, held, pairs, sharing, block_rows, (pieces, grouped)
    )
    outs = pl.pallas_call(
        kernel,
        grid_spec=pltpu.PrefetchScalarGridSpec(
            num_scalar_prefetch=2,
            grid=(slots // together,),
            in_specs=[pl.BlockSpec((half, width), lambda s, *_: (0, 0))] * slots
            + [pl.BlockSpec((together, 1, half), lambda s, *_: (s, 0, 0))]
            + [pl.BlockSpec(pair.shape, lambda s, *_: (0, 0)) for pair in pair_list]
            + [pl.BlockSpec(memory_space=pl.ANY)],
            out_specs=[pl.BlockSpec(shape.shape, lambda s, *_: (0, 0)) for shape in shapes],
            scratch_shapes=[
                pltpu.VMEM((pairs, tall, HD), jnp.bfloat16),
                pltpu.VMEM((blocks, pairs, block_rows, HD), jnp.bfloat16),
                pltpu.VMEM((blocks, pairs, HD + SUM_ROWS, block_rows), jnp.bfloat16),
                pltpu.VMEM((pairs, 8, tall), jnp.float32),
                pltpu.VMEM((pairs, HD + SUM_ROWS, tall), jnp.float32),
                pltpu.VMEM((slots * half, width), jnp.bfloat16),
                pltpu.VMEM(weight.shape, weight.dtype),
                pltpu.SemaphoreType.DMA,
            ],
        ),
        out_shape=shapes,
        compiler_params=pltpu.CompilerParams(vmem_limit_bytes=VMEM_LARGE),
        cost_estimate=pl.CostEstimate(
            flops=40 * slots * half * width * count,
            bytes_accessed=2 * (2 * slots * half * width + count * 2 * pairs * HD + weight.size),
            transcendentals=slots * half * width // HD * count,
        ),
    )(order, mine, *queries, places, *pair_list, weight)
    return by_piece(outs, slots, pieces, grouped)


def expert_kernel(plan, pieces, *refs):
    mine, refs = refs[0], refs[1:]
    sources = []
    for count in plan:
        sources.append(refs[:count])
        refs = refs[count:]
    gate_weight, up_weight, down_weights, refs = refs[0], refs[1], refs[2:4], refs[4:]
    outs, (chosen, acts) = refs[:-2], refs[-2:]
    step = pl.program_id(0)
    tile = gate_weight.shape[1]
    first = acts.shape[1] // tile

    def place(s, source):
        rows, width = source[0].shape
        for c, ref in enumerate(source):
            chosen[s * rows : (s + 1) * rows, c * width : (c + 1) * width] = ref[...]

    @pl.when(step == 0)
    def _():
        place(0, sources[0])
        for s in range(1, (len(plan) + 1) // 2):
            right, left = sources[s], sources[len(plan) - s]

            @pl.when(mine[0] >= s)
            def _():
                place(s, right)

            @pl.when(mine[0] < s)
            def _():
                place(s, left)

    @pl.when(step < first)
    def _():
        gate = jnp.dot(chosen[...], gate_weight[...], preferred_element_type=jnp.float32)
        upward = jnp.dot(chosen[...], up_weight[...], preferred_element_type=jnp.float32)
        columns = pl.ds(pl.multiple_of(step * tile, tile), tile)
        acts[:, columns] = (gate / (1.0 + jnp.exp(-gate)) * upward).astype(jnp.bfloat16)

    @pl.when(step >= first)
    def _():
        strip = down_weights[0].shape[1]
        pairs = outs[0].shape[1] // (2 * strip)
        for j, down_weight in enumerate(down_weights):
            value = jnp.dot(acts[...], down_weight[...], preferred_element_type=jnp.float32)
            for c in range(pieces):

                @pl.when((step - first) // pairs == c)
                def _():
                    at = (2 * (step - first - c * pairs) + j) * strip
                    share_out(outs[c * len(outs) // pieces :], pl.ds(pl.multiple_of(at, strip), strip), value)


def expert_rows(mine, sources, gate_weight, up_weight, down_weight, slots, pieces, grouped):
    flat = [piece for source in sources for piece in source]
    rows = flat[0].shape[0] * ((len(sources) + 1) // 2)
    depth, width = gate_weight.shape
    tile, strip = min(TILE, width), 2 * TILE
    first = width // tile
    shapes = piece_shapes(rows, depth, slots, pieces, grouped)
    in_place = pl.BlockSpec(memory_space=pltpu.VMEM)
    weight = pl.BlockSpec((depth, tile), lambda n, *_: (0, jnp.minimum(n, first - 1)))
    outs = pl.pallas_call(
        functools.partial(expert_kernel, [len(source) for source in sources], pieces),
        grid_spec=pltpu.PrefetchScalarGridSpec(
            num_scalar_prefetch=1,
            grid=(first + depth // (2 * strip),),
            in_specs=[in_place] * len(flat)
            + [weight, weight]
            + [
                pl.BlockSpec((width, strip), functools.partial(lambda j, n, *_: (0, 2 * jnp.maximum(n - first, 0) + j), j))
                for j in range(2)
            ],
            out_specs=[in_place] * len(shapes),
            scratch_shapes=[pltpu.VMEM((rows, depth), jnp.bfloat16), pltpu.VMEM((rows, width), jnp.bfloat16)],
        ),
        out_shape=shapes,
        compiler_params=pltpu.CompilerParams(vmem_limit_bytes=VMEM_LARGE),
        cost_estimate=pl.CostEstimate(
            flops=6 * rows * depth * width, bytes_accessed=6 * depth * width, transcendentals=rows * width
        ),
    )(mine, *flat, gate_weight, up_weight, down_weight, down_weight)
    return by_piece(outs, slots, pieces, grouped)


def pack_pairs_kernel(shards, mine, keys_ref, values_ref, *outs):
    width = keys_ref.shape[1] // shards
    for s in range(shards):
        columns = pl.ds(pl.multiple_of(lax.rem(mine[0] + s, shards) * width, width), width)
        outs[s][:, :width] = keys_ref[:, columns]
        outs[s][:, width:] = values_ref[:, columns]


def pack_pairs(mine, keys, values, shards):
    rows, width = keys.shape
    spec = pl.BlockSpec((rows, width), lambda k, *_: (0, 0))
    out = (rows, 2 * width // shards)
    return pl.pallas_call(
        functools.partial(pack_pairs_kernel, shards),
        grid_spec=pltpu.PrefetchScalarGridSpec(
            num_scalar_prefetch=1,
            grid=(1,),
            in_specs=[spec, spec],
            out_specs=[pl.BlockSpec(out, lambda k, *_: (0, 0))] * shards,
        ),
        out_shape=[jax.ShapeDtypeStruct(out, keys.dtype)] * shards,
    )(mine, keys, values)


def pack_queries_kernel(slots, halves, mine, picked_ref, query_ref, *outs):
    shards = len(slots)
    rows = query_ref.shape[0]
    half = rows // halves
    width = query_ref.shape[1] // shards
    packed, outs = outs[: halves * shards], outs[halves * shards :]
    place_refs, (order_ref, count_ref) = outs[:halves], outs[halves:]
    me = mine[0]
    across = lax.broadcasted_iota(jnp.int32, (rows, rows), 1)
    down = lax.broadcasted_iota(jnp.int32, (rows, rows), 0)
    up_to = jnp.where(down <= across, 1.0, 0.0).astype(jnp.bfloat16)
    picked = picked_ref[...]
    seen = jnp.dot(picked.astype(jnp.bfloat16), up_to, preferred_element_type=jnp.float32).astype(jnp.int32)
    count = seen[:, rows - 1 : rows]
    row_ids = lax.broadcasted_iota(jnp.int32, seen.shape, 1)
    slot = jnp.where(picked > 0, seen - 1, count + row_ids - seen)
    count_ref[...] = jnp.broadcast_to(jnp.max(count, axis=0, keepdims=True), count_ref.shape).astype(jnp.float32)
    ids = row_ids.astype(jnp.bfloat16)
    for s in range(shards):
        shard = lax.rem(me - s + shards, shards)
        mine_slot = slot[0:1]
        for other in range(1, shards):
            mine_slot = jnp.where(shard == other, slot[other : other + 1], mine_slot)
        at_slot = jnp.where(mine_slot == down, 1.0, 0.0).astype(jnp.bfloat16)
        rows_at = lax.dot_general(ids, at_slot, (((1,), (1,)), ((), ())), preferred_element_type=jnp.float32)
        for h in range(halves):
            here = rows_at[0:1, h * half : (h + 1) * half]
            place_refs[h][slots.index(s)] = here.astype(jnp.int32) + shard * rows
        if s == 0:
            order_ref[...] = at_slot
    for s in range(shards):
        columns = pl.ds(pl.multiple_of(lax.rem(me + s, shards) * width, width), width)
        ordered = jnp.dot(order_ref[...], query_ref[:, columns], preferred_element_type=jnp.float32)
        ordered = ordered.astype(jnp.bfloat16)
        for h in range(halves):
            packed[h * shards + s][...] = ordered[h * half : (h + 1) * half]


def pack_queries(mine, picked, queries, slots, halves):
    shards = len(slots)
    rows, width = queries.shape
    packed = (rows // halves, width // shards)
    shapes = [jax.ShapeDtypeStruct(packed, jnp.bfloat16)] * (halves * shards)
    shapes += [jax.ShapeDtypeStruct((shards, 1, rows // halves), jnp.int32)] * halves
    shapes += [jax.ShapeDtypeStruct((rows, rows), jnp.bfloat16), jax.ShapeDtypeStruct((8, 128), jnp.float32)]

    def whole(shape):
        return pl.BlockSpec(shape, lambda k, *_: (0,) * len(shape))

    got = pl.pallas_call(
        functools.partial(pack_queries_kernel, slots, halves),
        grid_spec=pltpu.PrefetchScalarGridSpec(
            num_scalar_prefetch=1,
            grid=(1,),
            in_specs=[whole(picked.shape), whole(queries.shape)],
            out_specs=[whole(shape.shape) for shape in shapes],
        ),
        out_shape=shapes,
    )(mine, picked, queries)
    packed, got = got[: halves * shards], got[halves * shards :]
    return [packed[h * shards : (h + 1) * shards] for h in range(halves)], got[:halves], *got[halves:]


def on_device(
    hidden_in,
    queries,
    keys,
    values,
    block_order,
    routes,
    out_weight,
    norm_gain,
    router_weight,
    gate_weight,
    up_weight,
    down_weight,
):
    shards = lax.axis_size("tp")
    blocks = lax.axis_size("ctx")
    me = lax.axis_index("tp")
    rows, model = hidden_in.shape
    block_rows = rows * shards
    per_device = HEADS // shards
    grouping = HEADS // KV_HEADS
    repeat_by = max(1, grouping // per_device)
    pairs = max(1, per_device // grouping)
    sharing = per_device // pairs
    half = rows // 2 if rows % 32 == 0 else rows
    halves = rows // half
    line = shards <= LINE
    pieces = 2 if line else 1
    cuts = [slice(c * (model // pieces), (c + 1) * (model // pieces)) for c in range(pieces)]
    slots = [s for s in range(1, shards, 2)] + [s for s in range(2, shards, 2)] + [0]
    shard_of = lax.rem(me - jnp.arange(shards, dtype=jnp.int32) + shards, shards)

    def shift(parts):
        moves = [[(i, (i + s) % shards) for i in range(shards)] for s in range(shards)]
        return [parts[0]] + [lax.ppermute(parts[s], "tp", moves[s]) for s in range(1, shards)]

    def exchange(source):
        got = lax.all_to_all(source, "tp", split_axis=1, concat_axis=0, tiled=True)
        got = got.reshape(shards, rows, source.shape[2])
        return [lax.dynamic_index_in_dim(got, shard_of[s], 0, keepdims=False) for s in range(shards)]

    def rights(count):
        return [(i, i + 1) for i in range(count)]

    def lefts(count):
        return [(i, i - 1) for i in range(shards - count, shards)]

    def reduce_line(pieces_terms):
        if not line:
            by_shard = [jnp.take(jnp.stack(terms), shard_of, axis=0).reshape(-1, terms[0].shape[1]) for terms in pieces_terms]
            return [
                lax.psum_scatter(term, "tp", scatter_dimension=0, tiled=True).astype(jnp.float32) for term in by_shard
            ], None
        got = [None] * len(pieces_terms)
        marks = []
        for s in range(1, shards):
            for c, terms in enumerate(pieces_terms):
                if got[c] is None:
                    sent = (terms[s], terms[shards - s])
                else:
                    arrived = got[c]
                    sent = (terms[s] + arrived[0], terms[shards - s] + arrived[1])
                right = lax.ppermute(sent[0], "tp", rights(s))
                left = lax.ppermute(sent[1], "tp", lefts(s))
                got[c] = lax.optimization_barrier((right, left))
            marks.append(got[0])
        return [
            terms[0].astype(jnp.float32) + right.astype(jnp.float32) + left.astype(jnp.float32)
            for terms, (right, left) in zip(pieces_terms, got)
        ], marks

    def gather_line(source, terms=None):
        if not line:
            got = lax.all_gather(source, "tp", axis=0)
            return [[jnp.take(got, shard_of, axis=0).reshape(shards * half, -1)]], None
        first_right = lax.ppermute(source, "tp", rights(shards - 1))
        first_left = lax.ppermute(source, "tp", lefts(shards - 1))
        first_right, first_left = lax.optimization_barrier((first_right, first_left))
        got = [(first_right[:, cut], first_left[:, cut]) for cut in cuts]
        from_left, from_right = [], []
        for s in range(2, shards):
            if terms is None:
                sent = got
                to_right = [(i, i + 1) for i in range(s - 1, shards - 1)]
                to_left = [(i, i - 1) for i in range(1, shards - s + 1)]
            else:
                sent = [
                    (
                        jnp.where(me >= s - 1, right, right + term[s - 1]),
                        jnp.where(me <= shards - s, left, left + term[shards - s + 1]),
                    )
                    for (right, left), term in zip(got, terms)
                ]
                to_right, to_left = rights(shards - 1), lefts(shards - 1)
            from_left.append([right for right, _ in sent])
            from_right.append([left for _, left in sent])
            got = [
                lax.optimization_barrier((lax.ppermute(right, "tp", to_right), lax.ppermute(left, "tp", to_left)))
                for right, left in sent
            ]
        from_left.append([right for right, _ in got])
        from_right.append([left for _, left in got])
        total = None
        if terms is not None:
            right = jnp.concatenate([right + term[shards - 1] for (right, _), term in zip(got, terms)], axis=1)
            left = jnp.concatenate([left + term[1] for (_, left), term in zip(got, terms)], axis=1)
            right = lax.ppermute(right, "tp", rights(shards - 1)).astype(jnp.float32)
            left = lax.ppermute(left, "tp", lefts(shards - 1)).astype(jnp.float32)
            total = jnp.concatenate([term[0] for term in terms], axis=1).astype(jnp.float32) + right + left
        return [[source]] + from_left + from_right, total

    picked = ((routes[:, 0] == 0) | (routes[:, 1] == 0)).reshape(shards, rows)
    if line:
        sent_pairs = pack_pairs(me[None], keys, values, shards)
        own_pairs = jnp.concatenate(shift(sent_pairs), axis=0)
        picked, _ = lax.optimization_barrier((picked.astype(jnp.int32), sent_pairs))
        packed, places, order, fullest = pack_queries(me[None], picked, queries, slots, halves)
        asked = [shift(packed[0])]
    else:

        def spread(source):
            widened = jnp.repeat(source.reshape(rows, KV_HEADS, HD), repeat_by, axis=1)
            return widened.reshape(rows, shards, pairs * HD)

        own_pairs = exchange(jnp.concatenate([spread(keys), spread(values)], axis=2))
        own_pairs = jnp.concatenate(own_pairs, axis=0)
        row_ids = jnp.arange(rows, dtype=jnp.int32)
        seen = jnp.cumsum(picked.astype(jnp.int32), axis=1)
        slot = jnp.where(picked, seen - 1, seen[:, -1:] + row_ids[None, :] - seen)
        at_slot = slot[:, None, :] == row_ids[None, :, None]
        row_of_slot = jnp.sum(jnp.where(at_slot, row_ids[None, None, :], 0), axis=2)
        places = row_of_slot + jnp.arange(shards, dtype=jnp.int32)[:, None] * rows
        places = [jnp.stack([jnp.take(places, shard_of[s], axis=0) for s in slots])[:, None, :]]
        order = lax.dynamic_index_in_dim(at_slot, me, 0, keepdims=False).astype(jnp.bfloat16)
        ordered = jnp.dot(order, queries, preferred_element_type=jnp.float32).astype(jnp.bfloat16)
        asked = [exchange(ordered.reshape(rows, shards, per_device * HD))]

    pair_list, held = [own_pairs], [[0]]
    offset = blocks // 2
    while offset >= 1:
        pair_list += [lax.ppermute(part, "ctx", [(i, i ^ offset) for i in range(blocks)]) for part in pair_list]
        held += [[other ^ offset for other in group] for group in held]
        if line and len(pair_list) == 2:
            pair_list[1], asked[0] = lax.optimization_barrier((pair_list[1], asked[0]))
        offset //= 2

    def reorder(source):
        return jnp.dot(order, source, preferred_element_type=jnp.float32).astype(jnp.bfloat16)

    def restore(parts):
        whole = jnp.concatenate(parts, axis=0) if len(parts) > 1 else parts[0]
        return lax.dot_general(
            order, whole, (((0,), (0,)), ((), ())), preferred_element_type=jnp.float32
        ).astype(jnp.bfloat16)

    mine = lax.axis_index("ctx").astype(jnp.int32)[None]
    expert_ids = jnp.arange(router_weight.shape[1], dtype=jnp.int32)

    def project(which):
        terms = attend(
            block_order,
            jnp.stack([lax.axis_index("ctx"), me]).astype(jnp.int32),
            [asked[which][s] for s in slots],
            places[which],
            pair_list,
            held,
            pairs,
            sharing,
            block_rows,
            out_weight,
            pieces,
            line,
        )
        return [[term[slots.index(s)] for s in range(shards)] for term in terms]

    def finish(which, head_sums):
        base = hidden[which * half : (which + 1) * half].astype(jnp.float32)
        return jnp.concatenate(
            [(base[:, cut] + head_sum).astype(jnp.bfloat16) for cut, head_sum in zip(cuts, head_sums)], axis=1
        )

    def normalise(attended):
        widened = attended.astype(jnp.float32)
        return (
            widened * lax.rsqrt(jnp.mean(widened * widened, axis=1, keepdims=True) + 1e-05) * norm_gain
        ).astype(jnp.bfloat16)

    def share_of(which, normed):
        logits = jnp.dot(normed, router_weight, preferred_element_type=jnp.float32)
        named = my_routes[which * half : (which + 1) * half]
        first = jnp.sum(jnp.where(named[:, 0:1] == expert_ids[None, :], logits, 0.0), axis=1)
        second = jnp.sum(jnp.where(named[:, 1:2] == expert_ids[None, :], logits, 0.0), axis=1)
        share = jnp.where(named[:, 0] == 0, 1.0 / (1.0 + jnp.exp(second - first)), 0.0)
        return share + jnp.where(named[:, 1] == 0, 1.0 / (1.0 + jnp.exp(first - second)), 0.0)

    def expert(which, normed, sources, beside=None):
        terms = expert_rows(me[None], sources, gate_weight, up_weight, down_weight, shards, pieces, line)
        if beside is not None:
            terms, beside = lax.optimization_barrier((terms, beside))
        sums, marks = reduce_line(terms)
        if beside is not None:
            beside = (beside[0], lax.optimization_barrier((beside[1], marks[0]))[0][0, 0] > half)
        if line:
            normed, _ = lax.optimization_barrier((normed, marks[0]))
        share = share_of(which, normed)
        parts = [(total * share[:, None]).astype(jnp.bfloat16) for total in sums]
        return jnp.concatenate(parts, axis=1), beside

    def late_expert(source):
        normed = normalise(source)
        return expert(1, normed, gather_line(normed)[0])[0]

    terms = project(0)
    if halves > 1:
        asked.append(shift(packed[1]))
        terms, asked[1] = lax.optimization_barrier((terms, asked[1]))
    totals, marks = reduce_line(terms)
    if line:
        hidden_in, order, _ = lax.optimization_barrier((hidden_in, order, marks[0]))
    hidden = reorder(hidden_in)
    my_routes = lax.dynamic_slice_in_dim(routes, me * rows, rows, 0).astype(jnp.bfloat16)
    my_routes = reorder(my_routes).astype(jnp.int32)
    first_half = finish(0, totals)
    normed = normalise(first_half)
    if halves == 1:
        return (restore([first_half]), restore([expert(0, normed, gather_line(normed)[0])[0]]))
    asked[1], _ = lax.optimization_barrier((asked[1], normed))
    sources, second_sum = gather_line(normed, project(1))
    second_half = (hidden[half:].astype(jnp.float32) + second_sum).astype(jnp.bfloat16)
    part, (second_half, crowded) = expert(0, normed, sources, (second_half, fullest))
    part, late, crowded = lax.optimization_barrier((part, second_half, crowded))
    late = lax.cond(crowded, late_expert, jnp.zeros_like, late)
    return (restore([first_half, second_half]), restore([part, late]))


def solution(mesh):
    return jax.shard_map(
        on_device,
        mesh=mesh,
        in_specs=(
            P(("req", "ctx", "tp"), None),
            P(("req", "ctx", "tp"), None),
            P(("req", "ctx", "tp"), None),
            P(("req", "ctx", "tp"), None),
            P("req"),
            P(("req", "ctx"), None),
            P("tp", None),
            P(),
            P(),
            P(None, "tp"),
            P(None, "tp"),
            P("tp", None),
        ),
        out_specs=(P(("req", "ctx", "tp"), None), P(("req", "ctx", "tp"), None)),
        check_vma=False,
    )
```

```python
import functools
import math

import jax
import jax.numpy as jnp
from jax import lax
from jax.experimental import pallas as pl
from jax.experimental.pallas import tpu as pltpu
from jax.sharding import PartitionSpec as P

HEADS = 32
KV_HEADS = 8
HD = 128
FACTOR = math.log2(math.e) / math.sqrt(HD)
LINE = 4
SUM_ROWS = 16
TILE = 256
VMEM_HELD = 21 * 1024 * 1024
VMEM_LARGE = 28 * 1024 * 1024


def attention_kernel(slots, together, held, pairs, sharing, block_rows, plan, *refs):
    pieces, grouped = plan
    (order, mine), refs = refs[:2], refs[2:]
    query_refs, refs = refs[:slots], refs[slots:]
    place_ref, refs = refs[0], refs[1:]
    pair_refs, weight, refs = refs[: len(held)], refs[len(held)], refs[len(held) + 1 :]
    outs, refs = refs[: pieces * (slots if grouped else 1)], refs[pieces * (slots if grouped else 1) :]
    query_ref, key_ref, value_ref, top_ref, total_ref, head_ref, weight_ref, arrived = refs
    half = query_refs[0].shape[0]
    step = pl.program_id(0)
    me = mine[0]
    my_block = order[me]
    blocks = [(ref, index, offset) for ref, group in zip(pair_refs, held) for index, offset in enumerate(group)]
    weight_copy = pltpu.make_async_copy(weight, weight_ref, arrived)

    @pl.when(step == 0)
    def _():
        weight_copy.start()
        value_ref[:, :, HD:, :] = jnp.ones((len(blocks), pairs, SUM_ROWS, block_rows), jnp.bfloat16)

    for at, (ref, index, offset) in enumerate(blocks):

        @pl.when((step == 0) & (order[me ^ offset] <= my_block))
        def _():
            for p in range(pairs):
                rows = slice(index * block_rows, (index + 1) * block_rows)
                key_ref[at, p] = ref[rows, p * HD : (p + 1) * HD]
                value_ref[at, p, :HD, :] = ref[rows, (pairs + p) * HD : (pairs + p + 1) * HD].T

    for at in range(slots):

        @pl.when(step == at // together)
        def _():
            for p in range(pairs):
                for g in range(sharing):
                    column = (p * sharing + g) * HD
                    row = (at % together * sharing + g) * half
                    query_ref[p, row : row + half, :] = query_refs[at][:, column : column + HD]

    def scores_of(p, at):
        return lax.dot_general(
            key_ref[at, p], query_ref[p], (((1,), (1,)), ((), ())), preferred_element_type=jnp.float32
        )

    def mixed_of(p, at, weights):
        return jnp.dot(value_ref[at, p], weights, preferred_element_type=jnp.float32)

    place = jnp.concatenate([place_ref[i] for i in range(together) for _ in range(sharing)], axis=1)
    rows = block_rows // slots
    down = lax.broadcasted_iota(jnp.int32, (rows, place.shape[1]), 0)
    visible = jnp.concatenate(
        [down <= place - lax.rem(mine[1] - s + slots, slots) * rows for s in range(slots)], axis=0
    )
    for p in range(pairs):
        scores = jnp.where(visible, scores_of(p, 0), -1e30)
        top = jnp.max(scores, axis=0, keepdims=True)
        weights = jnp.exp2((scores - top) * FACTOR).astype(jnp.bfloat16)
        top_ref[p, 0:1, :] = top
        total_ref[p] = mixed_of(p, 0, weights)

    @pl.loop(1, len(blocks))
    def _(at):
        offset = blocks[1][2] if len(blocks) > 1 else 0
        for other in range(2, len(blocks)):
            offset = jnp.where(at == other, blocks[other][2], offset)

        @pl.when(order[me ^ offset] < my_block)
        def _():
            for p in range(pairs):
                top = top_ref[p, 0:1, :]
                scores = scores_of(p, at)
                raised = jnp.maximum(top, jnp.max(scores, axis=0, keepdims=True))
                weights = jnp.exp2((scores - raised) * FACTOR).astype(jnp.bfloat16)
                top_ref[p, 0:1, :] = raised
                total_ref[p] = total_ref[p] * jnp.exp2((top - raised) * FACTOR) + mixed_of(p, at, weights)

    for p in range(pairs):
        mixed = (total_ref[p, :HD, :] / total_ref[p, HD : HD + 1, :]).T.astype(jnp.bfloat16)
        for i in range(together):
            for g in range(sharing):
                column = (p * sharing + g) * HD
                row = (i * sharing + g) * half
                at = pl.multiple_of((step * together + i) * half, half)
                head_ref[pl.ds(at, half), column : column + HD] = mixed[row : row + half]

    @pl.when(step == pl.num_programs(0) - 1)
    def _():
        weight_copy.wait()
        width = weight.shape[1] // pieces
        tile = 2 * TILE
        for c in range(pieces):

            @pl.loop(0, width // tile)
            def _(n):
                columns = pl.ds(pl.multiple_of(c * width + n * tile, tile), tile)
                value = jnp.dot(head_ref[...], weight_ref[:, columns], preferred_element_type=jnp.float32)
                share_out(outs[c * len(outs) // pieces :], pl.ds(pl.multiple_of(n * tile, tile), tile), value)


def share_out(outs, columns, value):
    rows = outs[0].shape[0]
    for g in range(value.shape[0] // rows):
        outs[g][:, columns] = value[g * rows : (g + 1) * rows].astype(jnp.bfloat16)


def piece_shapes(rows, width, slots, pieces, grouped):
    return [jax.ShapeDtypeStruct((rows // slots if grouped else rows, width // pieces), jnp.bfloat16)] * (
        pieces * (slots if grouped else 1)
    )


def by_piece(outs, slots, pieces, grouped):
    if grouped:
        return [outs[c * slots : (c + 1) * slots] for c in range(pieces)]
    return [[out[s * (out.shape[0] // slots) : (s + 1) * (out.shape[0] // slots)] for s in range(slots)] for out in outs]


def attend(order, mine, queries, places, pair_list, held, pairs, sharing, block_rows, weight, pieces, grouped):
    slots = len(queries)
    half, width = queries[0].shape
    together = 2 if slots <= LINE else 1
    tall = together * sharing * half
    blocks = sum(len(group) for group in held)
    count = blocks * block_rows
    shapes = piece_shapes(slots * half, weight.shape[1], slots, pieces, grouped)
    kernel = functools.partial(
        attention_kernel, slots, together, held, pairs, sharing, block_rows, (pieces, grouped)
    )
    outs = pl.pallas_call(
        kernel,
        grid_spec=pltpu.PrefetchScalarGridSpec(
            num_scalar_prefetch=2,
            grid=(slots // together,),
            in_specs=[pl.BlockSpec((half, width), lambda s, *_: (0, 0))] * slots
            + [pl.BlockSpec((together, 1, half), lambda s, *_: (s, 0, 0))]
            + [pl.BlockSpec(pair.shape, lambda s, *_: (0, 0)) for pair in pair_list]
            + [pl.BlockSpec(memory_space=pl.ANY)],
            out_specs=[pl.BlockSpec(shape.shape, lambda s, *_: (0, 0)) for shape in shapes],
            scratch_shapes=[
                pltpu.VMEM((pairs, tall, HD), jnp.bfloat16),
                pltpu.VMEM((blocks, pairs, block_rows, HD), jnp.bfloat16),
                pltpu.VMEM((blocks, pairs, HD + SUM_ROWS, block_rows), jnp.bfloat16),
                pltpu.VMEM((pairs, 8, tall), jnp.float32),
                pltpu.VMEM((pairs, HD + SUM_ROWS, tall), jnp.float32),
                pltpu.VMEM((slots * half, width), jnp.bfloat16),
                pltpu.VMEM(weight.shape, weight.dtype),
                pltpu.SemaphoreType.DMA,
            ],
        ),
        out_shape=shapes,
        compiler_params=pltpu.CompilerParams(vmem_limit_bytes=VMEM_HELD),
        cost_estimate=pl.CostEstimate(
            flops=40 * slots * half * width * count,
            bytes_accessed=2 * (2 * slots * half * width + count * 2 * pairs * HD + weight.size),
            transcendentals=slots * half * width // HD * count,
        ),
    )(order, mine, *queries, places, *pair_list, weight)
    return by_piece(outs, slots, pieces, grouped)


def expert_kernel(plan, pieces, *refs):
    mine, refs = refs[0], refs[1:]
    sources = []
    for count in plan:
        sources.append(refs[:count])
        refs = refs[count:]
    gate_weight, up_weight, down_weights, refs = refs[0], refs[1], refs[2:4], refs[4:]
    outs, (chosen, acts) = refs[:-2], refs[-2:]
    step = pl.program_id(0)
    tile = gate_weight.shape[1]
    first = acts.shape[1] // tile

    def place(s, source):
        rows, width = source[0].shape
        for c, ref in enumerate(source):
            chosen[s * rows : (s + 1) * rows, c * width : (c + 1) * width] = ref[...]

    @pl.when(step == 0)
    def _():
        place(0, sources[0])
        for s in range(1, (len(plan) + 1) // 2):
            right, left = sources[s], sources[len(plan) - s]

            @pl.when(mine[0] >= s)
            def _():
                place(s, right)

            @pl.when(mine[0] < s)
            def _():
                place(s, left)

    @pl.when(step < first)
    def _():
        gate = jnp.dot(chosen[...], gate_weight[...], preferred_element_type=jnp.float32)
        upward = jnp.dot(chosen[...], up_weight[...], preferred_element_type=jnp.float32)
        columns = pl.ds(pl.multiple_of(step * tile, tile), tile)
        acts[:, columns] = (gate / (1.0 + jnp.exp(-gate)) * upward).astype(jnp.bfloat16)

    @pl.when(step >= first)
    def _():
        strip = down_weights[0].shape[1]
        pairs = outs[0].shape[1] // (2 * strip)
        for j, down_weight in enumerate(down_weights):
            value = jnp.dot(acts[...], down_weight[...], preferred_element_type=jnp.float32)
            for c in range(pieces):

                @pl.when((step - first) // pairs == c)
                def _():
                    at = (2 * (step - first - c * pairs) + j) * strip
                    share_out(outs[c * len(outs) // pieces :], pl.ds(pl.multiple_of(at, strip), strip), value)


def expert_rows(mine, sources, gate_weight, up_weight, down_weight, slots, pieces, grouped):
    flat = [piece for source in sources for piece in source]
    rows = flat[0].shape[0] * ((len(sources) + 1) // 2)
    depth, width = gate_weight.shape
    tile, strip = min(TILE, width), 2 * TILE
    first = width // tile
    shapes = piece_shapes(rows, depth, slots, pieces, grouped)
    in_place = pl.BlockSpec(memory_space=pltpu.VMEM)
    weight = pl.BlockSpec((depth, tile), lambda n, *_: (0, jnp.minimum(n, first - 1)))
    outs = pl.pallas_call(
        functools.partial(expert_kernel, [len(source) for source in sources], pieces),
        grid_spec=pltpu.PrefetchScalarGridSpec(
            num_scalar_prefetch=1,
            grid=(first + depth // (2 * strip),),
            in_specs=[in_place] * len(flat)
            + [weight, weight]
            + [
                pl.BlockSpec((width, strip), functools.partial(lambda j, n, *_: (0, 2 * jnp.maximum(n - first, 0) + j), j))
                for j in range(2)
            ],
            out_specs=[in_place] * len(shapes),
            scratch_shapes=[pltpu.VMEM((rows, depth), jnp.bfloat16), pltpu.VMEM((rows, width), jnp.bfloat16)],
        ),
        out_shape=shapes,
        compiler_params=pltpu.CompilerParams(vmem_limit_bytes=VMEM_LARGE),
        cost_estimate=pl.CostEstimate(
            flops=6 * rows * depth * width, bytes_accessed=6 * depth * width, transcendentals=rows * width
        ),
    )(mine, *flat, gate_weight, up_weight, down_weight, down_weight)
    return by_piece(outs, slots, pieces, grouped)


def pack_pairs_kernel(shards, mine, keys_ref, values_ref, *outs):
    width = keys_ref.shape[1] // shards
    for s in range(shards):
        columns = pl.ds(pl.multiple_of(lax.rem(mine[0] + s, shards) * width, width), width)
        outs[s][:, :width] = keys_ref[:, columns]
        outs[s][:, width:] = values_ref[:, columns]


def pack_pairs(mine, keys, values, shards):
    rows, width = keys.shape
    spec = pl.BlockSpec((rows, width), lambda k, *_: (0, 0))
    out = (rows, 2 * width // shards)
    return pl.pallas_call(
        functools.partial(pack_pairs_kernel, shards),
        grid_spec=pltpu.PrefetchScalarGridSpec(
            num_scalar_prefetch=1,
            grid=(1,),
            in_specs=[spec, spec],
            out_specs=[pl.BlockSpec(out, lambda k, *_: (0, 0))] * shards,
        ),
        out_shape=[jax.ShapeDtypeStruct(out, keys.dtype)] * shards,
    )(mine, keys, values)


def pack_queries_kernel(slots, halves, mine, picked_ref, query_ref, *outs):
    shards = len(slots)
    rows = query_ref.shape[0]
    half = rows // halves
    width = query_ref.shape[1] // shards
    packed, outs = outs[: halves * shards], outs[halves * shards :]
    place_refs, (order_ref, count_ref) = outs[:halves], outs[halves:]
    me = mine[0]
    across = lax.broadcasted_iota(jnp.int32, (rows, rows), 1)
    down = lax.broadcasted_iota(jnp.int32, (rows, rows), 0)
    up_to = jnp.where(down <= across, 1.0, 0.0).astype(jnp.bfloat16)
    picked = picked_ref[...]
    seen = jnp.dot(picked.astype(jnp.bfloat16), up_to, preferred_element_type=jnp.float32).astype(jnp.int32)
    count = seen[:, rows - 1 : rows]
    row_ids = lax.broadcasted_iota(jnp.int32, seen.shape, 1)
    slot = jnp.where(picked > 0, seen - 1, count + row_ids - seen)
    count_ref[...] = jnp.broadcast_to(jnp.max(count, axis=0, keepdims=True), count_ref.shape).astype(jnp.float32)
    ids = row_ids.astype(jnp.bfloat16)
    for s in range(shards):
        shard = lax.rem(me - s + shards, shards)
        mine_slot = slot[0:1]
        for other in range(1, shards):
            mine_slot = jnp.where(shard == other, slot[other : other + 1], mine_slot)
        at_slot = jnp.where(mine_slot == down, 1.0, 0.0).astype(jnp.bfloat16)
        rows_at = lax.dot_general(ids, at_slot, (((1,), (1,)), ((), ())), preferred_element_type=jnp.float32)
        for h in range(halves):
            here = rows_at[0:1, h * half : (h + 1) * half]
            place_refs[h][slots.index(s)] = here.astype(jnp.int32) + shard * rows
        if s == 0:
            order_ref[...] = at_slot
    for s in range(shards):
        columns = pl.ds(pl.multiple_of(lax.rem(me + s, shards) * width, width), width)
        ordered = jnp.dot(order_ref[...], query_ref[:, columns], preferred_element_type=jnp.float32)
        ordered = ordered.astype(jnp.bfloat16)
        for h in range(halves):
            packed[h * shards + s][...] = ordered[h * half : (h + 1) * half]


def pack_queries(mine, picked, queries, slots, halves):
    shards = len(slots)
    rows, width = queries.shape
    packed = (rows // halves, width // shards)
    shapes = [jax.ShapeDtypeStruct(packed, jnp.bfloat16)] * (halves * shards)
    shapes += [jax.ShapeDtypeStruct((shards, 1, rows // halves), jnp.int32)] * halves
    shapes += [jax.ShapeDtypeStruct((rows, rows), jnp.bfloat16), jax.ShapeDtypeStruct((8, 128), jnp.float32)]

    def whole(shape):
        return pl.BlockSpec(shape, lambda k, *_: (0,) * len(shape))

    got = pl.pallas_call(
        functools.partial(pack_queries_kernel, slots, halves),
        grid_spec=pltpu.PrefetchScalarGridSpec(
            num_scalar_prefetch=1,
            grid=(1,),
            in_specs=[whole(picked.shape), whole(queries.shape)],
            out_specs=[whole(shape.shape) for shape in shapes],
        ),
        out_shape=shapes,
    )(mine, picked, queries)
    packed, got = got[: halves * shards], got[halves * shards :]
    return [packed[h * shards : (h + 1) * shards] for h in range(halves)], got[:halves], *got[halves:]


def on_device(
    hidden_in,
    queries,
    keys,
    values,
    block_order,
    routes,
    out_weight,
    norm_gain,
    router_weight,
    gate_weight,
    up_weight,
    down_weight,
):
    shards = lax.axis_size("tp")
    blocks = lax.axis_size("ctx")
    me = lax.axis_index("tp")
    rows, model = hidden_in.shape
    block_rows = rows * shards
    per_device = HEADS // shards
    grouping = HEADS // KV_HEADS
    repeat_by = max(1, grouping // per_device)
    pairs = max(1, per_device // grouping)
    sharing = per_device // pairs
    half = rows // 2 if rows % 32 == 0 else rows
    halves = rows // half
    line = shards <= LINE
    pieces = 2 if line else 1
    cuts = [slice(c * (model // pieces), (c + 1) * (model // pieces)) for c in range(pieces)]
    slots = [s for s in range(1, shards, 2)] + [s for s in range(2, shards, 2)] + [0]
    shard_of = lax.rem(me - jnp.arange(shards, dtype=jnp.int32) + shards, shards)

    def shift(parts):
        moves = [[(i, (i + s) % shards) for i in range(shards)] for s in range(shards)]
        return [parts[0]] + [lax.ppermute(parts[s], "tp", moves[s]) for s in range(1, shards)]

    def exchange(source):
        got = lax.all_to_all(source, "tp", split_axis=1, concat_axis=0, tiled=True)
        got = got.reshape(shards, rows, source.shape[2])
        return [lax.dynamic_index_in_dim(got, shard_of[s], 0, keepdims=False) for s in range(shards)]

    def rights(count):
        return [(i, i + 1) for i in range(count)]

    def lefts(count):
        return [(i, i - 1) for i in range(shards - count, shards)]

    def reduce_line(pieces_terms):
        if not line:
            by_shard = [jnp.take(jnp.stack(terms), shard_of, axis=0).reshape(-1, terms[0].shape[1]) for terms in pieces_terms]
            return [
                lax.psum_scatter(term, "tp", scatter_dimension=0, tiled=True).astype(jnp.float32) for term in by_shard
            ], None
        got = [None] * len(pieces_terms)
        marks = []
        for s in range(1, shards):
            for c, terms in enumerate(pieces_terms):
                if got[c] is None:
                    sent = (terms[s], terms[shards - s])
                else:
                    arrived = got[c]
                    sent = (terms[s] + arrived[0], terms[shards - s] + arrived[1])
                right = lax.ppermute(sent[0], "tp", rights(s))
                left = lax.ppermute(sent[1], "tp", lefts(s))
                got[c] = lax.optimization_barrier((right, left))
            marks.append(got[0])
        return [
            terms[0].astype(jnp.float32) + right.astype(jnp.float32) + left.astype(jnp.float32)
            for terms, (right, left) in zip(pieces_terms, got)
        ], marks

    def gather_line(source, terms=None):
        if not line:
            got = lax.all_gather(source, "tp", axis=0)
            return [[jnp.take(got, shard_of, axis=0).reshape(shards * half, -1)]], None
        first_right = lax.ppermute(source, "tp", rights(shards - 1))
        first_left = lax.ppermute(source, "tp", lefts(shards - 1))
        first_right, first_left = lax.optimization_barrier((first_right, first_left))
        got = [(first_right[:, cut], first_left[:, cut]) for cut in cuts]
        from_left, from_right = [], []
        for s in range(2, shards):
            if terms is None:
                sent = got
                to_right = [(i, i + 1) for i in range(s - 1, shards - 1)]
                to_left = [(i, i - 1) for i in range(1, shards - s + 1)]
            else:
                sent = [
                    (
                        jnp.where(me >= s - 1, right, right + term[s - 1]),
                        jnp.where(me <= shards - s, left, left + term[shards - s + 1]),
                    )
                    for (right, left), term in zip(got, terms)
                ]
                to_right, to_left = rights(shards - 1), lefts(shards - 1)
            from_left.append([right for right, _ in sent])
            from_right.append([left for _, left in sent])
            got = [
                lax.optimization_barrier((lax.ppermute(right, "tp", to_right), lax.ppermute(left, "tp", to_left)))
                for right, left in sent
            ]
        from_left.append([right for right, _ in got])
        from_right.append([left for _, left in got])
        total = None
        if terms is not None:
            right = jnp.concatenate([right + term[shards - 1] for (right, _), term in zip(got, terms)], axis=1)
            left = jnp.concatenate([left + term[1] for (_, left), term in zip(got, terms)], axis=1)
            right = lax.ppermute(right, "tp", rights(shards - 1)).astype(jnp.float32)
            left = lax.ppermute(left, "tp", lefts(shards - 1)).astype(jnp.float32)
            total = jnp.concatenate([term[0] for term in terms], axis=1).astype(jnp.float32) + right + left
        return [[source]] + from_left + from_right, total

    picked = ((routes[:, 0] == 0) | (routes[:, 1] == 0)).reshape(shards, rows)
    if line:
        sent_pairs = pack_pairs(me[None], keys, values, shards)
        own_pairs = jnp.concatenate(shift(sent_pairs), axis=0)
        picked, _ = lax.optimization_barrier((picked.astype(jnp.int32), sent_pairs))
        packed, places, order, fullest = pack_queries(me[None], picked, queries, slots, halves)
        asked = [shift(packed[0])]
    else:

        def spread(source):
            widened = jnp.repeat(source.reshape(rows, KV_HEADS, HD), repeat_by, axis=1)
            return widened.reshape(rows, shards, pairs * HD)

        own_pairs = exchange(jnp.concatenate([spread(keys), spread(values)], axis=2))
        own_pairs = jnp.concatenate(own_pairs, axis=0)
        row_ids = jnp.arange(rows, dtype=jnp.int32)
        seen = jnp.cumsum(picked.astype(jnp.int32), axis=1)
        slot = jnp.where(picked, seen - 1, seen[:, -1:] + row_ids[None, :] - seen)
        at_slot = slot[:, None, :] == row_ids[None, :, None]
        row_of_slot = jnp.sum(jnp.where(at_slot, row_ids[None, None, :], 0), axis=2)
        places = row_of_slot + jnp.arange(shards, dtype=jnp.int32)[:, None] * rows
        places = [jnp.stack([jnp.take(places, shard_of[s], axis=0) for s in slots])[:, None, :]]
        order = lax.dynamic_index_in_dim(at_slot, me, 0, keepdims=False).astype(jnp.bfloat16)
        ordered = jnp.dot(order, queries, preferred_element_type=jnp.float32).astype(jnp.bfloat16)
        asked = [exchange(ordered.reshape(rows, shards, per_device * HD))]

    pair_list, held = [own_pairs], [[0]]
    offset = blocks // 2
    while offset >= 1:
        pair_list += [lax.ppermute(part, "ctx", [(i, i ^ offset) for i in range(blocks)]) for part in pair_list]
        held += [[other ^ offset for other in group] for group in held]
        if line and len(pair_list) == 2:
            pair_list[1], asked[0] = lax.optimization_barrier((pair_list[1], asked[0]))
        offset //= 2

    def reorder(source):
        return jnp.dot(order, source, preferred_element_type=jnp.float32).astype(jnp.bfloat16)

    def restore(parts):
        whole = jnp.concatenate(parts, axis=0) if len(parts) > 1 else parts[0]
        return lax.dot_general(
            order, whole, (((0,), (0,)), ((), ())), preferred_element_type=jnp.float32
        ).astype(jnp.bfloat16)

    mine = lax.axis_index("ctx").astype(jnp.int32)[None]
    expert_ids = jnp.arange(router_weight.shape[1], dtype=jnp.int32)

    def project(which):
        terms = attend(
            block_order,
            jnp.stack([lax.axis_index("ctx"), me]).astype(jnp.int32),
            [asked[which][s] for s in slots],
            places[which],
            pair_list,
            held,
            pairs,
            sharing,
            block_rows,
            out_weight,
            pieces,
            line,
        )
        return [[term[slots.index(s)] for s in range(shards)] for term in terms]

    def finish(which, head_sums):
        base = hidden[which * half : (which + 1) * half].astype(jnp.float32)
        return jnp.concatenate(
            [(base[:, cut] + head_sum).astype(jnp.bfloat16) for cut, head_sum in zip(cuts, head_sums)], axis=1
        )

    def normalise(attended):
        widened = attended.astype(jnp.float32)
        return (
            widened * lax.rsqrt(jnp.mean(widened * widened, axis=1, keepdims=True) + 1e-05) * norm_gain
        ).astype(jnp.bfloat16)

    def share_of(which, normed):
        logits = jnp.dot(normed, router_weight, preferred_element_type=jnp.float32)
        named = my_routes[which * half : (which + 1) * half]
        first = jnp.sum(jnp.where(named[:, 0:1] == expert_ids[None, :], logits, 0.0), axis=1)
        second = jnp.sum(jnp.where(named[:, 1:2] == expert_ids[None, :], logits, 0.0), axis=1)
        share = jnp.where(named[:, 0] == 0, 1.0 / (1.0 + jnp.exp(second - first)), 0.0)
        return share + jnp.where(named[:, 1] == 0, 1.0 / (1.0 + jnp.exp(first - second)), 0.0)

    def expert(which, normed, sources, beside=None):
        terms = expert_rows(me[None], sources, gate_weight, up_weight, down_weight, shards, pieces, line)
        if beside is not None:
            terms, beside = lax.optimization_barrier((terms, beside))
        sums, marks = reduce_line(terms)
        if line:
            normed, _ = lax.optimization_barrier((normed, marks[0]))
        share = share_of(which, normed)
        parts = [(total * share[:, None]).astype(jnp.bfloat16) for total in sums]
        return jnp.concatenate(parts, axis=1), beside

    def late_expert(source):
        normed = normalise(source)
        return expert(1, normed, gather_line(normed)[0])[0]

    terms = project(0)
    if halves > 1:
        asked.append(shift(packed[1]))
        terms, asked[1] = lax.optimization_barrier((terms, asked[1]))
    totals, marks = reduce_line(terms)
    if line:
        hidden_in, order, _ = lax.optimization_barrier((hidden_in, order, marks[0]))
    hidden = reorder(hidden_in)
    my_routes = lax.dynamic_slice_in_dim(routes, me * rows, rows, 0).astype(jnp.bfloat16)
    my_routes = reorder(my_routes).astype(jnp.int32)
    first_half = finish(0, totals)
    normed = normalise(first_half)
    if halves == 1:
        return (restore([first_half]), restore([expert(0, normed, gather_line(normed)[0])[0]]))
    asked[1], _ = lax.optimization_barrier((asked[1], normed))
    sources, second_sum = gather_line(normed, project(1))
    second_half = (hidden[half:].astype(jnp.float32) + second_sum).astype(jnp.bfloat16)
    part, second_half = expert(0, normed, sources, second_half)
    part, late = lax.optimization_barrier((part, second_half))
    late = lax.cond(fullest[0, 0] > half, late_expert, jnp.zeros_like, late)
    return (restore([first_half, second_half]), restore([part, late]))


def solution(mesh):
    return jax.shard_map(
        on_device,
        mesh=mesh,
        in_specs=(
            P(("req", "ctx", "tp"), None),
            P(("req", "ctx", "tp"), None),
            P(("req", "ctx", "tp"), None),
            P(("req", "ctx", "tp"), None),
            P("req"),
            P(("req", "ctx"), None),
            P("tp", None),
            P(),
            P(),
            P(None, "tp"),
            P(None, "tp"),
            P("tp", None),
        ),
        out_specs=(P(("req", "ctx", "tp"), None), P(("req", "ctx", "tp"), None)),
        check_vma=False,
    )
```

```python
import functools
import math

import jax
import jax.numpy as jnp
from jax import lax
from jax.experimental import pallas as pl
from jax.experimental.pallas import tpu as pltpu
from jax.sharding import PartitionSpec as P

HEADS = 32
KV_HEADS = 8
HD = 128
FACTOR = math.log2(math.e) / math.sqrt(HD)
LINE = 4
SUM_ROWS = 16
TILE = 256
VMEM_HELD = 21 * 1024 * 1024
VMEM_LARGE = 28 * 1024 * 1024


def attention_kernel(slots, together, held, pairs, sharing, block_rows, plan, *refs):
    pieces, grouped = plan
    (order, mine), refs = refs[:2], refs[2:]
    sent_queries, refs = refs[:slots], refs[slots:]
    place_ref, refs = refs[0], refs[1:]
    sent_pairs, weight, refs = refs[: len(held)], refs[len(held)], refs[len(held) + 1 :]
    outs, refs = refs[: pieces * (slots if grouped else 1)], refs[pieces * (slots if grouped else 1) :]
    query_refs, pair_refs, refs = refs[:slots], refs[slots : slots + len(held)], refs[slots + len(held) :]
    query_ref, key_ref, value_ref, top_ref, total_ref, head_ref, weight_ref, arrived, here = refs
    half = query_refs[0].shape[0]
    step = pl.program_id(0)
    me = mine[0]
    my_block = order[me]
    blocks = [(ref, index, offset) for ref, group in zip(pair_refs, held) for index, offset in enumerate(group)]
    weight_copy = pltpu.make_async_copy(weight, weight_ref, arrived)
    moves = [
        pltpu.make_async_copy(source, target, here.at[i])
        for i, (source, target) in enumerate(
            list(zip(sent_pairs, pair_refs)) + list(zip(sent_queries, query_refs))
        )
    ]

    @pl.when(step == 0)
    def _():
        for move in moves:
            move.start()
        value_ref[:, :, HD:, :] = jnp.ones((len(blocks), pairs, SUM_ROWS, block_rows), jnp.bfloat16)

    @pl.when(step == 0)
    def _():
        for move in moves:
            move.wait()
        weight_copy.start()

    for at, (ref, index, offset) in enumerate(blocks):

        @pl.when((step == 0) & (order[me ^ offset] <= my_block))
        def _():
            for p in range(pairs):
                rows = slice(index * block_rows, (index + 1) * block_rows)
                key_ref[at, p] = ref[rows, p * HD : (p + 1) * HD]
                value_ref[at, p, :HD, :] = ref[rows, (pairs + p) * HD : (pairs + p + 1) * HD].T

    for at in range(slots):

        @pl.when(step == at // together)
        def _():
            for p in range(pairs):
                for g in range(sharing):
                    column = (p * sharing + g) * HD
                    row = (at % together * sharing + g) * half
                    query_ref[p, row : row + half, :] = query_refs[at][:, column : column + HD]

    def scores_of(p, at):
        return lax.dot_general(
            key_ref[at, p], query_ref[p], (((1,), (1,)), ((), ())), preferred_element_type=jnp.float32
        )

    def mixed_of(p, at, weights):
        return jnp.dot(value_ref[at, p], weights, preferred_element_type=jnp.float32)

    place = jnp.concatenate([place_ref[i] for i in range(together) for _ in range(sharing)], axis=1)
    rows = block_rows // slots
    down = lax.broadcasted_iota(jnp.int32, (rows, place.shape[1]), 0)
    visible = jnp.concatenate(
        [down <= place - lax.rem(mine[1] - s + slots, slots) * rows for s in range(slots)], axis=0
    )
    for p in range(pairs):
        scores = jnp.where(visible, scores_of(p, 0), -1e30)
        top = jnp.max(scores, axis=0, keepdims=True)
        weights = jnp.exp2((scores - top) * FACTOR).astype(jnp.bfloat16)
        top_ref[p, 0:1, :] = top
        total_ref[p] = mixed_of(p, 0, weights)

    @pl.loop(1, len(blocks))
    def _(at):
        offset = blocks[1][2] if len(blocks) > 1 else 0
        for other in range(2, len(blocks)):
            offset = jnp.where(at == other, blocks[other][2], offset)

        @pl.when(order[me ^ offset] < my_block)
        def _():
            for p in range(pairs):
                top = top_ref[p, 0:1, :]
                scores = scores_of(p, at)
                raised = jnp.maximum(top, jnp.max(scores, axis=0, keepdims=True))
                weights = jnp.exp2((scores - raised) * FACTOR).astype(jnp.bfloat16)
                top_ref[p, 0:1, :] = raised
                total_ref[p] = total_ref[p] * jnp.exp2((top - raised) * FACTOR) + mixed_of(p, at, weights)

    for p in range(pairs):
        mixed = (total_ref[p, :HD, :] / total_ref[p, HD : HD + 1, :]).T.astype(jnp.bfloat16)
        for i in range(together):
            for g in range(sharing):
                column = (p * sharing + g) * HD
                row = (i * sharing + g) * half
                at = pl.multiple_of((step * together + i) * half, half)
                head_ref[pl.ds(at, half), column : column + HD] = mixed[row : row + half]

    @pl.when(step == pl.num_programs(0) - 1)
    def _():
        weight_copy.wait()
        width = weight.shape[1] // pieces
        tile = 2 * TILE
        for c in range(pieces):

            @pl.loop(0, width // tile)
            def _(n):
                columns = pl.ds(pl.multiple_of(c * width + n * tile, tile), tile)
                value = jnp.dot(head_ref[...], weight_ref[:, columns], preferred_element_type=jnp.float32)
                share_out(outs[c * len(outs) // pieces :], pl.ds(pl.multiple_of(n * tile, tile), tile), value)


def share_out(outs, columns, value):
    rows = outs[0].shape[0]
    for g in range(value.shape[0] // rows):
        outs[g][:, columns] = value[g * rows : (g + 1) * rows].astype(jnp.bfloat16)


def piece_shapes(rows, width, slots, pieces, grouped):
    return [jax.ShapeDtypeStruct((rows // slots if grouped else rows, width // pieces), jnp.bfloat16)] * (
        pieces * (slots if grouped else 1)
    )


def by_piece(outs, slots, pieces, grouped):
    if grouped:
        return [outs[c * slots : (c + 1) * slots] for c in range(pieces)]
    return [[out[s * (out.shape[0] // slots) : (s + 1) * (out.shape[0] // slots)] for s in range(slots)] for out in outs]


def attend(order, mine, queries, places, pair_list, held, pairs, sharing, block_rows, weight, pieces, grouped):
    slots = len(queries)
    half, width = queries[0].shape
    together = 2 if slots <= LINE else 1
    tall = together * sharing * half
    blocks = sum(len(group) for group in held)
    count = blocks * block_rows
    shapes = piece_shapes(slots * half, weight.shape[1], slots, pieces, grouped)
    kernel = functools.partial(
        attention_kernel, slots, together, held, pairs, sharing, block_rows, (pieces, grouped)
    )
    outs = pl.pallas_call(
        kernel,
        grid_spec=pltpu.PrefetchScalarGridSpec(
            num_scalar_prefetch=2,
            grid=(slots // together,),
            in_specs=[pl.BlockSpec(memory_space=pl.ANY)] * slots
            + [pl.BlockSpec((together, 1, half), lambda s, *_: (s, 0, 0))]
            + [pl.BlockSpec(memory_space=pl.ANY)] * len(pair_list)
            + [pl.BlockSpec(memory_space=pltpu.HBM)],
            out_specs=[pl.BlockSpec(shape.shape, lambda s, *_: (0, 0)) for shape in shapes],
            scratch_shapes=[pltpu.VMEM((half, width), jnp.bfloat16)] * slots
            + [pltpu.VMEM(pair.shape, pair.dtype) for pair in pair_list]
            + [
                pltpu.VMEM((pairs, tall, HD), jnp.bfloat16),
                pltpu.VMEM((blocks, pairs, block_rows, HD), jnp.bfloat16),
                pltpu.VMEM((blocks, pairs, HD + SUM_ROWS, block_rows), jnp.bfloat16),
                pltpu.VMEM((pairs, 8, tall), jnp.float32),
                pltpu.VMEM((pairs, HD + SUM_ROWS, tall), jnp.float32),
                pltpu.VMEM((slots * half, width), jnp.bfloat16),
                pltpu.VMEM(weight.shape, weight.dtype),
                pltpu.SemaphoreType.DMA,
                pltpu.SemaphoreType.DMA((slots + len(pair_list),)),
            ],
        ),
        out_shape=shapes,
        compiler_params=pltpu.CompilerParams(vmem_limit_bytes=VMEM_HELD),
        cost_estimate=pl.CostEstimate(
            flops=40 * slots * half * width * count,
            bytes_accessed=2 * (2 * slots * half * width + count * 2 * pairs * HD + weight.size),
            transcendentals=slots * half * width // HD * count,
        ),
    )(order, mine, *queries, places, *pair_list, pltpu.with_memory_space_constraint(weight, pltpu.HBM))
    return by_piece(outs, slots, pieces, grouped)


def expert_kernel(plan, pieces, *refs):
    mine, refs = refs[0], refs[1:]
    sources = []
    for count in plan:
        sources.append(refs[:count])
        refs = refs[count:]
    gate_weight, up_weight, down_weights, refs = refs[0], refs[1], refs[2:4], refs[4:]
    outs, (chosen, acts) = refs[:-2], refs[-2:]
    step = pl.program_id(0)
    tile = gate_weight.shape[1]
    first = acts.shape[1] // tile

    def place(s, source):
        rows, width = source[0].shape
        for c, ref in enumerate(source):
            chosen[s * rows : (s + 1) * rows, c * width : (c + 1) * width] = ref[...]

    @pl.when(step == 0)
    def _():
        place(0, sources[0])
        for s in range(1, (len(plan) + 1) // 2):
            right, left = sources[s], sources[len(plan) - s]

            @pl.when(mine[0] >= s)
            def _():
                place(s, right)

            @pl.when(mine[0] < s)
            def _():
                place(s, left)

    @pl.when(step < first)
    def _():
        gate = jnp.dot(chosen[...], gate_weight[...], preferred_element_type=jnp.float32)
        upward = jnp.dot(chosen[...], up_weight[...], preferred_element_type=jnp.float32)
        columns = pl.ds(pl.multiple_of(step * tile, tile), tile)
        acts[:, columns] = (gate / (1.0 + jnp.exp(-gate)) * upward).astype(jnp.bfloat16)

    @pl.when(step >= first)
    def _():
        strip = down_weights[0].shape[1]
        pairs = outs[0].shape[1] // (2 * strip)
        for j, down_weight in enumerate(down_weights):
            value = jnp.dot(acts[...], down_weight[...], preferred_element_type=jnp.float32)
            for c in range(pieces):

                @pl.when((step - first) // pairs == c)
                def _():
                    at = (2 * (step - first - c * pairs) + j) * strip
                    share_out(outs[c * len(outs) // pieces :], pl.ds(pl.multiple_of(at, strip), strip), value)


def expert_rows(mine, sources, gate_weight, up_weight, down_weight, slots, pieces, grouped):
    flat = [piece for source in sources for piece in source]
    rows = flat[0].shape[0] * ((len(sources) + 1) // 2)
    depth, width = gate_weight.shape
    tile, strip = min(TILE, width), 2 * TILE
    first = width // tile
    shapes = piece_shapes(rows, depth, slots, pieces, grouped)
    in_place = pl.BlockSpec(memory_space=pltpu.VMEM)
    weight = pl.BlockSpec((depth, tile), lambda n, *_: (0, jnp.minimum(n, first - 1)))
    outs = pl.pallas_call(
        functools.partial(expert_kernel, [len(source) for source in sources], pieces),
        grid_spec=pltpu.PrefetchScalarGridSpec(
            num_scalar_prefetch=1,
            grid=(first + depth // (2 * strip),),
            in_specs=[in_place] * len(flat)
            + [weight, weight]
            + [
                pl.BlockSpec((width, strip), functools.partial(lambda j, n, *_: (0, 2 * jnp.maximum(n - first, 0) + j), j))
                for j in range(2)
            ],
            out_specs=[in_place] * len(shapes),
            scratch_shapes=[pltpu.VMEM((rows, depth), jnp.bfloat16), pltpu.VMEM((rows, width), jnp.bfloat16)],
        ),
        out_shape=shapes,
        compiler_params=pltpu.CompilerParams(vmem_limit_bytes=VMEM_LARGE),
        cost_estimate=pl.CostEstimate(
            flops=6 * rows * depth * width, bytes_accessed=6 * depth * width, transcendentals=rows * width
        ),
    )(mine, *flat, gate_weight, up_weight, down_weight, down_weight)
    return by_piece(outs, slots, pieces, grouped)


def pack_pairs_kernel(shards, mine, keys_ref, values_ref, *outs):
    width = keys_ref.shape[1] // shards
    for s in range(shards):
        columns = pl.ds(pl.multiple_of(lax.rem(mine[0] + s, shards) * width, width), width)
        outs[s][:, :width] = keys_ref[:, columns]
        outs[s][:, width:] = values_ref[:, columns]


def pack_pairs(mine, keys, values, shards):
    rows, width = keys.shape
    spec = pl.BlockSpec((rows, width), lambda k, *_: (0, 0))
    out = (rows, 2 * width // shards)
    return pl.pallas_call(
        functools.partial(pack_pairs_kernel, shards),
        grid_spec=pltpu.PrefetchScalarGridSpec(
            num_scalar_prefetch=1,
            grid=(1,),
            in_specs=[spec, spec],
            out_specs=[pl.BlockSpec(out, lambda k, *_: (0, 0))] * shards,
        ),
        out_shape=[jax.ShapeDtypeStruct(out, keys.dtype)] * shards,
    )(mine, keys, values)


def pack_queries_kernel(slots, halves, mine, picked_ref, query_ref, *outs):
    shards = len(slots)
    rows = query_ref.shape[0]
    half = rows // halves
    width = query_ref.shape[1] // shards
    packed, outs = outs[: halves * shards], outs[halves * shards :]
    place_refs, (order_ref, count_ref) = outs[:halves], outs[halves:]
    me = mine[0]
    across = lax.broadcasted_iota(jnp.int32, (rows, rows), 1)
    down = lax.broadcasted_iota(jnp.int32, (rows, rows), 0)
    up_to = jnp.where(down <= across, 1.0, 0.0).astype(jnp.bfloat16)
    picked = picked_ref[...]
    seen = jnp.dot(picked.astype(jnp.bfloat16), up_to, preferred_element_type=jnp.float32).astype(jnp.int32)
    count = seen[:, rows - 1 : rows]
    row_ids = lax.broadcasted_iota(jnp.int32, seen.shape, 1)
    slot = jnp.where(picked > 0, seen - 1, count + row_ids - seen)
    count_ref[0] = jnp.max(jnp.where(count > half, 1, 0))
    ids = row_ids.astype(jnp.bfloat16)
    for s in range(shards):
        shard = lax.rem(me - s + shards, shards)
        mine_slot = slot[0:1]
        for other in range(1, shards):
            mine_slot = jnp.where(shard == other, slot[other : other + 1], mine_slot)
        at_slot = jnp.where(mine_slot == down, 1.0, 0.0).astype(jnp.bfloat16)
        rows_at = lax.dot_general(ids, at_slot, (((1,), (1,)), ((), ())), preferred_element_type=jnp.float32)
        for h in range(halves):
            here = rows_at[0:1, h * half : (h + 1) * half]
            place_refs[h][slots.index(s)] = here.astype(jnp.int32) + shard * rows
        if s == 0:
            order_ref[...] = at_slot
    for s in range(shards):
        columns = pl.ds(pl.multiple_of(lax.rem(me + s, shards) * width, width), width)
        ordered = jnp.dot(order_ref[...], query_ref[:, columns], preferred_element_type=jnp.float32)
        ordered = ordered.astype(jnp.bfloat16)
        for h in range(halves):
            packed[h * shards + s][...] = ordered[h * half : (h + 1) * half]


def pack_queries(mine, picked, queries, slots, halves):
    shards = len(slots)
    rows, width = queries.shape
    packed = (rows // halves, width // shards)
    shapes = [jax.ShapeDtypeStruct(packed, jnp.bfloat16)] * (halves * shards)
    shapes += [jax.ShapeDtypeStruct((shards, 1, rows // halves), jnp.int32)] * halves
    shapes += [jax.ShapeDtypeStruct((rows, rows), jnp.bfloat16), jax.ShapeDtypeStruct((1,), jnp.int32)]

    def whole(shape):
        return pl.BlockSpec(shape, lambda k, *_: (0,) * len(shape))

    got = pl.pallas_call(
        functools.partial(pack_queries_kernel, slots, halves),
        grid_spec=pltpu.PrefetchScalarGridSpec(
            num_scalar_prefetch=1,
            grid=(1,),
            in_specs=[whole(picked.shape), whole(queries.shape)],
            out_specs=[whole(shape.shape) for shape in shapes[:-1]] + [pl.BlockSpec(memory_space=pltpu.SMEM)],
        ),
        out_shape=shapes,
    )(mine, picked, queries)
    packed, got = got[: halves * shards], got[halves * shards :]
    return [packed[h * shards : (h + 1) * shards] for h in range(halves)], got[:halves], *got[halves:]


def on_device(
    hidden_in,
    queries,
    keys,
    values,
    block_order,
    routes,
    out_weight,
    norm_gain,
    router_weight,
    gate_weight,
    up_weight,
    down_weight,
):
    shards = lax.axis_size("tp")
    blocks = lax.axis_size("ctx")
    me = lax.axis_index("tp")
    rows, model = hidden_in.shape
    block_rows = rows * shards
    per_device = HEADS // shards
    grouping = HEADS // KV_HEADS
    repeat_by = max(1, grouping // per_device)
    pairs = max(1, per_device // grouping)
    sharing = per_device // pairs
    half = rows // 2 if rows % 32 == 0 else rows
    halves = rows // half
    line = shards <= LINE
    pieces = 2 if line else 1
    cuts = [slice(c * (model // pieces), (c + 1) * (model // pieces)) for c in range(pieces)]
    slots = [s for s in range(1, shards, 2)] + [s for s in range(2, shards, 2)] + [0]
    shard_of = lax.rem(me - jnp.arange(shards, dtype=jnp.int32) + shards, shards)

    def shift(parts):
        moves = [[(i, (i + s) % shards) for i in range(shards)] for s in range(shards)]
        return [parts[0]] + [lax.ppermute(parts[s], "tp", moves[s]) for s in range(1, shards)]

    def exchange(source):
        got = lax.all_to_all(source, "tp", split_axis=1, concat_axis=0, tiled=True)
        got = got.reshape(shards, rows, source.shape[2])
        return [lax.dynamic_index_in_dim(got, shard_of[s], 0, keepdims=False) for s in range(shards)]

    def rights(count):
        return [(i, i + 1) for i in range(count)]

    def lefts(count):
        return [(i, i - 1) for i in range(shards - count, shards)]

    def reduce_line(pieces_terms):
        if not line:
            by_shard = [jnp.take(jnp.stack(terms), shard_of, axis=0).reshape(-1, terms[0].shape[1]) for terms in pieces_terms]
            return [
                lax.psum_scatter(term, "tp", scatter_dimension=0, tiled=True).astype(jnp.float32) for term in by_shard
            ], None
        got = [None] * len(pieces_terms)
        marks = []
        for s in range(1, shards):
            for c, terms in enumerate(pieces_terms):
                if got[c] is None:
                    sent = (terms[s], terms[shards - s])
                else:
                    arrived = got[c]
                    sent = (terms[s] + arrived[0], terms[shards - s] + arrived[1])
                right = lax.ppermute(sent[0], "tp", rights(s))
                left = lax.ppermute(sent[1], "tp", lefts(s))
                got[c] = lax.optimization_barrier((right, left))
            marks.append(got[0])
        return [
            terms[0].astype(jnp.float32) + right.astype(jnp.float32) + left.astype(jnp.float32)
            for terms, (right, left) in zip(pieces_terms, got)
        ], marks

    def gather_line(source, terms=None):
        if not line:
            got = lax.all_gather(source, "tp", axis=0)
            return [[jnp.take(got, shard_of, axis=0).reshape(shards * half, -1)]], None
        first_right = lax.ppermute(source, "tp", rights(shards - 1))
        first_left = lax.ppermute(source, "tp", lefts(shards - 1))
        first_right, first_left = lax.optimization_barrier((first_right, first_left))
        got = [(first_right[:, cut], first_left[:, cut]) for cut in cuts]
        from_left, from_right = [], []
        for s in range(2, shards):
            if terms is None:
                sent = got
                to_right = [(i, i + 1) for i in range(s - 1, shards - 1)]
                to_left = [(i, i - 1) for i in range(1, shards - s + 1)]
            else:
                sent = [
                    (
                        jnp.where(me >= s - 1, right, right + term[s - 1]),
                        jnp.where(me <= shards - s, left, left + term[shards - s + 1]),
                    )
                    for (right, left), term in zip(got, terms)
                ]
                to_right, to_left = rights(shards - 1), lefts(shards - 1)
            from_left.append([right for right, _ in sent])
            from_right.append([left for _, left in sent])
            got = [
                lax.optimization_barrier((lax.ppermute(right, "tp", to_right), lax.ppermute(left, "tp", to_left)))
                for right, left in sent
            ]
        from_left.append([right for right, _ in got])
        from_right.append([left for _, left in got])
        total = None
        if terms is not None:
            right = jnp.concatenate([right + term[shards - 1] for (right, _), term in zip(got, terms)], axis=1)
            left = jnp.concatenate([left + term[1] for (_, left), term in zip(got, terms)], axis=1)
            right = lax.ppermute(right, "tp", rights(shards - 1)).astype(jnp.float32)
            left = lax.ppermute(left, "tp", lefts(shards - 1)).astype(jnp.float32)
            total = jnp.concatenate([term[0] for term in terms], axis=1).astype(jnp.float32) + right + left
        return [[source]] + from_left + from_right, total

    picked = ((routes[:, 0] == 0) | (routes[:, 1] == 0)).reshape(shards, rows)
    if line:
        sent_pairs = pack_pairs(me[None], keys, values, shards)
        own_pairs = jnp.concatenate(shift(sent_pairs), axis=0)
        picked, _ = lax.optimization_barrier((picked.astype(jnp.int32), sent_pairs))
        packed, places, order, crowded = pack_queries(me[None], picked, queries, slots, halves)
        asked = [shift(packed[0])]
    else:

        def spread(source):
            widened = jnp.repeat(source.reshape(rows, KV_HEADS, HD), repeat_by, axis=1)
            return widened.reshape(rows, shards, pairs * HD)

        own_pairs = exchange(jnp.concatenate([spread(keys), spread(values)], axis=2))
        own_pairs = jnp.concatenate(own_pairs, axis=0)
        row_ids = jnp.arange(rows, dtype=jnp.int32)
        seen = jnp.cumsum(picked.astype(jnp.int32), axis=1)
        slot = jnp.where(picked, seen - 1, seen[:, -1:] + row_ids[None, :] - seen)
        at_slot = slot[:, None, :] == row_ids[None, :, None]
        row_of_slot = jnp.sum(jnp.where(at_slot, row_ids[None, None, :], 0), axis=2)
        places = row_of_slot + jnp.arange(shards, dtype=jnp.int32)[:, None] * rows
        places = [jnp.stack([jnp.take(places, shard_of[s], axis=0) for s in slots])[:, None, :]]
        order = lax.dynamic_index_in_dim(at_slot, me, 0, keepdims=False).astype(jnp.bfloat16)
        ordered = jnp.dot(order, queries, preferred_element_type=jnp.float32).astype(jnp.bfloat16)
        asked = [exchange(ordered.reshape(rows, shards, per_device * HD))]

    pair_list, held = [own_pairs], [[0]]
    offset = blocks // 2
    while offset >= 1:
        pair_list += [lax.ppermute(part, "ctx", [(i, i ^ offset) for i in range(blocks)]) for part in pair_list]
        held += [[other ^ offset for other in group] for group in held]
        if line and len(pair_list) == 2:
            pair_list[1], asked[0] = lax.optimization_barrier((pair_list[1], asked[0]))
        offset //= 2

    def reorder(source):
        return jnp.dot(order, source, preferred_element_type=jnp.float32).astype(jnp.bfloat16)

    def restore(parts):
        whole = jnp.concatenate(parts, axis=0) if len(parts) > 1 else parts[0]
        return lax.dot_general(
            order, whole, (((0,), (0,)), ((), ())), preferred_element_type=jnp.float32
        ).astype(jnp.bfloat16)

    mine = lax.axis_index("ctx").astype(jnp.int32)[None]
    expert_ids = jnp.arange(router_weight.shape[1], dtype=jnp.int32)

    def project(which):
        terms = attend(
            block_order,
            jnp.stack([lax.axis_index("ctx"), me]).astype(jnp.int32),
            [asked[which][s] for s in slots],
            places[which],
            pair_list,
            held,
            pairs,
            sharing,
            block_rows,
            out_weight,
            pieces,
            line,
        )
        return [[term[slots.index(s)] for s in range(shards)] for term in terms]

    def finish(which, head_sums):
        base = hidden[which * half : (which + 1) * half].astype(jnp.float32)
        return jnp.concatenate(
            [(base[:, cut] + head_sum).astype(jnp.bfloat16) for cut, head_sum in zip(cuts, head_sums)], axis=1
        )

    def normalise(attended):
        widened = attended.astype(jnp.float32)
        return (
            widened * lax.rsqrt(jnp.mean(widened * widened, axis=1, keepdims=True) + 1e-05) * norm_gain
        ).astype(jnp.bfloat16)

    def share_of(which, normed):
        logits = jnp.dot(normed, router_weight, preferred_element_type=jnp.float32)
        named = my_routes[which * half : (which + 1) * half]
        first = jnp.sum(jnp.where(named[:, 0:1] == expert_ids[None, :], logits, 0.0), axis=1)
        second = jnp.sum(jnp.where(named[:, 1:2] == expert_ids[None, :], logits, 0.0), axis=1)
        share = jnp.where(named[:, 0] == 0, 1.0 / (1.0 + jnp.exp(second - first)), 0.0)
        return share + jnp.where(named[:, 1] == 0, 1.0 / (1.0 + jnp.exp(first - second)), 0.0)

    def expert(which, normed, sources, beside=None):
        terms = expert_rows(me[None], sources, gate_weight, up_weight, down_weight, shards, pieces, line)
        if beside is not None:
            terms, beside = lax.optimization_barrier((terms, beside))
        sums, marks = reduce_line(terms)
        if line:
            normed, _ = lax.optimization_barrier((normed, marks[0]))
        share = share_of(which, normed)
        parts = [(total * share[:, None]).astype(jnp.bfloat16) for total in sums]
        return jnp.concatenate(parts, axis=1), beside

    def late_expert(source):
        normed = normalise(source)
        return expert(1, normed, gather_line(normed)[0])[0]

    terms = project(0)
    if halves > 1:
        asked.append(shift(packed[1]))
        terms, asked[1] = lax.optimization_barrier((terms, asked[1]))
    totals, marks = reduce_line(terms)
    if line:
        hidden_in, order, _ = lax.optimization_barrier((hidden_in, order, marks[0]))
    hidden = reorder(hidden_in)
    my_routes = lax.dynamic_slice_in_dim(routes, me * rows, rows, 0).astype(jnp.bfloat16)
    my_routes = reorder(my_routes).astype(jnp.int32)
    first_half = finish(0, totals)
    normed = normalise(first_half)
    if halves == 1:
        return (restore([first_half]), restore([expert(0, normed, gather_line(normed)[0])[0]]))
    asked[1], _ = lax.optimization_barrier((asked[1], normed))
    sources, second_sum = gather_line(normed, project(1))
    second_half = (hidden[half:].astype(jnp.float32) + second_sum).astype(jnp.bfloat16)
    part, second_half = expert(0, normed, sources, second_half)
    part, late = lax.optimization_barrier((part, second_half))
    late = lax.cond(crowded[0] > 0, late_expert, jnp.zeros_like, late)
    return (restore([first_half, second_half]), restore([part, late]))


def solution(mesh):
    return jax.shard_map(
        on_device,
        mesh=mesh,
        in_specs=(
            P(("req", "ctx", "tp"), None),
            P(("req", "ctx", "tp"), None),
            P(("req", "ctx", "tp"), None),
            P(("req", "ctx", "tp"), None),
            P("req"),
            P(("req", "ctx"), None),
            P("tp", None),
            P(),
            P(),
            P(None, "tp"),
            P(None, "tp"),
            P("tp", None),
        ),
        out_specs=(P(("req", "ctx", "tp"), None), P(("req", "ctx", "tp"), None)),
        check_vma=False,
    )
```

```python
import functools
import math

import jax
import jax.numpy as jnp
from jax import lax
from jax.experimental import pallas as pl
from jax.experimental.pallas import tpu as pltpu
from jax.sharding import PartitionSpec as P

HEADS = 32
KV_HEADS = 8
HD = 128
FACTOR = math.log2(math.e) / math.sqrt(HD)
LINE = 4
SUM_ROWS = 16
TILE = 256
VMEM_HELD = 21 * 1024 * 1024
VMEM_LARGE = 28 * 1024 * 1024


def attention_kernel(slots, together, held, pairs, sharing, block_rows, plan, *refs):
    pieces, grouped = plan
    (order, mine), refs = refs[:2], refs[2:]
    sent_queries, refs = refs[:slots], refs[slots:]
    place_ref, refs = refs[0], refs[1:]
    sent_pairs, weight, refs = refs[: len(held)], refs[len(held)], refs[len(held) + 1 :]
    outs, refs = refs[: pieces * (slots if grouped else 1)], refs[pieces * (slots if grouped else 1) :]
    query_refs, pair_refs, refs = refs[:slots], refs[slots : slots + len(held)], refs[slots + len(held) :]
    query_ref, key_ref, value_ref, top_ref, total_ref, head_ref, weight_ref, arrived, here = refs
    half = query_refs[0].shape[0]
    step = pl.program_id(0)
    me = mine[0]
    my_block = order[me]
    blocks = [(ref, index, offset) for ref, group in zip(pair_refs, held) for index, offset in enumerate(group)]
    weight_copy = pltpu.make_async_copy(weight, weight_ref, arrived)
    moves = [
        pltpu.make_async_copy(source, target, here.at[i])
        for i, (source, target) in enumerate(
            list(zip(sent_pairs, pair_refs)) + list(zip(sent_queries, query_refs))
        )
    ]

    @pl.when(step == 0)
    def _():
        for move in moves:
            move.start()
        value_ref[:, :, HD:, :] = jnp.ones((len(blocks), pairs, SUM_ROWS, block_rows), jnp.bfloat16)

    @pl.when(step == 0)
    def _():
        for move in moves:
            move.wait()
        weight_copy.start()

    for at, (ref, index, offset) in enumerate(blocks):

        @pl.when((step == 0) & (order[me ^ offset] <= my_block))
        def _():
            for p in range(pairs):
                rows = slice(index * block_rows, (index + 1) * block_rows)
                key_ref[at, p] = ref[rows, p * HD : (p + 1) * HD]
                value_ref[at, p, :HD, :] = ref[rows, (pairs + p) * HD : (pairs + p + 1) * HD].T

    for at in range(slots):

        @pl.when(step == at // together)
        def _():
            for p in range(pairs):
                for g in range(sharing):
                    column = (p * sharing + g) * HD
                    row = (at % together * sharing + g) * half
                    query_ref[p, row : row + half, :] = query_refs[at][:, column : column + HD]

    def scores_of(p, at):
        return lax.dot_general(
            key_ref[at, p], query_ref[p], (((1,), (1,)), ((), ())), preferred_element_type=jnp.float32
        )

    def mixed_of(p, at, weights):
        return jnp.dot(value_ref[at, p], weights, preferred_element_type=jnp.float32)

    place = jnp.concatenate([place_ref[i] for i in range(together) for _ in range(sharing)], axis=1)
    rows = block_rows // slots
    down = lax.broadcasted_iota(jnp.int32, (rows, place.shape[1]), 0)
    visible = jnp.concatenate(
        [down <= place - lax.rem(mine[1] - s + slots, slots) * rows for s in range(slots)], axis=0
    )
    for p in range(pairs):
        scores = jnp.where(visible, scores_of(p, 0), -1e30)
        top = jnp.max(scores, axis=0, keepdims=True)
        weights = jnp.exp2((scores - top) * FACTOR).astype(jnp.bfloat16)
        top_ref[p, 0:1, :] = top
        total_ref[p] = mixed_of(p, 0, weights)

    @pl.loop(1, len(blocks))
    def _(at):
        offset = blocks[1][2] if len(blocks) > 1 else 0
        for other in range(2, len(blocks)):
            offset = jnp.where(at == other, blocks[other][2], offset)

        @pl.when(order[me ^ offset] < my_block)
        def _():
            for p in range(pairs):
                top = top_ref[p, 0:1, :]
                scores = scores_of(p, at)
                raised = jnp.maximum(top, jnp.max(scores, axis=0, keepdims=True))
                weights = jnp.exp2((scores - raised) * FACTOR).astype(jnp.bfloat16)
                top_ref[p, 0:1, :] = raised
                total_ref[p] = total_ref[p] * jnp.exp2((top - raised) * FACTOR) + mixed_of(p, at, weights)

    for p in range(pairs):
        mixed = (total_ref[p, :HD, :] / total_ref[p, HD : HD + 1, :]).T.astype(jnp.bfloat16)
        for i in range(together):
            for g in range(sharing):
                column = (p * sharing + g) * HD
                row = (i * sharing + g) * half
                at = pl.multiple_of((step * together + i) * half, half)
                head_ref[pl.ds(at, half), column : column + HD] = mixed[row : row + half]

    @pl.when(step == pl.num_programs(0) - 1)
    def _():
        weight_copy.wait()
        width = weight.shape[1] // pieces
        tile = 2 * TILE
        for c in range(pieces):

            @pl.loop(0, width // tile)
            def _(n):
                columns = pl.ds(pl.multiple_of(c * width + n * tile, tile), tile)
                value = jnp.dot(head_ref[...], weight_ref[:, columns], preferred_element_type=jnp.float32)
                share_out(outs[c * len(outs) // pieces :], pl.ds(pl.multiple_of(n * tile, tile), tile), value)


def share_out(outs, columns, value):
    rows = outs[0].shape[0]
    for g in range(value.shape[0] // rows):
        outs[g][:, columns] = value[g * rows : (g + 1) * rows].astype(jnp.bfloat16)


def piece_shapes(rows, width, slots, pieces, grouped):
    return [jax.ShapeDtypeStruct((rows // slots if grouped else rows, width // pieces), jnp.bfloat16)] * (
        pieces * (slots if grouped else 1)
    )


def by_piece(outs, slots, pieces, grouped):
    if grouped:
        return [outs[c * slots : (c + 1) * slots] for c in range(pieces)]
    return [[out[s * (out.shape[0] // slots) : (s + 1) * (out.shape[0] // slots)] for s in range(slots)] for out in outs]


def in_hbm(arrays):
    return [pltpu.with_memory_space_constraint(array, pltpu.HBM) for array in arrays]


def attend(order, mine, queries, places, pair_list, held, pairs, sharing, block_rows, weight, pieces, grouped):
    slots = len(queries)
    half, width = queries[0].shape
    together = 2 if slots <= LINE else 1
    tall = together * sharing * half
    blocks = sum(len(group) for group in held)
    count = blocks * block_rows
    shapes = piece_shapes(slots * half, weight.shape[1], slots, pieces, grouped)
    kernel = functools.partial(
        attention_kernel, slots, together, held, pairs, sharing, block_rows, (pieces, grouped)
    )
    outs = pl.pallas_call(
        kernel,
        grid_spec=pltpu.PrefetchScalarGridSpec(
            num_scalar_prefetch=2,
            grid=(slots // together,),
            in_specs=[pl.BlockSpec(memory_space=pltpu.HBM)] * slots
            + [pl.BlockSpec((together, 1, half), lambda s, *_: (s, 0, 0))]
            + [pl.BlockSpec(memory_space=pltpu.HBM)] * (len(pair_list) + 1),
            out_specs=[pl.BlockSpec(shape.shape, lambda s, *_: (0, 0)) for shape in shapes],
            scratch_shapes=[pltpu.VMEM((half, width), jnp.bfloat16)] * slots
            + [pltpu.VMEM(pair.shape, pair.dtype) for pair in pair_list]
            + [
                pltpu.VMEM((pairs, tall, HD), jnp.bfloat16),
                pltpu.VMEM((blocks, pairs, block_rows, HD), jnp.bfloat16),
                pltpu.VMEM((blocks, pairs, HD + SUM_ROWS, block_rows), jnp.bfloat16),
                pltpu.VMEM((pairs, 8, tall), jnp.float32),
                pltpu.VMEM((pairs, HD + SUM_ROWS, tall), jnp.float32),
                pltpu.VMEM((slots * half, width), jnp.bfloat16),
                pltpu.VMEM(weight.shape, weight.dtype),
                pltpu.SemaphoreType.DMA,
                pltpu.SemaphoreType.DMA((slots + len(pair_list),)),
            ],
        ),
        out_shape=shapes,
        compiler_params=pltpu.CompilerParams(vmem_limit_bytes=VMEM_HELD),
        cost_estimate=pl.CostEstimate(
            flops=40 * slots * half * width * count,
            bytes_accessed=2 * (2 * slots * half * width + count * 2 * pairs * HD + weight.size),
            transcendentals=slots * half * width // HD * count,
        ),
    )(order, mine, *in_hbm(queries), places, *in_hbm(pair_list), *in_hbm([weight]))
    return by_piece(outs, slots, pieces, grouped)


def expert_kernel(plan, pieces, *refs):
    mine, refs = refs[0], refs[1:]
    sources = []
    for count in plan:
        sources.append(refs[:count])
        refs = refs[count:]
    gate_weight, up_weight, down_weights, refs = refs[0], refs[1], refs[2:4], refs[4:]
    outs, (chosen, acts) = refs[:-2], refs[-2:]
    step = pl.program_id(0)
    tile = gate_weight.shape[1]
    first = acts.shape[1] // tile

    def place(s, source):
        rows, width = source[0].shape
        for c, ref in enumerate(source):
            chosen[s * rows : (s + 1) * rows, c * width : (c + 1) * width] = ref[...]

    @pl.when(step == 0)
    def _():
        place(0, sources[0])
        for s in range(1, (len(plan) + 1) // 2):
            right, left = sources[s], sources[len(plan) - s]

            @pl.when(mine[0] >= s)
            def _():
                place(s, right)

            @pl.when(mine[0] < s)
            def _():
                place(s, left)

    @pl.when(step < first)
    def _():
        gate = jnp.dot(chosen[...], gate_weight[...], preferred_element_type=jnp.float32)
        upward = jnp.dot(chosen[...], up_weight[...], preferred_element_type=jnp.float32)
        columns = pl.ds(pl.multiple_of(step * tile, tile), tile)
        acts[:, columns] = (gate / (1.0 + jnp.exp(-gate)) * upward).astype(jnp.bfloat16)

    @pl.when(step >= first)
    def _():
        strip = down_weights[0].shape[1]
        pairs = outs[0].shape[1] // (2 * strip)
        for j, down_weight in enumerate(down_weights):
            value = jnp.dot(acts[...], down_weight[...], preferred_element_type=jnp.float32)
            for c in range(pieces):

                @pl.when((step - first) // pairs == c)
                def _():
                    at = (2 * (step - first - c * pairs) + j) * strip
                    share_out(outs[c * len(outs) // pieces :], pl.ds(pl.multiple_of(at, strip), strip), value)


def expert_rows(mine, sources, gate_weight, up_weight, down_weight, slots, pieces, grouped):
    flat = [piece for source in sources for piece in source]
    rows = flat[0].shape[0] * ((len(sources) + 1) // 2)
    depth, width = gate_weight.shape
    tile, strip = min(TILE, width), 2 * TILE
    first = width // tile
    shapes = piece_shapes(rows, depth, slots, pieces, grouped)
    in_place = pl.BlockSpec(memory_space=pltpu.VMEM)
    weight = pl.BlockSpec((depth, tile), lambda n, *_: (0, jnp.minimum(n, first - 1)))
    outs = pl.pallas_call(
        functools.partial(expert_kernel, [len(source) for source in sources], pieces),
        grid_spec=pltpu.PrefetchScalarGridSpec(
            num_scalar_prefetch=1,
            grid=(first + depth // (2 * strip),),
            in_specs=[in_place] * len(flat)
            + [weight, weight]
            + [
                pl.BlockSpec((width, strip), functools.partial(lambda j, n, *_: (0, 2 * jnp.maximum(n - first, 0) + j), j))
                for j in range(2)
            ],
            out_specs=[in_place] * len(shapes),
            scratch_shapes=[pltpu.VMEM((rows, depth), jnp.bfloat16), pltpu.VMEM((rows, width), jnp.bfloat16)],
        ),
        out_shape=shapes,
        compiler_params=pltpu.CompilerParams(vmem_limit_bytes=VMEM_LARGE),
        cost_estimate=pl.CostEstimate(
            flops=6 * rows * depth * width, bytes_accessed=6 * depth * width, transcendentals=rows * width
        ),
    )(mine, *flat, gate_weight, up_weight, down_weight, down_weight)
    return by_piece(outs, slots, pieces, grouped)


def pack_pairs_kernel(shards, mine, keys_ref, values_ref, *outs):
    width = keys_ref.shape[1] // shards
    for s in range(shards):
        columns = pl.ds(pl.multiple_of(lax.rem(mine[0] + s, shards) * width, width), width)
        outs[s][:, :width] = keys_ref[:, columns]
        outs[s][:, width:] = values_ref[:, columns]


def pack_pairs(mine, keys, values, shards):
    rows, width = keys.shape
    spec = pl.BlockSpec((rows, width), lambda k, *_: (0, 0))
    out = (rows, 2 * width // shards)
    return pl.pallas_call(
        functools.partial(pack_pairs_kernel, shards),
        grid_spec=pltpu.PrefetchScalarGridSpec(
            num_scalar_prefetch=1,
            grid=(1,),
            in_specs=[spec, spec],
            out_specs=[pl.BlockSpec(out, lambda k, *_: (0, 0))] * shards,
        ),
        out_shape=[jax.ShapeDtypeStruct(out, keys.dtype)] * shards,
    )(mine, keys, values)


def pack_queries_kernel(slots, halves, mine, picked_ref, query_ref, *outs):
    shards = len(slots)
    rows = query_ref.shape[0]
    half = rows // halves
    width = query_ref.shape[1] // shards
    packed, outs = outs[: halves * shards], outs[halves * shards :]
    place_refs, (order_ref, count_ref) = outs[:halves], outs[halves:]
    me = mine[0]
    across = lax.broadcasted_iota(jnp.int32, (rows, rows), 1)
    down = lax.broadcasted_iota(jnp.int32, (rows, rows), 0)
    up_to = jnp.where(down <= across, 1.0, 0.0).astype(jnp.bfloat16)
    picked = picked_ref[...]
    seen = jnp.dot(picked.astype(jnp.bfloat16), up_to, preferred_element_type=jnp.float32).astype(jnp.int32)
    count = seen[:, rows - 1 : rows]
    row_ids = lax.broadcasted_iota(jnp.int32, seen.shape, 1)
    slot = jnp.where(picked > 0, seen - 1, count + row_ids - seen)
    count_ref[0] = jnp.max(jnp.where(count > half, 1, 0))
    ids = row_ids.astype(jnp.bfloat16)
    for s in range(shards):
        shard = lax.rem(me - s + shards, shards)
        mine_slot = slot[0:1]
        for other in range(1, shards):
            mine_slot = jnp.where(shard == other, slot[other : other + 1], mine_slot)
        at_slot = jnp.where(mine_slot == down, 1.0, 0.0).astype(jnp.bfloat16)
        rows_at = lax.dot_general(ids, at_slot, (((1,), (1,)), ((), ())), preferred_element_type=jnp.float32)
        for h in range(halves):
            here = rows_at[0:1, h * half : (h + 1) * half]
            place_refs[h][slots.index(s)] = here.astype(jnp.int32) + shard * rows
        if s == 0:
            order_ref[...] = at_slot
    for s in range(shards):
        columns = pl.ds(pl.multiple_of(lax.rem(me + s, shards) * width, width), width)
        ordered = jnp.dot(order_ref[...], query_ref[:, columns], preferred_element_type=jnp.float32)
        ordered = ordered.astype(jnp.bfloat16)
        for h in range(halves):
            packed[h * shards + s][...] = ordered[h * half : (h + 1) * half]


def pack_queries(mine, picked, queries, slots, halves):
    shards = len(slots)
    rows, width = queries.shape
    packed = (rows // halves, width // shards)
    shapes = [jax.ShapeDtypeStruct(packed, jnp.bfloat16)] * (halves * shards)
    shapes += [jax.ShapeDtypeStruct((shards, 1, rows // halves), jnp.int32)] * halves
    shapes += [jax.ShapeDtypeStruct((rows, rows), jnp.bfloat16), jax.ShapeDtypeStruct((1,), jnp.int32)]

    def whole(shape):
        return pl.BlockSpec(shape, lambda k, *_: (0,) * len(shape))

    got = pl.pallas_call(
        functools.partial(pack_queries_kernel, slots, halves),
        grid_spec=pltpu.PrefetchScalarGridSpec(
            num_scalar_prefetch=1,
            grid=(1,),
            in_specs=[whole(picked.shape), whole(queries.shape)],
            out_specs=[whole(shape.shape) for shape in shapes[:-1]] + [pl.BlockSpec(memory_space=pltpu.SMEM)],
        ),
        out_shape=shapes,
    )(mine, picked, queries)
    packed, got = got[: halves * shards], got[halves * shards :]
    return [packed[h * shards : (h + 1) * shards] for h in range(halves)], got[:halves], *got[halves:]


def on_device(
    hidden_in,
    queries,
    keys,
    values,
    block_order,
    routes,
    out_weight,
    norm_gain,
    router_weight,
    gate_weight,
    up_weight,
    down_weight,
):
    shards = lax.axis_size("tp")
    blocks = lax.axis_size("ctx")
    me = lax.axis_index("tp")
    rows, model = hidden_in.shape
    block_rows = rows * shards
    per_device = HEADS // shards
    grouping = HEADS // KV_HEADS
    repeat_by = max(1, grouping // per_device)
    pairs = max(1, per_device // grouping)
    sharing = per_device // pairs
    half = rows // 2 if rows % 32 == 0 else rows
    halves = rows // half
    line = shards <= LINE
    pieces = 2 if line else 1
    cuts = [slice(c * (model // pieces), (c + 1) * (model // pieces)) for c in range(pieces)]
    slots = [s for s in range(1, shards, 2)] + [s for s in range(2, shards, 2)] + [0]
    shard_of = lax.rem(me - jnp.arange(shards, dtype=jnp.int32) + shards, shards)

    def shift(parts):
        moves = [[(i, (i + s) % shards) for i in range(shards)] for s in range(shards)]
        return [parts[0]] + [lax.ppermute(parts[s], "tp", moves[s]) for s in range(1, shards)]

    def exchange(source):
        got = lax.all_to_all(source, "tp", split_axis=1, concat_axis=0, tiled=True)
        got = got.reshape(shards, rows, source.shape[2])
        return [lax.dynamic_index_in_dim(got, shard_of[s], 0, keepdims=False) for s in range(shards)]

    def rights(count):
        return [(i, i + 1) for i in range(count)]

    def lefts(count):
        return [(i, i - 1) for i in range(shards - count, shards)]

    def reduce_line(pieces_terms):
        if not line:
            by_shard = [jnp.take(jnp.stack(terms), shard_of, axis=0).reshape(-1, terms[0].shape[1]) for terms in pieces_terms]
            return [
                lax.psum_scatter(term, "tp", scatter_dimension=0, tiled=True).astype(jnp.float32) for term in by_shard
            ], None
        got = [None] * len(pieces_terms)
        marks = []
        for s in range(1, shards):
            for c, terms in enumerate(pieces_terms):
                if got[c] is None:
                    sent = (terms[s], terms[shards - s])
                else:
                    arrived = got[c]
                    sent = (terms[s] + arrived[0], terms[shards - s] + arrived[1])
                right = lax.ppermute(sent[0], "tp", rights(s))
                left = lax.ppermute(sent[1], "tp", lefts(s))
                got[c] = lax.optimization_barrier((right, left))
            marks.append(got[0])
        return [
            terms[0].astype(jnp.float32) + right.astype(jnp.float32) + left.astype(jnp.float32)
            for terms, (right, left) in zip(pieces_terms, got)
        ], marks

    def gather_line(source, terms=None):
        if not line:
            got = lax.all_gather(source, "tp", axis=0)
            return [[jnp.take(got, shard_of, axis=0).reshape(shards * half, -1)]], None
        first_right = lax.ppermute(source, "tp", rights(shards - 1))
        first_left = lax.ppermute(source, "tp", lefts(shards - 1))
        first_right, first_left = lax.optimization_barrier((first_right, first_left))
        got = [(first_right[:, cut], first_left[:, cut]) for cut in cuts]
        from_left, from_right = [], []
        for s in range(2, shards):
            if terms is None:
                sent = got
                to_right = [(i, i + 1) for i in range(s - 1, shards - 1)]
                to_left = [(i, i - 1) for i in range(1, shards - s + 1)]
            else:
                sent = [
                    (
                        jnp.where(me >= s - 1, right, right + term[s - 1]),
                        jnp.where(me <= shards - s, left, left + term[shards - s + 1]),
                    )
                    for (right, left), term in zip(got, terms)
                ]
                to_right, to_left = rights(shards - 1), lefts(shards - 1)
            from_left.append([right for right, _ in sent])
            from_right.append([left for _, left in sent])
            got = [
                lax.optimization_barrier((lax.ppermute(right, "tp", to_right), lax.ppermute(left, "tp", to_left)))
                for right, left in sent
            ]
        from_left.append([right for right, _ in got])
        from_right.append([left for _, left in got])
        total = None
        if terms is not None:
            right = jnp.concatenate([right + term[shards - 1] for (right, _), term in zip(got, terms)], axis=1)
            left = jnp.concatenate([left + term[1] for (_, left), term in zip(got, terms)], axis=1)
            right = lax.ppermute(right, "tp", rights(shards - 1)).astype(jnp.float32)
            left = lax.ppermute(left, "tp", lefts(shards - 1)).astype(jnp.float32)
            total = jnp.concatenate([term[0] for term in terms], axis=1).astype(jnp.float32) + right + left
        return [[source]] + from_left + from_right, total

    picked = ((routes[:, 0] == 0) | (routes[:, 1] == 0)).reshape(shards, rows)
    if line:
        sent_pairs = pack_pairs(me[None], keys, values, shards)
        own_pairs = jnp.concatenate(shift(sent_pairs), axis=0)
        picked, _ = lax.optimization_barrier((picked.astype(jnp.int32), sent_pairs))
        packed, places, order, crowded = pack_queries(me[None], picked, queries, slots, halves)
        asked = [shift(packed[0])]
    else:

        def spread(source):
            widened = jnp.repeat(source.reshape(rows, KV_HEADS, HD), repeat_by, axis=1)
            return widened.reshape(rows, shards, pairs * HD)

        own_pairs = exchange(jnp.concatenate([spread(keys), spread(values)], axis=2))
        own_pairs = jnp.concatenate(own_pairs, axis=0)
        row_ids = jnp.arange(rows, dtype=jnp.int32)
        seen = jnp.cumsum(picked.astype(jnp.int32), axis=1)
        slot = jnp.where(picked, seen - 1, seen[:, -1:] + row_ids[None, :] - seen)
        at_slot = slot[:, None, :] == row_ids[None, :, None]
        row_of_slot = jnp.sum(jnp.where(at_slot, row_ids[None, None, :], 0), axis=2)
        places = row_of_slot + jnp.arange(shards, dtype=jnp.int32)[:, None] * rows
        places = [jnp.stack([jnp.take(places, shard_of[s], axis=0) for s in slots])[:, None, :]]
        order = lax.dynamic_index_in_dim(at_slot, me, 0, keepdims=False).astype(jnp.bfloat16)
        ordered = jnp.dot(order, queries, preferred_element_type=jnp.float32).astype(jnp.bfloat16)
        asked = [exchange(ordered.reshape(rows, shards, per_device * HD))]

    pair_list, held = [own_pairs], [[0]]
    offset = blocks // 2
    while offset >= 1:
        pair_list += [lax.ppermute(part, "ctx", [(i, i ^ offset) for i in range(blocks)]) for part in pair_list]
        held += [[other ^ offset for other in group] for group in held]
        if line and len(pair_list) == 2:
            pair_list[1], asked[0] = lax.optimization_barrier((pair_list[1], asked[0]))
        offset //= 2

    def reorder(source):
        return jnp.dot(order, source, preferred_element_type=jnp.float32).astype(jnp.bfloat16)

    def restore(parts):
        whole = jnp.concatenate(parts, axis=0) if len(parts) > 1 else parts[0]
        return lax.dot_general(
            order, whole, (((0,), (0,)), ((), ())), preferred_element_type=jnp.float32
        ).astype(jnp.bfloat16)

    mine = lax.axis_index("ctx").astype(jnp.int32)[None]
    expert_ids = jnp.arange(router_weight.shape[1], dtype=jnp.int32)

    def project(which):
        terms = attend(
            block_order,
            jnp.stack([lax.axis_index("ctx"), me]).astype(jnp.int32),
            [asked[which][s] for s in slots],
            places[which],
            pair_list,
            held,
            pairs,
            sharing,
            block_rows,
            out_weight,
            pieces,
            line,
        )
        return [[term[slots.index(s)] for s in range(shards)] for term in terms]

    def finish(which, head_sums):
        base = hidden[which * half : (which + 1) * half].astype(jnp.float32)
        return jnp.concatenate(
            [(base[:, cut] + head_sum).astype(jnp.bfloat16) for cut, head_sum in zip(cuts, head_sums)], axis=1
        )

    def normalise(attended):
        widened = attended.astype(jnp.float32)
        return (
            widened * lax.rsqrt(jnp.mean(widened * widened, axis=1, keepdims=True) + 1e-05) * norm_gain
        ).astype(jnp.bfloat16)

    def share_of(which, normed):
        logits = jnp.dot(normed, router_weight, preferred_element_type=jnp.float32)
        named = my_routes[which * half : (which + 1) * half]
        first = jnp.sum(jnp.where(named[:, 0:1] == expert_ids[None, :], logits, 0.0), axis=1)
        second = jnp.sum(jnp.where(named[:, 1:2] == expert_ids[None, :], logits, 0.0), axis=1)
        share = jnp.where(named[:, 0] == 0, 1.0 / (1.0 + jnp.exp(second - first)), 0.0)
        return share + jnp.where(named[:, 1] == 0, 1.0 / (1.0 + jnp.exp(first - second)), 0.0)

    def expert(which, normed, sources, beside=None):
        terms = expert_rows(me[None], sources, gate_weight, up_weight, down_weight, shards, pieces, False)
        if beside is not None:
            terms, beside = lax.optimization_barrier((terms, beside))
        sums, marks = reduce_line(terms)
        if line:
            normed, _ = lax.optimization_barrier((normed, marks[0]))
        share = share_of(which, normed)
        parts = [(total * share[:, None]).astype(jnp.bfloat16) for total in sums]
        return jnp.concatenate(parts, axis=1), beside

    def late_expert(source):
        normed = normalise(source)
        return expert(1, normed, gather_line(normed)[0])[0]

    terms = project(0)
    if halves > 1:
        asked.append(shift(packed[1]))
        terms, asked[1] = lax.optimization_barrier((terms, asked[1]))
    totals, marks = reduce_line(terms)
    if line:
        hidden_in, order, _ = lax.optimization_barrier((hidden_in, order, marks[0]))
    hidden = reorder(hidden_in)
    my_routes = lax.dynamic_slice_in_dim(routes, me * rows, rows, 0).astype(jnp.bfloat16)
    my_routes = reorder(my_routes).astype(jnp.int32)
    first_half = finish(0, totals)
    normed = normalise(first_half)
    if halves == 1:
        return (restore([first_half]), restore([expert(0, normed, gather_line(normed)[0])[0]]))
    asked[1], _ = lax.optimization_barrier((asked[1], normed))
    sources, second_sum = gather_line(normed, project(1))
    second_half = (hidden[half:].astype(jnp.float32) + second_sum).astype(jnp.bfloat16)
    part, second_half = expert(0, normed, sources, second_half)
    part, late = lax.optimization_barrier((part, second_half))
    late = lax.cond(crowded[0] > 0, late_expert, jnp.zeros_like, late)
    return (restore([first_half, second_half]), restore([part, late]))


def solution(mesh):
    return jax.shard_map(
        on_device,
        mesh=mesh,
        in_specs=(
            P(("req", "ctx", "tp"), None),
            P(("req", "ctx", "tp"), None),
            P(("req", "ctx", "tp"), None),
            P(("req", "ctx", "tp"), None),
            P("req"),
            P(("req", "ctx"), None),
            P("tp", None),
            P(),
            P(),
            P(None, "tp"),
            P(None, "tp"),
            P("tp", None),
        ),
        out_specs=(P(("req", "ctx", "tp"), None), P(("req", "ctx", "tp"), None)),
        check_vma=False,
    )
```

```python
import functools
import math

import jax
import jax.numpy as jnp
from jax import lax
from jax.experimental import pallas as pl
from jax.experimental.pallas import tpu as pltpu
from jax.sharding import PartitionSpec as P

HEADS = 32
KV_HEADS = 8
HD = 128
FACTOR = math.log2(math.e) / math.sqrt(HD)
LINE = 4
SUM_ROWS = 16
TILE = 256
VMEM_HELD = 21 * 1024 * 1024
VMEM_LARGE = 28 * 1024 * 1024


def attention_kernel(slots, together, held, pairs, sharing, block_rows, plan, *refs):
    pieces, grouped = plan
    (order, mine), refs = refs[:2], refs[2:]
    sent_queries, refs = refs[:slots], refs[slots:]
    place_ref, refs = refs[0], refs[1:]
    sent_pairs, weight, refs = refs[: len(held)], refs[len(held)], refs[len(held) + 1 :]
    outs, refs = refs[: pieces * (slots if grouped else 1)], refs[pieces * (slots if grouped else 1) :]
    query_refs, pair_refs, refs = refs[:slots], refs[slots : slots + len(held)], refs[slots + len(held) :]
    query_ref, key_ref, value_ref, top_ref, total_ref, head_ref, weight_ref, arrived, here = refs
    half = query_refs[0].shape[0]
    step = pl.program_id(0)
    me = mine[0]
    my_block = order[me]
    blocks = [(ref, index, offset) for ref, group in zip(pair_refs, held) for index, offset in enumerate(group)]
    weight_copy = pltpu.make_async_copy(weight, weight_ref, arrived)
    moves = [
        pltpu.make_async_copy(source, target, here.at[i])
        for i, (source, target) in enumerate(
            list(zip(sent_pairs, pair_refs)) + list(zip(sent_queries, query_refs))
        )
    ]

    @pl.when(step == 0)
    def _():
        for move in moves:
            move.start()
        value_ref[:, :, HD:, :] = jnp.ones((len(blocks), pairs, SUM_ROWS, block_rows), jnp.bfloat16)

    @pl.when(step == 0)
    def _():
        for move in moves:
            move.wait()
        weight_copy.start()

    for at, (ref, index, offset) in enumerate(blocks):

        @pl.when((step == 0) & (order[me ^ offset] <= my_block))
        def _():
            for p in range(pairs):
                rows = slice(index * block_rows, (index + 1) * block_rows)
                key_ref[at, p] = ref[rows, p * HD : (p + 1) * HD]
                value_ref[at, p, :HD, :] = ref[rows, (pairs + p) * HD : (pairs + p + 1) * HD].T

    for at in range(slots):

        @pl.when(step == at // together)
        def _():
            for p in range(pairs):
                for g in range(sharing):
                    column = (p * sharing + g) * HD
                    row = (at % together * sharing + g) * half
                    query_ref[p, row : row + half, :] = query_refs[at][:, column : column + HD]

    def scores_of(p, at):
        return lax.dot_general(
            key_ref[at, p], query_ref[p], (((1,), (1,)), ((), ())), preferred_element_type=jnp.float32
        )

    def mixed_of(p, at, weights):
        return jnp.dot(value_ref[at, p], weights, preferred_element_type=jnp.float32)

    place = jnp.concatenate([place_ref[i] for i in range(together) for _ in range(sharing)], axis=1)
    rows = block_rows // slots
    down = lax.broadcasted_iota(jnp.int32, (rows, place.shape[1]), 0)
    visible = jnp.concatenate(
        [down <= place - lax.rem(mine[1] - s + slots, slots) * rows for s in range(slots)], axis=0
    )
    for p in range(pairs):
        scores = jnp.where(visible, scores_of(p, 0), -1e30)
        top = jnp.max(scores, axis=0, keepdims=True)
        weights = jnp.exp2((scores - top) * FACTOR).astype(jnp.bfloat16)
        top_ref[p, 0:1, :] = top
        total_ref[p] = mixed_of(p, 0, weights)

    @pl.loop(1, len(blocks))
    def _(at):
        offset = blocks[1][2] if len(blocks) > 1 else 0
        for other in range(2, len(blocks)):
            offset = jnp.where(at == other, blocks[other][2], offset)

        @pl.when(order[me ^ offset] < my_block)
        def _():
            for p in range(pairs):
                top = top_ref[p, 0:1, :]
                scores = scores_of(p, at)
                raised = jnp.maximum(top, jnp.max(scores, axis=0, keepdims=True))
                weights = jnp.exp2((scores - raised) * FACTOR).astype(jnp.bfloat16)
                top_ref[p, 0:1, :] = raised
                total_ref[p] = total_ref[p] * jnp.exp2((top - raised) * FACTOR) + mixed_of(p, at, weights)

    for p in range(pairs):
        mixed = (total_ref[p, :HD, :] / total_ref[p, HD : HD + 1, :]).T.astype(jnp.bfloat16)
        for i in range(together):
            for g in range(sharing):
                column = (p * sharing + g) * HD
                row = (i * sharing + g) * half
                at = pl.multiple_of((step * together + i) * half, half)
                head_ref[pl.ds(at, half), column : column + HD] = mixed[row : row + half]

    @pl.when(step == pl.num_programs(0) - 1)
    def _():
        weight_copy.wait()
        width = weight.shape[1] // pieces
        tile = 2 * TILE
        for c in range(pieces):

            @pl.loop(0, width // tile)
            def _(n):
                columns = pl.ds(pl.multiple_of(c * width + n * tile, tile), tile)
                value = jnp.dot(head_ref[...], weight_ref[:, columns], preferred_element_type=jnp.float32)
                share_out(outs[c * len(outs) // pieces :], pl.ds(pl.multiple_of(n * tile, tile), tile), value)


def share_out(outs, columns, value):
    rows = outs[0].shape[0]
    for g in range(value.shape[0] // rows):
        outs[g][:, columns] = value[g * rows : (g + 1) * rows].astype(jnp.bfloat16)


def piece_shapes(rows, width, slots, pieces, grouped):
    return [jax.ShapeDtypeStruct((rows // slots if grouped else rows, width // pieces), jnp.bfloat16)] * (
        pieces * (slots if grouped else 1)
    )


def by_piece(outs, slots, pieces, grouped):
    if grouped:
        return [outs[c * slots : (c + 1) * slots] for c in range(pieces)]
    return [[out[s * (out.shape[0] // slots) : (s + 1) * (out.shape[0] // slots)] for s in range(slots)] for out in outs]


def in_hbm(arrays):
    return [pltpu.with_memory_space_constraint(array, pltpu.HBM) for array in arrays]


def attend(order, mine, queries, places, pair_list, held, pairs, sharing, block_rows, weight, pieces, grouped):
    slots = len(queries)
    half, width = queries[0].shape
    together = 2 if slots <= LINE else 1
    tall = together * sharing * half
    blocks = sum(len(group) for group in held)
    count = blocks * block_rows
    shapes = piece_shapes(slots * half, weight.shape[1], slots, pieces, grouped)
    kernel = functools.partial(
        attention_kernel, slots, together, held, pairs, sharing, block_rows, (pieces, grouped)
    )
    outs = pl.pallas_call(
        kernel,
        grid_spec=pltpu.PrefetchScalarGridSpec(
            num_scalar_prefetch=2,
            grid=(slots // together,),
            in_specs=[pl.BlockSpec(memory_space=pltpu.HBM)] * slots
            + [pl.BlockSpec((together, 1, half), lambda s, *_: (s, 0, 0))]
            + [pl.BlockSpec(memory_space=pltpu.HBM)] * (len(pair_list) + 1),
            out_specs=[pl.BlockSpec(shape.shape, lambda s, *_: (0, 0)) for shape in shapes],
            scratch_shapes=[pltpu.VMEM((half, width), jnp.bfloat16)] * slots
            + [pltpu.VMEM(pair.shape, pair.dtype) for pair in pair_list]
            + [
                pltpu.VMEM((pairs, tall, HD), jnp.bfloat16),
                pltpu.VMEM((blocks, pairs, block_rows, HD), jnp.bfloat16),
                pltpu.VMEM((blocks, pairs, HD + SUM_ROWS, block_rows), jnp.bfloat16),
                pltpu.VMEM((pairs, 8, tall), jnp.float32),
                pltpu.VMEM((pairs, HD + SUM_ROWS, tall), jnp.float32),
                pltpu.VMEM((slots * half, width), jnp.bfloat16),
                pltpu.VMEM(weight.shape, weight.dtype),
                pltpu.SemaphoreType.DMA,
                pltpu.SemaphoreType.DMA((slots + len(pair_list),)),
            ],
        ),
        out_shape=shapes,
        compiler_params=pltpu.CompilerParams(vmem_limit_bytes=VMEM_HELD),
        cost_estimate=pl.CostEstimate(
            flops=40 * slots * half * width * count,
            bytes_accessed=2 * (2 * slots * half * width + count * 2 * pairs * HD + weight.size),
            transcendentals=slots * half * width // HD * count,
        ),
    )(order, mine, *in_hbm(queries), places, *in_hbm(pair_list), *in_hbm([weight]))
    return by_piece(outs, slots, pieces, grouped)


def expert_kernel(plan, pieces, *refs):
    mine, refs = refs[0], refs[1:]
    sources = []
    for count in plan:
        sources.append(refs[:count])
        refs = refs[count:]
    gate_weight, up_weight, down_weights, refs = refs[0], refs[1], refs[2:4], refs[4:]
    outs, (chosen, acts) = refs[:-2], refs[-2:]
    step = pl.program_id(0)
    tile = gate_weight.shape[1]
    first = acts.shape[1] // tile

    def place(s, source):
        rows, width = source[0].shape
        for c, ref in enumerate(source):
            chosen[s * rows : (s + 1) * rows, c * width : (c + 1) * width] = ref[...]

    @pl.when(step == 0)
    def _():
        place(0, sources[0])
        for s in range(1, (len(plan) + 1) // 2):
            right, left = sources[s], sources[len(plan) - s]

            @pl.when(mine[0] >= s)
            def _():
                place(s, right)

            @pl.when(mine[0] < s)
            def _():
                place(s, left)

    @pl.when(step < first)
    def _():
        gate = jnp.dot(chosen[...], gate_weight[...], preferred_element_type=jnp.float32)
        upward = jnp.dot(chosen[...], up_weight[...], preferred_element_type=jnp.float32)
        columns = pl.ds(pl.multiple_of(step * tile, tile), tile)
        acts[:, columns] = (gate / (1.0 + jnp.exp(-gate)) * upward).astype(jnp.bfloat16)

    @pl.when(step >= first)
    def _():
        strip = down_weights[0].shape[1]
        pairs = outs[0].shape[1] // (2 * strip)
        for j, down_weight in enumerate(down_weights):
            value = jnp.dot(acts[...], down_weight[...], preferred_element_type=jnp.float32)
            for c in range(pieces):

                @pl.when((step - first) // pairs == c)
                def _():
                    at = (2 * (step - first - c * pairs) + j) * strip
                    share_out(outs[c * len(outs) // pieces :], pl.ds(pl.multiple_of(at, strip), strip), value)


def expert_rows(mine, sources, gate_weight, up_weight, down_weight, slots, pieces, grouped):
    flat = [piece for source in sources for piece in source]
    rows = flat[0].shape[0] * ((len(sources) + 1) // 2)
    depth, width = gate_weight.shape
    tile, strip = min(TILE, width), 2 * TILE
    first = width // tile
    shapes = piece_shapes(rows, depth, slots, pieces, grouped)
    in_place = pl.BlockSpec(memory_space=pltpu.VMEM)
    weight = pl.BlockSpec((depth, tile), lambda n, *_: (0, jnp.minimum(n, first - 1)))
    outs = pl.pallas_call(
        functools.partial(expert_kernel, [len(source) for source in sources], pieces),
        grid_spec=pltpu.PrefetchScalarGridSpec(
            num_scalar_prefetch=1,
            grid=(first + depth // (2 * strip),),
            in_specs=[in_place] * len(flat)
            + [weight, weight]
            + [
                pl.BlockSpec((width, strip), functools.partial(lambda j, n, *_: (0, 2 * jnp.maximum(n - first, 0) + j), j))
                for j in range(2)
            ],
            out_specs=[in_place] * len(shapes),
            scratch_shapes=[pltpu.VMEM((rows, depth), jnp.bfloat16), pltpu.VMEM((rows, width), jnp.bfloat16)],
        ),
        out_shape=shapes,
        compiler_params=pltpu.CompilerParams(vmem_limit_bytes=VMEM_LARGE),
        cost_estimate=pl.CostEstimate(
            flops=6 * rows * depth * width, bytes_accessed=6 * depth * width, transcendentals=rows * width
        ),
    )(mine, *flat, gate_weight, up_weight, down_weight, down_weight)
    return by_piece(outs, slots, pieces, grouped)


def pack_pairs_kernel(shards, mine, keys_ref, values_ref, *outs):
    width = keys_ref.shape[1] // shards
    for s in range(shards):
        columns = pl.ds(pl.multiple_of(lax.rem(mine[0] + s, shards) * width, width), width)
        outs[s][:, :width] = keys_ref[:, columns]
        outs[s][:, width:] = values_ref[:, columns]


def pack_pairs(mine, keys, values, shards):
    rows, width = keys.shape
    spec = pl.BlockSpec((rows, width), lambda k, *_: (0, 0))
    out = (rows, 2 * width // shards)
    return pl.pallas_call(
        functools.partial(pack_pairs_kernel, shards),
        grid_spec=pltpu.PrefetchScalarGridSpec(
            num_scalar_prefetch=1,
            grid=(1,),
            in_specs=[spec, spec],
            out_specs=[pl.BlockSpec(out, lambda k, *_: (0, 0))] * shards,
        ),
        out_shape=[jax.ShapeDtypeStruct(out, keys.dtype)] * shards,
    )(mine, keys, values)


def pack_queries_kernel(slots, halves, mine, picked_ref, query_ref, *outs):
    shards = len(slots)
    rows = query_ref.shape[0]
    half = rows // halves
    width = query_ref.shape[1] // shards
    packed, outs = outs[: halves * shards], outs[halves * shards :]
    place_refs, (order_ref, count_ref) = outs[:halves], outs[halves:]
    me = mine[0]
    across = lax.broadcasted_iota(jnp.int32, (rows, rows), 1)
    down = lax.broadcasted_iota(jnp.int32, (rows, rows), 0)
    up_to = jnp.where(down <= across, 1.0, 0.0).astype(jnp.bfloat16)
    picked = picked_ref[...]
    seen = jnp.dot(picked.astype(jnp.bfloat16), up_to, preferred_element_type=jnp.float32).astype(jnp.int32)
    count = seen[:, rows - 1 : rows]
    row_ids = lax.broadcasted_iota(jnp.int32, seen.shape, 1)
    slot = jnp.where(picked > 0, seen - 1, count + row_ids - seen)
    count_ref[0] = jnp.max(jnp.where(count > half, 1, 0))
    ids = row_ids.astype(jnp.bfloat16)
    for s in range(shards):
        shard = lax.rem(me - s + shards, shards)
        mine_slot = slot[0:1]
        for other in range(1, shards):
            mine_slot = jnp.where(shard == other, slot[other : other + 1], mine_slot)
        at_slot = jnp.where(mine_slot == down, 1.0, 0.0).astype(jnp.bfloat16)
        rows_at = lax.dot_general(ids, at_slot, (((1,), (1,)), ((), ())), preferred_element_type=jnp.float32)
        for h in range(halves):
            here = rows_at[0:1, h * half : (h + 1) * half]
            place_refs[h][slots.index(s)] = here.astype(jnp.int32) + shard * rows
        if s == 0:
            order_ref[...] = at_slot
    for s in range(shards):
        columns = pl.ds(pl.multiple_of(lax.rem(me + s, shards) * width, width), width)
        ordered = jnp.dot(order_ref[...], query_ref[:, columns], preferred_element_type=jnp.float32)
        ordered = ordered.astype(jnp.bfloat16)
        for h in range(halves):
            packed[h * shards + s][...] = ordered[h * half : (h + 1) * half]


def pack_queries(mine, picked, queries, slots, halves):
    shards = len(slots)
    rows, width = queries.shape
    packed = (rows // halves, width // shards)
    shapes = [jax.ShapeDtypeStruct(packed, jnp.bfloat16)] * (halves * shards)
    shapes += [jax.ShapeDtypeStruct((shards, 1, rows // halves), jnp.int32)] * halves
    shapes += [jax.ShapeDtypeStruct((rows, rows), jnp.bfloat16), jax.ShapeDtypeStruct((1,), jnp.int32)]

    def whole(shape):
        return pl.BlockSpec(shape, lambda k, *_: (0,) * len(shape))

    got = pl.pallas_call(
        functools.partial(pack_queries_kernel, slots, halves),
        grid_spec=pltpu.PrefetchScalarGridSpec(
            num_scalar_prefetch=1,
            grid=(1,),
            in_specs=[whole(picked.shape), whole(queries.shape)],
            out_specs=[whole(shape.shape) for shape in shapes[:-1]] + [pl.BlockSpec(memory_space=pltpu.SMEM)],
        ),
        out_shape=shapes,
    )(mine, picked, queries)
    packed, got = got[: halves * shards], got[halves * shards :]
    return [packed[h * shards : (h + 1) * shards] for h in range(halves)], got[:halves], *got[halves:]


def on_device(
    hidden_in,
    queries,
    keys,
    values,
    block_order,
    routes,
    out_weight,
    norm_gain,
    router_weight,
    gate_weight,
    up_weight,
    down_weight,
):
    shards = lax.axis_size("tp")
    blocks = lax.axis_size("ctx")
    me = lax.axis_index("tp")
    rows, model = hidden_in.shape
    block_rows = rows * shards
    per_device = HEADS // shards
    grouping = HEADS // KV_HEADS
    repeat_by = max(1, grouping // per_device)
    pairs = max(1, per_device // grouping)
    sharing = per_device // pairs
    half = rows // 2 if rows % 32 == 0 else rows
    halves = rows // half
    line = shards <= LINE
    pieces = 2 if line else 1
    cuts = [slice(c * (model // pieces), (c + 1) * (model // pieces)) for c in range(pieces)]
    slots = [s for s in range(1, shards, 2)] + [s for s in range(2, shards, 2)] + [0]
    shard_of = lax.rem(me - jnp.arange(shards, dtype=jnp.int32) + shards, shards)

    def shift(parts):
        moves = [[(i, (i + s) % shards) for i in range(shards)] for s in range(shards)]
        return [parts[0]] + [lax.ppermute(parts[s], "tp", moves[s]) for s in range(1, shards)]

    def exchange(source):
        got = lax.all_to_all(source, "tp", split_axis=1, concat_axis=0, tiled=True)
        got = got.reshape(shards, rows, source.shape[2])
        return [lax.dynamic_index_in_dim(got, shard_of[s], 0, keepdims=False) for s in range(shards)]

    def rights(count):
        return [(i, i + 1) for i in range(count)]

    def lefts(count):
        return [(i, i - 1) for i in range(shards - count, shards)]

    def reduce_line(pieces_terms):
        if not line:
            by_shard = [jnp.take(jnp.stack(terms), shard_of, axis=0).reshape(-1, terms[0].shape[1]) for terms in pieces_terms]
            return [
                lax.psum_scatter(term, "tp", scatter_dimension=0, tiled=True).astype(jnp.float32) for term in by_shard
            ], None
        got = [None] * len(pieces_terms)
        marks = []
        for s in range(1, shards):
            for c, terms in enumerate(pieces_terms):
                if got[c] is None:
                    sent = (terms[s], terms[shards - s])
                else:
                    arrived = got[c]
                    sent = (terms[s] + arrived[0], terms[shards - s] + arrived[1])
                right = lax.ppermute(sent[0], "tp", rights(s))
                left = lax.ppermute(sent[1], "tp", lefts(s))
                got[c] = lax.optimization_barrier((right, left))
            marks.append(got[0])
        return [
            terms[0].astype(jnp.float32) + right.astype(jnp.float32) + left.astype(jnp.float32)
            for terms, (right, left) in zip(pieces_terms, got)
        ], marks

    def gather_line(source, terms=None):
        if not line:
            got = lax.all_gather(source, "tp", axis=0)
            return [[jnp.take(got, shard_of, axis=0).reshape(shards * half, -1)]], None
        first_right = lax.ppermute(source, "tp", rights(shards - 1))
        first_left = lax.ppermute(source, "tp", lefts(shards - 1))
        first_right, first_left = lax.optimization_barrier((first_right, first_left))
        got = [(first_right[:, cut], first_left[:, cut]) for cut in cuts]
        from_left, from_right = [], []
        for s in range(2, shards):
            if terms is None:
                sent = got
                to_right = [(i, i + 1) for i in range(s - 1, shards - 1)]
                to_left = [(i, i - 1) for i in range(1, shards - s + 1)]
            else:
                sent = [
                    (
                        jnp.where(me >= s - 1, right, right + term[s - 1]),
                        jnp.where(me <= shards - s, left, left + term[shards - s + 1]),
                    )
                    for (right, left), term in zip(got, terms)
                ]
                to_right, to_left = rights(shards - 1), lefts(shards - 1)
            from_left.append([right for right, _ in sent])
            from_right.append([left for _, left in sent])
            got = [
                lax.optimization_barrier((lax.ppermute(right, "tp", to_right), lax.ppermute(left, "tp", to_left)))
                for right, left in sent
            ]
        from_left.append([right for right, _ in got])
        from_right.append([left for _, left in got])
        total = None
        if terms is not None:
            right = jnp.concatenate([right + term[shards - 1] for (right, _), term in zip(got, terms)], axis=1)
            left = jnp.concatenate([left + term[1] for (_, left), term in zip(got, terms)], axis=1)
            right = lax.ppermute(right, "tp", rights(shards - 1))
            left = lax.ppermute(left, "tp", lefts(shards - 1))
            total = (right, left)
        return [[source]] + from_left + from_right, total

    picked = ((routes[:, 0] == 0) | (routes[:, 1] == 0)).reshape(shards, rows)
    if line:
        sent_pairs = pack_pairs(me[None], keys, values, shards)
        own_pairs = jnp.concatenate(shift(sent_pairs), axis=0)
        picked, _ = lax.optimization_barrier((picked.astype(jnp.int32), sent_pairs))
        packed, places, order, crowded = pack_queries(me[None], picked, queries, slots, halves)
        asked = [shift(packed[0])]
    else:

        def spread(source):
            widened = jnp.repeat(source.reshape(rows, KV_HEADS, HD), repeat_by, axis=1)
            return widened.reshape(rows, shards, pairs * HD)

        own_pairs = exchange(jnp.concatenate([spread(keys), spread(values)], axis=2))
        own_pairs = jnp.concatenate(own_pairs, axis=0)
        row_ids = jnp.arange(rows, dtype=jnp.int32)
        seen = jnp.cumsum(picked.astype(jnp.int32), axis=1)
        slot = jnp.where(picked, seen - 1, seen[:, -1:] + row_ids[None, :] - seen)
        at_slot = slot[:, None, :] == row_ids[None, :, None]
        row_of_slot = jnp.sum(jnp.where(at_slot, row_ids[None, None, :], 0), axis=2)
        places = row_of_slot + jnp.arange(shards, dtype=jnp.int32)[:, None] * rows
        places = [jnp.stack([jnp.take(places, shard_of[s], axis=0) for s in slots])[:, None, :]]
        order = lax.dynamic_index_in_dim(at_slot, me, 0, keepdims=False).astype(jnp.bfloat16)
        ordered = jnp.dot(order, queries, preferred_element_type=jnp.float32).astype(jnp.bfloat16)
        asked = [exchange(ordered.reshape(rows, shards, per_device * HD))]

    pair_list, held = [own_pairs], [[0]]
    offset = blocks // 2
    while offset >= 1:
        pair_list += [lax.ppermute(part, "ctx", [(i, i ^ offset) for i in range(blocks)]) for part in pair_list]
        held += [[other ^ offset for other in group] for group in held]
        if line and len(pair_list) == 2:
            pair_list[1], asked[0] = lax.optimization_barrier((pair_list[1], asked[0]))
        offset //= 2

    def reorder(source):
        return jnp.dot(order, source, preferred_element_type=jnp.float32).astype(jnp.bfloat16)

    def restore(parts):
        whole = jnp.concatenate(parts, axis=0) if len(parts) > 1 else parts[0]
        return lax.dot_general(
            order, whole, (((0,), (0,)), ((), ())), preferred_element_type=jnp.float32
        ).astype(jnp.bfloat16)

    mine = lax.axis_index("ctx").astype(jnp.int32)[None]
    expert_ids = jnp.arange(router_weight.shape[1], dtype=jnp.int32)

    def project(which):
        terms = attend(
            block_order,
            jnp.stack([lax.axis_index("ctx"), me]).astype(jnp.int32),
            [asked[which][s] for s in slots],
            places[which],
            pair_list,
            held,
            pairs,
            sharing,
            block_rows,
            out_weight,
            pieces,
            False,
        )
        return [[term[slots.index(s)] for s in range(shards)] for term in terms]

    def finish(which, head_sums):
        base = hidden[which * half : (which + 1) * half].astype(jnp.float32)
        return jnp.concatenate(
            [(base[:, cut] + head_sum).astype(jnp.bfloat16) for cut, head_sum in zip(cuts, head_sums)], axis=1
        )

    def normalise(attended):
        widened = attended.astype(jnp.float32)
        return (
            widened * lax.rsqrt(jnp.mean(widened * widened, axis=1, keepdims=True) + 1e-05) * norm_gain
        ).astype(jnp.bfloat16)

    def share_of(which, normed):
        logits = jnp.dot(normed, router_weight, preferred_element_type=jnp.float32)
        named = my_routes[which * half : (which + 1) * half]
        first = jnp.sum(jnp.where(named[:, 0:1] == expert_ids[None, :], logits, 0.0), axis=1)
        second = jnp.sum(jnp.where(named[:, 1:2] == expert_ids[None, :], logits, 0.0), axis=1)
        share = jnp.where(named[:, 0] == 0, 1.0 / (1.0 + jnp.exp(second - first)), 0.0)
        return share + jnp.where(named[:, 1] == 0, 1.0 / (1.0 + jnp.exp(first - second)), 0.0)

    def expert(which, normed, sources, beside=None):
        terms = expert_rows(me[None], sources, gate_weight, up_weight, down_weight, shards, pieces, False)
        if beside is not None:
            terms, beside = lax.optimization_barrier((terms, beside))
        sums, marks = reduce_line(terms)
        if line:
            normed, _ = lax.optimization_barrier((normed, marks[0]))
        share = share_of(which, normed)
        parts = [(total * share[:, None]).astype(jnp.bfloat16) for total in sums]
        return jnp.concatenate(parts, axis=1), beside

    def late_expert(source):
        normed = normalise(source)
        return expert(1, normed, gather_line(normed)[0])[0]

    terms = project(0)
    if halves > 1:
        asked.append(shift(packed[1]))
        terms, asked[1] = lax.optimization_barrier((terms, asked[1]))
    totals, marks = reduce_line(terms)
    if line:
        hidden_in, order, _ = lax.optimization_barrier((hidden_in, order, marks[0]))
    hidden = reorder(hidden_in)
    my_routes = lax.dynamic_slice_in_dim(routes, me * rows, rows, 0).astype(jnp.bfloat16)
    my_routes = reorder(my_routes).astype(jnp.int32)
    first_half = finish(0, totals)
    normed = normalise(first_half)
    if halves == 1:
        return (restore([first_half]), restore([expert(0, normed, gather_line(normed)[0])[0]]))
    asked[1], _ = lax.optimization_barrier((asked[1], normed))
    terms = project(1)
    sources, arrived = gather_line(normed, terms)
    part, (right, left) = expert(0, normed, sources, arrived)
    own = jnp.concatenate([term[0] for term in terms], axis=1).astype(jnp.float32)
    second_sum = own + right.astype(jnp.float32) + left.astype(jnp.float32)
    second_half = (hidden[half:].astype(jnp.float32) + second_sum).astype(jnp.bfloat16)
    part, late = lax.optimization_barrier((part, second_half))
    late = lax.cond(crowded[0] > 0, late_expert, jnp.zeros_like, late)
    return (restore([first_half, second_half]), restore([part, late]))


def solution(mesh):
    return jax.shard_map(
        on_device,
        mesh=mesh,
        in_specs=(
            P(("req", "ctx", "tp"), None),
            P(("req", "ctx", "tp"), None),
            P(("req", "ctx", "tp"), None),
            P(("req", "ctx", "tp"), None),
            P("req"),
            P(("req", "ctx"), None),
            P("tp", None),
            P(),
            P(),
            P(None, "tp"),
            P(None, "tp"),
            P("tp", None),
        ),
        out_specs=(P(("req", "ctx", "tp"), None), P(("req", "ctx", "tp"), None)),
        check_vma=False,
    )
```

```python
import functools
import math

import jax
import jax.numpy as jnp
from jax import lax
from jax.experimental import pallas as pl
from jax.experimental.pallas import tpu as pltpu
from jax.sharding import PartitionSpec as P

HEADS = 32
KV_HEADS = 8
HD = 128
FACTOR = math.log2(math.e) / math.sqrt(HD)
LINE = 4
SUM_ROWS = 16
TILE = 256
VMEM_HELD = 21 * 1024 * 1024
VMEM_LARGE = 28 * 1024 * 1024


def attention_kernel(slots, together, held, pairs, sharing, block_rows, plan, *refs):
    pieces, grouped = plan
    (order, mine), refs = refs[:2], refs[2:]
    sent_queries, refs = refs[:slots], refs[slots:]
    place_ref, refs = refs[0], refs[1:]
    sent_pairs, weight, refs = refs[: len(held)], refs[len(held)], refs[len(held) + 1 :]
    outs, refs = refs[: pieces * (slots if grouped else 1)], refs[pieces * (slots if grouped else 1) :]
    query_refs, pair_refs, refs = refs[:slots], refs[slots : slots + len(held)], refs[slots + len(held) :]
    query_ref, key_ref, value_ref, top_ref, total_ref, head_ref, weight_ref, arrived, here = refs
    half = query_refs[0].shape[0]
    step = pl.program_id(0)
    me = mine[0]
    my_block = order[me]
    blocks = [(ref, index, offset) for ref, group in zip(pair_refs, held) for index, offset in enumerate(group)]
    weight_copy = pltpu.make_async_copy(weight, weight_ref, arrived)
    moves = [
        pltpu.make_async_copy(source, target, here.at[i])
        for i, (source, target) in enumerate(
            list(zip(sent_pairs, pair_refs)) + list(zip(sent_queries, query_refs))
        )
    ]

    @pl.when(step == 0)
    def _():
        for move in moves:
            move.start()
        value_ref[:, :, HD:, :] = jnp.ones((len(blocks), pairs, SUM_ROWS, block_rows), jnp.bfloat16)

    @pl.when(step == 0)
    def _():
        for move in moves:
            move.wait()
        weight_copy.start()

    for at, (ref, index, offset) in enumerate(blocks):

        @pl.when((step == 0) & (order[me ^ offset] <= my_block))
        def _():
            for p in range(pairs):
                rows = slice(index * block_rows, (index + 1) * block_rows)
                key_ref[at, p] = ref[rows, p * HD : (p + 1) * HD]
                value_ref[at, p, :HD, :] = ref[rows, (pairs + p) * HD : (pairs + p + 1) * HD].T

    for at in range(slots):

        @pl.when(step == at // together)
        def _():
            for p in range(pairs):
                for g in range(sharing):
                    column = (p * sharing + g) * HD
                    row = (at % together * sharing + g) * half
                    query_ref[p, row : row + half, :] = query_refs[at][:, column : column + HD]

    def scores_of(p, at):
        return lax.dot_general(
            key_ref[at, p], query_ref[p], (((1,), (1,)), ((), ())), preferred_element_type=jnp.float32
        )

    def mixed_of(p, at, weights):
        return jnp.dot(value_ref[at, p], weights, preferred_element_type=jnp.float32)

    place = jnp.concatenate([place_ref[i] for i in range(together) for _ in range(sharing)], axis=1)
    rows = block_rows // slots
    down = lax.broadcasted_iota(jnp.int32, (rows, place.shape[1]), 0)
    visible = jnp.concatenate(
        [down <= place - lax.rem(mine[1] - s + slots, slots) * rows for s in range(slots)], axis=0
    )
    for p in range(pairs):
        scores = jnp.where(visible, scores_of(p, 0), -1e30)
        top = jnp.max(scores, axis=0, keepdims=True)
        weights = jnp.exp2((scores - top) * FACTOR).astype(jnp.bfloat16)
        top_ref[p, 0:1, :] = top
        total_ref[p] = mixed_of(p, 0, weights)

    @pl.loop(1, len(blocks))
    def _(at):
        offset = blocks[1][2] if len(blocks) > 1 else 0
        for other in range(2, len(blocks)):
            offset = jnp.where(at == other, blocks[other][2], offset)

        @pl.when(order[me ^ offset] < my_block)
        def _():
            for p in range(pairs):
                top = top_ref[p, 0:1, :]
                scores = scores_of(p, at)
                raised = jnp.maximum(top, jnp.max(scores, axis=0, keepdims=True))
                weights = jnp.exp2((scores - raised) * FACTOR).astype(jnp.bfloat16)
                top_ref[p, 0:1, :] = raised
                total_ref[p] = total_ref[p] * jnp.exp2((top - raised) * FACTOR) + mixed_of(p, at, weights)

    for p in range(pairs):
        mixed = (total_ref[p, :HD, :] / total_ref[p, HD : HD + 1, :]).T.astype(jnp.bfloat16)
        for i in range(together):
            for g in range(sharing):
                column = (p * sharing + g) * HD
                row = (i * sharing + g) * half
                at = pl.multiple_of((step * together + i) * half, half)
                head_ref[pl.ds(at, half), column : column + HD] = mixed[row : row + half]

    @pl.when(step == pl.num_programs(0) - 1)
    def _():
        weight_copy.wait()
        width = weight.shape[1] // pieces
        tile = 2 * TILE
        for c in range(pieces):

            @pl.loop(0, width // tile)
            def _(n):
                columns = pl.ds(pl.multiple_of(c * width + n * tile, tile), tile)
                value = jnp.dot(head_ref[...], weight_ref[:, columns], preferred_element_type=jnp.float32)
                share_out(outs[c * len(outs) // pieces :], pl.ds(pl.multiple_of(n * tile, tile), tile), value)


def share_out(outs, columns, value):
    rows = outs[0].shape[0]
    for g in range(value.shape[0] // rows):
        outs[g][:, columns] = value[g * rows : (g + 1) * rows].astype(jnp.bfloat16)


def piece_shapes(rows, width, slots, pieces, grouped):
    return [jax.ShapeDtypeStruct((rows // slots if grouped else rows, width // pieces), jnp.bfloat16)] * (
        pieces * (slots if grouped else 1)
    )


def by_piece(outs, slots, pieces, grouped):
    if grouped:
        return [outs[c * slots : (c + 1) * slots] for c in range(pieces)]
    return [[out[s * (out.shape[0] // slots) : (s + 1) * (out.shape[0] // slots)] for s in range(slots)] for out in outs]


def in_hbm(arrays):
    return [pltpu.with_memory_space_constraint(array, pltpu.HBM) for array in arrays]


def attend(order, mine, queries, places, pair_list, held, pairs, sharing, block_rows, weight, pieces, grouped):
    slots = len(queries)
    half, width = queries[0].shape
    together = 2 if slots <= LINE else 1
    tall = together * sharing * half
    blocks = sum(len(group) for group in held)
    count = blocks * block_rows
    shapes = piece_shapes(slots * half, weight.shape[1], slots, pieces, grouped)
    kernel = functools.partial(
        attention_kernel, slots, together, held, pairs, sharing, block_rows, (pieces, grouped)
    )
    outs = pl.pallas_call(
        kernel,
        grid_spec=pltpu.PrefetchScalarGridSpec(
            num_scalar_prefetch=2,
            grid=(slots // together,),
            in_specs=[pl.BlockSpec(memory_space=pltpu.HBM)] * slots
            + [pl.BlockSpec((together, 1, half), lambda s, *_: (s, 0, 0))]
            + [pl.BlockSpec(memory_space=pltpu.HBM)] * (len(pair_list) + 1),
            out_specs=[pl.BlockSpec(shape.shape, lambda s, *_: (0, 0)) for shape in shapes],
            scratch_shapes=[pltpu.VMEM((half, width), jnp.bfloat16)] * slots
            + [pltpu.VMEM(pair.shape, pair.dtype) for pair in pair_list]
            + [
                pltpu.VMEM((pairs, tall, HD), jnp.bfloat16),
                pltpu.VMEM((blocks, pairs, block_rows, HD), jnp.bfloat16),
                pltpu.VMEM((blocks, pairs, HD + SUM_ROWS, block_rows), jnp.bfloat16),
                pltpu.VMEM((pairs, 8, tall), jnp.float32),
                pltpu.VMEM((pairs, HD + SUM_ROWS, tall), jnp.float32),
                pltpu.VMEM((slots * half, width), jnp.bfloat16),
                pltpu.VMEM(weight.shape, weight.dtype),
                pltpu.SemaphoreType.DMA,
                pltpu.SemaphoreType.DMA((slots + len(pair_list),)),
            ],
        ),
        out_shape=shapes,
        compiler_params=pltpu.CompilerParams(vmem_limit_bytes=VMEM_HELD),
        cost_estimate=pl.CostEstimate(
            flops=40 * slots * half * width * count,
            bytes_accessed=2 * (2 * slots * half * width + count * 2 * pairs * HD + weight.size),
            transcendentals=slots * half * width // HD * count,
        ),
    )(order, mine, *in_hbm(queries), places, *in_hbm(pair_list), *in_hbm([weight]))
    return by_piece(outs, slots, pieces, grouped)


def expert_kernel(plan, pieces, *refs):
    mine, refs = refs[0], refs[1:]
    sources = []
    for count in plan:
        sources.append(refs[:count])
        refs = refs[count:]
    gate_weight, up_weight, down_weight, refs = refs[0], refs[1], refs[2], refs[3:]
    outs, (chosen, acts, strips_ref, arrived) = refs[:-4], refs[-4:]
    step = pl.program_id(0)
    tile = gate_weight.shape[1]
    first = acts.shape[1] // tile

    def place(s, source):
        rows, width = source[0].shape
        for c, ref in enumerate(source):
            chosen[s * rows : (s + 1) * rows, c * width : (c + 1) * width] = ref[...]

    @pl.when(step == 0)
    def _():
        place(0, sources[0])
        for s in range(1, (len(plan) + 1) // 2):
            right, left = sources[s], sources[len(plan) - s]

            @pl.when(mine[0] >= s)
            def _():
                place(s, right)

            @pl.when(mine[0] < s)
            def _():
                place(s, left)

    @pl.when(step < first)
    def _():
        gate = jnp.dot(chosen[...], gate_weight[...], preferred_element_type=jnp.float32)
        upward = jnp.dot(chosen[...], up_weight[...], preferred_element_type=jnp.float32)
        columns = pl.ds(pl.multiple_of(step * tile, tile), tile)
        acts[:, columns] = (gate / (1.0 + jnp.exp(-gate)) * upward).astype(jnp.bfloat16)

    strip = strips_ref.shape[2]

    def strip_copy(n):
        slot = lax.rem(n, 2)
        columns = pl.ds(pl.multiple_of(n * strip, strip), strip)
        return pltpu.make_async_copy(down_weight.at[:, columns], strips_ref.at[slot], arrived.at[slot])

    @pl.when((step >= first - 1) & (step < pl.num_programs(0) - 1))
    def _():
        strip_copy(step - first + 1).start()

    @pl.when(step >= first)
    def _():
        n = step - first
        strip_copy(n).wait()
        value = jnp.dot(acts[...], strips_ref[lax.rem(n, 2)], preferred_element_type=jnp.float32)
        per_piece = outs[0].shape[1] // strip
        for c in range(pieces):

            @pl.when(n // per_piece == c)
            def _():
                at = pl.multiple_of((n - c * per_piece) * strip, strip)
                share_out(outs[c * len(outs) // pieces :], pl.ds(at, strip), value)


def expert_rows(mine, sources, gate_weight, up_weight, down_weight, slots, pieces, grouped):
    flat = [piece for source in sources for piece in source]
    rows = flat[0].shape[0] * ((len(sources) + 1) // 2)
    depth, width = gate_weight.shape
    tile, strip = min(TILE, width), 4 * TILE
    first = width // tile
    shapes = piece_shapes(rows, depth, slots, pieces, grouped)
    in_place = pl.BlockSpec(memory_space=pltpu.VMEM)
    weight = pl.BlockSpec((depth, tile), lambda n, *_: (0, jnp.minimum(n, first - 1)))
    outs = pl.pallas_call(
        functools.partial(expert_kernel, [len(source) for source in sources], pieces),
        grid_spec=pltpu.PrefetchScalarGridSpec(
            num_scalar_prefetch=1,
            grid=(first + depth // strip,),
            in_specs=[in_place] * len(flat) + [weight, weight, pl.BlockSpec(memory_space=pltpu.HBM)],
            out_specs=[in_place] * len(shapes),
            scratch_shapes=[
                pltpu.VMEM((rows, depth), jnp.bfloat16),
                pltpu.VMEM((rows, width), jnp.bfloat16),
                pltpu.VMEM((2, width, strip), jnp.bfloat16),
                pltpu.SemaphoreType.DMA((2,)),
            ],
        ),
        out_shape=shapes,
        compiler_params=pltpu.CompilerParams(vmem_limit_bytes=VMEM_LARGE),
        cost_estimate=pl.CostEstimate(
            flops=6 * rows * depth * width, bytes_accessed=6 * depth * width, transcendentals=rows * width
        ),
    )(mine, *flat, gate_weight, up_weight, *in_hbm([down_weight]))
    return by_piece(outs, slots, pieces, grouped)


def pack_pairs_kernel(shards, mine, keys_ref, values_ref, *outs):
    width = keys_ref.shape[1] // shards
    for s in range(shards):
        columns = pl.ds(pl.multiple_of(lax.rem(mine[0] + s, shards) * width, width), width)
        outs[s][:, :width] = keys_ref[:, columns]
        outs[s][:, width:] = values_ref[:, columns]


def pack_pairs(mine, keys, values, shards):
    rows, width = keys.shape
    spec = pl.BlockSpec((rows, width), lambda k, *_: (0, 0))
    out = (rows, 2 * width // shards)
    return pl.pallas_call(
        functools.partial(pack_pairs_kernel, shards),
        grid_spec=pltpu.PrefetchScalarGridSpec(
            num_scalar_prefetch=1,
            grid=(1,),
            in_specs=[spec, spec],
            out_specs=[pl.BlockSpec(out, lambda k, *_: (0, 0))] * shards,
        ),
        out_shape=[jax.ShapeDtypeStruct(out, keys.dtype)] * shards,
    )(mine, keys, values)


def pack_queries_kernel(slots, halves, mine, picked_ref, query_ref, *outs):
    shards = len(slots)
    rows = query_ref.shape[0]
    half = rows // halves
    width = query_ref.shape[1] // shards
    packed, outs = outs[: halves * shards], outs[halves * shards :]
    place_refs, (order_ref, count_ref) = outs[:halves], outs[halves:]
    me = mine[0]
    across = lax.broadcasted_iota(jnp.int32, (rows, rows), 1)
    down = lax.broadcasted_iota(jnp.int32, (rows, rows), 0)
    up_to = jnp.where(down <= across, 1.0, 0.0).astype(jnp.bfloat16)
    picked = picked_ref[...]
    seen = jnp.dot(picked.astype(jnp.bfloat16), up_to, preferred_element_type=jnp.float32).astype(jnp.int32)
    count = seen[:, rows - 1 : rows]
    row_ids = lax.broadcasted_iota(jnp.int32, seen.shape, 1)
    slot = jnp.where(picked > 0, seen - 1, count + row_ids - seen)
    count_ref[0] = jnp.max(jnp.where(count > half, 1, 0))
    ids = row_ids.astype(jnp.bfloat16)
    for s in range(shards):
        shard = lax.rem(me - s + shards, shards)
        mine_slot = slot[0:1]
        for other in range(1, shards):
            mine_slot = jnp.where(shard == other, slot[other : other + 1], mine_slot)
        at_slot = jnp.where(mine_slot == down, 1.0, 0.0).astype(jnp.bfloat16)
        rows_at = lax.dot_general(ids, at_slot, (((1,), (1,)), ((), ())), preferred_element_type=jnp.float32)
        for h in range(halves):
            here = rows_at[0:1, h * half : (h + 1) * half]
            place_refs[h][slots.index(s)] = here.astype(jnp.int32) + shard * rows
        if s == 0:
            order_ref[...] = at_slot
    for s in range(shards):
        columns = pl.ds(pl.multiple_of(lax.rem(me + s, shards) * width, width), width)
        ordered = jnp.dot(order_ref[...], query_ref[:, columns], preferred_element_type=jnp.float32)
        ordered = ordered.astype(jnp.bfloat16)
        for h in range(halves):
            packed[h * shards + s][...] = ordered[h * half : (h + 1) * half]


def pack_queries(mine, picked, queries, slots, halves):
    shards = len(slots)
    rows, width = queries.shape
    packed = (rows // halves, width // shards)
    shapes = [jax.ShapeDtypeStruct(packed, jnp.bfloat16)] * (halves * shards)
    shapes += [jax.ShapeDtypeStruct((shards, 1, rows // halves), jnp.int32)] * halves
    shapes += [jax.ShapeDtypeStruct((rows, rows), jnp.bfloat16), jax.ShapeDtypeStruct((1,), jnp.int32)]

    def whole(shape):
        return pl.BlockSpec(shape, lambda k, *_: (0,) * len(shape))

    got = pl.pallas_call(
        functools.partial(pack_queries_kernel, slots, halves),
        grid_spec=pltpu.PrefetchScalarGridSpec(
            num_scalar_prefetch=1,
            grid=(1,),
            in_specs=[whole(picked.shape), whole(queries.shape)],
            out_specs=[whole(shape.shape) for shape in shapes[:-1]] + [pl.BlockSpec(memory_space=pltpu.SMEM)],
        ),
        out_shape=shapes,
    )(mine, picked, queries)
    packed, got = got[: halves * shards], got[halves * shards :]
    return [packed[h * shards : (h + 1) * shards] for h in range(halves)], got[:halves], *got[halves:]


def on_device(
    hidden_in,
    queries,
    keys,
    values,
    block_order,
    routes,
    out_weight,
    norm_gain,
    router_weight,
    gate_weight,
    up_weight,
    down_weight,
):
    shards = lax.axis_size("tp")
    blocks = lax.axis_size("ctx")
    me = lax.axis_index("tp")
    rows, model = hidden_in.shape
    block_rows = rows * shards
    per_device = HEADS // shards
    grouping = HEADS // KV_HEADS
    repeat_by = max(1, grouping // per_device)
    pairs = max(1, per_device // grouping)
    sharing = per_device // pairs
    half = rows // 2 if rows % 32 == 0 else rows
    halves = rows // half
    line = shards <= LINE
    pieces = 2 if line else 1
    cuts = [slice(c * (model // pieces), (c + 1) * (model // pieces)) for c in range(pieces)]
    slots = [s for s in range(1, shards, 2)] + [s for s in range(2, shards, 2)] + [0]
    shard_of = lax.rem(me - jnp.arange(shards, dtype=jnp.int32) + shards, shards)

    def shift(parts):
        moves = [[(i, (i + s) % shards) for i in range(shards)] for s in range(shards)]
        return [parts[0]] + [lax.ppermute(parts[s], "tp", moves[s]) for s in range(1, shards)]

    def exchange(source):
        got = lax.all_to_all(source, "tp", split_axis=1, concat_axis=0, tiled=True)
        got = got.reshape(shards, rows, source.shape[2])
        return [lax.dynamic_index_in_dim(got, shard_of[s], 0, keepdims=False) for s in range(shards)]

    def rights(count):
        return [(i, i + 1) for i in range(count)]

    def lefts(count):
        return [(i, i - 1) for i in range(shards - count, shards)]

    def reduce_line(pieces_terms):
        if not line:
            by_shard = [jnp.take(jnp.stack(terms), shard_of, axis=0).reshape(-1, terms[0].shape[1]) for terms in pieces_terms]
            return [
                lax.psum_scatter(term, "tp", scatter_dimension=0, tiled=True).astype(jnp.float32) for term in by_shard
            ], None
        got = [None] * len(pieces_terms)
        marks = []
        for s in range(1, shards):
            for c, terms in enumerate(pieces_terms):
                if got[c] is None:
                    sent = (terms[s], terms[shards - s])
                else:
                    arrived = got[c]
                    sent = (terms[s] + arrived[0], terms[shards - s] + arrived[1])
                right = lax.ppermute(sent[0], "tp", rights(s))
                left = lax.ppermute(sent[1], "tp", lefts(s))
                got[c] = lax.optimization_barrier((right, left))
            marks.append(got[0])
        return [
            terms[0].astype(jnp.float32) + right.astype(jnp.float32) + left.astype(jnp.float32)
            for terms, (right, left) in zip(pieces_terms, got)
        ], marks

    def gather_line(source, terms=None):
        if not line:
            got = lax.all_gather(source, "tp", axis=0)
            return [[jnp.take(got, shard_of, axis=0).reshape(shards * half, -1)]], None
        first_right = lax.ppermute(source, "tp", rights(shards - 1))
        first_left = lax.ppermute(source, "tp", lefts(shards - 1))
        first_right, first_left = lax.optimization_barrier((first_right, first_left))
        got = [(first_right[:, cut], first_left[:, cut]) for cut in cuts]
        from_left, from_right = [], []
        for s in range(2, shards):
            if terms is None:
                sent = got
                to_right = [(i, i + 1) for i in range(s - 1, shards - 1)]
                to_left = [(i, i - 1) for i in range(1, shards - s + 1)]
            else:
                sent = [
                    (
                        jnp.where(me >= s - 1, right, right + term[s - 1]),
                        jnp.where(me <= shards - s, left, left + term[shards - s + 1]),
                    )
                    for (right, left), term in zip(got, terms)
                ]
                to_right, to_left = rights(shards - 1), lefts(shards - 1)
            from_left.append([right for right, _ in sent])
            from_right.append([left for _, left in sent])
            got = [
                lax.optimization_barrier((lax.ppermute(right, "tp", to_right), lax.ppermute(left, "tp", to_left)))
                for right, left in sent
            ]
        from_left.append([right for right, _ in got])
        from_right.append([left for _, left in got])
        total = None
        if terms is not None:
            right = jnp.concatenate([right + term[shards - 1] for (right, _), term in zip(got, terms)], axis=1)
            left = jnp.concatenate([left + term[1] for (_, left), term in zip(got, terms)], axis=1)
            right = lax.ppermute(right, "tp", rights(shards - 1))
            left = lax.ppermute(left, "tp", lefts(shards - 1))
            total = (right, left)
        return [[source]] + from_left + from_right, total

    picked = ((routes[:, 0] == 0) | (routes[:, 1] == 0)).reshape(shards, rows)
    if line:
        sent_pairs = pack_pairs(me[None], keys, values, shards)
        own_pairs = jnp.concatenate(shift(sent_pairs), axis=0)
        picked, _ = lax.optimization_barrier((picked.astype(jnp.int32), sent_pairs))
        packed, places, order, crowded = pack_queries(me[None], picked, queries, slots, halves)
        asked = [shift(packed[0])]
    else:

        def spread(source):
            widened = jnp.repeat(source.reshape(rows, KV_HEADS, HD), repeat_by, axis=1)
            return widened.reshape(rows, shards, pairs * HD)

        own_pairs = exchange(jnp.concatenate([spread(keys), spread(values)], axis=2))
        own_pairs = jnp.concatenate(own_pairs, axis=0)
        row_ids = jnp.arange(rows, dtype=jnp.int32)
        seen = jnp.cumsum(picked.astype(jnp.int32), axis=1)
        slot = jnp.where(picked, seen - 1, seen[:, -1:] + row_ids[None, :] - seen)
        at_slot = slot[:, None, :] == row_ids[None, :, None]
        row_of_slot = jnp.sum(jnp.where(at_slot, row_ids[None, None, :], 0), axis=2)
        places = row_of_slot + jnp.arange(shards, dtype=jnp.int32)[:, None] * rows
        places = [jnp.stack([jnp.take(places, shard_of[s], axis=0) for s in slots])[:, None, :]]
        order = lax.dynamic_index_in_dim(at_slot, me, 0, keepdims=False).astype(jnp.bfloat16)
        ordered = jnp.dot(order, queries, preferred_element_type=jnp.float32).astype(jnp.bfloat16)
        asked = [exchange(ordered.reshape(rows, shards, per_device * HD))]

    pair_list, held = [own_pairs], [[0]]
    offset = blocks // 2
    while offset >= 1:
        pair_list += [lax.ppermute(part, "ctx", [(i, i ^ offset) for i in range(blocks)]) for part in pair_list]
        held += [[other ^ offset for other in group] for group in held]
        if line and len(pair_list) == 2:
            pair_list[1], asked[0] = lax.optimization_barrier((pair_list[1], asked[0]))
        offset //= 2

    def reorder(source):
        return jnp.dot(order, source, preferred_element_type=jnp.float32).astype(jnp.bfloat16)

    def restore(parts):
        whole = jnp.concatenate(parts, axis=0) if len(parts) > 1 else parts[0]
        return lax.dot_general(
            order, whole, (((0,), (0,)), ((), ())), preferred_element_type=jnp.float32
        ).astype(jnp.bfloat16)

    mine = lax.axis_index("ctx").astype(jnp.int32)[None]
    expert_ids = jnp.arange(router_weight.shape[1], dtype=jnp.int32)

    def project(which, grouped=False):
        terms = attend(
            block_order,
            jnp.stack([lax.axis_index("ctx"), me]).astype(jnp.int32),
            [asked[which][s] for s in slots],
            places[which],
            pair_list,
            held,
            pairs,
            sharing,
            block_rows,
            out_weight,
            pieces,
            grouped,
        )
        return [[term[slots.index(s)] for s in range(shards)] for term in terms]

    def finish(which, head_sums):
        base = hidden[which * half : (which + 1) * half].astype(jnp.float32)
        return jnp.concatenate(
            [(base[:, cut] + head_sum).astype(jnp.bfloat16) for cut, head_sum in zip(cuts, head_sums)], axis=1
        )

    def normalise(attended):
        widened = attended.astype(jnp.float32)
        return (
            widened * lax.rsqrt(jnp.mean(widened * widened, axis=1, keepdims=True) + 1e-05) * norm_gain
        ).astype(jnp.bfloat16)

    def share_of(which, normed):
        logits = jnp.dot(normed, router_weight, preferred_element_type=jnp.float32)
        named = my_routes[which * half : (which + 1) * half]
        first = jnp.sum(jnp.where(named[:, 0:1] == expert_ids[None, :], logits, 0.0), axis=1)
        second = jnp.sum(jnp.where(named[:, 1:2] == expert_ids[None, :], logits, 0.0), axis=1)
        share = jnp.where(named[:, 0] == 0, 1.0 / (1.0 + jnp.exp(second - first)), 0.0)
        return share + jnp.where(named[:, 1] == 0, 1.0 / (1.0 + jnp.exp(first - second)), 0.0)

    def expert(which, normed, sources, beside=None):
        terms = expert_rows(me[None], sources, gate_weight, up_weight, down_weight, shards, pieces, False)
        if beside is not None:
            terms, beside = lax.optimization_barrier((terms, beside))
        sums, marks = reduce_line(terms)
        if line:
            normed, _ = lax.optimization_barrier((normed, marks[0]))
        share = share_of(which, normed)
        parts = [(total * share[:, None]).astype(jnp.bfloat16) for total in sums]
        return jnp.concatenate(parts, axis=1), beside

    def late_expert(source):
        normed = normalise(source)
        return expert(1, normed, gather_line(normed)[0])[0]

    terms = project(0)
    if halves > 1:
        asked.append(shift(packed[1]))
        terms, asked[1] = lax.optimization_barrier((terms, asked[1]))
    totals, marks = reduce_line(terms)
    if line:
        hidden_in, order, _ = lax.optimization_barrier((hidden_in, order, marks[0]))
    hidden = reorder(hidden_in)
    my_routes = lax.dynamic_slice_in_dim(routes, me * rows, rows, 0).astype(jnp.bfloat16)
    my_routes = reorder(my_routes).astype(jnp.int32)
    first_half = finish(0, totals)
    normed = normalise(first_half)
    if halves == 1:
        return (restore([first_half]), restore([expert(0, normed, gather_line(normed)[0])[0]]))
    asked[1], _ = lax.optimization_barrier((asked[1], normed))
    terms = project(1, line)
    sources, arrived = gather_line(normed, terms)
    part, (right, left) = expert(0, normed, sources, arrived)
    own = jnp.concatenate([term[0] for term in terms], axis=1).astype(jnp.float32)
    second_sum = own + right.astype(jnp.float32) + left.astype(jnp.float32)
    second_half = (hidden[half:].astype(jnp.float32) + second_sum).astype(jnp.bfloat16)
    part, late = lax.optimization_barrier((part, second_half))
    late = lax.cond(crowded[0] > 0, late_expert, jnp.zeros_like, late)
    return (restore([first_half, second_half]), restore([part, late]))


def solution(mesh):
    return jax.shard_map(
        on_device,
        mesh=mesh,
        in_specs=(
            P(("req", "ctx", "tp"), None),
            P(("req", "ctx", "tp"), None),
            P(("req", "ctx", "tp"), None),
            P(("req", "ctx", "tp"), None),
            P("req"),
            P(("req", "ctx"), None),
            P("tp", None),
            P(),
            P(),
            P(None, "tp"),
            P(None, "tp"),
            P("tp", None),
        ),
        out_specs=(P(("req", "ctx", "tp"), None), P(("req", "ctx", "tp"), None)),
        check_vma=False,
    )
```

```python
import functools
import math

import jax
import jax.numpy as jnp
from jax import lax
from jax.experimental import pallas as pl
from jax.experimental.pallas import tpu as pltpu
from jax.sharding import PartitionSpec as P

HEADS = 32
KV_HEADS = 8
HD = 128
FACTOR = math.log2(math.e) / math.sqrt(HD)
LINE = 4
SUM_ROWS = 16
TILE = 256
VMEM_HELD = 21 * 1024 * 1024
VMEM_LARGE = 28 * 1024 * 1024


def attention_kernel(slots, together, held, pairs, sharing, block_rows, plan, *refs):
    pieces, grouped = plan
    (order, mine), refs = refs[:2], refs[2:]
    sent_queries, refs = refs[:slots], refs[slots:]
    place_ref, refs = refs[0], refs[1:]
    sent_pairs, weight, refs = refs[: len(held)], refs[len(held)], refs[len(held) + 1 :]
    outs, refs = refs[: pieces * (slots if grouped else 1)], refs[pieces * (slots if grouped else 1) :]
    query_refs, pair_refs, refs = refs[:slots], refs[slots : slots + len(held)], refs[slots + len(held) :]
    query_ref, key_ref, value_ref, top_ref, total_ref, head_ref, weight_ref, arrived, here = refs
    half = query_refs[0].shape[0]
    step = pl.program_id(0)
    me = mine[0]
    my_block = order[me]
    blocks = [(ref, index, offset) for ref, group in zip(pair_refs, held) for index, offset in enumerate(group)]
    weight_copy = pltpu.make_async_copy(weight, weight_ref, arrived)
    moves = [
        pltpu.make_async_copy(source, target, here.at[i])
        for i, (source, target) in enumerate(
            list(zip(sent_pairs, pair_refs)) + list(zip(sent_queries, query_refs))
        )
    ]

    @pl.when(step == 0)
    def _():
        for move in moves:
            move.start()
        value_ref[:, :, HD:, :] = jnp.ones((len(blocks), pairs, SUM_ROWS, block_rows), jnp.bfloat16)

    @pl.when(step == 0)
    def _():
        for move in moves:
            move.wait()
        weight_copy.start()

    for at, (ref, index, offset) in enumerate(blocks):

        @pl.when((step == 0) & (order[me ^ offset] <= my_block))
        def _():
            for p in range(pairs):
                rows = slice(index * block_rows, (index + 1) * block_rows)
                key_ref[at, p] = ref[rows, p * HD : (p + 1) * HD]
                value_ref[at, p, :HD, :] = ref[rows, (pairs + p) * HD : (pairs + p + 1) * HD].T

    for at in range(slots):

        @pl.when(step == at // together)
        def _():
            for p in range(pairs):
                for g in range(sharing):
                    column = (p * sharing + g) * HD
                    row = (at % together * sharing + g) * half
                    query_ref[p, row : row + half, :] = query_refs[at][:, column : column + HD]

    def scores_of(p, at):
        return lax.dot_general(
            key_ref[at, p], query_ref[p], (((1,), (1,)), ((), ())), preferred_element_type=jnp.float32
        )

    def mixed_of(p, at, weights):
        return jnp.dot(value_ref[at, p], weights, preferred_element_type=jnp.float32)

    place = jnp.concatenate([place_ref[i] for i in range(together) for _ in range(sharing)], axis=1)
    rows = block_rows // slots
    down = lax.broadcasted_iota(jnp.int32, (rows, place.shape[1]), 0)
    visible = jnp.concatenate(
        [down <= place - lax.rem(mine[1] - s + slots, slots) * rows for s in range(slots)], axis=0
    )
    for p in range(pairs):
        scores = jnp.where(visible, scores_of(p, 0), -1e30)
        top = jnp.max(scores, axis=0, keepdims=True)
        weights = jnp.exp2((scores - top) * FACTOR).astype(jnp.bfloat16)
        top_ref[p, 0:1, :] = top
        total_ref[p] = mixed_of(p, 0, weights)

    @pl.loop(1, len(blocks))
    def _(at):
        offset = blocks[1][2] if len(blocks) > 1 else 0
        for other in range(2, len(blocks)):
            offset = jnp.where(at == other, blocks[other][2], offset)

        @pl.when(order[me ^ offset] < my_block)
        def _():
            for p in range(pairs):
                top = top_ref[p, 0:1, :]
                scores = scores_of(p, at)
                raised = jnp.maximum(top, jnp.max(scores, axis=0, keepdims=True))
                weights = jnp.exp2((scores - raised) * FACTOR).astype(jnp.bfloat16)
                top_ref[p, 0:1, :] = raised
                total_ref[p] = total_ref[p] * jnp.exp2((top - raised) * FACTOR) + mixed_of(p, at, weights)

    for p in range(pairs):
        mixed = (total_ref[p, :HD, :] / total_ref[p, HD : HD + 1, :]).T.astype(jnp.bfloat16)
        for i in range(together):
            for g in range(sharing):
                column = (p * sharing + g) * HD
                row = (i * sharing + g) * half
                at = pl.multiple_of((step * together + i) * half, half)
                head_ref[pl.ds(at, half), column : column + HD] = mixed[row : row + half]

    @pl.when(step == pl.num_programs(0) - 1)
    def _():
        weight_copy.wait()
        width = weight.shape[1] // pieces
        tile = 2 * TILE
        for c in range(pieces):

            @pl.loop(0, width // tile)
            def _(n):
                columns = pl.ds(pl.multiple_of(c * width + n * tile, tile), tile)
                value = jnp.dot(head_ref[...], weight_ref[:, columns], preferred_element_type=jnp.float32)
                share_out(outs[c * len(outs) // pieces :], pl.ds(pl.multiple_of(n * tile, tile), tile), value)


def share_out(outs, columns, value):
    rows = outs[0].shape[0]
    for g in range(value.shape[0] // rows):
        outs[g][:, columns] = value[g * rows : (g + 1) * rows].astype(jnp.bfloat16)


def piece_shapes(rows, width, slots, pieces, grouped):
    return [jax.ShapeDtypeStruct((rows // slots if grouped else rows, width // pieces), jnp.bfloat16)] * (
        pieces * (slots if grouped else 1)
    )


def by_piece(outs, slots, pieces, grouped):
    if grouped:
        return [outs[c * slots : (c + 1) * slots] for c in range(pieces)]
    return [[out[s * (out.shape[0] // slots) : (s + 1) * (out.shape[0] // slots)] for s in range(slots)] for out in outs]


def in_hbm(arrays):
    return [pltpu.with_memory_space_constraint(array, pltpu.HBM) for array in arrays]


def attend(order, mine, queries, places, pair_list, held, pairs, sharing, block_rows, weight, pieces, grouped):
    slots = len(queries)
    half, width = queries[0].shape
    together = 2 if slots <= LINE else 1
    tall = together * sharing * half
    blocks = sum(len(group) for group in held)
    count = blocks * block_rows
    shapes = piece_shapes(slots * half, weight.shape[1], slots, pieces, grouped)
    kernel = functools.partial(
        attention_kernel, slots, together, held, pairs, sharing, block_rows, (pieces, grouped)
    )
    outs = pl.pallas_call(
        kernel,
        grid_spec=pltpu.PrefetchScalarGridSpec(
            num_scalar_prefetch=2,
            grid=(slots // together,),
            in_specs=[pl.BlockSpec(memory_space=pltpu.HBM)] * slots
            + [pl.BlockSpec((together, 1, half), lambda s, *_: (s, 0, 0))]
            + [pl.BlockSpec(memory_space=pltpu.HBM)] * (len(pair_list) + 1),
            out_specs=[pl.BlockSpec(shape.shape, lambda s, *_: (0, 0)) for shape in shapes],
            scratch_shapes=[pltpu.VMEM((half, width), jnp.bfloat16)] * slots
            + [pltpu.VMEM(pair.shape, pair.dtype) for pair in pair_list]
            + [
                pltpu.VMEM((pairs, tall, HD), jnp.bfloat16),
                pltpu.VMEM((blocks, pairs, block_rows, HD), jnp.bfloat16),
                pltpu.VMEM((blocks, pairs, HD + SUM_ROWS, block_rows), jnp.bfloat16),
                pltpu.VMEM((pairs, 8, tall), jnp.float32),
                pltpu.VMEM((pairs, HD + SUM_ROWS, tall), jnp.float32),
                pltpu.VMEM((slots * half, width), jnp.bfloat16),
                pltpu.VMEM(weight.shape, weight.dtype),
                pltpu.SemaphoreType.DMA,
                pltpu.SemaphoreType.DMA((slots + len(pair_list),)),
            ],
        ),
        out_shape=shapes,
        compiler_params=pltpu.CompilerParams(vmem_limit_bytes=VMEM_HELD),
        cost_estimate=pl.CostEstimate(
            flops=40 * slots * half * width * count,
            bytes_accessed=2 * (2 * slots * half * width + count * 2 * pairs * HD + weight.size),
            transcendentals=slots * half * width // HD * count,
        ),
    )(order, mine, *in_hbm(queries), places, *in_hbm(pair_list), *in_hbm([weight]))
    return by_piece(outs, slots, pieces, grouped)


def expert_kernel(plan, pieces, *refs):
    mine, refs = refs[0], refs[1:]
    sources = []
    for count in plan:
        sources.append(refs[:count])
        refs = refs[count:]
    gate_weight, up_weight, down_weights, refs = refs[0], refs[1], refs[2:4], refs[4:]
    outs, (chosen, acts) = refs[:-2], refs[-2:]
    step = pl.program_id(0)
    tile = gate_weight.shape[1]
    first = acts.shape[1] // tile

    def place(s, source):
        rows, width = source[0].shape
        for c, ref in enumerate(source):
            chosen[s * rows : (s + 1) * rows, c * width : (c + 1) * width] = ref[...]

    @pl.when(step == 0)
    def _():
        place(0, sources[0])
        for s in range(1, (len(plan) + 1) // 2):
            right, left = sources[s], sources[len(plan) - s]

            @pl.when(mine[0] >= s)
            def _():
                place(s, right)

            @pl.when(mine[0] < s)
            def _():
                place(s, left)

    @pl.when(step < first)
    def _():
        gate = jnp.dot(chosen[...], gate_weight[...], preferred_element_type=jnp.float32)
        upward = jnp.dot(chosen[...], up_weight[...], preferred_element_type=jnp.float32)
        columns = pl.ds(pl.multiple_of(step * tile, tile), tile)
        acts[:, columns] = (gate / (1.0 + jnp.exp(-gate)) * upward).astype(jnp.bfloat16)

    @pl.when(step >= first)
    def _():
        strip = down_weights[0].shape[1]
        pairs = outs[0].shape[1] // (2 * strip)
        for j, down_weight in enumerate(down_weights):
            value = jnp.dot(acts[...], down_weight[...], preferred_element_type=jnp.float32)
            for c in range(pieces):

                @pl.when((step - first) // pairs == c)
                def _():
                    at = (2 * (step - first - c * pairs) + j) * strip
                    share_out(outs[c * len(outs) // pieces :], pl.ds(pl.multiple_of(at, strip), strip), value)


def expert_rows(mine, sources, gate_weight, up_weight, down_weight, slots, pieces, grouped):
    flat = [piece for source in sources for piece in source]
    rows = flat[0].shape[0] * ((len(sources) + 1) // 2)
    depth, width = gate_weight.shape
    tile, strip = min(TILE, width), 2 * TILE
    first = width // tile
    shapes = piece_shapes(rows, depth, slots, pieces, grouped)
    in_place = pl.BlockSpec(memory_space=pltpu.VMEM)
    weight = pl.BlockSpec((depth, tile), lambda n, *_: (0, jnp.minimum(n, first - 1)))
    outs = pl.pallas_call(
        functools.partial(expert_kernel, [len(source) for source in sources], pieces),
        grid_spec=pltpu.PrefetchScalarGridSpec(
            num_scalar_prefetch=1,
            grid=(first + depth // (2 * strip),),
            in_specs=[in_place] * len(flat)
            + [weight, weight]
            + [
                pl.BlockSpec((width, strip), functools.partial(lambda j, n, *_: (0, 2 * jnp.maximum(n - first, 0) + j), j))
                for j in range(2)
            ],
            out_specs=[in_place] * len(shapes),
            scratch_shapes=[pltpu.VMEM((rows, depth), jnp.bfloat16), pltpu.VMEM((rows, width), jnp.bfloat16)],
        ),
        out_shape=shapes,
        compiler_params=pltpu.CompilerParams(vmem_limit_bytes=VMEM_LARGE),
        cost_estimate=pl.CostEstimate(
            flops=6 * rows * depth * width, bytes_accessed=6 * depth * width, transcendentals=rows * width
        ),
    )(mine, *flat, gate_weight, up_weight, down_weight, down_weight)
    return by_piece(outs, slots, pieces, grouped)


def pack_pairs_kernel(shards, mine, keys_ref, values_ref, *outs):
    width = keys_ref.shape[1] // shards
    for s in range(shards):
        columns = pl.ds(pl.multiple_of(lax.rem(mine[0] + s, shards) * width, width), width)
        outs[s][:, :width] = keys_ref[:, columns]
        outs[s][:, width:] = values_ref[:, columns]


def pack_pairs(mine, keys, values, shards):
    rows, width = keys.shape
    spec = pl.BlockSpec((rows, width), lambda k, *_: (0, 0))
    out = (rows, 2 * width // shards)
    return pl.pallas_call(
        functools.partial(pack_pairs_kernel, shards),
        grid_spec=pltpu.PrefetchScalarGridSpec(
            num_scalar_prefetch=1,
            grid=(1,),
            in_specs=[spec, spec],
            out_specs=[pl.BlockSpec(out, lambda k, *_: (0, 0))] * shards,
        ),
        out_shape=[jax.ShapeDtypeStruct(out, keys.dtype)] * shards,
    )(mine, keys, values)


def pack_queries_kernel(slots, halves, mine, picked_ref, query_ref, *outs):
    shards = len(slots)
    rows = query_ref.shape[0]
    half = rows // halves
    width = query_ref.shape[1] // shards
    packed, outs = outs[: halves * shards], outs[halves * shards :]
    place_refs, (order_ref, count_ref) = outs[:halves], outs[halves:]
    me = mine[0]
    across = lax.broadcasted_iota(jnp.int32, (rows, rows), 1)
    down = lax.broadcasted_iota(jnp.int32, (rows, rows), 0)
    up_to = jnp.where(down <= across, 1.0, 0.0).astype(jnp.bfloat16)
    picked = picked_ref[...]
    seen = jnp.dot(picked.astype(jnp.bfloat16), up_to, preferred_element_type=jnp.float32).astype(jnp.int32)
    count = seen[:, rows - 1 : rows]
    row_ids = lax.broadcasted_iota(jnp.int32, seen.shape, 1)
    slot = jnp.where(picked > 0, seen - 1, count + row_ids - seen)
    count_ref[0] = jnp.max(jnp.where(count > half, 1, 0))
    ids = row_ids.astype(jnp.bfloat16)
    for s in range(shards):
        shard = lax.rem(me - s + shards, shards)
        mine_slot = slot[0:1]
        for other in range(1, shards):
            mine_slot = jnp.where(shard == other, slot[other : other + 1], mine_slot)
        at_slot = jnp.where(mine_slot == down, 1.0, 0.0).astype(jnp.bfloat16)
        rows_at = lax.dot_general(ids, at_slot, (((1,), (1,)), ((), ())), preferred_element_type=jnp.float32)
        for h in range(halves):
            here = rows_at[0:1, h * half : (h + 1) * half]
            place_refs[h][slots.index(s)] = here.astype(jnp.int32) + shard * rows
        if s == 0:
            order_ref[...] = at_slot
    for s in range(shards):
        columns = pl.ds(pl.multiple_of(lax.rem(me + s, shards) * width, width), width)
        ordered = jnp.dot(order_ref[...], query_ref[:, columns], preferred_element_type=jnp.float32)
        ordered = ordered.astype(jnp.bfloat16)
        for h in range(halves):
            packed[h * shards + s][...] = ordered[h * half : (h + 1) * half]


def pack_queries(mine, picked, queries, slots, halves):
    shards = len(slots)
    rows, width = queries.shape
    packed = (rows // halves, width // shards)
    shapes = [jax.ShapeDtypeStruct(packed, jnp.bfloat16)] * (halves * shards)
    shapes += [jax.ShapeDtypeStruct((shards, 1, rows // halves), jnp.int32)] * halves
    shapes += [jax.ShapeDtypeStruct((rows, rows), jnp.bfloat16), jax.ShapeDtypeStruct((1,), jnp.int32)]

    def whole(shape):
        return pl.BlockSpec(shape, lambda k, *_: (0,) * len(shape))

    got = pl.pallas_call(
        functools.partial(pack_queries_kernel, slots, halves),
        grid_spec=pltpu.PrefetchScalarGridSpec(
            num_scalar_prefetch=1,
            grid=(1,),
            in_specs=[whole(picked.shape), whole(queries.shape)],
            out_specs=[whole(shape.shape) for shape in shapes[:-1]] + [pl.BlockSpec(memory_space=pltpu.SMEM)],
        ),
        out_shape=shapes,
    )(mine, picked, queries)
    packed, got = got[: halves * shards], got[halves * shards :]
    return [packed[h * shards : (h + 1) * shards] for h in range(halves)], got[:halves], *got[halves:]


def on_device(
    hidden_in,
    queries,
    keys,
    values,
    block_order,
    routes,
    out_weight,
    norm_gain,
    router_weight,
    gate_weight,
    up_weight,
    down_weight,
):
    shards = lax.axis_size("tp")
    blocks = lax.axis_size("ctx")
    me = lax.axis_index("tp")
    rows, model = hidden_in.shape
    block_rows = rows * shards
    per_device = HEADS // shards
    grouping = HEADS // KV_HEADS
    repeat_by = max(1, grouping // per_device)
    pairs = max(1, per_device // grouping)
    sharing = per_device // pairs
    half = rows // 2 if rows % 32 == 0 else rows
    halves = rows // half
    line = shards <= LINE
    pieces = 2 if line else 1
    cuts = [slice(c * (model // pieces), (c + 1) * (model // pieces)) for c in range(pieces)]
    slots = [s for s in range(1, shards, 2)] + [s for s in range(2, shards, 2)] + [0]
    shard_of = lax.rem(me - jnp.arange(shards, dtype=jnp.int32) + shards, shards)

    def shift(parts):
        moves = [[(i, (i + s) % shards) for i in range(shards)] for s in range(shards)]
        return [parts[0]] + [lax.ppermute(parts[s], "tp", moves[s]) for s in range(1, shards)]

    def exchange(source):
        got = lax.all_to_all(source, "tp", split_axis=1, concat_axis=0, tiled=True)
        got = got.reshape(shards, rows, source.shape[2])
        return [lax.dynamic_index_in_dim(got, shard_of[s], 0, keepdims=False) for s in range(shards)]

    def rights(count):
        return [(i, i + 1) for i in range(count)]

    def lefts(count):
        return [(i, i - 1) for i in range(shards - count, shards)]

    def reduce_line(pieces_terms):
        if not line:
            by_shard = [jnp.take(jnp.stack(terms), shard_of, axis=0).reshape(-1, terms[0].shape[1]) for terms in pieces_terms]
            return [
                lax.psum_scatter(term, "tp", scatter_dimension=0, tiled=True).astype(jnp.float32) for term in by_shard
            ], None
        got = [None] * len(pieces_terms)
        marks = []
        for s in range(1, shards):
            for c, terms in enumerate(pieces_terms):
                if s == 1:
                    sent = jnp.where(me == 0, terms[1], terms[shards - 1])
                    arrived = lax.ppermute(sent, "tp", [(0, 1), (shards - 1, shards - 2)])
                    got[c] = (arrived, arrived)
                    continue
                if s == 2:
                    to_right = to_left = terms[s] + got[c][0]
                else:
                    to_right, to_left = terms[s] + got[c][0], terms[shards - s] + got[c][1]
                right = lax.ppermute(to_right, "tp", rights(s))
                left = lax.ppermute(to_left, "tp", lefts(s))
                got[c] = lax.optimization_barrier((right, left))
            marks.append(got[0])
        return [
            terms[0].astype(jnp.float32) + right.astype(jnp.float32) + left.astype(jnp.float32)
            for terms, (right, left) in zip(pieces_terms, got)
        ], marks

    def gather_line(source, terms=None):
        if not line:
            got = lax.all_gather(source, "tp", axis=0)
            return [[jnp.take(got, shard_of, axis=0).reshape(shards * half, -1)]], None
        first_right = lax.ppermute(source, "tp", rights(shards - 1))
        first_left = lax.ppermute(source, "tp", lefts(shards - 1))
        first_right, first_left = lax.optimization_barrier((first_right, first_left))
        got = [(first_right[:, cut], first_left[:, cut]) for cut in cuts]
        from_left, from_right = [], []
        for s in range(2, shards):
            if terms is None:
                sent = got
                to_right = [(i, i + 1) for i in range(s - 1, shards - 1)]
                to_left = [(i, i - 1) for i in range(1, shards - s + 1)]
            else:
                sent = [
                    (
                        jnp.where(me >= s - 1, right, right + term[s - 1]),
                        jnp.where(me <= shards - s, left, left + term[shards - s + 1]),
                    )
                    for (right, left), term in zip(got, terms)
                ]
                to_right, to_left = rights(shards - 1), lefts(shards - 1)
            from_left.append([right for right, _ in sent])
            from_right.append([left for _, left in sent])
            got = [
                lax.optimization_barrier((lax.ppermute(right, "tp", to_right), lax.ppermute(left, "tp", to_left)))
                for right, left in sent
            ]
        from_left.append([right for right, _ in got])
        from_right.append([left for _, left in got])
        total = None
        if terms is not None:
            right = jnp.concatenate([right + term[shards - 1] for (right, _), term in zip(got, terms)], axis=1)
            left = jnp.concatenate([left + term[1] for (_, left), term in zip(got, terms)], axis=1)
            right = lax.ppermute(right, "tp", rights(shards - 1)).astype(jnp.float32)
            left = lax.ppermute(left, "tp", lefts(shards - 1)).astype(jnp.float32)
            total = jnp.concatenate([term[0] for term in terms], axis=1).astype(jnp.float32) + right + left
        return [[source]] + from_left + from_right, total

    picked = ((routes[:, 0] == 0) | (routes[:, 1] == 0)).reshape(shards, rows)
    if line:
        sent_pairs = pack_pairs(me[None], keys, values, shards)
        own_pairs = jnp.concatenate(shift(sent_pairs), axis=0)
        picked, _ = lax.optimization_barrier((picked.astype(jnp.int32), sent_pairs))
        packed, places, order, crowded = pack_queries(me[None], picked, queries, slots, halves)
        asked = [shift(packed[0])]
    else:

        def spread(source):
            widened = jnp.repeat(source.reshape(rows, KV_HEADS, HD), repeat_by, axis=1)
            return widened.reshape(rows, shards, pairs * HD)

        own_pairs = exchange(jnp.concatenate([spread(keys), spread(values)], axis=2))
        own_pairs = jnp.concatenate(own_pairs, axis=0)
        row_ids = jnp.arange(rows, dtype=jnp.int32)
        seen = jnp.cumsum(picked.astype(jnp.int32), axis=1)
        slot = jnp.where(picked, seen - 1, seen[:, -1:] + row_ids[None, :] - seen)
        at_slot = slot[:, None, :] == row_ids[None, :, None]
        row_of_slot = jnp.sum(jnp.where(at_slot, row_ids[None, None, :], 0), axis=2)
        places = row_of_slot + jnp.arange(shards, dtype=jnp.int32)[:, None] * rows
        places = [jnp.stack([jnp.take(places, shard_of[s], axis=0) for s in slots])[:, None, :]]
        order = lax.dynamic_index_in_dim(at_slot, me, 0, keepdims=False).astype(jnp.bfloat16)
        ordered = jnp.dot(order, queries, preferred_element_type=jnp.float32).astype(jnp.bfloat16)
        asked = [exchange(ordered.reshape(rows, shards, per_device * HD))]

    pair_list, held = [own_pairs], [[0]]
    offset = blocks // 2
    while offset >= 1:
        pair_list += [lax.ppermute(part, "ctx", [(i, i ^ offset) for i in range(blocks)]) for part in pair_list]
        held += [[other ^ offset for other in group] for group in held]
        if line and len(pair_list) == 2:
            pair_list[1], asked[0] = lax.optimization_barrier((pair_list[1], asked[0]))
        offset //= 2

    def reorder(source):
        return jnp.dot(order, source, preferred_element_type=jnp.float32).astype(jnp.bfloat16)

    def restore(parts):
        whole = jnp.concatenate(parts, axis=0) if len(parts) > 1 else parts[0]
        return lax.dot_general(
            order, whole, (((0,), (0,)), ((), ())), preferred_element_type=jnp.float32
        ).astype(jnp.bfloat16)

    mine = lax.axis_index("ctx").astype(jnp.int32)[None]
    expert_ids = jnp.arange(router_weight.shape[1], dtype=jnp.int32)

    def project(which):
        terms = attend(
            block_order,
            jnp.stack([lax.axis_index("ctx"), me]).astype(jnp.int32),
            [asked[which][s] for s in slots],
            places[which],
            pair_list,
            held,
            pairs,
            sharing,
            block_rows,
            out_weight,
            pieces,
            line,
        )
        return [[term[slots.index(s)] for s in range(shards)] for term in terms]

    def finish(which, head_sums):
        base = hidden[which * half : (which + 1) * half].astype(jnp.float32)
        return jnp.concatenate(
            [(base[:, cut] + head_sum).astype(jnp.bfloat16) for cut, head_sum in zip(cuts, head_sums)], axis=1
        )

    def normalise(attended):
        widened = attended.astype(jnp.float32)
        return (
            widened * lax.rsqrt(jnp.mean(widened * widened, axis=1, keepdims=True) + 1e-05) * norm_gain
        ).astype(jnp.bfloat16)

    def share_of(which, normed):
        logits = jnp.dot(normed, router_weight, preferred_element_type=jnp.float32)
        named = my_routes[which * half : (which + 1) * half]
        first = jnp.sum(jnp.where(named[:, 0:1] == expert_ids[None, :], logits, 0.0), axis=1)
        second = jnp.sum(jnp.where(named[:, 1:2] == expert_ids[None, :], logits, 0.0), axis=1)
        share = jnp.where(named[:, 0] == 0, 1.0 / (1.0 + jnp.exp(second - first)), 0.0)
        return share + jnp.where(named[:, 1] == 0, 1.0 / (1.0 + jnp.exp(first - second)), 0.0)

    def expert(which, normed, sources, beside=None):
        terms = expert_rows(me[None], sources, gate_weight, up_weight, down_weight, shards, pieces, False)
        if beside is not None:
            terms, beside = lax.optimization_barrier((terms, beside))
        sums, marks = reduce_line(terms)
        if line:
            normed, _ = lax.optimization_barrier((normed, marks[0]))
        share = share_of(which, normed)
        parts = [(total * share[:, None]).astype(jnp.bfloat16) for total in sums]
        return jnp.concatenate(parts, axis=1), beside

    def late_expert(source):
        normed = normalise(source)
        return expert(1, normed, gather_line(normed)[0])[0]

    terms = project(0)
    if halves > 1:
        asked.append(shift(packed[1]))
        terms, asked[1] = lax.optimization_barrier((terms, asked[1]))
    totals, marks = reduce_line(terms)
    if line:
        hidden_in, order, _ = lax.optimization_barrier((hidden_in, order, marks[0]))
    hidden = reorder(hidden_in)
    my_routes = lax.dynamic_slice_in_dim(routes, me * rows, rows, 0).astype(jnp.bfloat16)
    my_routes = reorder(my_routes).astype(jnp.int32)
    first_half = finish(0, totals)
    normed = normalise(first_half)
    if halves == 1:
        return (restore([first_half]), restore([expert(0, normed, gather_line(normed)[0])[0]]))
    asked[1], _ = lax.optimization_barrier((asked[1], normed))
    sources, second_sum = gather_line(normed, project(1))
    second_half = (hidden[half:].astype(jnp.float32) + second_sum).astype(jnp.bfloat16)
    part, second_half = expert(0, normed, sources, second_half)
    part, late = lax.optimization_barrier((part, second_half))
    late = lax.cond(crowded[0] > 0, late_expert, jnp.zeros_like, late)
    return (restore([first_half, second_half]), restore([part, late]))


def solution(mesh):
    return jax.shard_map(
        on_device,
        mesh=mesh,
        in_specs=(
            P(("req", "ctx", "tp"), None),
            P(("req", "ctx", "tp"), None),
            P(("req", "ctx", "tp"), None),
            P(("req", "ctx", "tp"), None),
            P("req"),
            P(("req", "ctx"), None),
            P("tp", None),
            P(),
            P(),
            P(None, "tp"),
            P(None, "tp"),
            P("tp", None),
        ),
        out_specs=(P(("req", "ctx", "tp"), None), P(("req", "ctx", "tp"), None)),
        check_vma=False,
    )
```

```python
import functools
import math

import jax
import jax.numpy as jnp
from jax import lax
from jax.experimental import pallas as pl
from jax.experimental.pallas import tpu as pltpu
from jax.sharding import PartitionSpec as P

HEADS = 32
KV_HEADS = 8
HD = 128
FACTOR = math.log2(math.e) / math.sqrt(HD)
LINE = 4
SUM_ROWS = 16
TILE = 256
VMEM_HELD = 21 * 1024 * 1024
VMEM_LARGE = 28 * 1024 * 1024


def attention_kernel(slots, together, held, pairs, sharing, block_rows, plan, *refs):
    pieces, grouped = plan
    (order, mine), refs = refs[:2], refs[2:]
    sent_queries, refs = refs[:slots], refs[slots:]
    place_ref, refs = refs[0], refs[1:]
    sent_pairs, weight, refs = refs[: len(held)], refs[len(held)], refs[len(held) + 1 :]
    outs, refs = refs[: pieces * (slots if grouped else 1)], refs[pieces * (slots if grouped else 1) :]
    query_refs, pair_refs, refs = refs[:slots], refs[slots : slots + len(held)], refs[slots + len(held) :]
    query_ref, key_ref, value_ref, top_ref, total_ref, head_ref, weight_ref, arrived, here = refs
    half = query_refs[0].shape[0]
    step = pl.program_id(0)
    me = mine[0]
    my_block = order[me]
    blocks = [(ref, index, offset) for ref, group in zip(pair_refs, held) for index, offset in enumerate(group)]
    weight_copy = pltpu.make_async_copy(weight, weight_ref, arrived)
    moves = [
        pltpu.make_async_copy(source, target, here.at[i])
        for i, (source, target) in enumerate(
            list(zip(sent_pairs, pair_refs)) + list(zip(sent_queries, query_refs))
        )
    ]

    @pl.when(step == 0)
    def _():
        for move in moves:
            move.start()
        value_ref[:, :, HD:, :] = jnp.ones((len(blocks), pairs, SUM_ROWS, block_rows), jnp.bfloat16)

    @pl.when(step == 0)
    def _():
        for move in moves:
            move.wait()
        weight_copy.start()

    for at, (ref, index, offset) in enumerate(blocks):

        @pl.when((step == 0) & (order[me ^ offset] <= my_block))
        def _():
            for p in range(pairs):
                rows = slice(index * block_rows, (index + 1) * block_rows)
                key_ref[at, p] = ref[rows, p * HD : (p + 1) * HD]
                value_ref[at, p, :HD, :] = ref[rows, (pairs + p) * HD : (pairs + p + 1) * HD].T

    for at in range(slots):

        @pl.when(step == at // together)
        def _():
            for p in range(pairs):
                for g in range(sharing):
                    column = (p * sharing + g) * HD
                    row = (at % together * sharing + g) * half
                    query_ref[p, row : row + half, :] = query_refs[at][:, column : column + HD]

    def scores_of(p, at):
        return lax.dot_general(
            key_ref[at, p], query_ref[p], (((1,), (1,)), ((), ())), preferred_element_type=jnp.float32
        )

    def mixed_of(p, at, weights):
        return jnp.dot(value_ref[at, p], weights, preferred_element_type=jnp.float32)

    place = jnp.concatenate([place_ref[i] for i in range(together) for _ in range(sharing)], axis=1)
    rows = block_rows // slots
    down = lax.broadcasted_iota(jnp.int32, (rows, place.shape[1]), 0)
    visible = jnp.concatenate(
        [down <= place - lax.rem(mine[1] - s + slots, slots) * rows for s in range(slots)], axis=0
    )
    for p in range(pairs):
        scores = jnp.where(visible, scores_of(p, 0), -1e30)
        top = jnp.max(scores, axis=0, keepdims=True)
        weights = jnp.exp2((scores - top) * FACTOR).astype(jnp.bfloat16)
        top_ref[p, 0:1, :] = top
        total_ref[p] = mixed_of(p, 0, weights)

    @pl.loop(1, len(blocks))
    def _(at):
        offset = blocks[1][2] if len(blocks) > 1 else 0
        for other in range(2, len(blocks)):
            offset = jnp.where(at == other, blocks[other][2], offset)

        @pl.when(order[me ^ offset] < my_block)
        def _():
            for p in range(pairs):
                top = top_ref[p, 0:1, :]
                scores = scores_of(p, at)
                raised = jnp.maximum(top, jnp.max(scores, axis=0, keepdims=True))
                weights = jnp.exp2((scores - raised) * FACTOR).astype(jnp.bfloat16)
                top_ref[p, 0:1, :] = raised
                total_ref[p] = total_ref[p] * jnp.exp2((top - raised) * FACTOR) + mixed_of(p, at, weights)

    for p in range(pairs):
        mixed = (total_ref[p, :HD, :] / total_ref[p, HD : HD + 1, :]).T.astype(jnp.bfloat16)
        for i in range(together):
            for g in range(sharing):
                column = (p * sharing + g) * HD
                row = (i * sharing + g) * half
                at = pl.multiple_of((step * together + i) * half, half)
                head_ref[pl.ds(at, half), column : column + HD] = mixed[row : row + half]

    @pl.when(step == pl.num_programs(0) - 1)
    def _():
        weight_copy.wait()
        width = weight.shape[1] // pieces
        tile = 2 * TILE
        for c in range(pieces):

            @pl.loop(0, width // tile)
            def _(n):
                columns = pl.ds(pl.multiple_of(c * width + n * tile, tile), tile)
                value = jnp.dot(head_ref[...], weight_ref[:, columns], preferred_element_type=jnp.float32)
                share_out(outs[c * len(outs) // pieces :], pl.ds(pl.multiple_of(n * tile, tile), tile), value)


def share_out(outs, columns, value):
    rows = outs[0].shape[0]
    for g in range(value.shape[0] // rows):
        outs[g][:, columns] = value[g * rows : (g + 1) * rows].astype(jnp.bfloat16)


def piece_shapes(rows, width, slots, pieces, grouped):
    return [jax.ShapeDtypeStruct((rows // slots if grouped else rows, width // pieces), jnp.bfloat16)] * (
        pieces * (slots if grouped else 1)
    )


def by_piece(outs, slots, pieces, grouped):
    if grouped:
        return [outs[c * slots : (c + 1) * slots] for c in range(pieces)]
    return [[out[s * (out.shape[0] // slots) : (s + 1) * (out.shape[0] // slots)] for s in range(slots)] for out in outs]


def in_hbm(arrays):
    return [pltpu.with_memory_space_constraint(array, pltpu.HBM) for array in arrays]


def attend(order, mine, queries, places, pair_list, held, pairs, sharing, block_rows, weight, pieces, grouped):
    slots = len(queries)
    half, width = queries[0].shape
    together = 2 if slots <= LINE else 1
    tall = together * sharing * half
    blocks = sum(len(group) for group in held)
    count = blocks * block_rows
    shapes = piece_shapes(slots * half, weight.shape[1], slots, pieces, grouped)
    kernel = functools.partial(
        attention_kernel, slots, together, held, pairs, sharing, block_rows, (pieces, grouped)
    )
    outs = pl.pallas_call(
        kernel,
        grid_spec=pltpu.PrefetchScalarGridSpec(
            num_scalar_prefetch=2,
            grid=(slots // together,),
            in_specs=[pl.BlockSpec(memory_space=pltpu.HBM)] * slots
            + [pl.BlockSpec((together, 1, half), lambda s, *_: (s, 0, 0))]
            + [pl.BlockSpec(memory_space=pltpu.HBM)] * (len(pair_list) + 1),
            out_specs=[pl.BlockSpec(shape.shape, lambda s, *_: (0, 0)) for shape in shapes],
            scratch_shapes=[pltpu.VMEM((half, width), jnp.bfloat16)] * slots
            + [pltpu.VMEM(pair.shape, pair.dtype) for pair in pair_list]
            + [
                pltpu.VMEM((pairs, tall, HD), jnp.bfloat16),
                pltpu.VMEM((blocks, pairs, block_rows, HD), jnp.bfloat16),
                pltpu.VMEM((blocks, pairs, HD + SUM_ROWS, block_rows), jnp.bfloat16),
                pltpu.VMEM((pairs, 8, tall), jnp.float32),
                pltpu.VMEM((pairs, HD + SUM_ROWS, tall), jnp.float32),
                pltpu.VMEM((slots * half, width), jnp.bfloat16),
                pltpu.VMEM(weight.shape, weight.dtype),
                pltpu.SemaphoreType.DMA,
                pltpu.SemaphoreType.DMA((slots + len(pair_list),)),
            ],
        ),
        out_shape=shapes,
        compiler_params=pltpu.CompilerParams(vmem_limit_bytes=VMEM_HELD),
        cost_estimate=pl.CostEstimate(
            flops=40 * slots * half * width * count,
            bytes_accessed=2 * (2 * slots * half * width + count * 2 * pairs * HD + weight.size),
            transcendentals=slots * half * width // HD * count,
        ),
    )(order, mine, *in_hbm(queries), places, *in_hbm(pair_list), *in_hbm([weight]))
    return by_piece(outs, slots, pieces, grouped)


def expert_kernel(plan, pieces, *refs):
    mine, refs = refs[0], refs[1:]
    sources = []
    for count in plan:
        sources.append(refs[:count])
        refs = refs[count:]
    gate_weight, up_weight, down_weights, refs = refs[0], refs[1], refs[2:4], refs[4:]
    outs, (chosen, acts) = refs[:-2], refs[-2:]
    step = pl.program_id(0)
    tile = gate_weight.shape[1]
    first = acts.shape[1] // tile

    def place(s, source):
        rows, width = source[0].shape
        for c, ref in enumerate(source):
            chosen[s * rows : (s + 1) * rows, c * width : (c + 1) * width] = ref[...]

    @pl.when(step == 0)
    def _():
        place(0, sources[0])
        for s in range(1, (len(plan) + 1) // 2):
            right, left = sources[s], sources[len(plan) - s]

            @pl.when(mine[0] >= s)
            def _():
                place(s, right)

            @pl.when(mine[0] < s)
            def _():
                place(s, left)

    @pl.when(step < first)
    def _():
        gate = jnp.dot(chosen[...], gate_weight[...], preferred_element_type=jnp.float32)
        upward = jnp.dot(chosen[...], up_weight[...], preferred_element_type=jnp.float32)
        columns = pl.ds(pl.multiple_of(step * tile, tile), tile)
        acts[:, columns] = (gate / (1.0 + jnp.exp(-gate)) * upward).astype(jnp.bfloat16)

    @pl.when(step >= first)
    def _():
        strip = down_weights[0].shape[1]
        pairs = outs[0].shape[1] // (2 * strip)
        for j, down_weight in enumerate(down_weights):
            value = jnp.dot(acts[...], down_weight[...], preferred_element_type=jnp.float32)
            for c in range(pieces):

                @pl.when((step - first) // pairs == c)
                def _():
                    at = (2 * (step - first - c * pairs) + j) * strip
                    share_out(outs[c * len(outs) // pieces :], pl.ds(pl.multiple_of(at, strip), strip), value)


def expert_rows(mine, sources, gate_weight, up_weight, down_weight, slots, pieces, grouped):
    flat = [piece for source in sources for piece in source]
    rows = flat[0].shape[0] * ((len(sources) + 1) // 2)
    depth, width = gate_weight.shape
    tile, strip = min(TILE, width), 2 * TILE
    first = width // tile
    shapes = piece_shapes(rows, depth, slots, pieces, grouped)
    in_place = pl.BlockSpec(memory_space=pltpu.VMEM)
    weight = pl.BlockSpec((depth, tile), lambda n, *_: (0, jnp.minimum(n, first - 1)))
    outs = pl.pallas_call(
        functools.partial(expert_kernel, [len(source) for source in sources], pieces),
        grid_spec=pltpu.PrefetchScalarGridSpec(
            num_scalar_prefetch=1,
            grid=(first + depth // (2 * strip),),
            in_specs=[in_place] * len(flat)
            + [weight, weight]
            + [
                pl.BlockSpec((width, strip), functools.partial(lambda j, n, *_: (0, 2 * jnp.maximum(n - first, 0) + j), j))
                for j in range(2)
            ],
            out_specs=[in_place] * len(shapes),
            scratch_shapes=[pltpu.VMEM((rows, depth), jnp.bfloat16), pltpu.VMEM((rows, width), jnp.bfloat16)],
        ),
        out_shape=shapes,
        compiler_params=pltpu.CompilerParams(vmem_limit_bytes=VMEM_LARGE),
        cost_estimate=pl.CostEstimate(
            flops=6 * rows * depth * width, bytes_accessed=6 * depth * width, transcendentals=rows * width
        ),
    )(mine, *flat, gate_weight, up_weight, down_weight, down_weight)
    return by_piece(outs, slots, pieces, grouped)


def pack_pairs_kernel(shards, mine, keys_ref, values_ref, *outs):
    width = keys_ref.shape[1] // shards
    for s in range(shards):
        columns = pl.ds(pl.multiple_of(lax.rem(mine[0] + s, shards) * width, width), width)
        outs[s][:, :width] = keys_ref[:, columns]
        outs[s][:, width:] = values_ref[:, columns]


def pack_pairs(mine, keys, values, shards):
    rows, width = keys.shape
    spec = pl.BlockSpec((rows, width), lambda k, *_: (0, 0))
    out = (rows, 2 * width // shards)
    return pl.pallas_call(
        functools.partial(pack_pairs_kernel, shards),
        grid_spec=pltpu.PrefetchScalarGridSpec(
            num_scalar_prefetch=1,
            grid=(1,),
            in_specs=[spec, spec],
            out_specs=[pl.BlockSpec(out, lambda k, *_: (0, 0))] * shards,
        ),
        out_shape=[jax.ShapeDtypeStruct(out, keys.dtype)] * shards,
    )(mine, keys, values)


def pack_queries_kernel(slots, halves, mine, picked_ref, query_ref, *outs):
    shards = len(slots)
    rows = query_ref.shape[0]
    half = rows // halves
    width = query_ref.shape[1] // shards
    packed, outs = outs[: halves * shards], outs[halves * shards :]
    place_refs, (order_ref, count_ref) = outs[:halves], outs[halves:]
    me = mine[0]
    across = lax.broadcasted_iota(jnp.int32, (rows, rows), 1)
    down = lax.broadcasted_iota(jnp.int32, (rows, rows), 0)
    up_to = jnp.where(down <= across, 1.0, 0.0).astype(jnp.bfloat16)
    picked = picked_ref[...]
    seen = jnp.dot(picked.astype(jnp.bfloat16), up_to, preferred_element_type=jnp.float32).astype(jnp.int32)
    count = seen[:, rows - 1 : rows]
    row_ids = lax.broadcasted_iota(jnp.int32, seen.shape, 1)
    slot = jnp.where(picked > 0, seen - 1, count + row_ids - seen)
    count_ref[0] = jnp.max(jnp.where(count > half, 1, 0))
    ids = row_ids.astype(jnp.bfloat16)
    for s in range(shards):
        shard = lax.rem(me - s + shards, shards)
        mine_slot = slot[0:1]
        for other in range(1, shards):
            mine_slot = jnp.where(shard == other, slot[other : other + 1], mine_slot)
        at_slot = jnp.where(mine_slot == down, 1.0, 0.0).astype(jnp.bfloat16)
        rows_at = lax.dot_general(ids, at_slot, (((1,), (1,)), ((), ())), preferred_element_type=jnp.float32)
        for h in range(halves):
            here = rows_at[0:1, h * half : (h + 1) * half]
            place_refs[h][slots.index(s)] = here.astype(jnp.int32) + shard * rows
        if s == 0:
            order_ref[...] = at_slot
    for s in range(shards):
        columns = pl.ds(pl.multiple_of(lax.rem(me + s, shards) * width, width), width)
        ordered = jnp.dot(order_ref[...], query_ref[:, columns], preferred_element_type=jnp.float32)
        ordered = ordered.astype(jnp.bfloat16)
        for h in range(halves):
            packed[h * shards + s][...] = ordered[h * half : (h + 1) * half]


def pack_queries(mine, picked, queries, slots, halves):
    shards = len(slots)
    rows, width = queries.shape
    packed = (rows // halves, width // shards)
    shapes = [jax.ShapeDtypeStruct(packed, jnp.bfloat16)] * (halves * shards)
    shapes += [jax.ShapeDtypeStruct((shards, 1, rows // halves), jnp.int32)] * halves
    shapes += [jax.ShapeDtypeStruct((rows, rows), jnp.bfloat16), jax.ShapeDtypeStruct((1,), jnp.int32)]

    def whole(shape):
        return pl.BlockSpec(shape, lambda k, *_: (0,) * len(shape))

    got = pl.pallas_call(
        functools.partial(pack_queries_kernel, slots, halves),
        grid_spec=pltpu.PrefetchScalarGridSpec(
            num_scalar_prefetch=1,
            grid=(1,),
            in_specs=[whole(picked.shape), whole(queries.shape)],
            out_specs=[whole(shape.shape) for shape in shapes[:-1]] + [pl.BlockSpec(memory_space=pltpu.SMEM)],
        ),
        out_shape=shapes,
    )(mine, picked, queries)
    packed, got = got[: halves * shards], got[halves * shards :]
    return [packed[h * shards : (h + 1) * shards] for h in range(halves)], got[:halves], *got[halves:]


def on_device(
    hidden_in,
    queries,
    keys,
    values,
    block_order,
    routes,
    out_weight,
    norm_gain,
    router_weight,
    gate_weight,
    up_weight,
    down_weight,
):
    shards = lax.axis_size("tp")
    blocks = lax.axis_size("ctx")
    me = lax.axis_index("tp")
    rows, model = hidden_in.shape
    block_rows = rows * shards
    per_device = HEADS // shards
    grouping = HEADS // KV_HEADS
    repeat_by = max(1, grouping // per_device)
    pairs = max(1, per_device // grouping)
    sharing = per_device // pairs
    half = rows // 2 if rows % 32 == 0 else rows
    halves = rows // half
    line = shards <= LINE
    pieces = 2 if line else 1
    cuts = [slice(c * (model // pieces), (c + 1) * (model // pieces)) for c in range(pieces)]
    slots = [s for s in range(1, shards, 2)] + [s for s in range(2, shards, 2)] + [0]
    shard_of = lax.rem(me - jnp.arange(shards, dtype=jnp.int32) + shards, shards)

    def shift(parts):
        moves = [[(i, (i + s) % shards) for i in range(shards)] for s in range(shards)]
        return [parts[0]] + [lax.ppermute(parts[s], "tp", moves[s]) for s in range(1, shards)]

    def exchange(source):
        got = lax.all_to_all(source, "tp", split_axis=1, concat_axis=0, tiled=True)
        got = got.reshape(shards, rows, source.shape[2])
        return [lax.dynamic_index_in_dim(got, shard_of[s], 0, keepdims=False) for s in range(shards)]

    def rights(count):
        return [(i, i + 1) for i in range(count)]

    def lefts(count):
        return [(i, i - 1) for i in range(shards - count, shards)]

    def reduce_line(pieces_terms, merged=False):
        if not line:
            by_shard = [jnp.take(jnp.stack(terms), shard_of, axis=0).reshape(-1, terms[0].shape[1]) for terms in pieces_terms]
            return [
                lax.psum_scatter(term, "tp", scatter_dimension=0, tiled=True).astype(jnp.float32) for term in by_shard
            ], None
        got = [None] * len(pieces_terms)
        marks = []
        for s in range(1, shards):
            for c, terms in enumerate(pieces_terms):
                if s == 1 and merged:
                    sent = jnp.where(me == 0, terms[1], terms[shards - 1])
                    arrived = lax.ppermute(sent, "tp", [(0, 1), (shards - 1, shards - 2)])
                    got[c] = (arrived, arrived)
                    continue
                if s == 1:
                    to_right, to_left = terms[s], terms[shards - s]
                elif s == 2 and merged:
                    to_right = to_left = terms[s] + got[c][0]
                else:
                    to_right, to_left = terms[s] + got[c][0], terms[shards - s] + got[c][1]
                right = lax.ppermute(to_right, "tp", rights(s))
                left = lax.ppermute(to_left, "tp", lefts(s))
                got[c] = lax.optimization_barrier((right, left))
            marks.append(got[0])
        return [
            terms[0].astype(jnp.float32) + right.astype(jnp.float32) + left.astype(jnp.float32)
            for terms, (right, left) in zip(pieces_terms, got)
        ], marks

    def gather_line(source, terms=None):
        if not line:
            got = lax.all_gather(source, "tp", axis=0)
            return [[jnp.take(got, shard_of, axis=0).reshape(shards * half, -1)]], None
        first_right = lax.ppermute(source, "tp", rights(shards - 1))
        first_left = lax.ppermute(source, "tp", lefts(shards - 1))
        first_right, first_left = lax.optimization_barrier((first_right, first_left))
        got = [(first_right[:, cut], first_left[:, cut]) for cut in cuts]
        from_left, from_right = [], []
        for s in range(2, shards):
            if terms is None:
                sent = got
                to_right = [(i, i + 1) for i in range(s - 1, shards - 1)]
                to_left = [(i, i - 1) for i in range(1, shards - s + 1)]
            else:
                sent = [
                    (
                        jnp.where(me >= s - 1, right, right + term[s - 1]),
                        jnp.where(me <= shards - s, left, left + term[shards - s + 1]),
                    )
                    for (right, left), term in zip(got, terms)
                ]
                to_right, to_left = rights(shards - 1), lefts(shards - 1)
            from_left.append([right for right, _ in sent])
            from_right.append([left for _, left in sent])
            got = [
                lax.optimization_barrier((lax.ppermute(right, "tp", to_right), lax.ppermute(left, "tp", to_left)))
                for right, left in sent
            ]
        from_left.append([right for right, _ in got])
        from_right.append([left for _, left in got])
        total = None
        if terms is not None:
            right = jnp.concatenate([right + term[shards - 1] for (right, _), term in zip(got, terms)], axis=1)
            left = jnp.concatenate([left + term[1] for (_, left), term in zip(got, terms)], axis=1)
            right = lax.ppermute(right, "tp", rights(shards - 1)).astype(jnp.float32)
            left = lax.ppermute(left, "tp", lefts(shards - 1)).astype(jnp.float32)
            total = jnp.concatenate([term[0] for term in terms], axis=1).astype(jnp.float32) + right + left
        return [[source]] + from_left + from_right, total

    picked = ((routes[:, 0] == 0) | (routes[:, 1] == 0)).reshape(shards, rows)
    if line:
        sent_pairs = pack_pairs(me[None], keys, values, shards)
        own_pairs = jnp.concatenate(shift(sent_pairs), axis=0)
        picked, _ = lax.optimization_barrier((picked.astype(jnp.int32), sent_pairs))
        packed, places, order, crowded = pack_queries(me[None], picked, queries, slots, halves)
        asked = [shift(packed[0])]
    else:

        def spread(source):
            widened = jnp.repeat(source.reshape(rows, KV_HEADS, HD), repeat_by, axis=1)
            return widened.reshape(rows, shards, pairs * HD)

        own_pairs = exchange(jnp.concatenate([spread(keys), spread(values)], axis=2))
        own_pairs = jnp.concatenate(own_pairs, axis=0)
        row_ids = jnp.arange(rows, dtype=jnp.int32)
        seen = jnp.cumsum(picked.astype(jnp.int32), axis=1)
        slot = jnp.where(picked, seen - 1, seen[:, -1:] + row_ids[None, :] - seen)
        at_slot = slot[:, None, :] == row_ids[None, :, None]
        row_of_slot = jnp.sum(jnp.where(at_slot, row_ids[None, None, :], 0), axis=2)
        places = row_of_slot + jnp.arange(shards, dtype=jnp.int32)[:, None] * rows
        places = [jnp.stack([jnp.take(places, shard_of[s], axis=0) for s in slots])[:, None, :]]
        order = lax.dynamic_index_in_dim(at_slot, me, 0, keepdims=False).astype(jnp.bfloat16)
        ordered = jnp.dot(order, queries, preferred_element_type=jnp.float32).astype(jnp.bfloat16)
        asked = [exchange(ordered.reshape(rows, shards, per_device * HD))]

    pair_list, held = [own_pairs], [[0]]
    offset = blocks // 2
    while offset >= 1:
        pair_list += [lax.ppermute(part, "ctx", [(i, i ^ offset) for i in range(blocks)]) for part in pair_list]
        held += [[other ^ offset for other in group] for group in held]
        if line and len(pair_list) == 2:
            pair_list[1], asked[0] = lax.optimization_barrier((pair_list[1], asked[0]))
        offset //= 2

    def reorder(source):
        return jnp.dot(order, source, preferred_element_type=jnp.float32).astype(jnp.bfloat16)

    def restore(parts):
        whole = jnp.concatenate(parts, axis=0) if len(parts) > 1 else parts[0]
        return lax.dot_general(
            order, whole, (((0,), (0,)), ((), ())), preferred_element_type=jnp.float32
        ).astype(jnp.bfloat16)

    mine = lax.axis_index("ctx").astype(jnp.int32)[None]
    expert_ids = jnp.arange(router_weight.shape[1], dtype=jnp.int32)

    def project(which):
        terms = attend(
            block_order,
            jnp.stack([lax.axis_index("ctx"), me]).astype(jnp.int32),
            [asked[which][s] for s in slots],
            places[which],
            pair_list,
            held,
            pairs,
            sharing,
            block_rows,
            out_weight,
            pieces,
            line,
        )
        return [[term[slots.index(s)] for s in range(shards)] for term in terms]

    def finish(which, head_sums):
        base = hidden[which * half : (which + 1) * half].astype(jnp.float32)
        return jnp.concatenate(
            [(base[:, cut] + head_sum).astype(jnp.bfloat16) for cut, head_sum in zip(cuts, head_sums)], axis=1
        )

    def normalise(attended):
        widened = attended.astype(jnp.float32)
        return (
            widened * lax.rsqrt(jnp.mean(widened * widened, axis=1, keepdims=True) + 1e-05) * norm_gain
        ).astype(jnp.bfloat16)

    def share_of(which, normed):
        logits = jnp.dot(normed, router_weight, preferred_element_type=jnp.float32)
        named = my_routes[which * half : (which + 1) * half]
        first = jnp.sum(jnp.where(named[:, 0:1] == expert_ids[None, :], logits, 0.0), axis=1)
        second = jnp.sum(jnp.where(named[:, 1:2] == expert_ids[None, :], logits, 0.0), axis=1)
        share = jnp.where(named[:, 0] == 0, 1.0 / (1.0 + jnp.exp(second - first)), 0.0)
        return share + jnp.where(named[:, 1] == 0, 1.0 / (1.0 + jnp.exp(first - second)), 0.0)

    def expert(which, normed, sources, beside=None):
        terms = expert_rows(me[None], sources, gate_weight, up_weight, down_weight, shards, pieces, False)
        if beside is not None:
            terms, beside = lax.optimization_barrier((terms, beside))
        sums, marks = reduce_line(terms)
        if line:
            normed, _ = lax.optimization_barrier((normed, marks[0]))
        share = share_of(which, normed)
        parts = [(total * share[:, None]).astype(jnp.bfloat16) for total in sums]
        return jnp.concatenate(parts, axis=1), beside

    def late_expert(source):
        normed = normalise(source)
        return expert(1, normed, gather_line(normed)[0])[0]

    terms = project(0)
    if halves > 1:
        asked.append(shift(packed[1]))
        terms, asked[1] = lax.optimization_barrier((terms, asked[1]))
    totals, marks = reduce_line(terms, True)
    if line:
        hidden_in, order, _ = lax.optimization_barrier((hidden_in, order, marks[0]))
    hidden = reorder(hidden_in)
    my_routes = lax.dynamic_slice_in_dim(routes, me * rows, rows, 0).astype(jnp.bfloat16)
    my_routes = reorder(my_routes).astype(jnp.int32)
    first_half = finish(0, totals)
    normed = normalise(first_half)
    if halves == 1:
        return (restore([first_half]), restore([expert(0, normed, gather_line(normed)[0])[0]]))
    asked[1], _ = lax.optimization_barrier((asked[1], normed))
    sources, second_sum = gather_line(normed, project(1))
    second_half = (hidden[half:].astype(jnp.float32) + second_sum).astype(jnp.bfloat16)
    part, second_half = expert(0, normed, sources, second_half)
    part, late = lax.optimization_barrier((part, second_half))
    late = lax.cond(crowded[0] > 0, late_expert, jnp.zeros_like, late)
    return (restore([first_half, second_half]), restore([part, late]))


def solution(mesh):
    return jax.shard_map(
        on_device,
        mesh=mesh,
        in_specs=(
            P(("req", "ctx", "tp"), None),
            P(("req", "ctx", "tp"), None),
            P(("req", "ctx", "tp"), None),
            P(("req", "ctx", "tp"), None),
            P("req"),
            P(("req", "ctx"), None),
            P("tp", None),
            P(),
            P(),
            P(None, "tp"),
            P(None, "tp"),
            P("tp", None),
        ),
        out_specs=(P(("req", "ctx", "tp"), None), P(("req", "ctx", "tp"), None)),
        check_vma=False,
    )
```

```python
import functools
import math

import jax
import jax.numpy as jnp
from jax import lax
from jax.experimental import pallas as pl
from jax.experimental.pallas import tpu as pltpu
from jax.sharding import PartitionSpec as P

HEADS = 32
KV_HEADS = 8
HD = 128
FACTOR = math.log2(math.e) / math.sqrt(HD)
LINE = 4
SUM_ROWS = 16
TILE = 256
VMEM_HELD = 21 * 1024 * 1024
VMEM_LARGE = 28 * 1024 * 1024


def attention_kernel(slots, together, held, pairs, sharing, block_rows, plan, *refs):
    pieces, grouped = plan
    (order, mine), refs = refs[:2], refs[2:]
    sent_queries, refs = refs[:slots], refs[slots:]
    place_ref, refs = refs[0], refs[1:]
    sent_pairs, weight, refs = refs[: len(held)], refs[len(held)], refs[len(held) + 1 :]
    outs, refs = refs[: pieces * (slots if grouped else 1)], refs[pieces * (slots if grouped else 1) :]
    query_refs, pair_refs, refs = refs[:slots], refs[slots : slots + len(held)], refs[slots + len(held) :]
    query_ref, key_ref, value_ref, top_ref, total_ref, head_ref, weight_ref, arrived, here = refs
    half = query_refs[0].shape[0]
    step = pl.program_id(0)
    me = mine[0]
    my_block = order[me]
    blocks = [(ref, index, offset) for ref, group in zip(pair_refs, held) for index, offset in enumerate(group)]
    weight_copy = pltpu.make_async_copy(weight, weight_ref, arrived)
    moves = [
        pltpu.make_async_copy(source, target, here.at[i])
        for i, (source, target) in enumerate(
            list(zip(sent_pairs, pair_refs)) + list(zip(sent_queries, query_refs))
        )
    ]

    @pl.when(step == 0)
    def _():
        for move in moves:
            move.start()
        value_ref[:, :, HD:, :] = jnp.ones((len(blocks), pairs, SUM_ROWS, block_rows), jnp.bfloat16)

    @pl.when(step == 0)
    def _():
        for move in moves:
            move.wait()
        weight_copy.start()

    for at, (ref, index, offset) in enumerate(blocks):

        @pl.when((step == 0) & (order[me ^ offset] <= my_block))
        def _():
            for p in range(pairs):
                rows = slice(index * block_rows, (index + 1) * block_rows)
                key_ref[at, p] = ref[rows, p * HD : (p + 1) * HD]
                value_ref[at, p, :HD, :] = ref[rows, (pairs + p) * HD : (pairs + p + 1) * HD].T

    for at in range(slots):

        @pl.when(step == at // together)
        def _():
            for p in range(pairs):
                for g in range(sharing):
                    column = (p * sharing + g) * HD
                    row = (at % together * sharing + g) * half
                    query_ref[p, row : row + half, :] = query_refs[at][:, column : column + HD]

    def scores_of(p, at):
        return lax.dot_general(
            key_ref[at, p], query_ref[p], (((1,), (1,)), ((), ())), preferred_element_type=jnp.float32
        )

    def mixed_of(p, at, weights):
        return jnp.dot(value_ref[at, p], weights, preferred_element_type=jnp.float32)

    place = jnp.concatenate([place_ref[i] for i in range(together) for _ in range(sharing)], axis=1)
    rows = block_rows // slots
    down = lax.broadcasted_iota(jnp.int32, (rows, place.shape[1]), 0)
    visible = jnp.concatenate(
        [down <= place - lax.rem(mine[1] - s + slots, slots) * rows for s in range(slots)], axis=0
    )
    for p in range(pairs):
        scores = jnp.where(visible, scores_of(p, 0), -1e30)
        top = jnp.max(scores, axis=0, keepdims=True)
        weights = jnp.exp2((scores - top) * FACTOR).astype(jnp.bfloat16)
        top_ref[p, 0:1, :] = top
        total_ref[p] = mixed_of(p, 0, weights)

    @pl.loop(1, len(blocks))
    def _(at):
        offset = blocks[1][2] if len(blocks) > 1 else 0
        for other in range(2, len(blocks)):
            offset = jnp.where(at == other, blocks[other][2], offset)

        @pl.when(order[me ^ offset] < my_block)
        def _():
            for p in range(pairs):
                top = top_ref[p, 0:1, :]
                scores = scores_of(p, at)
                raised = jnp.maximum(top, jnp.max(scores, axis=0, keepdims=True))
                weights = jnp.exp2((scores - raised) * FACTOR).astype(jnp.bfloat16)
                top_ref[p, 0:1, :] = raised
                total_ref[p] = total_ref[p] * jnp.exp2((top - raised) * FACTOR) + mixed_of(p, at, weights)

    for p in range(pairs):
        mixed = (total_ref[p, :HD, :] / total_ref[p, HD : HD + 1, :]).T.astype(jnp.bfloat16)
        for i in range(together):
            for g in range(sharing):
                column = (p * sharing + g) * HD
                row = (i * sharing + g) * half
                at = pl.multiple_of((step * together + i) * half, half)
                head_ref[pl.ds(at, half), column : column + HD] = mixed[row : row + half]

    @pl.when(step == pl.num_programs(0) - 1)
    def _():
        weight_copy.wait()
        width = weight.shape[1] // pieces
        tile = 2 * TILE
        for c in range(pieces):

            @pl.loop(0, width // tile)
            def _(n):
                columns = pl.ds(pl.multiple_of(c * width + n * tile, tile), tile)
                value = jnp.dot(head_ref[...], weight_ref[:, columns], preferred_element_type=jnp.float32)
                share_out(outs[c * len(outs) // pieces :], pl.ds(pl.multiple_of(n * tile, tile), tile), value)


def share_out(outs, columns, value):
    rows = outs[0].shape[0]
    for g in range(value.shape[0] // rows):
        outs[g][:, columns] = value[g * rows : (g + 1) * rows].astype(jnp.bfloat16)


def piece_shapes(rows, width, slots, pieces, grouped):
    return [jax.ShapeDtypeStruct((rows // slots if grouped else rows, width // pieces), jnp.bfloat16)] * (
        pieces * (slots if grouped else 1)
    )


def by_piece(outs, slots, pieces, grouped):
    if grouped:
        return [outs[c * slots : (c + 1) * slots] for c in range(pieces)]
    return [[out[s * (out.shape[0] // slots) : (s + 1) * (out.shape[0] // slots)] for s in range(slots)] for out in outs]


def in_hbm(arrays):
    return [pltpu.with_memory_space_constraint(array, pltpu.HBM) for array in arrays]


def attend(order, mine, queries, places, pair_list, held, pairs, sharing, block_rows, weight, pieces, grouped):
    slots = len(queries)
    half, width = queries[0].shape
    together = 2 if slots <= LINE else 1
    tall = together * sharing * half
    blocks = sum(len(group) for group in held)
    count = blocks * block_rows
    shapes = piece_shapes(slots * half, weight.shape[1], slots, pieces, grouped)
    kernel = functools.partial(
        attention_kernel, slots, together, held, pairs, sharing, block_rows, (pieces, grouped)
    )
    outs = pl.pallas_call(
        kernel,
        grid_spec=pltpu.PrefetchScalarGridSpec(
            num_scalar_prefetch=2,
            grid=(slots // together,),
            in_specs=[pl.BlockSpec(memory_space=pltpu.HBM)] * slots
            + [pl.BlockSpec((together, 1, half), lambda s, *_: (s, 0, 0))]
            + [pl.BlockSpec(memory_space=pltpu.HBM)] * (len(pair_list) + 1),
            out_specs=[pl.BlockSpec(shape.shape, lambda s, *_: (0, 0)) for shape in shapes],
            scratch_shapes=[pltpu.VMEM((half, width), jnp.bfloat16)] * slots
            + [pltpu.VMEM(pair.shape, pair.dtype) for pair in pair_list]
            + [
                pltpu.VMEM((pairs, tall, HD), jnp.bfloat16),
                pltpu.VMEM((blocks, pairs, block_rows, HD), jnp.bfloat16),
                pltpu.VMEM((blocks, pairs, HD + SUM_ROWS, block_rows), jnp.bfloat16),
                pltpu.VMEM((pairs, 8, tall), jnp.float32),
                pltpu.VMEM((pairs, HD + SUM_ROWS, tall), jnp.float32),
                pltpu.VMEM((slots * half, width), jnp.bfloat16),
                pltpu.VMEM(weight.shape, weight.dtype),
                pltpu.SemaphoreType.DMA,
                pltpu.SemaphoreType.DMA((slots + len(pair_list),)),
            ],
        ),
        out_shape=shapes,
        compiler_params=pltpu.CompilerParams(vmem_limit_bytes=VMEM_HELD),
        cost_estimate=pl.CostEstimate(
            flops=40 * slots * half * width * count,
            bytes_accessed=2 * (2 * slots * half * width + count * 2 * pairs * HD + weight.size),
            transcendentals=slots * half * width // HD * count,
        ),
    )(order, mine, *in_hbm(queries), places, *in_hbm(pair_list), *in_hbm([weight]))
    return by_piece(outs, slots, pieces, grouped)


def expert_kernel(plan, pieces, *refs):
    mine, refs = refs[0], refs[1:]
    sources = []
    for count in plan:
        sources.append(refs[:count])
        refs = refs[count:]
    gate_weight, up_weight, down_weights, refs = refs[0], refs[1], refs[2:4], refs[4:]
    outs, (chosen, acts) = refs[:-2], refs[-2:]
    step = pl.program_id(0)
    tile = gate_weight.shape[1]
    first = acts.shape[1] // tile

    def place(s, source):
        rows, width = source[0].shape
        for c, ref in enumerate(source):
            chosen[s * rows : (s + 1) * rows, c * width : (c + 1) * width] = ref[...]

    @pl.when(step == 0)
    def _():
        place(0, sources[0])
        for s in range(1, (len(plan) + 1) // 2):
            right, left = sources[s], sources[len(plan) - s]

            @pl.when(mine[0] >= s)
            def _():
                place(s, right)

            @pl.when(mine[0] < s)
            def _():
                place(s, left)

    @pl.when(step < first)
    def _():
        gate = jnp.dot(chosen[...], gate_weight[...], preferred_element_type=jnp.float32)
        upward = jnp.dot(chosen[...], up_weight[...], preferred_element_type=jnp.float32)
        columns = pl.ds(pl.multiple_of(step * tile, tile), tile)
        acts[:, columns] = (gate / (1.0 + jnp.exp(-gate)) * upward).astype(jnp.bfloat16)

    @pl.when(step >= first)
    def _():
        strip = down_weights[0].shape[1]
        pairs = outs[0].shape[1] // (2 * strip)
        for j, down_weight in enumerate(down_weights):
            value = jnp.dot(acts[...], down_weight[...], preferred_element_type=jnp.float32)
            for c in range(pieces):

                @pl.when((step - first) // pairs == c)
                def _():
                    at = (2 * (step - first - c * pairs) + j) * strip
                    share_out(outs[c * len(outs) // pieces :], pl.ds(pl.multiple_of(at, strip), strip), value)


def expert_rows(mine, sources, gate_weight, up_weight, down_weight, slots, pieces, grouped):
    flat = [piece for source in sources for piece in source]
    rows = flat[0].shape[0] * ((len(sources) + 1) // 2)
    depth, width = gate_weight.shape
    tile, strip = min(TILE, width), 2 * TILE
    first = width // tile
    shapes = piece_shapes(rows, depth, slots, pieces, grouped)
    in_place = pl.BlockSpec(memory_space=pltpu.VMEM)
    weight = pl.BlockSpec((depth, tile), lambda n, *_: (0, jnp.minimum(n, first - 1)))
    outs = pl.pallas_call(
        functools.partial(expert_kernel, [len(source) for source in sources], pieces),
        grid_spec=pltpu.PrefetchScalarGridSpec(
            num_scalar_prefetch=1,
            grid=(first + depth // (2 * strip),),
            in_specs=[in_place] * len(flat)
            + [weight, weight]
            + [
                pl.BlockSpec((width, strip), functools.partial(lambda j, n, *_: (0, 2 * jnp.maximum(n - first, 0) + j), j))
                for j in range(2)
            ],
            out_specs=[in_place] * len(shapes),
            scratch_shapes=[pltpu.VMEM((rows, depth), jnp.bfloat16), pltpu.VMEM((rows, width), jnp.bfloat16)],
        ),
        out_shape=shapes,
        compiler_params=pltpu.CompilerParams(vmem_limit_bytes=VMEM_LARGE),
        cost_estimate=pl.CostEstimate(
            flops=6 * rows * depth * width, bytes_accessed=6 * depth * width, transcendentals=rows * width
        ),
    )(mine, *flat, gate_weight, up_weight, down_weight, down_weight)
    return by_piece(outs, slots, pieces, grouped)


def pack_pairs_kernel(shards, mine, keys_ref, values_ref, *outs):
    width = keys_ref.shape[1] // shards
    for s in range(shards):
        columns = pl.ds(pl.multiple_of(lax.rem(mine[0] + s, shards) * width, width), width)
        outs[s][:, :width] = keys_ref[:, columns]
        outs[s][:, width:] = values_ref[:, columns]


def pack_pairs(mine, keys, values, shards):
    rows, width = keys.shape
    spec = pl.BlockSpec((rows, width), lambda k, *_: (0, 0))
    out = (rows, 2 * width // shards)
    return pl.pallas_call(
        functools.partial(pack_pairs_kernel, shards),
        grid_spec=pltpu.PrefetchScalarGridSpec(
            num_scalar_prefetch=1,
            grid=(1,),
            in_specs=[spec, spec],
            out_specs=[pl.BlockSpec(out, lambda k, *_: (0, 0))] * shards,
        ),
        out_shape=[jax.ShapeDtypeStruct(out, keys.dtype)] * shards,
    )(mine, keys, values)


def pack_queries_kernel(slots, halves, mine, picked_ref, query_ref, *outs):
    shards = len(slots)
    rows = query_ref.shape[0]
    half = rows // halves
    width = query_ref.shape[1] // shards
    packed, outs = outs[: halves * shards], outs[halves * shards :]
    place_refs, (order_ref, count_ref) = outs[:halves], outs[halves:]
    me = mine[0]
    across = lax.broadcasted_iota(jnp.int32, (rows, rows), 1)
    down = lax.broadcasted_iota(jnp.int32, (rows, rows), 0)
    up_to = jnp.where(down <= across, 1.0, 0.0).astype(jnp.bfloat16)
    picked = picked_ref[...]
    seen = jnp.dot(picked.astype(jnp.bfloat16), up_to, preferred_element_type=jnp.float32).astype(jnp.int32)
    count = seen[:, rows - 1 : rows]
    row_ids = lax.broadcasted_iota(jnp.int32, seen.shape, 1)
    slot = jnp.where(picked > 0, seen - 1, count + row_ids - seen)
    count_ref[0] = jnp.max(jnp.where(count > half, 1, 0))
    ids = row_ids.astype(jnp.bfloat16)
    for s in range(shards):
        shard = lax.rem(me - s + shards, shards)
        mine_slot = slot[0:1]
        for other in range(1, shards):
            mine_slot = jnp.where(shard == other, slot[other : other + 1], mine_slot)
        at_slot = jnp.where(mine_slot == down, 1.0, 0.0).astype(jnp.bfloat16)
        rows_at = lax.dot_general(ids, at_slot, (((1,), (1,)), ((), ())), preferred_element_type=jnp.float32)
        for h in range(halves):
            here = rows_at[0:1, h * half : (h + 1) * half]
            place_refs[h][slots.index(s)] = here.astype(jnp.int32) + shard * rows
        if s == 0:
            order_ref[...] = at_slot
    for s in range(shards):
        columns = pl.ds(pl.multiple_of(lax.rem(me + s, shards) * width, width), width)
        ordered = jnp.dot(order_ref[...], query_ref[:, columns], preferred_element_type=jnp.float32)
        ordered = ordered.astype(jnp.bfloat16)
        for h in range(halves):
            packed[h * shards + s][...] = ordered[h * half : (h + 1) * half]


def pack_queries(mine, picked, queries, slots, halves):
    shards = len(slots)
    rows, width = queries.shape
    packed = (rows // halves, width // shards)
    shapes = [jax.ShapeDtypeStruct(packed, jnp.bfloat16)] * (halves * shards)
    shapes += [jax.ShapeDtypeStruct((shards, 1, rows // halves), jnp.int32)] * halves
    shapes += [jax.ShapeDtypeStruct((rows, rows), jnp.bfloat16), jax.ShapeDtypeStruct((1,), jnp.int32)]

    def whole(shape):
        return pl.BlockSpec(shape, lambda k, *_: (0,) * len(shape))

    got = pl.pallas_call(
        functools.partial(pack_queries_kernel, slots, halves),
        grid_spec=pltpu.PrefetchScalarGridSpec(
            num_scalar_prefetch=1,
            grid=(1,),
            in_specs=[whole(picked.shape), whole(queries.shape)],
            out_specs=[whole(shape.shape) for shape in shapes[:-1]] + [pl.BlockSpec(memory_space=pltpu.SMEM)],
        ),
        out_shape=shapes,
    )(mine, picked, queries)
    packed, got = got[: halves * shards], got[halves * shards :]
    return [packed[h * shards : (h + 1) * shards] for h in range(halves)], got[:halves], *got[halves:]


def on_device(
    hidden_in,
    queries,
    keys,
    values,
    block_order,
    routes,
    out_weight,
    norm_gain,
    router_weight,
    gate_weight,
    up_weight,
    down_weight,
):
    shards = lax.axis_size("tp")
    blocks = lax.axis_size("ctx")
    me = lax.axis_index("tp")
    rows, model = hidden_in.shape
    block_rows = rows * shards
    per_device = HEADS // shards
    grouping = HEADS // KV_HEADS
    repeat_by = max(1, grouping // per_device)
    pairs = max(1, per_device // grouping)
    sharing = per_device // pairs
    half = rows // 2 if rows % 32 == 0 else rows
    halves = rows // half
    line = shards <= LINE
    pieces = 2 if line else 1
    cuts = [slice(c * (model // pieces), (c + 1) * (model // pieces)) for c in range(pieces)]
    slots = [s for s in range(1, shards, 2)] + [s for s in range(2, shards, 2)] + [0]
    shard_of = lax.rem(me - jnp.arange(shards, dtype=jnp.int32) + shards, shards)

    def shift(parts):
        moves = [[(i, (i + s) % shards) for i in range(shards)] for s in range(shards)]
        return [parts[0]] + [lax.ppermute(parts[s], "tp", moves[s]) for s in range(1, shards)]

    def exchange(source):
        got = lax.all_to_all(source, "tp", split_axis=1, concat_axis=0, tiled=True)
        got = got.reshape(shards, rows, source.shape[2])
        return [lax.dynamic_index_in_dim(got, shard_of[s], 0, keepdims=False) for s in range(shards)]

    def rights(count):
        return [(i, i + 1) for i in range(count)]

    def lefts(count):
        return [(i, i - 1) for i in range(shards - count, shards)]

    def reduce_line(pieces_terms, merged=False, beside=None):
        if not line:
            by_shard = [jnp.take(jnp.stack(terms), shard_of, axis=0).reshape(-1, terms[0].shape[1]) for terms in pieces_terms]
            return [
                lax.psum_scatter(term, "tp", scatter_dimension=0, tiled=True).astype(jnp.float32) for term in by_shard
            ], None
        got = [None] * len(pieces_terms)
        marks = []
        for s in range(1, shards):
            for c, terms in enumerate(pieces_terms):
                if s == 1 and merged:
                    sent = jnp.where(me == 0, terms[1], terms[shards - 1])
                    arrived = lax.ppermute(sent, "tp", [(0, 1), (shards - 1, shards - 2)])
                    got[c] = (arrived, arrived)
                    continue
                if s == 1:
                    to_right, to_left = terms[s], terms[shards - s]
                elif s == 2 and merged:
                    to_right = to_left = terms[s] + got[c][0]
                else:
                    to_right, to_left = terms[s] + got[c][0], terms[shards - s] + got[c][1]
                right = lax.ppermute(to_right, "tp", rights(s))
                left = lax.ppermute(to_left, "tp", lefts(s))
                got[c] = lax.optimization_barrier((right, left))
            marks.append(got[0])
            if s == 1 and beside is not None:
                got[0], beside = lax.optimization_barrier((got[0], beside))
        marks.append(beside)
        return [
            terms[0].astype(jnp.float32) + right.astype(jnp.float32) + left.astype(jnp.float32)
            for terms, (right, left) in zip(pieces_terms, got)
        ], marks

    def gather_line(source, terms=None):
        if not line:
            got = lax.all_gather(source, "tp", axis=0)
            return [[jnp.take(got, shard_of, axis=0).reshape(shards * half, -1)]], None
        first_right = lax.ppermute(source, "tp", rights(shards - 1))
        first_left = lax.ppermute(source, "tp", lefts(shards - 1))
        first_right, first_left = lax.optimization_barrier((first_right, first_left))
        got = [(first_right[:, cut], first_left[:, cut]) for cut in cuts]
        from_left, from_right = [], []
        for s in range(2, shards):
            if terms is None:
                sent = got
                to_right = [(i, i + 1) for i in range(s - 1, shards - 1)]
                to_left = [(i, i - 1) for i in range(1, shards - s + 1)]
            else:
                sent = [
                    (
                        jnp.where(me >= s - 1, right, right + term[s - 1]),
                        jnp.where(me <= shards - s, left, left + term[shards - s + 1]),
                    )
                    for (right, left), term in zip(got, terms)
                ]
                to_right, to_left = rights(shards - 1), lefts(shards - 1)
            from_left.append([right for right, _ in sent])
            from_right.append([left for _, left in sent])
            got = [
                lax.optimization_barrier((lax.ppermute(right, "tp", to_right), lax.ppermute(left, "tp", to_left)))
                for right, left in sent
            ]
        from_left.append([right for right, _ in got])
        from_right.append([left for _, left in got])
        total = None
        if terms is not None:
            right = jnp.concatenate([right + term[shards - 1] for (right, _), term in zip(got, terms)], axis=1)
            left = jnp.concatenate([left + term[1] for (_, left), term in zip(got, terms)], axis=1)
            right = lax.ppermute(right, "tp", rights(shards - 1)).astype(jnp.float32)
            left = lax.ppermute(left, "tp", lefts(shards - 1)).astype(jnp.float32)
            total = jnp.concatenate([term[0] for term in terms], axis=1).astype(jnp.float32) + right + left
        return [[source]] + from_left + from_right, total

    picked = ((routes[:, 0] == 0) | (routes[:, 1] == 0)).reshape(shards, rows)
    if line:
        sent_pairs = pack_pairs(me[None], keys, values, shards)
        own_pairs = jnp.concatenate(shift(sent_pairs), axis=0)
        picked, _ = lax.optimization_barrier((picked.astype(jnp.int32), sent_pairs))
        packed, places, order, crowded = pack_queries(me[None], picked, queries, slots, halves)
        asked = [shift(packed[0])]
    else:

        def spread(source):
            widened = jnp.repeat(source.reshape(rows, KV_HEADS, HD), repeat_by, axis=1)
            return widened.reshape(rows, shards, pairs * HD)

        own_pairs = exchange(jnp.concatenate([spread(keys), spread(values)], axis=2))
        own_pairs = jnp.concatenate(own_pairs, axis=0)
        row_ids = jnp.arange(rows, dtype=jnp.int32)
        seen = jnp.cumsum(picked.astype(jnp.int32), axis=1)
        slot = jnp.where(picked, seen - 1, seen[:, -1:] + row_ids[None, :] - seen)
        at_slot = slot[:, None, :] == row_ids[None, :, None]
        row_of_slot = jnp.sum(jnp.where(at_slot, row_ids[None, None, :], 0), axis=2)
        places = row_of_slot + jnp.arange(shards, dtype=jnp.int32)[:, None] * rows
        places = [jnp.stack([jnp.take(places, shard_of[s], axis=0) for s in slots])[:, None, :]]
        order = lax.dynamic_index_in_dim(at_slot, me, 0, keepdims=False).astype(jnp.bfloat16)
        ordered = jnp.dot(order, queries, preferred_element_type=jnp.float32).astype(jnp.bfloat16)
        asked = [exchange(ordered.reshape(rows, shards, per_device * HD))]

    pair_list, held = [own_pairs], [[0]]
    offset = blocks // 2
    while offset >= 1:
        pair_list += [lax.ppermute(part, "ctx", [(i, i ^ offset) for i in range(blocks)]) for part in pair_list]
        held += [[other ^ offset for other in group] for group in held]
        if line and len(pair_list) == 2:
            pair_list[1], asked[0] = lax.optimization_barrier((pair_list[1], asked[0]))
        offset //= 2

    def reorder(source):
        return jnp.dot(order, source, preferred_element_type=jnp.float32).astype(jnp.bfloat16)

    def restore(parts):
        whole = jnp.concatenate(parts, axis=0) if len(parts) > 1 else parts[0]
        return lax.dot_general(
            order, whole, (((0,), (0,)), ((), ())), preferred_element_type=jnp.float32
        ).astype(jnp.bfloat16)

    mine = lax.axis_index("ctx").astype(jnp.int32)[None]
    expert_ids = jnp.arange(router_weight.shape[1], dtype=jnp.int32)

    def project(which):
        terms = attend(
            block_order,
            jnp.stack([lax.axis_index("ctx"), me]).astype(jnp.int32),
            [asked[which][s] for s in slots],
            places[which],
            pair_list,
            held,
            pairs,
            sharing,
            block_rows,
            out_weight,
            pieces,
            line,
        )
        return [[term[slots.index(s)] for s in range(shards)] for term in terms]

    def finish(which, head_sums):
        base = hidden[which * half : (which + 1) * half].astype(jnp.float32)
        return jnp.concatenate(
            [(base[:, cut] + head_sum).astype(jnp.bfloat16) for cut, head_sum in zip(cuts, head_sums)], axis=1
        )

    def normalise(attended):
        widened = attended.astype(jnp.float32)
        return (
            widened * lax.rsqrt(jnp.mean(widened * widened, axis=1, keepdims=True) + 1e-05) * norm_gain
        ).astype(jnp.bfloat16)

    def share_of(which, normed):
        logits = jnp.dot(normed, router_weight, preferred_element_type=jnp.float32)
        named = my_routes[which * half : (which + 1) * half]
        first = jnp.sum(jnp.where(named[:, 0:1] == expert_ids[None, :], logits, 0.0), axis=1)
        second = jnp.sum(jnp.where(named[:, 1:2] == expert_ids[None, :], logits, 0.0), axis=1)
        share = jnp.where(named[:, 0] == 0, 1.0 / (1.0 + jnp.exp(second - first)), 0.0)
        return share + jnp.where(named[:, 1] == 0, 1.0 / (1.0 + jnp.exp(first - second)), 0.0)

    def expert(which, normed, sources, beside=None):
        terms = expert_rows(me[None], sources, gate_weight, up_weight, down_weight, shards, pieces, False)
        if beside is not None:
            terms, beside = lax.optimization_barrier((terms, beside))
        sums, marks = reduce_line(terms)
        if line:
            normed, _ = lax.optimization_barrier((normed, marks[0]))
        share = share_of(which, normed)
        parts = [(total * share[:, None]).astype(jnp.bfloat16) for total in sums]
        return jnp.concatenate(parts, axis=1), beside

    def late_expert(source):
        normed = normalise(source)
        return expert(1, normed, gather_line(normed)[0])[0]

    terms = project(0)
    if halves > 1:
        asked.append(shift(packed[1]))
        terms, asked[1] = lax.optimization_barrier((terms, asked[1]))
    if line:
        hidden_in, order, terms = lax.optimization_barrier((hidden_in, order, terms))
    hidden = reorder(hidden_in)
    totals, marks = reduce_line(terms, True, hidden if line else None)
    if line:
        hidden = marks[-1]
    my_routes = lax.dynamic_slice_in_dim(routes, me * rows, rows, 0).astype(jnp.bfloat16)
    my_routes = reorder(my_routes).astype(jnp.int32)
    first_half = finish(0, totals)
    normed = normalise(first_half)
    if halves == 1:
        return (restore([first_half]), restore([expert(0, normed, gather_line(normed)[0])[0]]))
    asked[1], _ = lax.optimization_barrier((asked[1], normed))
    sources, second_sum = gather_line(normed, project(1))
    part, second_sum = expert(0, normed, sources, second_sum)
    second_half = (hidden[half:].astype(jnp.float32) + second_sum).astype(jnp.bfloat16)
    part, late = lax.optimization_barrier((part, second_half))
    late = lax.cond(crowded[0] > 0, late_expert, jnp.zeros_like, late)
    return (restore([first_half, second_half]), restore([part, late]))


def solution(mesh):
    return jax.shard_map(
        on_device,
        mesh=mesh,
        in_specs=(
            P(("req", "ctx", "tp"), None),
            P(("req", "ctx", "tp"), None),
            P(("req", "ctx", "tp"), None),
            P(("req", "ctx", "tp"), None),
            P("req"),
            P(("req", "ctx"), None),
            P("tp", None),
            P(),
            P(),
            P(None, "tp"),
            P(None, "tp"),
            P("tp", None),
        ),
        out_specs=(P(("req", "ctx", "tp"), None), P(("req", "ctx", "tp"), None)),
        check_vma=False,
    )
```

```python
import functools
import math

import jax
import jax.numpy as jnp
from jax import lax
from jax.experimental import pallas as pl
from jax.experimental.pallas import tpu as pltpu
from jax.sharding import PartitionSpec as P

HEADS = 32
KV_HEADS = 8
HD = 128
FACTOR = math.log2(math.e) / math.sqrt(HD)
LINE = 4
SUM_ROWS = 16
TILE = 256
VMEM_HELD = 21 * 1024 * 1024
VMEM_LARGE = 28 * 1024 * 1024


def attention_kernel(slots, together, held, pairs, sharing, block_rows, plan, *refs):
    pieces, grouped = plan
    (order, mine), refs = refs[:2], refs[2:]
    sent_queries, refs = refs[:slots], refs[slots:]
    place_ref, refs = refs[0], refs[1:]
    sent_pairs, weight, refs = refs[: len(held)], refs[len(held)], refs[len(held) + 1 :]
    outs, refs = refs[: pieces * (slots if grouped else 1)], refs[pieces * (slots if grouped else 1) :]
    query_refs, pair_refs, refs = refs[:slots], refs[slots : slots + len(held)], refs[slots + len(held) :]
    query_ref, key_ref, value_ref, top_ref, total_ref, head_ref, weight_ref, arrived, here = refs
    half = query_refs[0].shape[0]
    step = pl.program_id(0)
    me = mine[0]
    my_block = order[me]
    blocks = [(ref, index, offset) for ref, group in zip(pair_refs, held) for index, offset in enumerate(group)]
    weight_copy = pltpu.make_async_copy(weight, weight_ref, arrived)
    moves = [
        pltpu.make_async_copy(source, target, here.at[i])
        for i, (source, target) in enumerate(
            list(zip(sent_pairs, pair_refs)) + list(zip(sent_queries, query_refs))
        )
    ]

    @pl.when(step == 0)
    def _():
        for move in moves:
            move.start()
        value_ref[:, :, HD:, :] = jnp.ones((len(blocks), pairs, SUM_ROWS, block_rows), jnp.bfloat16)

    @pl.when(step == 0)
    def _():
        for move in moves:
            move.wait()
        weight_copy.start()

    for at, (ref, index, offset) in enumerate(blocks):

        @pl.when((step == 0) & (order[me ^ offset] <= my_block))
        def _():
            for p in range(pairs):
                rows = slice(index * block_rows, (index + 1) * block_rows)
                key_ref[at, p] = ref[rows, p * HD : (p + 1) * HD]
                value_ref[at, p, :HD, :] = ref[rows, (pairs + p) * HD : (pairs + p + 1) * HD].T

    for at in range(slots):

        @pl.when(step == at // together)
        def _():
            for p in range(pairs):
                for g in range(sharing):
                    column = (p * sharing + g) * HD
                    row = (at % together * sharing + g) * half
                    query_ref[p, row : row + half, :] = query_refs[at][:, column : column + HD]

    def scores_of(p, at):
        return lax.dot_general(
            key_ref[at, p], query_ref[p], (((1,), (1,)), ((), ())), preferred_element_type=jnp.float32
        )

    def mixed_of(p, at, weights):
        return jnp.dot(value_ref[at, p], weights, preferred_element_type=jnp.float32)

    place = jnp.concatenate([place_ref[i] for i in range(together) for _ in range(sharing)], axis=1)
    rows = block_rows // slots
    down = lax.broadcasted_iota(jnp.int32, (rows, place.shape[1]), 0)
    visible = jnp.concatenate(
        [down <= place - lax.rem(mine[1] - s + slots, slots) * rows for s in range(slots)], axis=0
    )
    for p in range(pairs):
        scores = jnp.where(visible, scores_of(p, 0), -1e30)
        top = jnp.max(scores, axis=0, keepdims=True)
        weights = jnp.exp2((scores - top) * FACTOR).astype(jnp.bfloat16)
        top_ref[p, 0:1, :] = top
        total_ref[p] = mixed_of(p, 0, weights)

    @pl.loop(1, len(blocks))
    def _(at):
        offset = blocks[1][2] if len(blocks) > 1 else 0
        for other in range(2, len(blocks)):
            offset = jnp.where(at == other, blocks[other][2], offset)

        @pl.when(order[me ^ offset] < my_block)
        def _():
            for p in range(pairs):
                top = top_ref[p, 0:1, :]
                scores = scores_of(p, at)
                raised = jnp.maximum(top, jnp.max(scores, axis=0, keepdims=True))
                weights = jnp.exp2((scores - raised) * FACTOR).astype(jnp.bfloat16)
                top_ref[p, 0:1, :] = raised
                total_ref[p] = total_ref[p] * jnp.exp2((top - raised) * FACTOR) + mixed_of(p, at, weights)

    for p in range(pairs):
        mixed = (total_ref[p, :HD, :] / total_ref[p, HD : HD + 1, :]).T.astype(jnp.bfloat16)
        for i in range(together):
            for g in range(sharing):
                column = (p * sharing + g) * HD
                row = (i * sharing + g) * half
                at = pl.multiple_of((step * together + i) * half, half)
                head_ref[pl.ds(at, half), column : column + HD] = mixed[row : row + half]

    @pl.when(step == pl.num_programs(0) - 1)
    def _():
        weight_copy.wait()
        width = weight.shape[1] // pieces
        tile = 2 * TILE
        for c in range(pieces):

            @pl.loop(0, width // tile)
            def _(n):
                columns = pl.ds(pl.multiple_of(c * width + n * tile, tile), tile)
                value = jnp.dot(head_ref[...], weight_ref[:, columns], preferred_element_type=jnp.float32)
                share_out(outs[c * len(outs) // pieces :], pl.ds(pl.multiple_of(n * tile, tile), tile), value)


def share_out(outs, columns, value):
    rows = outs[0].shape[0]
    for g in range(value.shape[0] // rows):
        outs[g][:, columns] = value[g * rows : (g + 1) * rows].astype(jnp.bfloat16)


def piece_shapes(rows, width, slots, pieces, grouped):
    return [jax.ShapeDtypeStruct((rows // slots if grouped else rows, width // pieces), jnp.bfloat16)] * (
        pieces * (slots if grouped else 1)
    )


def by_piece(outs, slots, pieces, grouped):
    if grouped:
        return [outs[c * slots : (c + 1) * slots] for c in range(pieces)]
    return [[out[s * (out.shape[0] // slots) : (s + 1) * (out.shape[0] // slots)] for s in range(slots)] for out in outs]


def in_hbm(arrays):
    return [pltpu.with_memory_space_constraint(array, pltpu.HBM) for array in arrays]


def attend(order, mine, queries, places, pair_list, held, pairs, sharing, block_rows, weight, pieces, grouped):
    slots = len(queries)
    half, width = queries[0].shape
    together = 2 if slots <= LINE else 1
    tall = together * sharing * half
    blocks = sum(len(group) for group in held)
    count = blocks * block_rows
    shapes = piece_shapes(slots * half, weight.shape[1], slots, pieces, grouped)
    kernel = functools.partial(
        attention_kernel, slots, together, held, pairs, sharing, block_rows, (pieces, grouped)
    )
    outs = pl.pallas_call(
        kernel,
        grid_spec=pltpu.PrefetchScalarGridSpec(
            num_scalar_prefetch=2,
            grid=(slots // together,),
            in_specs=[pl.BlockSpec(memory_space=pltpu.HBM)] * slots
            + [pl.BlockSpec((together, 1, half), lambda s, *_: (s, 0, 0))]
            + [pl.BlockSpec(memory_space=pltpu.HBM)] * (len(pair_list) + 1),
            out_specs=[pl.BlockSpec(shape.shape, lambda s, *_: (0, 0)) for shape in shapes],
            scratch_shapes=[pltpu.VMEM((half, width), jnp.bfloat16)] * slots
            + [pltpu.VMEM(pair.shape, pair.dtype) for pair in pair_list]
            + [
                pltpu.VMEM((pairs, tall, HD), jnp.bfloat16),
                pltpu.VMEM((blocks, pairs, block_rows, HD), jnp.bfloat16),
                pltpu.VMEM((blocks, pairs, HD + SUM_ROWS, block_rows), jnp.bfloat16),
                pltpu.VMEM((pairs, 8, tall), jnp.float32),
                pltpu.VMEM((pairs, HD + SUM_ROWS, tall), jnp.float32),
                pltpu.VMEM((slots * half, width), jnp.bfloat16),
                pltpu.VMEM(weight.shape, weight.dtype),
                pltpu.SemaphoreType.DMA,
                pltpu.SemaphoreType.DMA((slots + len(pair_list),)),
            ],
        ),
        out_shape=shapes,
        compiler_params=pltpu.CompilerParams(vmem_limit_bytes=VMEM_HELD),
        cost_estimate=pl.CostEstimate(
            flops=40 * slots * half * width * count,
            bytes_accessed=2 * (2 * slots * half * width + count * 2 * pairs * HD + weight.size),
            transcendentals=slots * half * width // HD * count,
        ),
    )(order, mine, *in_hbm(queries), places, *in_hbm(pair_list), *in_hbm([weight]))
    return by_piece(outs, slots, pieces, grouped)


def expert_kernel(plan, pieces, *refs):
    mine, refs = refs[0], refs[1:]
    sources = []
    for count in plan:
        sources.append(refs[:count])
        refs = refs[count:]
    gate_weight, up_weight, down_weights, refs = refs[0], refs[1], refs[2:4], refs[4:]
    outs, (chosen, acts) = refs[:-2], refs[-2:]
    step = pl.program_id(0)
    tile = gate_weight.shape[1]
    first = acts.shape[1] // tile

    def place(s, source):
        rows, width = source[0].shape
        for c, ref in enumerate(source):
            chosen[s * rows : (s + 1) * rows, c * width : (c + 1) * width] = ref[...]

    @pl.when(step == 0)
    def _():
        place(0, sources[0])
        for s in range(1, (len(plan) + 1) // 2):
            right, left = sources[s], sources[len(plan) - s]

            @pl.when(mine[0] >= s)
            def _():
                place(s, right)

            @pl.when(mine[0] < s)
            def _():
                place(s, left)

    @pl.when(step < first)
    def _():
        gate = jnp.dot(chosen[...], gate_weight[...], preferred_element_type=jnp.float32)
        upward = jnp.dot(chosen[...], up_weight[...], preferred_element_type=jnp.float32)
        columns = pl.ds(pl.multiple_of(step * tile, tile), tile)
        acts[:, columns] = (gate / (1.0 + jnp.exp(-gate)) * upward).astype(jnp.bfloat16)

    @pl.when(step >= first)
    def _():
        strip = down_weights[0].shape[1]
        pairs = outs[0].shape[1] // (2 * strip)
        for j, down_weight in enumerate(down_weights):
            value = jnp.dot(acts[...], down_weight[...], preferred_element_type=jnp.float32)
            for c in range(pieces):

                @pl.when((step - first) // pairs == c)
                def _():
                    at = (2 * (step - first - c * pairs) + j) * strip
                    share_out(outs[c * len(outs) // pieces :], pl.ds(pl.multiple_of(at, strip), strip), value)


def expert_rows(mine, sources, gate_weight, up_weight, down_weight, slots, pieces, grouped):
    flat = [piece for source in sources for piece in source]
    rows = flat[0].shape[0] * ((len(sources) + 1) // 2)
    depth, width = gate_weight.shape
    tile, strip = min(TILE, width), 2 * TILE
    first = width // tile
    shapes = piece_shapes(rows, depth, slots, pieces, grouped)
    in_place = pl.BlockSpec(memory_space=pltpu.VMEM)
    weight = pl.BlockSpec((depth, tile), lambda n, *_: (0, jnp.minimum(n, first - 1)))
    outs = pl.pallas_call(
        functools.partial(expert_kernel, [len(source) for source in sources], pieces),
        grid_spec=pltpu.PrefetchScalarGridSpec(
            num_scalar_prefetch=1,
            grid=(first + depth // (2 * strip),),
            in_specs=[in_place] * len(flat)
            + [weight, weight]
            + [
                pl.BlockSpec((width, strip), functools.partial(lambda j, n, *_: (0, 2 * jnp.maximum(n - first, 0) + j), j))
                for j in range(2)
            ],
            out_specs=[in_place] * len(shapes),
            scratch_shapes=[pltpu.VMEM((rows, depth), jnp.bfloat16), pltpu.VMEM((rows, width), jnp.bfloat16)],
        ),
        out_shape=shapes,
        compiler_params=pltpu.CompilerParams(vmem_limit_bytes=VMEM_LARGE),
        cost_estimate=pl.CostEstimate(
            flops=6 * rows * depth * width, bytes_accessed=6 * depth * width, transcendentals=rows * width
        ),
    )(mine, *flat, gate_weight, up_weight, down_weight, down_weight)
    return by_piece(outs, slots, pieces, grouped)


def pack_pairs_kernel(shards, mine, keys_ref, values_ref, *outs):
    width = keys_ref.shape[1] // shards
    for s in range(shards):
        columns = pl.ds(pl.multiple_of(lax.rem(mine[0] + s, shards) * width, width), width)
        outs[s][:, :width] = keys_ref[:, columns]
        outs[s][:, width:] = values_ref[:, columns]


def pack_pairs(mine, keys, values, shards):
    rows, width = keys.shape
    spec = pl.BlockSpec((rows, width), lambda k, *_: (0, 0))
    out = (rows, 2 * width // shards)
    return pl.pallas_call(
        functools.partial(pack_pairs_kernel, shards),
        grid_spec=pltpu.PrefetchScalarGridSpec(
            num_scalar_prefetch=1,
            grid=(1,),
            in_specs=[spec, spec],
            out_specs=[pl.BlockSpec(out, lambda k, *_: (0, 0))] * shards,
        ),
        out_shape=[jax.ShapeDtypeStruct(out, keys.dtype)] * shards,
    )(mine, keys, values)


def pack_queries_kernel(slots, halves, mine, picked_ref, query_ref, *outs):
    shards = len(slots)
    rows = query_ref.shape[0]
    half = rows // halves
    width = query_ref.shape[1] // shards
    packed, outs = outs[: halves * shards], outs[halves * shards :]
    place_refs, (order_ref, count_ref) = outs[:halves], outs[halves:]
    me = mine[0]
    across = lax.broadcasted_iota(jnp.int32, (rows, rows), 1)
    down = lax.broadcasted_iota(jnp.int32, (rows, rows), 0)
    up_to = jnp.where(down <= across, 1.0, 0.0).astype(jnp.bfloat16)
    picked = picked_ref[...]
    seen = jnp.dot(picked.astype(jnp.bfloat16), up_to, preferred_element_type=jnp.float32).astype(jnp.int32)
    count = seen[:, rows - 1 : rows]
    row_ids = lax.broadcasted_iota(jnp.int32, seen.shape, 1)
    slot = jnp.where(picked > 0, seen - 1, count + row_ids - seen)
    count_ref[0] = jnp.max(jnp.where(count > half, 1, 0))
    ids = row_ids.astype(jnp.bfloat16)
    for s in range(shards):
        shard = lax.rem(me - s + shards, shards)
        mine_slot = slot[0:1]
        for other in range(1, shards):
            mine_slot = jnp.where(shard == other, slot[other : other + 1], mine_slot)
        at_slot = jnp.where(mine_slot == down, 1.0, 0.0).astype(jnp.bfloat16)
        rows_at = lax.dot_general(ids, at_slot, (((1,), (1,)), ((), ())), preferred_element_type=jnp.float32)
        for h in range(halves):
            here = rows_at[0:1, h * half : (h + 1) * half]
            place_refs[h][slots.index(s)] = here.astype(jnp.int32) + shard * rows
        if s == 0:
            order_ref[...] = at_slot
    for s in range(shards):
        columns = pl.ds(pl.multiple_of(lax.rem(me + s, shards) * width, width), width)
        ordered = jnp.dot(order_ref[...], query_ref[:, columns], preferred_element_type=jnp.float32)
        ordered = ordered.astype(jnp.bfloat16)
        for h in range(halves):
            packed[h * shards + s][...] = ordered[h * half : (h + 1) * half]


def pack_queries(mine, picked, queries, slots, halves):
    shards = len(slots)
    rows, width = queries.shape
    packed = (rows // halves, width // shards)
    shapes = [jax.ShapeDtypeStruct(packed, jnp.bfloat16)] * (halves * shards)
    shapes += [jax.ShapeDtypeStruct((shards, 1, rows // halves), jnp.int32)] * halves
    shapes += [jax.ShapeDtypeStruct((rows, rows), jnp.bfloat16), jax.ShapeDtypeStruct((1,), jnp.int32)]

    def whole(shape):
        return pl.BlockSpec(shape, lambda k, *_: (0,) * len(shape))

    got = pl.pallas_call(
        functools.partial(pack_queries_kernel, slots, halves),
        grid_spec=pltpu.PrefetchScalarGridSpec(
            num_scalar_prefetch=1,
            grid=(1,),
            in_specs=[whole(picked.shape), whole(queries.shape)],
            out_specs=[whole(shape.shape) for shape in shapes[:-1]] + [pl.BlockSpec(memory_space=pltpu.SMEM)],
        ),
        out_shape=shapes,
    )(mine, picked, queries)
    packed, got = got[: halves * shards], got[halves * shards :]
    return [packed[h * shards : (h + 1) * shards] for h in range(halves)], got[:halves], *got[halves:]


def on_device(
    hidden_in,
    queries,
    keys,
    values,
    block_order,
    routes,
    out_weight,
    norm_gain,
    router_weight,
    gate_weight,
    up_weight,
    down_weight,
):
    shards = lax.axis_size("tp")
    blocks = lax.axis_size("ctx")
    me = lax.axis_index("tp")
    rows, model = hidden_in.shape
    block_rows = rows * shards
    per_device = HEADS // shards
    grouping = HEADS // KV_HEADS
    repeat_by = max(1, grouping // per_device)
    pairs = max(1, per_device // grouping)
    sharing = per_device // pairs
    half = rows // 2 if rows % 32 == 0 else rows
    halves = rows // half
    line = shards <= LINE
    pieces = 2 if line else 1
    cuts = [slice(c * (model // pieces), (c + 1) * (model // pieces)) for c in range(pieces)]
    slots = [s for s in range(1, shards, 2)] + [s for s in range(2, shards, 2)] + [0]
    shard_of = lax.rem(me - jnp.arange(shards, dtype=jnp.int32) + shards, shards)

    def shift(parts):
        moves = [[(i, (i + s) % shards) for i in range(shards)] for s in range(shards)]
        return [parts[0]] + [lax.ppermute(parts[s], "tp", moves[s]) for s in range(1, shards)]

    def exchange(source):
        got = lax.all_to_all(source, "tp", split_axis=1, concat_axis=0, tiled=True)
        got = got.reshape(shards, rows, source.shape[2])
        return [lax.dynamic_index_in_dim(got, shard_of[s], 0, keepdims=False) for s in range(shards)]

    def rights(count):
        return [(i, i + 1) for i in range(count)]

    def lefts(count):
        return [(i, i - 1) for i in range(shards - count, shards)]

    def reduce_line(pieces_terms, merged=False, beside=None):
        if not line:
            by_shard = [jnp.take(jnp.stack(terms), shard_of, axis=0).reshape(-1, terms[0].shape[1]) for terms in pieces_terms]
            return [
                lax.psum_scatter(term, "tp", scatter_dimension=0, tiled=True).astype(jnp.float32) for term in by_shard
            ], None
        got = [None] * len(pieces_terms)
        marks = []
        for s in range(1, shards):
            for c, terms in enumerate(pieces_terms):
                if s == 1 and merged:
                    sent = jnp.where(me == 0, terms[1], terms[shards - 1])
                    arrived = lax.ppermute(sent, "tp", [(0, 1), (shards - 1, shards - 2)])
                    got[c] = (arrived, arrived)
                    continue
                if s == 1:
                    to_right, to_left = terms[s], terms[shards - s]
                elif s == 2 and merged:
                    to_right = to_left = terms[s] + got[c][0]
                else:
                    to_right, to_left = terms[s] + got[c][0], terms[shards - s] + got[c][1]
                right = lax.ppermute(to_right, "tp", rights(s))
                left = lax.ppermute(to_left, "tp", lefts(s))
                got[c] = lax.optimization_barrier((right, left))
            marks.append(got[0])
            if s == 1 and beside is not None:
                got[0], beside = lax.optimization_barrier((got[0], beside))
        marks.append(beside)
        return [
            terms[0].astype(jnp.float32) + right.astype(jnp.float32) + left.astype(jnp.float32)
            for terms, (right, left) in zip(pieces_terms, got)
        ], marks

    def gather_line(source, terms=None):
        if not line:
            got = lax.all_gather(source, "tp", axis=0)
            return [[jnp.take(got, shard_of, axis=0).reshape(shards * half, -1)]], None
        first_right = lax.ppermute(source, "tp", rights(shards - 1))
        first_left = lax.ppermute(source, "tp", lefts(shards - 1))
        first_right, first_left = lax.optimization_barrier((first_right, first_left))
        got = [(first_right[:, cut], first_left[:, cut]) for cut in cuts]
        from_left, from_right = [], []
        for s in range(2, shards):
            if terms is None:
                sent = got
                to_right = [(i, i + 1) for i in range(s - 1, shards - 1)]
                to_left = [(i, i - 1) for i in range(1, shards - s + 1)]
            else:
                sent = [
                    (
                        jnp.where(me >= s - 1, right, right + term[s - 1]),
                        jnp.where(me <= shards - s, left, left + term[shards - s + 1]),
                    )
                    for (right, left), term in zip(got, terms)
                ]
                to_right, to_left = rights(shards - 1), lefts(shards - 1)
            from_left.append([right for right, _ in sent])
            from_right.append([left for _, left in sent])
            got = [
                lax.optimization_barrier((lax.ppermute(right, "tp", to_right), lax.ppermute(left, "tp", to_left)))
                for right, left in sent
            ]
        from_left.append([right for right, _ in got])
        from_right.append([left for _, left in got])
        total = None
        if terms is not None:
            right = jnp.concatenate([right + term[shards - 1] for (right, _), term in zip(got, terms)], axis=1)
            left = jnp.concatenate([left + term[1] for (_, left), term in zip(got, terms)], axis=1)
            right = lax.ppermute(right, "tp", rights(shards - 1)).astype(jnp.float32)
            left = lax.ppermute(left, "tp", lefts(shards - 1)).astype(jnp.float32)
            total = jnp.concatenate([term[0] for term in terms], axis=1).astype(jnp.float32) + right + left
        return [[source]] + from_left + from_right, total

    picked = ((routes[:, 0] == 0) | (routes[:, 1] == 0)).reshape(shards, rows)
    if line:
        sent_pairs = pack_pairs(me[None], keys, values, shards)
        own_pairs = jnp.concatenate(shift(sent_pairs), axis=0)
        picked, _ = lax.optimization_barrier((picked.astype(jnp.int32), sent_pairs))
        packed, places, order, crowded = pack_queries(me[None], picked, queries, slots, halves)
        asked = [shift(packed[0])]
    else:

        def spread(source):
            widened = jnp.repeat(source.reshape(rows, KV_HEADS, HD), repeat_by, axis=1)
            return widened.reshape(rows, shards, pairs * HD)

        own_pairs = exchange(jnp.concatenate([spread(keys), spread(values)], axis=2))
        own_pairs = jnp.concatenate(own_pairs, axis=0)
        row_ids = jnp.arange(rows, dtype=jnp.int32)
        seen = jnp.cumsum(picked.astype(jnp.int32), axis=1)
        slot = jnp.where(picked, seen - 1, seen[:, -1:] + row_ids[None, :] - seen)
        at_slot = slot[:, None, :] == row_ids[None, :, None]
        row_of_slot = jnp.sum(jnp.where(at_slot, row_ids[None, None, :], 0), axis=2)
        places = row_of_slot + jnp.arange(shards, dtype=jnp.int32)[:, None] * rows
        places = [jnp.stack([jnp.take(places, shard_of[s], axis=0) for s in slots])[:, None, :]]
        order = lax.dynamic_index_in_dim(at_slot, me, 0, keepdims=False).astype(jnp.bfloat16)
        ordered = jnp.dot(order, queries, preferred_element_type=jnp.float32).astype(jnp.bfloat16)
        asked = [exchange(ordered.reshape(rows, shards, per_device * HD))]

    pair_list, held = [own_pairs], [[0]]
    offset = blocks // 2
    while offset >= 1:
        pair_list += [lax.ppermute(part, "ctx", [(i, i ^ offset) for i in range(blocks)]) for part in pair_list]
        held += [[other ^ offset for other in group] for group in held]
        if line and len(pair_list) == 2:
            pair_list[1], asked[0] = lax.optimization_barrier((pair_list[1], asked[0]))
        offset //= 2

    def reorder(source):
        return jnp.dot(order, source, preferred_element_type=jnp.float32).astype(jnp.bfloat16)

    def restore(parts):
        whole = jnp.concatenate(parts, axis=0) if len(parts) > 1 else parts[0]
        return lax.dot_general(
            order, whole, (((0,), (0,)), ((), ())), preferred_element_type=jnp.float32
        ).astype(jnp.bfloat16)

    mine = lax.axis_index("ctx").astype(jnp.int32)[None]
    expert_ids = jnp.arange(router_weight.shape[1], dtype=jnp.int32)

    def project(which):
        terms = attend(
            block_order,
            jnp.stack([lax.axis_index("ctx"), me]).astype(jnp.int32),
            [asked[which][s] for s in slots],
            places[which],
            pair_list,
            held,
            pairs,
            sharing,
            block_rows,
            out_weight,
            pieces,
            line,
        )
        return [[term[slots.index(s)] for s in range(shards)] for term in terms]

    def finish(which, head_sums):
        base = hidden[which * half : (which + 1) * half].astype(jnp.float32)
        return jnp.concatenate(
            [(base[:, cut] + head_sum).astype(jnp.bfloat16) for cut, head_sum in zip(cuts, head_sums)], axis=1
        )

    def normalise(attended):
        widened = attended.astype(jnp.float32)
        return (
            widened * lax.rsqrt(jnp.mean(widened * widened, axis=1, keepdims=True) + 1e-05) * norm_gain
        ).astype(jnp.bfloat16)

    def share_of(which, normed):
        logits = jnp.dot(normed, router_weight, preferred_element_type=jnp.float32)
        named = my_routes[which * half : (which + 1) * half]
        first = jnp.sum(jnp.where(named[:, 0:1] == expert_ids[None, :], logits, 0.0), axis=1)
        second = jnp.sum(jnp.where(named[:, 1:2] == expert_ids[None, :], logits, 0.0), axis=1)
        share = jnp.where(named[:, 0] == 0, 1.0 / (1.0 + jnp.exp(second - first)), 0.0)
        return share + jnp.where(named[:, 1] == 0, 1.0 / (1.0 + jnp.exp(first - second)), 0.0)

    def expert(which, normed, sources, beside=None):
        terms = expert_rows(me[None], sources, gate_weight, up_weight, down_weight, shards, pieces, False)
        if beside is not None:
            terms, beside = lax.optimization_barrier((terms, beside))
        sums, marks = reduce_line(terms)
        if line:
            normed, _ = lax.optimization_barrier((normed, marks[0]))
        share = share_of(which, normed)
        parts = [(total * share[:, None]).astype(jnp.bfloat16) for total in sums]
        return jnp.concatenate(parts, axis=1), beside

    def late_expert(source):
        normed = normalise(source)
        return expert(1, normed, gather_line(normed)[0])[0]

    terms = project(0)
    if halves > 1:
        asked.append(shift(packed[1]))
        terms, asked[1] = lax.optimization_barrier((terms, asked[1]))
    if line:
        hidden_in, order, terms = lax.optimization_barrier((hidden_in, order, terms))
    hidden = reorder(hidden_in)
    totals, marks = reduce_line(terms, True, hidden if line else None)
    if line:
        hidden = marks[-1]
    my_routes = lax.dynamic_slice_in_dim(routes, me * rows, rows, 0).astype(jnp.bfloat16)
    my_routes = reorder(my_routes).astype(jnp.int32)
    first_half = finish(0, totals)
    normed = normalise(first_half)
    if halves == 1:
        return (restore([first_half]), restore([expert(0, normed, gather_line(normed)[0])[0]]))
    asked[1], _ = lax.optimization_barrier((asked[1], normed))
    sources, second_sum = gather_line(normed, project(1))
    second_half = (hidden[half:].astype(jnp.float32) + second_sum).astype(jnp.bfloat16)
    part, second_half = expert(0, normed, sources, second_half)
    part, late = lax.optimization_barrier((part, second_half))
    late = lax.cond(crowded[0] > 0, late_expert, jnp.zeros_like, late)
    return (restore([first_half, second_half]), restore([part, late]))


def solution(mesh):
    return jax.shard_map(
        on_device,
        mesh=mesh,
        in_specs=(
            P(("req", "ctx", "tp"), None),
            P(("req", "ctx", "tp"), None),
            P(("req", "ctx", "tp"), None),
            P(("req", "ctx", "tp"), None),
            P("req"),
            P(("req", "ctx"), None),
            P("tp", None),
            P(),
            P(),
            P(None, "tp"),
            P(None, "tp"),
            P("tp", None),
        ),
        out_specs=(P(("req", "ctx", "tp"), None), P(("req", "ctx", "tp"), None)),
        check_vma=False,
    )
```
